32 devices in a mesh: slab: 8 (over z, y), dom: 4 (over x, core).
Axes of the slice: x: 2, y: 2, z: 4, core: 2. Of those that a mesh axis runs over, the one named last changes fastest.
Arguments:
- base_cells: int32 [3, 8192], P(None, ('slab', 'dom')), may hold values from 0 to 511, as said below
- offsets: float32 [3, 8192], P(None, ('slab', 'dom')), may hold values from 0 to 1
- charges: float32 [8192], P(('slab', 'dom')), may hold values from -4 to 4
- bias_coupling: float32 [8192], P(('slab', 'dom')), may hold values from -4 to 4
- counts: int32 [32], P(('slab', 'dom')), may hold values from 128 to 256, as said below
- green: float32 [32, 512, 256], P(None, 'slab', 'dom'), as said below
Outputs:
- potential: float32 [32, 512, 512], P('slab', 'dom')
- gradient: float32 [8192], P(('slab', 'dom'))
The draws below stay inside these ranges and needn't reach their ends.
Inputs may be any that keep to these rules, and one draw needn't show every extreme that they name: `base_cells`: an atom in slot a belongs to device a // 256, which is slab index (a // 256) // 4 and dom index (a // 256) % 4 of the mesh; its base cell has first coordinate in that slab's 4 planes, second coordinate in that dom index's 128 rows, third coordinate anywhere in 0..511. `counts`: A multiple of 128 of at least half of 256; equal to 256 on at least one device; a device's atoms fill its first slots. `green`: zero at the zero wavenumber and positive elsewhere.
All inputs are finite; a program needn't handle non-finite values.
Results may differ from the reference program's by a relative error of at most 0.000086.
Values sent between devices are 32-bit elements; how exact they have to be, the bound alone decides.
No kernel may reach another device: no remote copies, remote signals or barrier semaphores. Data moves between devices by JAX's collectives and lax.ppermute only.
A program may use at most 64 MiB of HBM per device.

```python
import jax
import jax.numpy as jnp

XD = 4
NY = 512
NZ = 512
ATOM_DEV = 256
YD = 128
NX = 32
KH = 256
ATOMS = 8192
N_SLAB = 8
N_DOM = 4


def draw_base_cells(key, part):
    slot_index = jnp.arange(ATOMS, dtype=jnp.int32)
    owner = slot_index // ATOM_DEV
    slab_number = owner // N_DOM
    dom_number = owner % N_DOM
    key_x, key_y, key_z = jax.random.split(key, 3)
    cell_x = XD * slab_number + jax.random.randint(key_x, (ATOMS,), 0, XD)
    cell_y = YD * dom_number + jax.random.randint(key_y, (ATOMS,), 0, YD)
    cell_z = jax.random.randint(key_z, (ATOMS,), 0, NZ)
    return jnp.stack([cell_x, cell_y, cell_z]).astype(jnp.int32)


def draw_counts(key, part):
    total_devices = N_SLAB * N_DOM
    key_cut, key_full = jax.random.split(key)
    removed = jax.random.randint(key_cut, (total_devices,), 0, ATOM_DEV // 256 + 1)
    full_device = jax.random.randint(key_full, (), 0, total_devices)
    removed = jnp.where(jnp.arange(total_devices, dtype=jnp.int32) == full_device, 0, removed)
    return (ATOM_DEV - 128 * removed).astype(jnp.int32)


def draw_green(key, part):
    wave_x = jnp.arange(NX, dtype=jnp.int32)[:, None, None]
    wave_y = jnp.arange(NY, dtype=jnp.int32)[None, :, None]
    wave_z = jnp.arange(KH, dtype=jnp.int32)[None, None, :]
    sine_x = jnp.sin(jnp.pi * wave_x.astype(jnp.float32) / NX)
    sine_y = jnp.sin(jnp.pi * wave_y.astype(jnp.float32) / NY)
    sine_z = jnp.sin(jnp.pi * wave_z.astype(jnp.float32) / NZ)
    squared = 4.0 * (sine_x * sine_x + sine_y * sine_y + sine_z * sine_z)
    rough = jnp.exp(jax.random.uniform(key, (NX, NY, KH), jnp.float32, -0.693, 0.693))
    nonzero = wave_x + wave_y + wave_z > 0
    safe = jnp.where(nonzero, squared, 1.0)
    return jnp.where(nonzero, 8.0 * rough / safe, 0.0).astype(jnp.float32)


def steps_of(key, shape, pieces, low, top_value):
    loudness, own = 1.0, jax.random.fold_in(key, 6)
    for axis_at, parts in pieces:
        steps = jnp.exp(jax.random.uniform(jax.random.fold_in(own, axis_at), (parts,), jnp.float32, low / len(pieces), top_value / len(pieces)))
        loudness = loudness * jnp.repeat(steps, shape[axis_at] // parts).reshape([-1 if axis == axis_at else 1 for axis in range(len(shape))])
    return loudness


def centred(stream_key, shape, deviation, bound, cuts=(), kind=jnp.bfloat16):
    drawn = deviation * jax.random.normal(stream_key, shape, jnp.float32)
    if cuts:
        drawn = drawn * steps_of(stream_key, shape, cuts, -0.22, 0.18)
    return jnp.clip(drawn, -bound, bound).astype(kind)


def setup_inputs(seed: int = 0) -> dict:
    streams_of = jax.random.split(jax.random.key(seed), 7)
    base_cells = draw_base_cells(jax.random.fold_in(streams_of[6], 71), 0)
    offsets = jnp.clip(1.0 * jax.random.uniform(streams_of[1], (3, ATOMS), jnp.float32) ** steps_of(streams_of[1], (3, ATOMS), ((1, 32),), -0.2, 0.2), 0.0, 1.0)
    charges = centred(streams_of[2], (ATOMS,), 1.0, 4.0, ((0, 32),), jnp.float32)
    bias_coupling = centred(streams_of[3], (ATOMS,), 1.0, 4.0, ((0, 32),), jnp.float32)
    counts = draw_counts(jax.random.fold_in(streams_of[6], 71), 0)
    green = draw_green(jax.random.fold_in(streams_of[6], 71), 0)
    return {"base_cells": base_cells, "offsets": offsets, "charges": charges, "bias_coupling": bias_coupling, "counts": counts, "green": green}


def spline_rows(frac):
    inner = 1.0 - frac
    square = frac * frac
    cube = square * frac
    return jnp.stack([inner * inner * inner / 6.0, (3.0 * cube - 6.0 * square + 4.0) / 6.0, (-3.0 * cube + 3.0 * square + 3.0 * frac + 1.0) / 6.0, cube / 6.0])


def reference(base_cells, offsets, charges, bias_coupling, counts, green):
    slot_index = jnp.arange(ATOMS, dtype=jnp.int32)
    alive_mask = (slot_index % ATOM_DEV) < counts[slot_index // ATOM_DEV]
    weights = [spline_rows(offsets[axis_index]) for axis_index in range(3)]
    cell_list = []
    product_list = []
    for step_x in range(4):
        for step_y in range(4):
            for step_z in range(4):
                index_x = (base_cells[0] + step_x) % NX
                index_y = (base_cells[1] + step_y) % NY
                index_z = (base_cells[2] + step_z) % NZ
                cell_list.append(((index_x * NY + index_y) * NZ + index_z).astype(jnp.int32))
                product_list.append(weights[0][step_x] * weights[1][step_y] * weights[2][step_z])
    cell_index = jnp.stack(cell_list)
    products = jnp.stack(product_list)
    amounts = products * jnp.where(alive_mask, charges, 0.0)[None, :]
    flat_grid = jnp.zeros((NX * NY * NZ,), jnp.float32).at[cell_index.reshape(-1)].add(amounts.reshape(-1))
    spectrum = jnp.fft.rfftn(flat_grid.reshape(NX, NY, NZ))
    extended = jnp.concatenate([green, jnp.zeros((NX, NY, 1), jnp.float32)], 2)
    potential = jnp.fft.irfftn(spectrum * extended, s=(NX, NY, NZ)).astype(jnp.float32)
    sampled = jnp.sum(potential.reshape(-1)[cell_index] * products, 0)
    gradient = jnp.where(alive_mask, bias_coupling * sampled, 0.0)
    return potential, gradient
```

```python
import jax
import jax.numpy as jnp
import ml_dtypes
import numpy as np
from jax import lax
from jax.experimental import pallas as pl
from jax.experimental.pallas import tpu as pltpu
from jax.sharding import PartitionSpec as P

XD = 4
NY = 512
NZ = 512
KH = NZ // 2
LANES = 128
SPAN = XD + 3
MIB = 1 << 20
BF16 = jnp.bfloat16
F32 = jnp.float32


def polynomial(function, terms):
    nodes = 0.125 * (1.0 - np.cos(np.pi * (np.arange(64) + 0.5) / 64))
    powers = nodes[:, None] ** np.arange(terms)[None, :]
    return [float(v) for v in np.linalg.lstsq(powers, function(np.sqrt(nodes)), rcond=None)[0]]


SINE_TERMS = polynomial(lambda r: np.sin(np.pi * r) / r, 6)
COSINE_TERMS = polynomial(lambda r: np.cos(np.pi * r), 6)


def horner(terms, square):
    total = jnp.full_like(square, terms[-1])
    for term in terms[-2::-1]:
        total = total * square + term
    return total


def turn(fraction):
    left = fraction - jnp.floor(fraction + 0.5)
    square = left * left
    sine = left * horner(SINE_TERMS, square)
    cosine = horner(COSINE_TERMS, square)
    return 1.0 - 2.0 * sine * sine, 2.0 * sine * cosine


def spline(frac):
    inner = 1.0 - frac
    square = frac * frac
    cube = square * frac
    sixth = 1.0 / 6.0
    return (
        inner * inner * inner * sixth,
        (3.0 * cube - 6.0 * square + 4.0) * sixth,
        (-3.0 * cube + 3.0 * square + 3.0 * frac + 1.0) * sixth,
        cube * sixth,
    )


def split(value):
    high = value.astype(BF16)
    return high, (value - high.astype(F32)).astype(BF16)


def iota(shape, axis):
    return lax.broadcasted_iota(jnp.int32, shape, axis).astype(F32)


def step_waves(first, rows, width, length):
    wave = (first + iota((rows, width), 0)) * (1.0 / length)
    return [turn(wave * float(step)) for step in (1, 2, 3)]


def atom_waves(base, weights, first, rows, length, steps_ref):
    width = base.shape[1]
    blocks = rows // 8
    coarse_rows = -(-blocks // 8) * 8
    coarse = (first + 8.0 * iota((coarse_rows, width), 0)) * (base * (1.0 / length))
    coarse_cos, coarse_sin = turn(coarse)
    fine_cos, fine_sin = turn(iota((8, width), 0) * (base * (1.0 / length)))
    for block in range(blocks):
        at = slice(block, block + 1)
        cos_a, sin_a = coarse_cos[at], coarse_sin[at]
        cosine = cos_a * fine_cos - sin_a * fine_sin
        sine = sin_a * fine_cos + cos_a * fine_sin
        span = pl.ds(8 * block, 8)
        in_phase = weights[0] + sum(weights[r] * steps_ref[2 * r - 2, span, :] for r in (1, 2, 3))
        quarter = sum(weights[r] * steps_ref[2 * r - 1, span, :] for r in (1, 2, 3))
        yield block, cosine * in_phase - sine * quarter, sine * in_phase + cosine * quarter


def plane_weights(atoms, weights):
    row = iota((8, atoms.shape[1]), 0) - atoms[0:1]
    return sum(weights[r][3:4] * (row == float(r)).astype(F32) for r in range(4))


def swap(value):
    return pltpu.roll(value, LANES // 2, axis=value.ndim - 1)


def half_sign():
    lane = lax.broadcasted_iota(jnp.int32, (1, LANES), 1)
    return jnp.where(lane < LANES // 2, -1.0, 1.0).astype(F32)


def rotate(value, numer, denom, sign, halves):
    if numer == 0:
        return value
    if 4 * numer == denom:
        return swap(value) * (halves * sign)
    angle = 2.0 * np.pi * numer / denom
    return value * float(np.cos(angle)) + swap(value) * (halves * float(sign * np.sin(angle)))


def transform(values, sign, halves):
    count = len(values)
    if count == 1:
        return values
    even = transform(values[0::2], sign, halves)
    odd = transform(values[1::2], sign, halves)
    turned = [rotate(odd[k], k, count, sign, halves) for k in range(count // 2)]
    return [e + t for e, t in zip(even, turned)] + [e - t for e, t in zip(even, turned)]


def forward_kernel(place_ref, atoms_ref, out_ref, left_ref, right_ref, grid_ref, steps_y, steps_z):
    step = pl.program_id(0)
    cells_x = grid_ref.shape[0]
    rows = grid_ref.shape[1] // 2
    ky_local = rows - 8
    first_y = place_ref[0].astype(F32)
    first_z = place_ref[1].astype(F32)
    width = atoms_ref.shape[2]
    doms = atoms_ref.shape[0]
    half = LANES // 2

    @pl.when(step == 0)
    def _():
        grid_ref[...] = jnp.zeros_like(grid_ref)
        for index, (cosine, sine) in enumerate(step_waves(first_y, rows, width, NY)):
            steps_y[2 * index] = cosine
            steps_y[2 * index + 1] = sine
        for index, (cosine, sine) in enumerate(step_waves(first_z, half, width, NZ)):
            steps_z[2 * index] = cosine
            steps_z[2 * index + 1] = sine

    for dom in range(doms):
        atoms = atoms_ref[dom]
        lanes = pl.ds(dom * width, width)
        weights = spline(atoms)
        along_x = plane_weights(atoms, weights)
        weights_y = [w[4:5] for w in weights]
        weights_z = [w[5:6] * atoms[6:7] for w in weights]
        waves = list(atom_waves(atoms[2:3], weights_z, first_z, half, NZ, steps_z))
        for part in (1, 2):
            for pair in range(0, len(waves), 2):
                high, low = split(jnp.concatenate([waves[pair][part], waves[pair + 1][part]], 0))
                start = (part - 1) * half + 8 * pair
                right_ref[pl.ds(start, 16), lanes] = high
                right_ref[pl.ds(LANES + start, 16), lanes] = low
        for block, cosine, sine in atom_waves(atoms[1:2], weights_y, first_y, rows, NY, steps_y):
            both = jnp.concatenate([cosine, sine], 0)
            for plane in range(SPAN):
                high, low = split(both * along_x[plane : plane + 1])
                left_ref[plane, pl.ds(16 * block, 16), lanes] = high
                left_ref[plane, pl.ds(2 * rows + 16 * block, 16), lanes] = low

    right = right_ref[...]
    for plane in range(SPAN):
        product = lax.dot_general(
            left_ref[plane], right, (((1,), (1,)), ((), ())), preferred_element_type=F32
        )
        high, low = product[: 2 * rows], product[2 * rows :]
        total = (high[:, :LANES] + high[:, LANES:]) + (low[:, :LANES] + low[:, LANES:])
        at = lax.rem(step * XD + plane, cells_x)
        for block in range(rows // 8):
            grid_ref[at, pl.ds(8 * block, 8), :] += total[16 * block : 16 * block + 8]
            grid_ref[at, pl.ds(rows + 8 * block, 8), :] += total[16 * block + 8 : 16 * block + 16]

    @pl.when(step == pl.num_programs(0) - 1)
    def _():
        halves = half_sign()
        quarter_rows = ky_local // 2
        group = min(8, quarter_rows)
        for minus in (0, 1):
            for start in range(0, ky_local, group):
                row = start + minus
                values = []
                for x in range(cells_x):
                    top = grid_ref[x, pl.ds(row, group), :]
                    bottom = swap(grid_ref[x, pl.ds(rows + row, group), :])
                    values.append(bottom - top * halves if minus else -bottom - top * halves)
                at = 2 * minus + start // quarter_rows
                for x, value in enumerate(transform(values, -1.0, halves)):
                    out_ref[at, x, pl.ds(start % quarter_rows, group), :] = value


def inverse_x_kernel(side_ref, spectrum_ref, own_ref, mirrored_ref, *refs):
    outs, near_ref = refs[:XD], refs[XD]
    cells_x = spectrum_ref.shape[1]
    halves = half_sign()
    lane = lax.broadcasted_iota(jnp.int32, (1, LANES), 1)
    side = side_ref[0]
    for quarter in range(4):
        green_ref = own_ref if quarter < 2 else mirrored_ref
        values = []
        for kx in range(cells_x):
            green = green_ref[kx]
            keep = lane < LANES // 2 if quarter % 2 == 0 else lane >= LANES // 2
            values.append(spectrum_ref[quarter, kx] * jnp.where(keep, green, swap(green)))
        even = transform(values[0::2], 1.0, halves)
        odd = transform(values[1::2], 1.0, halves)
        for x in range(cells_x // 2):
            turned = rotate(odd[x], x, cells_x, 1.0, halves) * side
            plane = even[x] + turned
            outs[x % XD][x // XD, quarter] = plane
            near_ref[x, quarter] = plane
            if x < 3:
                near_ref[cells_x // 2 + x, quarter] = even[x] - turned


def inverse_y_kernel(side_ref, lines_ref, high_ref, low_ref, out_ref):
    lines = lines_ref[...]
    pairs = jnp.concatenate([lines, swap(lines) * half_sign()], 0)
    high, low = split(pairs)
    main = jnp.dot(high_ref[...], jnp.concatenate([high, low], 1), preferred_element_type=F32)
    rest = jnp.dot(low_ref[...], high, preferred_element_type=F32)
    row = lax.broadcasted_iota(jnp.int32, (NY, 1), 0)
    sign = jnp.where(row % 2 == 0, 1.0, side_ref[0])
    out_ref[...] = (main[:, :LANES] + main[:, LANES:] + rest) * sign


def inverse_z_kernel(*refs):
    ins, high_ref, low_ref, out_ref = refs[:XD], refs[XD], refs[XD + 1], refs[XD + 2]
    for x in range(XD):
        lines = jnp.concatenate([ins[x][d] for d in range(ins[x].shape[0])], 1)
        high, low = split(lines)
        total = jnp.dot(high, high_ref[...], preferred_element_type=F32)
        total += jnp.dot(low, high_ref[...], preferred_element_type=F32)
        total += jnp.dot(high, low_ref[...], preferred_element_type=F32)
        out_ref[x] = total


def gather_kernel(place_ref, atoms_ref, near_ref, out_ref, pair_ref, steps_y, steps_z, sine_y, sine_z):
    step = pl.program_id(0)
    half = LANES // 2
    rows = pair_ref.shape[1] // 2
    ky_local = rows - 8
    first_y = place_ref[0].astype(F32)
    first_z = place_ref[1].astype(F32)
    width = atoms_ref.shape[2]
    planes = near_ref.shape[0]
    halves = half_sign()

    @pl.when(step == 0)
    def _():
        out_ref[...] = jnp.zeros_like(out_ref)
        for index, (cosine, sine) in enumerate(step_waves(first_y, rows, width, NY)):
            steps_y[2 * index] = cosine
            steps_y[2 * index + 1] = sine
        for index, (cosine, sine) in enumerate(step_waves(first_z, half, width, NZ)):
            steps_z[2 * index] = cosine
            steps_z[2 * index + 1] = sine

        def build(x, carry):
            plus = near_ref[x, pl.ds(0, ky_local), :]
            minus = near_ref[x, pl.ds(ky_local, ky_local), :]
            for part in (0, rows):
                pair_ref[x, pl.ds(part + ky_local, 8), :] = jnp.zeros((8, LANES), F32)
            pair_ref[x, pl.ds(0, ky_local), :] = plus
            pair_ref[x, pl.ds(rows, ky_local), :] = swap(plus) * halves
            pair_ref[x, pl.ds(1, ky_local), :] += minus
            pair_ref[x, pl.ds(rows + 1, ky_local), :] -= swap(minus) * halves
            return carry

        lax.fori_loop(0, planes, build, 0)

    slot = place_ref[2] + step
    twice = jnp.where(first_z + iota((half, 1), 0) == 0.0, 1.0, 2.0)
    for dom in range(atoms_ref.shape[0]):
        atoms = atoms_ref[dom]
        weights = spline(atoms)
        along_x = plane_weights(atoms, weights)
        for block, cosine, sine in atom_waves(
            atoms[2:3], [w[5:6] for w in weights], first_z, half, NZ, steps_z
        ):
            sine_z[pl.ds(8 * block, 8), :] = cosine
            sine_z[pl.ds(half + 8 * block, 8), :] = -sine
        for block, cosine, sine in atom_waves(
            atoms[1:2], [w[4:5] for w in weights], first_y, rows, NY, steps_y
        ):
            sine_y[pl.ds(8 * block, 8), :] = cosine
            sine_y[pl.ds(rows + 8 * block, 8), :] = sine
        table_high, table_low = split(sine_y[...])
        dims = (((0,), (0,)), ((), ()))
        total = jnp.zeros((LANES, width), F32)
        for plane in range(SPAN):
            high, low = split(pair_ref[step * XD + plane])
            field = lax.dot_general(high, table_high, dims, preferred_element_type=F32)
            field += lax.dot_general(low, table_high, dims, preferred_element_type=F32)
            field += lax.dot_general(high, table_low, dims, preferred_element_type=F32)
            total += along_x[plane : plane + 1] * field
        scale = jnp.concatenate([twice, twice], 0)
        sampled = jnp.sum(total * sine_z[...] * scale, axis=0, keepdims=True)
        out_ref[slot, :, pl.ds(dom * width, width)] = sampled


def bf16_pair(table):
    high = table.astype(ml_dtypes.bfloat16)
    low = (table - high.astype(np.float64)).astype(ml_dtypes.bfloat16)
    return jnp.asarray(high), jnp.asarray(low)


def inverse_y_table(slab_half, ky_local):
    waves = []
    for slab in range(slab_half):
        first = slab * ky_local
        waves += [first + i for i in range(ky_local)] + [-(first + i + 1) for i in range(ky_local)]
    angle = 2.0 * np.pi * (np.outer(np.arange(NY), np.array(waves)) % NY) / NY
    return bf16_pair(np.concatenate([np.cos(angle), np.sin(angle)], 1))


def inverse_z_table(dom_count):
    kz = np.arange(KH)
    angle = 2.0 * np.pi * (np.outer(kz, np.arange(NZ)) % NZ) / NZ
    weight = np.where(kz == 0, 1.0, 2.0)[:, None]
    parts = [weight * np.cos(angle), -weight * np.sin(angle)]
    return bf16_pair(
        np.stack([p.reshape(dom_count, KH // dom_count, NZ) for p in parts], 1).reshape(2 * KH, NZ)
    )


def whole_spec(shape):
    return pl.BlockSpec(shape, lambda *_: (0,) * len(shape))


SMEM = pl.BlockSpec(memory_space=pltpu.SMEM)


def params(mib):
    return pltpu.CompilerParams(vmem_limit_bytes=mib * MIB)


def per_device(base_cells, offsets, charges, bias_coupling, counts, green):
    slabs = lax.axis_size("slab")
    doms = lax.axis_size("dom")
    slab = lax.axis_index("slab")
    dom = lax.axis_index("dom")
    atoms_local = charges.shape[0]
    cells_x = XD * slabs
    ky_local = NY // slabs
    kz_local = KH // doms
    slab_half = slabs // 2
    rows_local = NY // doms
    rows = ky_local + 8
    quarter_rows = ky_local // 2
    normalize = 1.0 / (cells_x * NY * NZ)
    upper = slab // slab_half
    place = jnp.stack([slab * ky_local, dom * kz_local, upper * slab_half]).astype(jnp.int32)
    side = jnp.where(upper == 0, 1.0, -1.0).astype(F32).reshape(1)

    alive = jnp.arange(atoms_local, dtype=jnp.int32) < counts[0]
    atoms = jnp.concatenate(
        [
            (base_cells[0:1] % XD).astype(F32),
            base_cells[1:3].astype(F32),
            offsets,
            jnp.where(alive, charges, 0.0)[None],
            jnp.zeros((1, atoms_local), F32),
        ],
        0,
    )
    gathered = lax.all_gather(atoms, ("slab", "dom"))

    scaled = green * normalize
    own = jnp.concatenate([scaled[:, :quarter_rows], scaled[:, quarter_rows:]], 2)
    flipped = scaled[:, ::-1]
    flipped = jnp.concatenate([flipped[:, :quarter_rows], flipped[:, quarter_rows:]], 2)
    mirrored = lax.ppermute(flipped, "slab", [(s, slabs - 1 - s) for s in range(slabs)])

    spectrum = pl.pallas_call(
        forward_kernel,
        grid=(slabs,),
        in_specs=[SMEM, pl.BlockSpec((doms, 8, atoms_local), lambda s: (s, 0, 0))],
        out_specs=whole_spec((4, cells_x, quarter_rows, LANES)),
        out_shape=jax.ShapeDtypeStruct((4, cells_x, quarter_rows, LANES), F32),
        scratch_shapes=[
            pltpu.VMEM((SPAN, 4 * rows, doms * atoms_local), BF16),
            pltpu.VMEM((2 * LANES, doms * atoms_local), BF16),
            pltpu.VMEM((cells_x, 2 * rows, LANES), F32),
            pltpu.VMEM((6, rows, atoms_local), F32),
            pltpu.VMEM((6, LANES // 2, atoms_local), F32),
        ],
        compiler_params=params(40),
        cost_estimate=pl.CostEstimate(flops=8 * 10**9, bytes_accessed=4 * MIB, transcendentals=0),
        name="forward",
    )(place, gathered)

    group = min(8, quarter_rows)
    near_planes = cells_x // 2 + 3
    chunk = (slab_half, 4, quarter_rows, LANES)
    *chunks, near = pl.pallas_call(
        inverse_x_kernel,
        grid=(quarter_rows // group,),
        in_specs=[
            SMEM,
            pl.BlockSpec((4, cells_x, group, LANES), lambda g: (0, 0, g, 0)),
            pl.BlockSpec((cells_x, group, LANES), lambda g: (0, g, 0)),
            pl.BlockSpec((cells_x, group, LANES), lambda g: (0, g, 0)),
        ],
        out_specs=[pl.BlockSpec((slab_half, 4, group, LANES), lambda g: (0, 0, g, 0))] * XD
        + [pl.BlockSpec((near_planes, 4, group, LANES), lambda g: (0, 0, g, 0))],
        out_shape=[jax.ShapeDtypeStruct(chunk, F32)] * XD
        + [jax.ShapeDtypeStruct((near_planes, 4, quarter_rows, LANES), F32)],
        compiler_params=params(32),
        cost_estimate=pl.CostEstimate(flops=10**8, bytes_accessed=6 * MIB, transcendentals=0),
        name="inverse_x",
    )(side, spectrum, own, mirrored)

    groups = [list(range(slab_half)), list(range(slab_half, slabs))]
    high_y, low_y = inverse_y_table(slab_half, ky_local)
    columns = []
    for piece in chunks:
        lines = lax.all_to_all(piece, "slab", 0, 0, axis_index_groups=groups, tiled=True)
        turned = pl.pallas_call(
            inverse_y_kernel,
            in_specs=[SMEM] + [pl.BlockSpec(memory_space=pltpu.VMEM)] * 3,
            out_specs=pl.BlockSpec(memory_space=pltpu.VMEM),
            out_shape=jax.ShapeDtypeStruct((NY, LANES), F32),
            compiler_params=params(24),
            cost_estimate=pl.CostEstimate(flops=4 * 10**8, bytes_accessed=3 * MIB, transcendentals=0),
            name="inverse_y",
        )(side, lines.reshape(NY, LANES), high_y, low_y)
        columns.append(
            lax.all_to_all(turned.reshape(doms, rows_local, LANES), "dom", 0, 0, tiled=True)
        )

    partial = pl.pallas_call(
        gather_kernel,
        grid_spec=pltpu.PrefetchScalarGridSpec(
            num_scalar_prefetch=1,
            grid=(slab_half,),
            in_specs=[
                pl.BlockSpec((doms, 8, atoms_local), lambda t, place: (place[2] + t, 0, 0)),
                pl.BlockSpec((near_planes, 2 * ky_local, LANES), lambda t, place: (0, 0, 0)),
            ],
            out_specs=pl.BlockSpec((slabs, 1, doms * atoms_local), lambda t, place: (0, 0, 0)),
            scratch_shapes=[
                pltpu.VMEM((near_planes, 2 * rows, LANES), F32),
                pltpu.VMEM((6, rows, atoms_local), F32),
                pltpu.VMEM((6, LANES // 2, atoms_local), F32),
                pltpu.VMEM((2 * rows, atoms_local), F32),
                pltpu.VMEM((LANES, atoms_local), F32),
            ],
        ),
        out_shape=jax.ShapeDtypeStruct((slabs, 1, doms * atoms_local), F32),
        compiler_params=params(24),
        cost_estimate=pl.CostEstimate(flops=6 * 10**9, bytes_accessed=3 * MIB, transcendentals=0),
        name="gather",
    )(place, gathered, near.reshape(near_planes, 2 * ky_local, LANES))
    sampled = lax.psum_scatter(
        partial.reshape(-1), ("slab", "dom"), scatter_dimension=0, tiled=True
    )
    gradient = jnp.where(alive, bias_coupling * sampled, 0.0)

    high_z, low_z = inverse_z_table(doms)
    potential = pl.pallas_call(
        inverse_z_kernel,
        in_specs=[pl.BlockSpec(memory_space=pltpu.VMEM)] * (XD + 2),
        out_specs=pl.BlockSpec(memory_space=pltpu.VMEM),
        out_shape=jax.ShapeDtypeStruct((XD, rows_local, NZ), F32),
        compiler_params=params(24),
        cost_estimate=pl.CostEstimate(flops=8 * 10**8, bytes_accessed=3 * MIB, transcendentals=0),
        name="inverse_z",
    )(*columns, high_z, low_z)
    return (potential, gradient)


def solution(mesh):
    placed = (
        P(None, ("slab", "dom")),
        P(None, ("slab", "dom")),
        P(("slab", "dom")),
        P(("slab", "dom")),
        P(("slab", "dom")),
        P(None, "slab", "dom"),
    )
    return jax.shard_map(
        per_device,
        mesh=mesh,
        in_specs=placed,
        out_specs=(P("slab", "dom", None), P(("slab", "dom"))),
        check_vma=False,
    )
```

```python
import functools

import jax
import jax.numpy as jnp
import ml_dtypes
import numpy as np
from jax import lax
from jax.experimental import pallas as pl
from jax.experimental.pallas import tpu as pltpu
from jax.sharding import PartitionSpec as P

XD = 4
NY = 512
NZ = 512
KH = NZ // 2
LANES = 128
SPAN = XD + 3
CHUNKS = 2
DEPTH = XD // CHUNKS
MIB = 1 << 20
BF16 = jnp.bfloat16
F32 = jnp.float32


def polynomial(function, terms):
    nodes = 0.125 * (1.0 - np.cos(np.pi * (np.arange(64) + 0.5) / 64))
    powers = nodes[:, None] ** np.arange(terms)[None, :]
    return [float(v) for v in np.linalg.lstsq(powers, function(np.sqrt(nodes)), rcond=None)[0]]


SINE_TERMS = polynomial(lambda r: np.sin(np.pi * r) / r, 6)
COSINE_TERMS = polynomial(lambda r: np.cos(np.pi * r), 6)


def horner(terms, square):
    total = jnp.full_like(square, terms[-1])
    for term in terms[-2::-1]:
        total = total * square + term
    return total


def turn(fraction):
    left = fraction - jnp.floor(fraction + 0.5)
    square = left * left
    sine = left * horner(SINE_TERMS, square)
    cosine = horner(COSINE_TERMS, square)
    return 1.0 - 2.0 * sine * sine, 2.0 * sine * cosine


def spline(frac):
    inner = 1.0 - frac
    square = frac * frac
    cube = square * frac
    sixth = 1.0 / 6.0
    return (
        inner * inner * inner * sixth,
        (3.0 * cube - 6.0 * square + 4.0) * sixth,
        (-3.0 * cube + 3.0 * square + 3.0 * frac + 1.0) * sixth,
        cube * sixth,
    )


def split(value):
    high = value.astype(BF16)
    return high, (value - high.astype(F32)).astype(BF16)


def iota(shape, axis):
    return lax.broadcasted_iota(jnp.int32, shape, axis).astype(F32)


def step_waves(first, rows, width, length):
    wave = (first + iota((rows, width), 0)) * (1.0 / length)
    return [turn(wave * float(step)) for step in (1, 2, 3)]


def atom_waves(base, weights, first, rows, length, steps_ref):
    width = base.shape[1]
    blocks = rows // 8
    coarse_rows = -(-blocks // 8) * 8
    coarse = (first + 8.0 * iota((coarse_rows, width), 0)) * (base * (1.0 / length))
    coarse_cos, coarse_sin = turn(coarse)
    fine_cos, fine_sin = turn(iota((8, width), 0) * (base * (1.0 / length)))
    for block in range(blocks):
        at = slice(block, block + 1)
        cos_a, sin_a = coarse_cos[at], coarse_sin[at]
        cosine = cos_a * fine_cos - sin_a * fine_sin
        sine = sin_a * fine_cos + cos_a * fine_sin
        span = pl.ds(8 * block, 8)
        in_phase = weights[0] + sum(weights[r] * steps_ref[2 * r - 2, span, :] for r in (1, 2, 3))
        quarter = sum(weights[r] * steps_ref[2 * r - 1, span, :] for r in (1, 2, 3))
        yield block, cosine * in_phase - sine * quarter, sine * in_phase + cosine * quarter


def plane_weights(atoms, weights):
    row = iota((8, atoms.shape[1]), 0) - atoms[0:1]
    return sum(weights[r][3:4] * (row == float(r)).astype(F32) for r in range(4))


def swap(value):
    return pltpu.roll(value, LANES // 2, axis=value.ndim - 1)


def half_sign():
    lane = lax.broadcasted_iota(jnp.int32, (1, LANES), 1)
    return jnp.where(lane < LANES // 2, -1.0, 1.0).astype(F32)


def rotate(value, numer, denom, sign, halves):
    if numer == 0:
        return value
    if 4 * numer == denom:
        return swap(value) * (halves * sign)
    angle = 2.0 * np.pi * numer / denom
    return value * float(np.cos(angle)) + swap(value) * (halves * float(sign * np.sin(angle)))


def transform(values, sign, halves):
    count = len(values)
    if count == 1:
        return values
    even = transform(values[0::2], sign, halves)
    odd = transform(values[1::2], sign, halves)
    turned = [rotate(odd[k], k, count, sign, halves) for k in range(count // 2)]
    return [e + t for e, t in zip(even, turned)] + [e - t for e, t in zip(even, turned)]


def forward_kernel(place_ref, atoms_ref, out_ref, left_ref, right_ref, grid_ref, steps_y, steps_z):
    step = pl.program_id(0)
    cells_x = grid_ref.shape[0]
    rows = grid_ref.shape[1] // 2
    ky_local = rows - 8
    first_y = place_ref[0].astype(F32)
    first_z = place_ref[1].astype(F32)
    width = atoms_ref.shape[2]
    doms = atoms_ref.shape[0]
    half = LANES // 2

    @pl.when(step == 0)
    def _():
        grid_ref[...] = jnp.zeros_like(grid_ref)
        for index, (cosine, sine) in enumerate(step_waves(first_y, rows, width, NY)):
            steps_y[2 * index] = cosine
            steps_y[2 * index + 1] = sine
        for index, (cosine, sine) in enumerate(step_waves(first_z, half, width, NZ)):
            steps_z[2 * index] = cosine
            steps_z[2 * index + 1] = sine

    for dom in range(doms):
        atoms = atoms_ref[dom]
        lanes = pl.ds(dom * width, width)
        weights = spline(atoms)
        along_x = plane_weights(atoms, weights)
        weights_y = [w[4:5] for w in weights]
        weights_z = [w[5:6] * atoms[6:7] for w in weights]
        waves = list(atom_waves(atoms[2:3], weights_z, first_z, half, NZ, steps_z))
        for part in (1, 2):
            for pair in range(0, len(waves), 2):
                high, low = split(jnp.concatenate([waves[pair][part], waves[pair + 1][part]], 0))
                start = (part - 1) * half + 8 * pair
                right_ref[pl.ds(start, 16), lanes] = high
                right_ref[pl.ds(LANES + start, 16), lanes] = low
        for block, cosine, sine in atom_waves(atoms[1:2], weights_y, first_y, rows, NY, steps_y):
            both = jnp.concatenate([cosine, sine], 0)
            for plane in range(SPAN):
                high, low = split(both * along_x[plane : plane + 1])
                left_ref[plane, pl.ds(16 * block, 16), lanes] = high
                left_ref[plane, pl.ds(2 * rows + 16 * block, 16), lanes] = low

    right = right_ref[...]
    for plane in range(SPAN):
        product = lax.dot_general(
            left_ref[plane], right, (((1,), (1,)), ((), ())), preferred_element_type=F32
        )
        high, low = product[: 2 * rows], product[2 * rows :]
        total = (high[:, :LANES] + high[:, LANES:]) + (low[:, :LANES] + low[:, LANES:])
        at = lax.rem(step * XD + plane, cells_x)
        for block in range(rows // 8):
            grid_ref[at, pl.ds(8 * block, 8), :] += total[16 * block : 16 * block + 8]
            grid_ref[at, pl.ds(rows + 8 * block, 8), :] += total[16 * block + 8 : 16 * block + 16]

    @pl.when(step == pl.num_programs(0) - 1)
    def _():
        halves = half_sign()
        quarter_rows = ky_local // 2
        group = min(8, quarter_rows)
        for minus in (0, 1):
            for start in range(0, ky_local, group):
                row = start + minus
                values = []
                for x in range(cells_x):
                    top = grid_ref[x, pl.ds(row, group), :]
                    bottom = swap(grid_ref[x, pl.ds(rows + row, group), :])
                    values.append(bottom - top * halves if minus else -bottom - top * halves)
                at = 2 * minus + start // quarter_rows
                for x, value in enumerate(transform(values, -1.0, halves)):
                    out_ref[at, x, pl.ds(start % quarter_rows, group), :] = value


def inverse_x_kernel(place_ref, spectrum_ref, own_ref, mirrored_ref, *refs):
    *outs, near_ref = refs
    slab_half = len(outs) // CHUNKS
    cells_x = spectrum_ref.shape[1]
    halves = half_sign()
    lane = lax.broadcasted_iota(jnp.int32, (1, LANES), 1)
    side = 1.0 - 2.0 * place_ref[3].astype(F32)
    for quarter in range(4):
        green_ref = own_ref if quarter < 2 else mirrored_ref
        values = []
        for kx in range(cells_x):
            green = green_ref[kx]
            keep = lane < LANES // 2 if quarter % 2 == 0 else lane >= LANES // 2
            values.append(spectrum_ref[quarter, kx] * jnp.where(keep, green, swap(green)))
        even = transform(values[0::2], 1.0, halves)
        odd = transform(values[1::2], 1.0, halves)
        for x in range(cells_x // 2):
            turned = rotate(odd[x], x, cells_x, 1.0, halves) * side
            near_ref[x, quarter] = even[x] + turned
            if x < 3:
                near_ref[cells_x // 2 + x, quarter] = even[x] - turned
    for k in range(slab_half):
        partner = lax.bitwise_xor(place_ref[4], k)
        for chunk in range(CHUNKS):
            outs[chunk * slab_half + k][...] = near_ref[pl.ds(partner * XD + chunk * DEPTH, DEPTH)]


def inverse_y_kernel(sources, place_ref, *refs):
    ins, (high_ref, low_ref) = refs[:sources], refs[sources : sources + 2]
    outs, (lines_ref, turned_ref) = refs[sources + 2 : -2], refs[-2:]
    for k in range(sources):
        lines_ref[lax.bitwise_xor(place_ref[4], k)] = ins[k][...]
    parts = []
    for x in range(DEPTH):
        lines = jnp.concatenate([lines_ref[source, x] for source in range(sources)], 0)
        pairs = jnp.concatenate([lines, swap(lines) * half_sign()], 0)
        parts.append(split(pairs))
    both = jnp.concatenate([value for part in parts for value in part], 1)
    main = jnp.dot(high_ref[...], both, preferred_element_type=F32)
    high = jnp.concatenate([part[0] for part in parts], 1)
    rest = jnp.dot(low_ref[...], high, preferred_element_type=F32)
    row = lax.broadcasted_iota(jnp.int32, (NY, 1), 0)
    sign = jnp.where((row % 2 == 1) & (place_ref[3] == 1), -1.0, 1.0)
    for x in range(DEPTH):
        total = main[:, 2 * x * LANES : (2 * x + 1) * LANES] + main[:, (2 * x + 1) * LANES : (2 * x + 2) * LANES]
        total = (total + rest[:, x * LANES : (x + 1) * LANES]) * sign
        turned_ref[:, x] = total.reshape(len(outs), -1, LANES)
    for k in range(len(outs)):
        outs[k][...] = turned_ref[lax.bitwise_xor(place_ref[5], k)]


def inverse_z_kernel(sources, place_ref, *refs):
    ins, (high_ref, low_ref) = refs[:sources], refs[sources : sources + 2]
    out_ref, lines_ref = refs[-2:]
    for k in range(sources):
        lines_ref[lax.bitwise_xor(place_ref[5], k)] = ins[k][...]
    for x in range(DEPTH):
        lines = jnp.concatenate([lines_ref[source, x] for source in range(sources)], 1)
        high, low = split(lines)
        total = jnp.dot(high, high_ref[...], preferred_element_type=F32)
        total += jnp.dot(low, high_ref[...], preferred_element_type=F32)
        total += jnp.dot(high, low_ref[...], preferred_element_type=F32)
        out_ref[x] = total


def gather_kernel(place_ref, atoms_ref, near_ref, out_ref, pair_ref, steps_y, steps_z, sine_y, sine_z):
    step = pl.program_id(0)
    half = LANES // 2
    rows = pair_ref.shape[1] // 2
    ky_local = rows - 8
    first_y = place_ref[0].astype(F32)
    first_z = place_ref[1].astype(F32)
    width = atoms_ref.shape[2]
    planes = near_ref.shape[0]
    halves = half_sign()

    @pl.when(step == 0)
    def _():
        for index, (cosine, sine) in enumerate(step_waves(first_y, rows, width, NY)):
            steps_y[2 * index] = cosine
            steps_y[2 * index + 1] = sine
        for index, (cosine, sine) in enumerate(step_waves(first_z, half, width, NZ)):
            steps_z[2 * index] = cosine
            steps_z[2 * index + 1] = sine

        def build(x, carry):
            plus = near_ref[x, pl.ds(0, ky_local), :]
            minus = near_ref[x, pl.ds(ky_local, ky_local), :]
            for part in (0, rows):
                pair_ref[x, pl.ds(part + ky_local, 8), :] = jnp.zeros((8, LANES), F32)
            pair_ref[x, pl.ds(0, ky_local), :] = plus
            pair_ref[x, pl.ds(rows, ky_local), :] = swap(plus) * halves
            pair_ref[x, pl.ds(1, ky_local), :] += minus
            pair_ref[x, pl.ds(rows + 1, ky_local), :] -= swap(minus) * halves
            return carry

        lax.fori_loop(0, planes, build, 0)

    twice = jnp.where(first_z + iota((half, 1), 0) == 0.0, 1.0, 2.0)
    for dom in range(atoms_ref.shape[0]):
        atoms = atoms_ref[dom]
        weights = spline(atoms)
        along_x = plane_weights(atoms, weights)
        for block, cosine, sine in atom_waves(
            atoms[2:3], [w[5:6] for w in weights], first_z, half, NZ, steps_z
        ):
            sine_z[pl.ds(8 * block, 8), :] = cosine
            sine_z[pl.ds(half + 8 * block, 8), :] = -sine
        for block, cosine, sine in atom_waves(
            atoms[1:2], [w[4:5] for w in weights], first_y, rows, NY, steps_y
        ):
            sine_y[pl.ds(8 * block, 8), :] = cosine
            sine_y[pl.ds(rows + 8 * block, 8), :] = sine
        table_high, table_low = split(sine_y[...])
        dims = (((0,), (0,)), ((), ()))
        total = jnp.zeros((LANES, width), F32)
        for plane in range(SPAN):
            high, low = split(pair_ref[step * XD + plane])
            field = lax.dot_general(high, table_high, dims, preferred_element_type=F32)
            field += lax.dot_general(low, table_high, dims, preferred_element_type=F32)
            field += lax.dot_general(high, table_low, dims, preferred_element_type=F32)
            total += along_x[plane : plane + 1] * field
        scale = jnp.concatenate([twice, twice], 0)
        sampled = jnp.sum(total * sine_z[...] * scale, axis=0, keepdims=True)
        out_ref[step, :, pl.ds(dom * width, width)] = sampled


def bf16_pair(table):
    high = table.astype(ml_dtypes.bfloat16)
    low = (table - high.astype(np.float64)).astype(ml_dtypes.bfloat16)
    return jnp.asarray(high), jnp.asarray(low)


def inverse_y_table(slab_half, ky_local):
    waves = []
    for slab in range(slab_half):
        first = slab * ky_local
        waves += [first + i for i in range(ky_local)] + [-(first + i + 1) for i in range(ky_local)]
    angle = 2.0 * np.pi * (np.outer(np.arange(NY), np.array(waves)) % NY) / NY
    return bf16_pair(np.concatenate([np.cos(angle), np.sin(angle)], 1))


def inverse_z_table(dom_count):
    kz = np.arange(KH)
    angle = 2.0 * np.pi * (np.outer(kz, np.arange(NZ)) % NZ) / NZ
    weight = np.where(kz == 0, 1.0, 2.0)[:, None]
    parts = [weight * np.cos(angle), -weight * np.sin(angle)]
    return bf16_pair(
        np.stack([p.reshape(dom_count, KH // dom_count, NZ) for p in parts], 1).reshape(2 * KH, NZ)
    )


def whole_spec(shape):
    return pl.BlockSpec(shape, lambda *_: (0,) * len(shape))


SMEM = pl.BlockSpec(memory_space=pltpu.SMEM)


def params(mib):
    return pltpu.CompilerParams(vmem_limit_bytes=mib * MIB)


def swapped(value, axis, distance):
    if distance == 0:
        return value
    return lax.ppermute(value, axis, [(i, i ^ distance) for i in range(lax.axis_size(axis))])


def per_device(base_cells, offsets, charges, bias_coupling, counts, green):
    slabs = lax.axis_size("slab")
    doms = lax.axis_size("dom")
    slab = lax.axis_index("slab")
    dom = lax.axis_index("dom")
    atoms_local = charges.shape[0]
    cells_x = XD * slabs
    ky_local = NY // slabs
    kz_local = KH // doms
    slab_half = slabs // 2
    rows_local = NY // doms
    rows = ky_local + 8
    quarter_rows = ky_local // 2
    normalize = 1.0 / (cells_x * NY * NZ)
    upper = slab // slab_half
    place = jnp.stack(
        [slab * ky_local, dom * kz_local, upper * slab_half, upper, slab % slab_half, dom]
    ).astype(jnp.int32)

    alive = jnp.arange(atoms_local, dtype=jnp.int32) < counts[0]
    atoms = jnp.concatenate(
        [
            (base_cells[0:1] % XD).astype(F32),
            base_cells[1:3].astype(F32),
            offsets,
            jnp.where(alive, charges, 0.0)[None],
            jnp.zeros((1, atoms_local), F32),
        ],
        0,
    )
    copies = jnp.broadcast_to(atoms[None], (slabs * doms,) + atoms.shape)
    copies, green = lax.optimization_barrier((copies, green))
    gathered = lax.all_to_all(copies, ("slab", "dom"), 0, 0, tiled=True)

    scaled = green * normalize
    own = jnp.concatenate([scaled[:, :quarter_rows], scaled[:, quarter_rows:]], 2)
    flipped = scaled[:, ::-1]
    flipped = jnp.concatenate([flipped[:, :quarter_rows], flipped[:, quarter_rows:]], 2)
    mirrored = lax.ppermute(flipped, "slab", [(s, slabs - 1 - s) for s in range(slabs)])

    spectrum = pl.pallas_call(
        forward_kernel,
        grid=(slabs,),
        in_specs=[SMEM, pl.BlockSpec((doms, 8, atoms_local), lambda s: (s, 0, 0))],
        out_specs=whole_spec((4, cells_x, quarter_rows, LANES)),
        out_shape=jax.ShapeDtypeStruct((4, cells_x, quarter_rows, LANES), F32),
        scratch_shapes=[
            pltpu.VMEM((SPAN, 4 * rows, doms * atoms_local), BF16),
            pltpu.VMEM((2 * LANES, doms * atoms_local), BF16),
            pltpu.VMEM((cells_x, 2 * rows, LANES), F32),
            pltpu.VMEM((6, rows, atoms_local), F32),
            pltpu.VMEM((6, LANES // 2, atoms_local), F32),
        ],
        compiler_params=params(40),
        cost_estimate=pl.CostEstimate(flops=8 * 10**9, bytes_accessed=4 * MIB, transcendentals=0),
        name="forward",
    )(place, gathered)

    group = min(8, quarter_rows)
    near_planes = cells_x // 2 + 3
    piece = (DEPTH, 4, quarter_rows, LANES)
    *pieces, near = pl.pallas_call(
        inverse_x_kernel,
        grid=(quarter_rows // group,),
        in_specs=[
            SMEM,
            pl.BlockSpec((4, cells_x, group, LANES), lambda g: (0, 0, g, 0)),
            pl.BlockSpec((cells_x, group, LANES), lambda g: (0, g, 0)),
            pl.BlockSpec((cells_x, group, LANES), lambda g: (0, g, 0)),
        ],
        out_specs=[pl.BlockSpec((DEPTH, 4, group, LANES), lambda g: (0, 0, g, 0))] * (CHUNKS * slab_half)
        + [pl.BlockSpec((near_planes, 4, group, LANES), lambda g: (0, 0, g, 0))],
        out_shape=[jax.ShapeDtypeStruct(piece, F32)] * (CHUNKS * slab_half)
        + [jax.ShapeDtypeStruct((near_planes, 4, quarter_rows, LANES), F32)],
        compiler_params=params(32),
        cost_estimate=pl.CostEstimate(flops=10**8, bytes_accessed=6 * MIB, transcendentals=0),
        name="inverse_x",
    )(place, spectrum, own, mirrored)

    high_y, low_y = inverse_y_table(slab_half, ky_local)
    high_z, low_z = inverse_z_table(doms)
    vmem = pl.BlockSpec(memory_space=pltpu.VMEM)
    potential = None
    for chunk in range(CHUNKS):
        lines = [
            swapped(value.reshape(DEPTH, 2 * ky_local, LANES), "slab", k)
            for k, value in enumerate(pieces[chunk * slab_half : (chunk + 1) * slab_half])
        ]
        turned = pl.pallas_call(
            functools.partial(inverse_y_kernel, slab_half),
            in_specs=[SMEM] + [vmem] * (slab_half + 2),
            out_specs=[vmem] * doms,
            out_shape=[jax.ShapeDtypeStruct((DEPTH, rows_local, LANES), F32)] * doms,
            scratch_shapes=[
                pltpu.VMEM((slab_half, DEPTH, 2 * ky_local, LANES), F32),
                pltpu.VMEM((doms, DEPTH, rows_local, LANES), F32),
            ],
            compiler_params=params(24),
            cost_estimate=pl.CostEstimate(flops=8 * 10**8, bytes_accessed=3 * MIB, transcendentals=0),
            name="inverse_y",
        )(place, *lines, high_y, low_y)
        columns = [swapped(value, "dom", k) for k, value in enumerate(turned)]
        earlier = [] if potential is None else [potential]
        potential = pl.pallas_call(
            functools.partial(inverse_z_kernel, doms),
            grid=(1,),
            in_specs=[SMEM]
            + [whole_spec((DEPTH, rows_local, LANES))] * doms
            + [whole_spec((2 * KH, NZ))] * 2
            + [pl.BlockSpec(memory_space=pl.ANY)] * len(earlier),
            out_specs=pl.BlockSpec((DEPTH, rows_local, NZ), lambda _, at=chunk: (at, 0, 0)),
            out_shape=jax.ShapeDtypeStruct((XD, rows_local, NZ), F32),
            scratch_shapes=[pltpu.VMEM((doms, DEPTH, rows_local, LANES), F32)],
            input_output_aliases={doms + 3: 0} if earlier else {},
            compiler_params=params(24),
            cost_estimate=pl.CostEstimate(flops=4 * 10**8, bytes_accessed=3 * MIB, transcendentals=0),
            name="inverse_z",
        )(place, *columns, high_z, low_z, *earlier)

    partial = pl.pallas_call(
        gather_kernel,
        grid_spec=pltpu.PrefetchScalarGridSpec(
            num_scalar_prefetch=1,
            grid=(slab_half,),
            in_specs=[
                pl.BlockSpec((doms, 8, atoms_local), lambda t, place: (place[2] + t, 0, 0)),
                pl.BlockSpec((near_planes, 2 * ky_local, LANES), lambda t, place: (0, 0, 0)),
            ],
            out_specs=pl.BlockSpec((slab_half, 1, doms * atoms_local), lambda t, place: (0, 0, 0)),
            scratch_shapes=[
                pltpu.VMEM((near_planes, 2 * rows, LANES), F32),
                pltpu.VMEM((6, rows, atoms_local), F32),
                pltpu.VMEM((6, LANES // 2, atoms_local), F32),
                pltpu.VMEM((2 * rows, atoms_local), F32),
                pltpu.VMEM((LANES, atoms_local), F32),
            ],
        ),
        out_shape=jax.ShapeDtypeStruct((slab_half, 1, doms * atoms_local), F32),
        compiler_params=params(24),
        cost_estimate=pl.CostEstimate(flops=6 * 10**9, bytes_accessed=3 * MIB, transcendentals=0),
        name="gather",
    )(place, gathered, near.reshape(near_planes, 2 * ky_local, LANES))
    members = slab_half * doms
    sampled = lax.all_to_all(
        partial.reshape(members, atoms_local),
        ("slab", "dom"),
        0,
        0,
        axis_index_groups=[list(range(members)), list(range(members, 2 * members))],
        tiled=True,
    )
    gradient = jnp.where(alive, bias_coupling * jnp.sum(sampled, 0), 0.0)
    return (potential, gradient)


def solution(mesh):
    placed = (
        P(None, ("slab", "dom")),
        P(None, ("slab", "dom")),
        P(("slab", "dom")),
        P(("slab", "dom")),
        P(("slab", "dom")),
        P(None, "slab", "dom"),
    )
    return jax.shard_map(
        per_device,
        mesh=mesh,
        in_specs=placed,
        out_specs=(P("slab", "dom", None), P(("slab", "dom"))),
        check_vma=False,
    )
```

```python
import functools

import jax
import jax.numpy as jnp
import ml_dtypes
import numpy as np
from jax import lax
from jax.experimental import pallas as pl
from jax.experimental.pallas import tpu as pltpu
from jax.sharding import PartitionSpec as P

XD = 4
NY = 512
NZ = 512
KH = NZ // 2
LANES = 128
SPAN = XD + 3
CHUNKS = 2
DEPTH = XD // CHUNKS
MIB = 1 << 20
BF16 = jnp.bfloat16
F32 = jnp.float32


def polynomial(function, terms):
    nodes = 0.125 * (1.0 - np.cos(np.pi * (np.arange(64) + 0.5) / 64))
    powers = nodes[:, None] ** np.arange(terms)[None, :]
    return [float(v) for v in np.linalg.lstsq(powers, function(np.sqrt(nodes)), rcond=None)[0]]


SINE_TERMS = polynomial(lambda r: np.sin(np.pi * r) / r, 6)
COSINE_TERMS = polynomial(lambda r: np.cos(np.pi * r), 6)


def horner(terms, square):
    total = jnp.full_like(square, terms[-1])
    for term in terms[-2::-1]:
        total = total * square + term
    return total


def turn(fraction):
    left = fraction - jnp.floor(fraction + 0.5)
    square = left * left
    sine = left * horner(SINE_TERMS, square)
    cosine = horner(COSINE_TERMS, square)
    return 1.0 - 2.0 * sine * sine, 2.0 * sine * cosine


def spline(frac):
    inner = 1.0 - frac
    square = frac * frac
    cube = square * frac
    sixth = 1.0 / 6.0
    return (
        inner * inner * inner * sixth,
        (3.0 * cube - 6.0 * square + 4.0) * sixth,
        (-3.0 * cube + 3.0 * square + 3.0 * frac + 1.0) * sixth,
        cube * sixth,
    )


def split(value):
    high = value.astype(BF16)
    return high, (value - high.astype(F32)).astype(BF16)


def iota(shape, axis):
    return lax.broadcasted_iota(jnp.int32, shape, axis).astype(F32)


def step_waves(first, rows, width, length):
    wave = (first + iota((rows, width), 0)) * (1.0 / length)
    return [turn(wave * float(step)) for step in (1, 2, 3)]


def atom_waves(base, weights, first, rows, length, steps_ref):
    width = base.shape[1]
    blocks = rows // 8
    coarse_rows = -(-blocks // 8) * 8
    coarse = (first + 8.0 * iota((coarse_rows, width), 0)) * (base * (1.0 / length))
    coarse_cos, coarse_sin = turn(coarse)
    fine_cos, fine_sin = turn(iota((8, width), 0) * (base * (1.0 / length)))
    for block in range(blocks):
        at = slice(block, block + 1)
        cos_a, sin_a = coarse_cos[at], coarse_sin[at]
        cosine = cos_a * fine_cos - sin_a * fine_sin
        sine = sin_a * fine_cos + cos_a * fine_sin
        span = pl.ds(8 * block, 8)
        in_phase = weights[0] + sum(weights[r] * steps_ref[2 * r - 2, span, :] for r in (1, 2, 3))
        quarter = sum(weights[r] * steps_ref[2 * r - 1, span, :] for r in (1, 2, 3))
        yield block, cosine * in_phase - sine * quarter, sine * in_phase + cosine * quarter


def plane_weights(atoms, weights):
    row = iota((8, atoms.shape[1]), 0) - atoms[0:1]
    return sum(weights[r][3:4] * (row == float(r)).astype(F32) for r in range(4))


def swap(value):
    return pltpu.roll(value, LANES // 2, axis=value.ndim - 1)


def half_sign():
    lane = lax.broadcasted_iota(jnp.int32, (1, LANES), 1)
    return jnp.where(lane < LANES // 2, -1.0, 1.0).astype(F32)


def rotate(value, numer, denom, sign, halves):
    if numer == 0:
        return value
    if 4 * numer == denom:
        return swap(value) * (halves * sign)
    angle = 2.0 * np.pi * numer / denom
    return value * float(np.cos(angle)) + swap(value) * (halves * float(sign * np.sin(angle)))


def transform(values, sign, halves):
    count = len(values)
    if count == 1:
        return values
    even = transform(values[0::2], sign, halves)
    odd = transform(values[1::2], sign, halves)
    turned = [rotate(odd[k], k, count, sign, halves) for k in range(count // 2)]
    return [e + t for e, t in zip(even, turned)] + [e - t for e, t in zip(even, turned)]


def pack_kernel(counts_ref, cells_ref, offsets_ref, charges_ref, out_ref):
    width = offsets_ref.shape[1]
    alive = lax.broadcasted_iota(jnp.int32, (1, width), 1) < counts_ref[0]
    atoms = jnp.concatenate(
        [
            lax.bitwise_and(cells_ref[0:1, :], XD - 1).astype(F32),
            cells_ref[1:3, :].astype(F32),
            offsets_ref[...],
            jnp.where(alive, charges_ref[...], 0.0),
            jnp.zeros((1, width), F32),
        ],
        0,
    )
    for copy in range(out_ref.shape[0]):
        out_ref[copy] = atoms


def forward_kernel(
    place_ref, atoms_ref, out_ref, left_ref, right_ref, grid_ref, table_ref, along_ref, steps_y, steps_z
):
    step = pl.program_id(0)
    cells_x = grid_ref.shape[0]
    rows = grid_ref.shape[1] // 2
    ky_local = rows - 8
    first_y = place_ref[0].astype(F32)
    first_z = place_ref[1].astype(F32)
    width = atoms_ref.shape[2]
    doms = table_ref.shape[1] // width
    half = LANES // 2

    @pl.when(step == 0)
    def _():
        grid_ref[...] = jnp.zeros_like(grid_ref)
        for index, (cosine, sine) in enumerate(step_waves(first_y, rows, width, NY)):
            steps_y[2 * index] = cosine
            steps_y[2 * index + 1] = sine
        for index, (cosine, sine) in enumerate(step_waves(first_z, half, width, NZ)):
            steps_z[2 * index] = cosine
            steps_z[2 * index + 1] = sine

    for dom in range(doms):
        atoms = atoms_ref[step * doms + dom]
        lanes = pl.ds(dom * width, width)
        weights = spline(atoms)
        along_ref[:, lanes] = plane_weights(atoms, weights)
        weights_y = [w[4:5] for w in weights]
        weights_z = [w[5:6] * atoms[6:7] for w in weights]
        waves = list(atom_waves(atoms[2:3], weights_z, first_z, half, NZ, steps_z))
        for part in (1, 2):
            for pair in range(0, len(waves), 2):
                high, low = split(jnp.concatenate([waves[pair][part], waves[pair + 1][part]], 0))
                start = (part - 1) * half + 8 * pair
                right_ref[pl.ds(start, 16), lanes] = high
                right_ref[pl.ds(LANES + start, 16), lanes] = low
        for block, cosine, sine in atom_waves(atoms[1:2], weights_y, first_y, rows, NY, steps_y):
            table_ref[pl.ds(16 * block, 8), lanes] = cosine
            table_ref[pl.ds(16 * block + 8, 8), lanes] = sine

    for plane in range(SPAN):
        for dom in range(doms):
            lanes = pl.ds(dom * width, width)
            along = along_ref[plane : plane + 1, lanes]
            for start in range(0, 2 * rows, 16):
                high, low = split(table_ref[pl.ds(start, 16), lanes] * along)
                left_ref[plane, pl.ds(start, 16), lanes] = high
                left_ref[plane, pl.ds(2 * rows + start, 16), lanes] = low
        product = lax.dot_general(
            left_ref[plane], right_ref[...], (((1,), (1,)), ((), ())), preferred_element_type=F32
        )
        high, low = product[: 2 * rows], product[2 * rows :]
        total = (high[:, :LANES] + high[:, LANES:]) + (low[:, :LANES] + low[:, LANES:])
        at = lax.rem(step * XD + plane, cells_x)
        for block in range(rows // 8):
            grid_ref[at, pl.ds(8 * block, 8), :] += total[16 * block : 16 * block + 8]
            grid_ref[at, pl.ds(rows + 8 * block, 8), :] += total[16 * block + 8 : 16 * block + 16]

    @pl.when(step == pl.num_programs(0) - 1)
    def _():
        halves = half_sign()
        quarter_rows = ky_local // 2
        group = min(8, quarter_rows)
        for minus in (0, 1):
            for start in range(0, ky_local, group):
                row = start + minus
                values = []
                for x in range(cells_x):
                    top = grid_ref[x, pl.ds(row, group), :]
                    bottom = swap(grid_ref[x, pl.ds(rows + row, group), :])
                    values.append(bottom - top * halves if minus else -bottom - top * halves)
                at = 2 * minus + start // quarter_rows
                for x, value in enumerate(transform(values, -1.0, halves)):
                    out_ref[at, x, pl.ds(start % quarter_rows, group), :] = value


def inverse_x_kernel(place_ref, spectrum_ref, own_ref, first_ref, second_ref, *refs):
    *outs, near_ref = refs
    slab_half = len(outs) // CHUNKS
    cells_x, quarter_rows = spectrum_ref.shape[1:3]
    group = min(8, quarter_rows)
    halves = half_sign()
    lane = lax.broadcasted_iota(jnp.int32, (1, LANES), 1)
    side = 1.0 - 2.0 * place_ref[3].astype(F32)

    def rows_of(step, carry):
        rows = pl.ds(pl.multiple_of(step * group, group), group)
        for quarter in range(4):
            values = []
            for kx in range(cells_x):
                if quarter < 2:
                    green = own_ref[kx, rows, :]
                elif kx < cells_x // 2:
                    green = first_ref[kx, rows, :]
                else:
                    green = second_ref[kx - cells_x // 2, rows, :]
                keep = lane < LANES // 2 if quarter % 2 == 0 else lane >= LANES // 2
                values.append(spectrum_ref[quarter, kx, rows, :] * jnp.where(keep, green, swap(green)))
            even = transform(values[0::2], 1.0, halves)
            odd = transform(values[1::2], 1.0, halves)
            for x in range(cells_x // 2):
                turned = rotate(odd[x], x, cells_x, 1.0, halves) * side
                near_ref[x, quarter, rows, :] = even[x] + turned
                if x < 3:
                    near_ref[cells_x // 2 + x, quarter, rows, :] = even[x] - turned
        return carry

    lax.fori_loop(0, quarter_rows // group, rows_of, 0)
    for chunk in range(CHUNKS):
        for k in range(slab_half):
            partner = lax.bitwise_xor(place_ref[4], k)
            outs[chunk * slab_half + k][...] = near_ref[pl.ds(partner * XD + chunk * DEPTH, DEPTH)]


def inverse_y_kernel(sources, place_ref, *refs):
    ins, (high_ref, low_ref) = refs[:sources], refs[sources : sources + 2]
    outs, (lines_ref, turned_ref) = refs[sources + 2 : -2], refs[-2:]
    for k in range(sources):
        lines_ref[lax.bitwise_xor(place_ref[4], k)] = ins[k][...]
    parts = []
    for x in range(DEPTH):
        lines = jnp.concatenate([lines_ref[source, x] for source in range(sources)], 0)
        pairs = jnp.concatenate([lines, swap(lines) * half_sign()], 0)
        parts.append(split(pairs))
    both = jnp.concatenate([value for part in parts for value in part], 1)
    main = jnp.dot(high_ref[...], both, preferred_element_type=F32)
    high = jnp.concatenate([part[0] for part in parts], 1)
    rest = jnp.dot(low_ref[...], high, preferred_element_type=F32)
    row = lax.broadcasted_iota(jnp.int32, (NY, 1), 0)
    sign = jnp.where((row % 2 == 1) & (place_ref[3] == 1), -1.0, 1.0)
    for x in range(DEPTH):
        total = main[:, 2 * x * LANES : (2 * x + 1) * LANES] + main[:, (2 * x + 1) * LANES : (2 * x + 2) * LANES]
        total = (total + rest[:, x * LANES : (x + 1) * LANES]) * sign
        turned_ref[:, x] = total.reshape(len(outs), -1, LANES)
    for k in range(len(outs)):
        outs[k][...] = turned_ref[lax.bitwise_xor(place_ref[5], k)]


def inverse_z_kernel(sources, place_ref, *refs):
    ins, (high_ref, low_ref) = refs[:sources], refs[sources : sources + 2]
    out_ref, lines_ref = refs[-2:]
    for k in range(sources):
        lines_ref[lax.bitwise_xor(place_ref[5], k)] = ins[k][...]
    for x in range(DEPTH):
        lines = jnp.concatenate([lines_ref[source, x] for source in range(sources)], 1)
        high, low = split(lines)
        total = jnp.dot(high, high_ref[...], preferred_element_type=F32)
        total += jnp.dot(low, high_ref[...], preferred_element_type=F32)
        total += jnp.dot(high, low_ref[...], preferred_element_type=F32)
        out_ref[x] = total


def gather_kernel(
    place_ref, atoms_ref, near_ref, out_ref, pair_ref, fields_ref, stack_ref, table_ref, waves_ref, steps_y, steps_z
):
    step = pl.program_id(0)
    half = LANES // 2
    rows = pair_ref.shape[0] // 2
    ky_local = rows - 8
    first_y = place_ref[0].astype(F32)
    first_z = place_ref[1].astype(F32)
    width = atoms_ref.shape[2]
    doms = out_ref.shape[2] // width
    planes = near_ref.shape[0]
    depth = stack_ref.shape[0]
    halves = half_sign()

    @pl.when(step == 0)
    def _():
        for index, (cosine, sine) in enumerate(step_waves(first_y, rows, width, NY)):
            steps_y[2 * index] = cosine
            steps_y[2 * index + 1] = sine
        for index, (cosine, sine) in enumerate(step_waves(first_z, half, width, NZ)):
            steps_z[2 * index] = cosine
            steps_z[2 * index + 1] = sine
        stack_ref[...] = jnp.zeros_like(stack_ref)

        def build(x, carry):
            plus = near_ref[x, pl.ds(0, ky_local), :]
            minus = near_ref[x, pl.ds(ky_local, ky_local), :]
            for part in (0, rows):
                pair_ref[pl.ds(part + ky_local, 8), :] = jnp.zeros((8, LANES), F32)
            pair_ref[pl.ds(0, ky_local), :] = plus
            pair_ref[pl.ds(rows, ky_local), :] = swap(plus) * halves
            pair_ref[pl.ds(1, ky_local), :] += minus
            pair_ref[pl.ds(rows + 1, ky_local), :] -= swap(minus) * halves
            pairs = pair_ref[...]
            high = pairs.astype(BF16).astype(F32)
            parts = [high, pairs - high, high, jnp.zeros((depth - 6 * rows, LANES), F32)]
            fields_ref[x] = jnp.concatenate(parts, 0).T.astype(BF16)
            return carry

        lax.fori_loop(0, planes, build, 0)

    twice = jnp.where(first_z + iota((half, 1), 0) == 0.0, 1.0, 2.0)
    fields = fields_ref[pl.ds(step * XD, SPAN)].reshape(SPAN * LANES, depth)
    for dom in range(doms):
        atoms = atoms_ref[(place_ref[2] + step) * doms + dom]
        weights = spline(atoms)
        along_x = plane_weights(atoms, weights)
        for block, cosine, sine in atom_waves(
            atoms[2:3], [w[5:6] for w in weights], first_z, half, NZ, steps_z
        ):
            scale = twice[8 * block : 8 * block + 8]
            waves_ref[pl.ds(8 * block, 8), :] = cosine * scale
            waves_ref[pl.ds(half + 8 * block, 8), :] = -sine * scale
        for block, cosine, sine in atom_waves(
            atoms[1:2], [w[4:5] for w in weights], first_y, rows, NY, steps_y
        ):
            table_ref[pl.ds(8 * block, 8), :] = cosine
            table_ref[pl.ds(rows + 8 * block, 8), :] = sine
        high, low = split(table_ref[...])
        lanes = pl.ds(dom * width, width)
        for part, value in enumerate((high, high, low)):
            stack_ref[pl.ds(2 * rows * part, 2 * rows), lanes] = value
        field = jnp.dot(fields, stack_ref[:, lanes], preferred_element_type=F32)
        total = sum(
            along_x[plane : plane + 1] * field[plane * LANES : (plane + 1) * LANES] for plane in range(SPAN)
        )
        out_ref[step, :, lanes] = jnp.sum(total * waves_ref[...], axis=0, keepdims=True)


def bf16_pair(table):
    high = table.astype(ml_dtypes.bfloat16)
    low = (table - high.astype(np.float64)).astype(ml_dtypes.bfloat16)
    return jnp.asarray(high), jnp.asarray(low)


def inverse_y_table(slab_half, ky_local):
    waves = []
    for slab in range(slab_half):
        first = slab * ky_local
        waves += [first + i for i in range(ky_local)] + [-(first + i + 1) for i in range(ky_local)]
    angle = 2.0 * np.pi * (np.outer(np.arange(NY), np.array(waves)) % NY) / NY
    return bf16_pair(np.concatenate([np.cos(angle), np.sin(angle)], 1))


def inverse_z_table(dom_count):
    kz = np.arange(KH)
    angle = 2.0 * np.pi * (np.outer(kz, np.arange(NZ)) % NZ) / NZ
    weight = np.where(kz == 0, 1.0, 2.0)[:, None]
    parts = [weight * np.cos(angle), -weight * np.sin(angle)]
    return bf16_pair(
        np.stack([p.reshape(dom_count, KH // dom_count, NZ) for p in parts], 1).reshape(2 * KH, NZ)
    )


def whole_spec(shape):
    return pl.BlockSpec(shape, lambda *_: (0,) * len(shape))


SMALL = pl.CostEstimate(flops=10**6, bytes_accessed=10**4, transcendentals=0)
SMEM = pl.BlockSpec(memory_space=pltpu.SMEM)


def params(mib):
    return pltpu.CompilerParams(vmem_limit_bytes=mib * MIB)


def swapped(value, axis, distance):
    if distance == 0:
        return value
    return lax.ppermute(value, axis, [(i, i ^ distance) for i in range(lax.axis_size(axis))])


def per_device(base_cells, offsets, charges, bias_coupling, counts, green):
    slabs = lax.axis_size("slab")
    doms = lax.axis_size("dom")
    slab = lax.axis_index("slab")
    dom = lax.axis_index("dom")
    atoms_local = charges.shape[0]
    cells_x = XD * slabs
    ky_local = NY // slabs
    kz_local = KH // doms
    slab_half = slabs // 2
    rows_local = NY // doms
    rows = ky_local + 8
    quarter_rows = ky_local // 2
    normalize = 1.0 / (cells_x * NY * NZ)
    upper = slab // slab_half
    place = jnp.stack(
        [slab * ky_local, dom * kz_local, upper * slab_half, upper, slab % slab_half, dom]
    ).astype(jnp.int32)

    vmem = pl.BlockSpec(memory_space=pltpu.VMEM)
    atoms = pl.pallas_call(
        pack_kernel,
        in_specs=[SMEM, vmem, vmem, vmem],
        out_specs=vmem,
        out_shape=jax.ShapeDtypeStruct((slabs * doms, 8, atoms_local), F32),
        name="pack",
    )(counts, base_cells, offsets, charges.reshape(1, atoms_local))
    gathered = lax.all_to_all(atoms, ("slab", "dom"), 0, 0, tiled=True)

    scaled = green * normalize
    own = jnp.concatenate([scaled[:, :quarter_rows], scaled[:, quarter_rows:]], 2)
    flipped = scaled[:, ::-1]
    flipped = jnp.concatenate([flipped[:, :quarter_rows], flipped[:, quarter_rows:]], 2)
    mirror = [(s, slabs - 1 - s) for s in range(slabs)]
    first_half = lax.ppermute(flipped[: cells_x // 2], "slab", mirror)
    gathered, late = lax.optimization_barrier((gathered, flipped[cells_x // 2 :]))
    second_half = lax.ppermute(late, "slab", mirror)

    spectrum = pl.pallas_call(
        forward_kernel,
        grid=(slabs,),
        in_specs=[SMEM, vmem],
        out_specs=vmem,
        out_shape=jax.ShapeDtypeStruct((4, cells_x, quarter_rows, LANES), F32),
        scratch_shapes=[
            pltpu.VMEM((SPAN, 4 * rows, doms * atoms_local), BF16),
            pltpu.VMEM((2 * LANES, doms * atoms_local), BF16),
            pltpu.VMEM((cells_x, 2 * rows, LANES), F32),
            pltpu.VMEM((2 * rows, doms * atoms_local), F32),
            pltpu.VMEM((8, doms * atoms_local), F32),
            pltpu.VMEM((6, rows, atoms_local), F32),
            pltpu.VMEM((6, LANES // 2, atoms_local), F32),
        ],
        compiler_params=params(40),
        cost_estimate=SMALL,
        name="forward",
    )(place, gathered)

    near_planes = cells_x // 2 + 3
    piece = (DEPTH, 4, quarter_rows, LANES)
    *pieces, near = pl.pallas_call(
        inverse_x_kernel,
        in_specs=[SMEM] + [vmem] * 4,
        out_specs=[vmem] * (CHUNKS * slab_half + 1),
        out_shape=[jax.ShapeDtypeStruct(piece, F32)] * (CHUNKS * slab_half)
        + [jax.ShapeDtypeStruct((near_planes, 4, quarter_rows, LANES), F32)],
        compiler_params=params(32),
        cost_estimate=SMALL,
        name="inverse_x",
    )(place, spectrum, own, first_half, second_half)

    atoms_slab = doms * atoms_local
    depth = -(-6 * rows // LANES) * LANES
    partial = pl.pallas_call(
        gather_kernel,
        grid=(slab_half,),
        in_specs=[SMEM, vmem, vmem],
        out_specs=vmem,
        out_shape=jax.ShapeDtypeStruct((slab_half, 1, atoms_slab), F32),
        scratch_shapes=[
            pltpu.VMEM((2 * rows, LANES), F32),
            pltpu.VMEM((near_planes, LANES, depth), BF16),
            pltpu.VMEM((depth, atoms_slab), BF16),
            pltpu.VMEM((2 * rows, atoms_local), F32),
            pltpu.VMEM((LANES, atoms_local), F32),
            pltpu.VMEM((6, rows, atoms_local), F32),
            pltpu.VMEM((6, LANES // 2, atoms_local), F32),
        ],
        compiler_params=params(32),
        cost_estimate=SMALL,
        name="gather",
    )(place, gathered, near.reshape(near_planes, 2 * ky_local, LANES))

    high_y, low_y = inverse_y_table(slab_half, ky_local)
    high_z, low_z = inverse_z_table(doms)
    potential = None
    for chunk in range(CHUNKS):
        lines = [
            swapped(value.reshape(DEPTH, 2 * ky_local, LANES), "slab", k)
            for k, value in enumerate(pieces[chunk * slab_half : (chunk + 1) * slab_half])
        ]
        if chunk == 0:
            partial, *lines = lax.optimization_barrier((partial, *lines))
        turned = pl.pallas_call(
            functools.partial(inverse_y_kernel, slab_half),
            in_specs=[SMEM] + [vmem] * (slab_half + 2),
            out_specs=[vmem] * doms,
            out_shape=[jax.ShapeDtypeStruct((DEPTH, rows_local, LANES), F32)] * doms,
            scratch_shapes=[
                pltpu.VMEM((slab_half, DEPTH, 2 * ky_local, LANES), F32),
                pltpu.VMEM((doms, DEPTH, rows_local, LANES), F32),
            ],
            compiler_params=params(24),
            cost_estimate=SMALL,
            name="inverse_y",
        )(place, *lines, high_y, low_y)
        if chunk == CHUNKS - 1:
            partial, *turned = lax.optimization_barrier((partial, *turned))
        columns = [swapped(value, "dom", k) for k, value in enumerate(turned)]
        earlier = [] if potential is None else [potential]
        potential = pl.pallas_call(
            functools.partial(inverse_z_kernel, doms),
            grid=(1,),
            in_specs=[SMEM]
            + [whole_spec((DEPTH, rows_local, LANES))] * doms
            + [whole_spec((2 * KH, NZ))] * 2
            + [pl.BlockSpec(memory_space=pl.ANY)] * len(earlier),
            out_specs=pl.BlockSpec((DEPTH, rows_local, NZ), lambda _, at=chunk: (at, 0, 0)),
            out_shape=jax.ShapeDtypeStruct((XD, rows_local, NZ), F32),
            scratch_shapes=[pltpu.VMEM((doms, DEPTH, rows_local, LANES), F32)],
            input_output_aliases={doms + 3: 0} if earlier else {},
            compiler_params=params(24),
            cost_estimate=SMALL,
            name="inverse_z",
        )(place, *columns, high_z, low_z, *earlier)

    members = slab_half * doms
    sampled = lax.all_to_all(
        partial.reshape(members, atoms_local),
        ("slab", "dom"),
        0,
        0,
        axis_index_groups=[list(range(members)), list(range(members, 2 * members))],
        tiled=True,
    )
    alive = jnp.arange(atoms_local, dtype=jnp.int32) < counts[0]
    gradient = jnp.where(alive, bias_coupling * jnp.sum(sampled, 0), 0.0)
    return (potential, gradient)


def solution(mesh):
    placed = (
        P(None, ("slab", "dom")),
        P(None, ("slab", "dom")),
        P(("slab", "dom")),
        P(("slab", "dom")),
        P(("slab", "dom")),
        P(None, "slab", "dom"),
    )
    return jax.shard_map(
        per_device,
        mesh=mesh,
        in_specs=placed,
        out_specs=(P("slab", "dom", None), P(("slab", "dom"))),
        check_vma=False,
    )
```

```python
import functools

import jax
import jax.numpy as jnp
import ml_dtypes
import numpy as np
from jax import lax
from jax.experimental import pallas as pl
from jax.experimental.pallas import tpu as pltpu
from jax.sharding import PartitionSpec as P

XD = 4
NY = 512
NZ = 512
KH = NZ // 2
LANES = 128
SPAN = XD + 3
CHUNKS = 2
DEPTH = XD // CHUNKS
MIB = 1 << 20
BF16 = jnp.bfloat16
F32 = jnp.float32


def polynomial(function, terms):
    nodes = 0.125 * (1.0 - np.cos(np.pi * (np.arange(64) + 0.5) / 64))
    powers = nodes[:, None] ** np.arange(terms)[None, :]
    return [float(v) for v in np.linalg.lstsq(powers, function(np.sqrt(nodes)), rcond=None)[0]]


SINE_TERMS = polynomial(lambda r: np.sin(np.pi * r) / r, 6)
COSINE_TERMS = polynomial(lambda r: np.cos(np.pi * r), 6)


def horner(terms, square):
    total = jnp.full_like(square, terms[-1])
    for term in terms[-2::-1]:
        total = total * square + term
    return total


def turn(fraction):
    left = fraction - jnp.floor(fraction + 0.5)
    square = left * left
    sine = left * horner(SINE_TERMS, square)
    cosine = horner(COSINE_TERMS, square)
    return 1.0 - 2.0 * sine * sine, 2.0 * sine * cosine


def spline(frac):
    inner = 1.0 - frac
    square = frac * frac
    cube = square * frac
    sixth = 1.0 / 6.0
    return (
        inner * inner * inner * sixth,
        (3.0 * cube - 6.0 * square + 4.0) * sixth,
        (-3.0 * cube + 3.0 * square + 3.0 * frac + 1.0) * sixth,
        cube * sixth,
    )


def split(value):
    high = value.astype(BF16)
    return high, (value - high.astype(F32)).astype(BF16)


def iota(shape, axis):
    return lax.broadcasted_iota(jnp.int32, shape, axis).astype(F32)


RADIX = 16
DIGITS = 32
TERMS = 256


def wave_factors(first, rows, length):
    lane = lax.broadcasted_iota(jnp.int32, (rows, TERMS), 1)
    section = lane // DIGITS
    digit = (lane % DIGITS).astype(F32) * jnp.where(section < 2, float(RADIX), 1.0)
    parts = []
    for value in turn((first + iota((rows, TERMS), 0)) * digit * (1.0 / length)):
        high = value.astype(BF16).astype(F32)
        parts.append(jnp.where((section == 1) | (section == 3), value - high, high))
    upper, lower = section < 2, (section >= 2) & (section < 5)
    masked = [jnp.where(mask, part, 0.0) for mask in (upper, lower) for part in parts]
    return jnp.concatenate(masked, 0).astype(BF16)


def wave_kernel(place_ref, out_y_ref, out_z_ref):
    out_y_ref[...] = wave_factors(place_ref[0].astype(F32), out_y_ref.shape[0] // 4, NY)
    out_z_ref[...] = wave_factors(place_ref[1].astype(F32), out_z_ref.shape[0] // 4, NZ)


def atom_waves(base, weights, factors_ref, digits_ref):
    width = base.shape[1]
    high_digit = jnp.floor(base * (1.0 / RADIX))
    row = iota((DIGITS, width), 0)
    chosen = jnp.where(row == high_digit, 1.0, 0.0).astype(BF16)
    step = row - (base - RADIX * high_digit)
    spread = jnp.where(step == 3.0, weights[3], 0.0)
    for r in (2, 1, 0):
        spread = jnp.where(step == float(r), weights[r], spread)
    high, low = split(spread)
    for section, value in enumerate((chosen, chosen, high, high, low)):
        digits_ref[pl.ds(DIGITS * section, DIGITS), :] = value
    product = jnp.dot(factors_ref[...], digits_ref[...], preferred_element_type=F32)
    rows = product.shape[0] // 4
    cos_a, sin_a, cos_b, sin_b = (product[i * rows : (i + 1) * rows] for i in range(4))
    return cos_a * cos_b - sin_a * sin_b, sin_a * cos_b + cos_a * sin_b


def plane_weights(atoms, weights):
    row = iota((8, atoms.shape[1]), 0) - atoms[0:1]
    return sum(weights[r][3:4] * (row == float(r)).astype(F32) for r in range(4))


def swap(value):
    return pltpu.roll(value, LANES // 2, axis=value.ndim - 1)


def half_sign():
    lane = lax.broadcasted_iota(jnp.int32, (1, LANES), 1)
    return jnp.where(lane < LANES // 2, -1.0, 1.0).astype(F32)


def rotate(value, numer, denom, sign, halves):
    if numer == 0:
        return value
    if 4 * numer == denom:
        return swap(value) * (halves * sign)
    angle = 2.0 * np.pi * numer / denom
    return value * float(np.cos(angle)) + swap(value) * (halves * float(sign * np.sin(angle)))


def transform(values, sign, halves):
    count = len(values)
    if count == 1:
        return values
    even = transform(values[0::2], sign, halves)
    odd = transform(values[1::2], sign, halves)
    turned = [rotate(odd[k], k, count, sign, halves) for k in range(count // 2)]
    return [e + t for e, t in zip(even, turned)] + [e - t for e, t in zip(even, turned)]


def pack_kernel(counts_ref, cells_ref, offsets_ref, charges_ref, out_ref):
    width = offsets_ref.shape[1]
    alive = lax.broadcasted_iota(jnp.int32, (1, width), 1) < counts_ref[0]
    atoms = jnp.concatenate(
        [
            lax.bitwise_and(cells_ref[0:1, :], XD - 1).astype(F32),
            cells_ref[1:3, :].astype(F32),
            offsets_ref[...],
            jnp.where(alive, charges_ref[...], 0.0),
            jnp.zeros((1, width), F32),
        ],
        0,
    )
    for copy in range(out_ref.shape[0]):
        out_ref[copy] = atoms


def atoms_of(refs, slab, slot, doms):
    half = doms // 2
    return refs[slot // half][slab * half + slot % half]


def forward_kernel(
    place_ref,
    same_ref,
    other_ref,
    factors_y,
    factors_z,
    out_ref,
    table_y,
    table_z,
    left_ref,
    right_ref,
    grid_ref,
    along_ref,
    digits_y,
    digits_z,
):
    step = pl.program_id(0)
    cells_x = grid_ref.shape[0]
    rows = grid_ref.shape[1] // 2
    ky_local = rows - 8
    width = same_ref.shape[2]
    doms = table_y.shape[2] // width
    kept = step - place_ref[2]
    kept = jnp.where((kept >= 0) & (kept < table_y.shape[0] - 1), kept, table_y.shape[0] - 1)

    @pl.when(step == 0)
    def _():
        grid_ref[...] = jnp.zeros_like(grid_ref)
        digits_y[...] = jnp.zeros_like(digits_y)
        digits_z[...] = jnp.zeros_like(digits_z)

    for slot in range(doms):
        atoms = atoms_of((same_ref, other_ref), step, slot, doms)
        lanes = pl.ds(slot * width, width)
        weights = spline(atoms)
        along_ref[:, lanes] = plane_weights(atoms, weights) * atoms[6:7]
        waves = atom_waves(atoms[2:3], [w[5:6] for w in weights], factors_z, digits_z.at[slot])
        waves = jnp.concatenate(waves, 0)
        table_z[kept, :, lanes] = waves
        high, low = split(waves.T)
        right_ref[lanes, :LANES] = high
        right_ref[lanes, LANES:] = low
        cosine, sine = atom_waves(atoms[1:2], [w[4:5] for w in weights], factors_y, digits_y.at[slot])
        table_y[kept, pl.ds(0, rows), lanes] = cosine
        table_y[kept, pl.ds(rows, rows), lanes] = sine

    for plane in range(SPAN):
        for slot in range(doms):
            lanes = pl.ds(slot * width, width)
            along = along_ref[plane : plane + 1, lanes]
            high, low = split(table_y[kept, :, lanes] * along)
            left_ref[plane, pl.ds(0, 2 * rows), lanes] = high
            left_ref[plane, pl.ds(2 * rows, 2 * rows), lanes] = low
        product = jnp.dot(left_ref[plane], right_ref[...], preferred_element_type=F32)
        high, low = product[: 2 * rows], product[2 * rows :]
        at = lax.rem(step * XD + plane, cells_x)
        grid_ref[at] += (high[:, :LANES] + high[:, LANES:]) + (low[:, :LANES] + low[:, LANES:])

    @pl.when(step == pl.num_programs(0) - 1)
    def _():
        halves = half_sign()
        quarter_rows = ky_local // 2
        group = min(8, quarter_rows)
        for minus in (0, 1):
            for start in range(0, ky_local, group):
                row = start + minus
                values = []
                for x in range(cells_x):
                    top = grid_ref[x, pl.ds(row, group), :]
                    bottom = swap(grid_ref[x, pl.ds(rows + row, group), :])
                    values.append(bottom - top * halves if minus else -bottom - top * halves)
                at = 2 * minus + start // quarter_rows
                for x, value in enumerate(transform(values, -1.0, halves)):
                    out_ref[at, x, pl.ds(start % quarter_rows, group), :] = value


def inverse_x_kernel(place_ref, spectrum_ref, own_ref, first_ref, second_ref, *refs):
    *outs, near_ref = refs
    slab_half = len(outs) // CHUNKS
    cells_x, quarter_rows = spectrum_ref.shape[1:3]
    group = min(8, quarter_rows)
    halves = half_sign()
    lane = lax.broadcasted_iota(jnp.int32, (1, LANES), 1)
    side = 1.0 - 2.0 * place_ref[3].astype(F32)

    def rows_of(step, carry):
        rows = pl.ds(pl.multiple_of(step * group, group), group)
        for quarter in range(4):
            values = []
            for kx in range(cells_x):
                if quarter < 2:
                    green = own_ref[kx, rows, :]
                elif kx < first_ref.shape[0]:
                    green = first_ref[kx, rows, :]
                else:
                    green = second_ref[kx - first_ref.shape[0], rows, :]
                keep = lane < LANES // 2 if quarter % 2 == 0 else lane >= LANES // 2
                values.append(spectrum_ref[quarter, kx, rows, :] * jnp.where(keep, green, swap(green)))
            even = transform(values[0::2], 1.0, halves)
            odd = transform(values[1::2], 1.0, halves)
            for x in range(cells_x // 2):
                turned = rotate(odd[x], x, cells_x, 1.0, halves) * side
                near_ref[x, quarter, rows, :] = even[x] + turned
                if x < 3:
                    near_ref[cells_x // 2 + x, quarter, rows, :] = even[x] - turned
        return carry

    lax.fori_loop(0, quarter_rows // group, rows_of, 0)
    for chunk in range(CHUNKS):
        for k in range(slab_half):
            partner = lax.bitwise_xor(place_ref[4], k)
            outs[chunk * slab_half + k][...] = near_ref[pl.ds(partner * XD + chunk * DEPTH, DEPTH)]


def inverse_y_kernel(sources, place_ref, *refs):
    ins, (high_ref, low_ref) = refs[:sources], refs[sources : sources + 2]
    outs, (lines_ref, turned_ref) = refs[sources + 2 : -2], refs[-2:]
    for k in range(sources):
        lines_ref[lax.bitwise_xor(place_ref[4], k)] = ins[k][...]
    parts = []
    for x in range(DEPTH):
        lines = jnp.concatenate([lines_ref[source, x] for source in range(sources)], 0)
        pairs = jnp.concatenate([lines, swap(lines) * half_sign()], 0)
        parts.append(split(pairs))
    both = jnp.concatenate([value for part in parts for value in part], 1)
    main = jnp.dot(high_ref[...], both, preferred_element_type=F32)
    high = jnp.concatenate([part[0] for part in parts], 1)
    rest = jnp.dot(low_ref[...], high, preferred_element_type=F32)
    row = lax.broadcasted_iota(jnp.int32, (NY, 1), 0)
    sign = jnp.where((row % 2 == 1) & (place_ref[3] == 1), -1.0, 1.0)
    for x in range(DEPTH):
        total = main[:, 2 * x * LANES : (2 * x + 1) * LANES] + main[:, (2 * x + 1) * LANES : (2 * x + 2) * LANES]
        total = (total + rest[:, x * LANES : (x + 1) * LANES]) * sign
        turned_ref[:, x] = total.reshape(len(outs), -1, LANES)
    for k in range(len(outs)):
        outs[k][...] = turned_ref[lax.bitwise_xor(place_ref[5], k)]


def inverse_z_kernel(sources, place_ref, *refs):
    ins, (high_ref, low_ref) = refs[:sources], refs[sources : sources + 2]
    out_ref, lines_ref = refs[-2:]
    for k in range(sources):
        lines_ref[lax.bitwise_xor(place_ref[5], k)] = ins[k][...]
    for x in range(DEPTH):
        lines = jnp.concatenate([lines_ref[source, x] for source in range(sources)], 1)
        high, low = split(lines)
        total = jnp.dot(high, high_ref[...], preferred_element_type=F32)
        total += jnp.dot(low, high_ref[...], preferred_element_type=F32)
        total += jnp.dot(high, low_ref[...], preferred_element_type=F32)
        out_ref[x] = total


def gather_kernel(
    place_ref, same_ref, other_ref, table_y, table_z, near_ref, out_ref, shift_ref, fields_ref, stack_ref
):
    step = pl.program_id(0)
    half = LANES // 2
    rows = table_y.shape[1] // 2
    ky_local = rows - 8
    width = same_ref.shape[2]
    doms = table_y.shape[2] // width
    planes = near_ref.shape[0]
    halves = half_sign()

    @pl.when(step == 0)
    def _():
        stack_ref[...] = jnp.zeros_like(stack_ref)
        shift_ref[...] = jnp.zeros_like(shift_ref)
        row = lax.broadcasted_iota(jnp.int32, (8, LANES), 0)

        def build(x, carry):
            plus = near_ref[x, pl.ds(0, ky_local), :]
            shift_ref[pl.ds(1, ky_local), :] = near_ref[x, pl.ds(ky_local, ky_local), :]
            minus = shift_ref[pl.ds(0, ky_local), :]
            last = shift_ref[pl.ds(ky_local, 8), :][0:1]
            main = [plus + minus, swap(plus - minus) * halves]
            if 2 * ky_local < LANES:
                main.append(jnp.zeros((LANES - 2 * ky_local, LANES), F32))
            rest = jnp.where(row % 2 == 0, last, -swap(jnp.broadcast_to(last, (8, LANES))) * halves)
            rest = jnp.where(row < 6, rest, 0.0)
            rest_high = rest.astype(BF16).astype(F32)
            rest = jnp.where((row == 2) | (row == 3), rest - rest_high, rest_high)
            high, low = split(jnp.concatenate(main, 0).T)
            fields_ref[x, :, pl.ds(0, LANES)] = high
            fields_ref[x, :, pl.ds(LANES, LANES)] = low
            fields_ref[x, :, pl.ds(2 * LANES, LANES)] = high
            rest = jnp.concatenate([rest, jnp.zeros((LANES - 8, LANES), F32)], 0)
            fields_ref[x, :, pl.ds(3 * LANES, LANES)] = rest.T.astype(BF16)
            return carry

        lax.fori_loop(0, planes, build, 0)

    first_z = place_ref[1].astype(F32)
    twice = jnp.where(first_z + iota((half, 1), 0) == 0.0, 1.0, 2.0)
    fields = fields_ref[pl.ds(step * XD, SPAN)].reshape(SPAN * LANES, 4 * LANES)
    for slot in range(doms):
        atoms = atoms_of((same_ref, other_ref), place_ref[2] + step, slot, doms)
        along_x = plane_weights(atoms, spline(atoms))
        lanes = pl.ds(slot * width, width)
        cosine = table_y[step, pl.ds(0, ky_local), lanes]
        sine = table_y[step, pl.ds(rows, ky_local), lanes]
        high, low = split(jnp.concatenate([cosine, sine], 0))
        for part, value in enumerate((high, high, low)):
            stack_ref[slot, pl.ds(LANES * part, 2 * ky_local), :] = value
        cosine = table_y[step, pl.ds(ky_local, 8), lanes][0:1]
        sine = table_y[step, pl.ds(rows + ky_local, 8), lanes][0:1]
        row = lax.broadcasted_iota(jnp.int32, (16, width), 0)
        rest = jnp.where(row % 2 == 0, cosine, sine)
        rest_high = rest.astype(BF16).astype(F32)
        rest = jnp.where(row < 4, rest_high, jnp.where(row < 6, rest - rest_high, 0.0))
        stack_ref[slot, pl.ds(3 * LANES, 16), :] = rest.astype(BF16)
        field = jnp.dot(fields, stack_ref[slot], preferred_element_type=F32)
        total = along_x[0:1] * field[:LANES]
        for plane in range(1, SPAN):
            total += along_x[plane : plane + 1] * field[plane * LANES : (plane + 1) * LANES]
        waves = total * table_z[step, :, lanes]
        sampled = jnp.sum((waves[:half] - waves[half:]) * twice, axis=0, keepdims=True)
        core = place_ref[5] % 2 if slot < doms // 2 else 1 - place_ref[5] % 2
        out_ref[step * doms + 2 * (slot % (doms // 2)) + core] = sampled


def bf16_pair(table):
    high = table.astype(ml_dtypes.bfloat16)
    low = (table - high.astype(np.float64)).astype(ml_dtypes.bfloat16)
    return jnp.asarray(high), jnp.asarray(low)


def inverse_y_table(slab_half, ky_local):
    waves = []
    for slab in range(slab_half):
        first = slab * ky_local
        waves += [first + i for i in range(ky_local)] + [-(first + i + 1) for i in range(ky_local)]
    angle = 2.0 * np.pi * (np.outer(np.arange(NY), np.array(waves)) % NY) / NY
    return bf16_pair(np.concatenate([np.cos(angle), np.sin(angle)], 1))


def inverse_z_table(dom_count):
    kz = np.arange(KH)
    angle = 2.0 * np.pi * (np.outer(kz, np.arange(NZ)) % NZ) / NZ
    weight = np.where(kz == 0, 1.0, 2.0)[:, None]
    parts = [weight * np.cos(angle), -weight * np.sin(angle)]
    return bf16_pair(
        np.stack([p.reshape(dom_count, KH // dom_count, NZ) for p in parts], 1).reshape(2 * KH, NZ)
    )


def whole_spec(shape):
    return pl.BlockSpec(shape, lambda *_: (0,) * len(shape))


SMALL = pl.CostEstimate(flops=10**6, bytes_accessed=10**4, transcendentals=0)
SMEM = pl.BlockSpec(memory_space=pltpu.SMEM)


def params(mib):
    return pltpu.CompilerParams(vmem_limit_bytes=mib * MIB)


def swapped(value, axis, distance):
    if distance == 0:
        return value
    return lax.ppermute(value, axis, [(i, i ^ distance) for i in range(lax.axis_size(axis))])


def per_device(base_cells, offsets, charges, bias_coupling, counts, green):
    slabs = lax.axis_size("slab")
    doms = lax.axis_size("dom")
    slab = lax.axis_index("slab")
    dom = lax.axis_index("dom")
    atoms_local = charges.shape[0]
    cells_x = XD * slabs
    ky_local = NY // slabs
    kz_local = KH // doms
    slab_half = slabs // 2
    rows_local = NY // doms
    rows = ky_local + 8
    quarter_rows = ky_local // 2
    normalize = 1.0 / (cells_x * NY * NZ)
    upper = slab // slab_half
    place = jnp.stack(
        [slab * ky_local, dom * kz_local, upper * slab_half, upper, slab % slab_half, dom]
    ).astype(jnp.int32)

    vmem = pl.BlockSpec(memory_space=pltpu.VMEM)
    atoms = pl.pallas_call(
        pack_kernel,
        in_specs=[SMEM, vmem, vmem, vmem],
        out_specs=vmem,
        out_shape=jax.ShapeDtypeStruct((slabs * doms // 2, 8, atoms_local), F32),
        name="pack",
    )(counts, base_cells, offsets, charges.reshape(1, atoms_local))
    everyone = list(range(slabs * doms))
    same = lax.all_to_all(
        atoms, ("slab", "dom"), 0, 0, axis_index_groups=[everyone[0::2], everyone[1::2]], tiled=True
    )
    other = swapped(same, "dom", 1)

    early = cells_x * 3 // 8
    mirror = [(s, slabs - 1 - s) for s in range(slabs)]

    def halves_beside(value):
        return jnp.concatenate([value[:, :quarter_rows], value[:, quarter_rows:]], 2) * normalize

    own = halves_beside(green)
    first_part = lax.ppermute(halves_beside(green[:early, ::-1]), "slab", mirror)
    same, late = lax.optimization_barrier((same, halves_beside(green[early:, ::-1])))
    second_part = lax.ppermute(late, "slab", mirror)

    factors_y, factors_z = pl.pallas_call(
        wave_kernel,
        in_specs=[SMEM],
        out_specs=[vmem] * 2,
        out_shape=[jax.ShapeDtypeStruct((4 * count, TERMS), BF16) for count in (rows, LANES // 2)],
        name="waves",
    )(place)
    atoms_slab = doms * atoms_local
    table_bytes = 4 * (slab_half + 1) * (2 * rows + LANES) * atoms_slab
    spectrum_bytes = 16 * cells_x * max(8, quarter_rows) * LANES
    spectrum, table_y, table_z = pl.pallas_call(
        forward_kernel,
        grid=(slabs,),
        in_specs=[SMEM] + [vmem] * 4,
        out_specs=[vmem] * 3,
        out_shape=[
            jax.ShapeDtypeStruct((4, cells_x, quarter_rows, LANES), F32),
            jax.ShapeDtypeStruct((slab_half + 1, 2 * rows, atoms_slab), F32),
            jax.ShapeDtypeStruct((slab_half + 1, LANES, atoms_slab), F32),
        ],
        scratch_shapes=[
            pltpu.VMEM((SPAN, 4 * rows, atoms_slab), BF16),
            pltpu.VMEM((atoms_slab, 2 * LANES), BF16),
            pltpu.VMEM((cells_x, 2 * rows, LANES), F32),
            pltpu.VMEM((8, atoms_slab), F32),
            pltpu.VMEM((doms, TERMS, atoms_local), BF16),
            pltpu.VMEM((doms, TERMS, atoms_local), BF16),
        ],
        compiler_params=params(16 + (table_bytes + spectrum_bytes) // MIB),
        cost_estimate=SMALL,
        name="forward",
    )(place, same, other, factors_y, factors_z)

    near_planes = cells_x // 2 + 3
    piece = (DEPTH, 4, quarter_rows, LANES)
    *pieces, near = pl.pallas_call(
        inverse_x_kernel,
        in_specs=[SMEM] + [vmem] * 4,
        out_specs=[vmem] * (CHUNKS * slab_half + 1),
        out_shape=[jax.ShapeDtypeStruct(piece, F32)] * (CHUNKS * slab_half)
        + [jax.ShapeDtypeStruct((near_planes, 4, quarter_rows, LANES), F32)],
        compiler_params=params(32),
        cost_estimate=SMALL,
        name="inverse_x",
    )(place, spectrum, own, first_part, second_part)

    partial = pl.pallas_call(
        gather_kernel,
        grid=(slab_half,),
        in_specs=[SMEM] + [vmem] * 5,
        out_specs=vmem,
        out_shape=jax.ShapeDtypeStruct((slab_half * doms, 1, atoms_local), F32),
        scratch_shapes=[
            pltpu.VMEM((rows, LANES), F32),
            pltpu.VMEM((near_planes, LANES, 4 * LANES), BF16),
            pltpu.VMEM((doms, 4 * LANES, atoms_local), BF16),
        ],
        compiler_params=params(8 + (table_bytes + 8 * near_planes * LANES * LANES) // MIB),
        cost_estimate=SMALL,
        name="gather",
    )(place, same, other, table_y, table_z, near.reshape(near_planes, 2 * ky_local, LANES))

    high_y, low_y = inverse_y_table(slab_half, ky_local)
    high_z, low_z = inverse_z_table(doms)
    potential = None
    for chunk in range(CHUNKS):
        lines = [
            swapped(value.reshape(DEPTH, 2 * ky_local, LANES), "slab", k)
            for k, value in enumerate(pieces[chunk * slab_half : (chunk + 1) * slab_half])
        ]
        if chunk == 0:
            partial, *lines = lax.optimization_barrier((partial, *lines))
        turned = pl.pallas_call(
            functools.partial(inverse_y_kernel, slab_half),
            in_specs=[SMEM] + [vmem] * (slab_half + 2),
            out_specs=[vmem] * doms,
            out_shape=[jax.ShapeDtypeStruct((DEPTH, rows_local, LANES), F32)] * doms,
            scratch_shapes=[
                pltpu.VMEM((slab_half, DEPTH, 2 * ky_local, LANES), F32),
                pltpu.VMEM((doms, DEPTH, rows_local, LANES), F32),
            ],
            compiler_params=params(24),
            cost_estimate=SMALL,
            name="inverse_y",
        )(place, *lines, high_y, low_y)
        if chunk == CHUNKS - 1:
            partial, *turned = lax.optimization_barrier((partial, *turned))
        columns = [swapped(value, "dom", k) for k, value in enumerate(turned)]
        earlier = [] if potential is None else [potential]
        potential = pl.pallas_call(
            functools.partial(inverse_z_kernel, doms),
            grid=(1,),
            in_specs=[SMEM]
            + [whole_spec((DEPTH, rows_local, LANES))] * doms
            + [whole_spec((2 * KH, NZ))] * 2
            + [pl.BlockSpec(memory_space=pl.ANY)] * len(earlier),
            out_specs=pl.BlockSpec((DEPTH, rows_local, NZ), lambda _, at=chunk: (at, 0, 0)),
            out_shape=jax.ShapeDtypeStruct((XD, rows_local, NZ), F32),
            scratch_shapes=[pltpu.VMEM((doms, DEPTH, rows_local, LANES), F32)],
            input_output_aliases={doms + 3: 0} if earlier else {},
            compiler_params=params(24),
            cost_estimate=SMALL,
            name="inverse_z",
        )(place, *columns, high_z, low_z, *earlier)

    members = slab_half * doms
    sampled = lax.all_to_all(
        partial.reshape(members, atoms_local),
        ("slab", "dom"),
        0,
        0,
        axis_index_groups=[list(range(members)), list(range(members, 2 * members))],
        tiled=True,
    )
    alive = jnp.arange(atoms_local, dtype=jnp.int32) < counts[0]
    gradient = jnp.where(alive, bias_coupling * jnp.sum(sampled, 0), 0.0)
    return (potential, gradient)


def solution(mesh):
    placed = (
        P(None, ("slab", "dom")),
        P(None, ("slab", "dom")),
        P(("slab", "dom")),
        P(("slab", "dom")),
        P(("slab", "dom")),
        P(None, "slab", "dom"),
    )
    return jax.shard_map(
        per_device,
        mesh=mesh,
        in_specs=placed,
        out_specs=(P("slab", "dom", None), P(("slab", "dom"))),
        check_vma=False,
    )
```

```python
import functools

import jax
import jax.numpy as jnp
import ml_dtypes
import numpy as np
from jax import lax
from jax.experimental import pallas as pl
from jax.experimental.pallas import tpu as pltpu
from jax.sharding import PartitionSpec as P

XD = 4
NY = 512
NZ = 512
KH = NZ // 2
LANES = 128
SPAN = XD + 3
CHUNKS = 2
DEPTH = XD // CHUNKS
MIB = 1 << 20
BF16 = jnp.bfloat16
F32 = jnp.float32


def polynomial(function, terms):
    nodes = 0.125 * (1.0 - np.cos(np.pi * (np.arange(64) + 0.5) / 64))
    powers = nodes[:, None] ** np.arange(terms)[None, :]
    return [float(v) for v in np.linalg.lstsq(powers, function(np.sqrt(nodes)), rcond=None)[0]]


SINE_TERMS = polynomial(lambda r: np.sin(np.pi * r) / r, 6)
COSINE_TERMS = polynomial(lambda r: np.cos(np.pi * r), 6)


def horner(terms, square):
    total = jnp.full_like(square, terms[-1])
    for term in terms[-2::-1]:
        total = total * square + term
    return total


def turn(fraction):
    left = fraction - jnp.floor(fraction + 0.5)
    square = left * left
    sine = left * horner(SINE_TERMS, square)
    cosine = horner(COSINE_TERMS, square)
    return 1.0 - 2.0 * sine * sine, 2.0 * sine * cosine


def spline(frac):
    inner = 1.0 - frac
    square = frac * frac
    cube = square * frac
    sixth = 1.0 / 6.0
    return (
        inner * inner * inner * sixth,
        (3.0 * cube - 6.0 * square + 4.0) * sixth,
        (-3.0 * cube + 3.0 * square + 3.0 * frac + 1.0) * sixth,
        cube * sixth,
    )


def split(value):
    high = value.astype(BF16)
    return high, (value - high.astype(F32)).astype(BF16)


def iota(shape, axis):
    return lax.broadcasted_iota(jnp.int32, shape, axis).astype(F32)


RADIX = 16
DIGITS = 32
TERMS = 256


def wave_factors(first, rows, length):
    lane = lax.broadcasted_iota(jnp.int32, (rows, TERMS), 1)
    section = lane // DIGITS
    digit = (lane % DIGITS).astype(F32) * jnp.where(section < 2, float(RADIX), 1.0)
    parts = []
    for value in turn((first + iota((rows, TERMS), 0)) * digit * (1.0 / length)):
        high = value.astype(BF16).astype(F32)
        parts.append(jnp.where((section == 1) | (section == 3), value - high, high))
    upper, lower = section < 2, (section >= 2) & (section < 5)
    masked = [jnp.where(mask, part, 0.0) for mask in (upper, lower) for part in parts]
    return jnp.concatenate(masked, 0).astype(BF16)


def wave_kernel(place_ref, out_y_ref, out_z_ref):
    out_y_ref[...] = wave_factors(place_ref[0].astype(F32), out_y_ref.shape[0] // 4, NY)
    out_z_ref[...] = wave_factors(place_ref[1].astype(F32), out_z_ref.shape[0] // 4, NZ)


def atom_waves(base, weights, factors_ref, digits_ref):
    width = base.shape[1]
    high_digit = jnp.floor(base * (1.0 / RADIX))
    row = iota((DIGITS, width), 0)
    chosen = jnp.where(row == high_digit, 1.0, 0.0).astype(BF16)
    step = row - (base - RADIX * high_digit)
    spread = jnp.where(step == 3.0, weights[3], 0.0)
    for r in (2, 1, 0):
        spread = jnp.where(step == float(r), weights[r], spread)
    high, low = split(spread)
    for section, value in enumerate((chosen, chosen, high, high, low)):
        digits_ref[pl.ds(DIGITS * section, DIGITS), :] = value
    product = jnp.dot(factors_ref[...], digits_ref[...], preferred_element_type=F32)
    rows = product.shape[0] // 4
    cos_a, sin_a, cos_b, sin_b = (product[i * rows : (i + 1) * rows] for i in range(4))
    return cos_a * cos_b - sin_a * sin_b, sin_a * cos_b + cos_a * sin_b


def plane_weights(atoms, weights):
    row = iota((8, atoms.shape[1]), 0) - atoms[0:1]
    return sum(weights[r][3:4] * (row == float(r)).astype(F32) for r in range(4))


def swap(value):
    return pltpu.roll(value, LANES // 2, axis=value.ndim - 1)


def half_sign():
    lane = lax.broadcasted_iota(jnp.int32, (1, LANES), 1)
    return jnp.where(lane < LANES // 2, -1.0, 1.0).astype(F32)


def rotate(value, numer, denom, sign, halves):
    if numer == 0:
        return value
    if 4 * numer == denom:
        return swap(value) * (halves * sign)
    angle = 2.0 * np.pi * numer / denom
    return value * float(np.cos(angle)) + swap(value) * (halves * float(sign * np.sin(angle)))


def transform(values, sign, halves):
    count = len(values)
    if count == 1:
        return values
    even = transform(values[0::2], sign, halves)
    odd = transform(values[1::2], sign, halves)
    turned = [rotate(odd[k], k, count, sign, halves) for k in range(count // 2)]
    return [e + t for e, t in zip(even, turned)] + [e - t for e, t in zip(even, turned)]


def pack_kernel(counts_ref, cells_ref, offsets_ref, charges_ref, out_ref):
    width = offsets_ref.shape[1]
    alive = lax.broadcasted_iota(jnp.int32, (1, width), 1) < counts_ref[0]
    atoms = jnp.concatenate(
        [
            lax.bitwise_and(cells_ref[0:1, :], XD - 1).astype(F32),
            cells_ref[1:3, :].astype(F32),
            offsets_ref[...],
            jnp.where(alive, charges_ref[...], 0.0),
            jnp.zeros((1, width), F32),
        ],
        0,
    )
    for copy in range(out_ref.shape[0]):
        out_ref[copy] = atoms


def exchange_order(slabs, doms):
    steps = [("slab", slabs >> (i + 1)) for i in range(slabs.bit_length() - 1)]
    return steps + [("dom", doms >> (i + 1)) for i in range(doms.bit_length() - 2)]


def atoms_of(refs, distance, slot, slabs, doms):
    half = doms // 2
    bits = slabs.bit_length() - 1
    at = sum(((distance >> (bits - 1 - i)) & 1) << i for i in range(bits))
    number = slot % half
    dom_bits = doms.bit_length() - 2
    dom_distance = sum(((number >> i) & 1) * (doms >> (i + 1)) for i in range(dom_bits))
    return refs[slot // half][number * slabs + at], dom_distance ^ (slot // half)


def forward_kernel(
    place_ref,
    same_ref,
    other_ref,
    factors_y,
    factors_z,
    out_ref,
    table_y,
    table_z,
    left_ref,
    right_ref,
    grid_ref,
    along_ref,
    digits_y,
    digits_z,
):
    step = pl.program_id(0)
    cells_x = grid_ref.shape[0]
    rows = grid_ref.shape[1] // 2
    ky_local = rows - 8
    width = same_ref.shape[2]
    doms = table_y.shape[2] // width
    slabs = cells_x // XD
    slab = lax.bitwise_xor(place_ref[6], step)
    kept = slab - place_ref[2]
    kept = jnp.where((kept >= 0) & (kept < table_y.shape[0] - 1), kept, table_y.shape[0] - 1)

    @pl.when(step == 0)
    def _():
        grid_ref[...] = jnp.zeros_like(grid_ref)
        digits_y[...] = jnp.zeros_like(digits_y)
        digits_z[...] = jnp.zeros_like(digits_z)

    for slot in range(doms):
        atoms, _ = atoms_of((same_ref, other_ref), step, slot, slabs, doms)
        lanes = pl.ds(slot * width, width)
        weights = spline(atoms)
        along_ref[:, lanes] = plane_weights(atoms, weights) * atoms[6:7]
        waves = atom_waves(atoms[2:3], [w[5:6] for w in weights], factors_z, digits_z.at[slot])
        waves = jnp.concatenate(waves, 0)
        table_z[kept, :, lanes] = waves
        high, low = split(waves.T)
        right_ref[lanes, :LANES] = high
        right_ref[lanes, LANES:] = low
        cosine, sine = atom_waves(atoms[1:2], [w[4:5] for w in weights], factors_y, digits_y.at[slot])
        table_y[kept, pl.ds(0, rows), lanes] = cosine
        table_y[kept, pl.ds(rows, rows), lanes] = sine

    for plane in range(SPAN):
        first = 4 * rows * plane
        for slot in range(doms):
            lanes = pl.ds(slot * width, width)
            along = along_ref[plane : plane + 1, lanes]
            high, low = split(table_y[kept, :, lanes] * along)
            left_ref[pl.ds(first, 2 * rows), lanes] = high
            left_ref[pl.ds(first + 2 * rows, 2 * rows), lanes] = low
    product = jnp.dot(left_ref[...], right_ref[...], preferred_element_type=F32)
    for plane in range(SPAN):
        first = 4 * rows * plane
        high, low = product[first : first + 2 * rows], product[first + 2 * rows : first + 4 * rows]
        at = lax.rem(slab * XD + plane, cells_x)
        grid_ref[at] += (high[:, :LANES] + high[:, LANES:]) + (low[:, :LANES] + low[:, LANES:])

    @pl.when(step == pl.num_programs(0) - 1)
    def _():
        halves = half_sign()
        quarter_rows = ky_local // 2
        group = min(8, quarter_rows)
        for minus in (0, 1):
            for start in range(0, ky_local, group):
                row = start + minus
                values = []
                for x in range(cells_x):
                    top = grid_ref[x, pl.ds(row, group), :]
                    bottom = swap(grid_ref[x, pl.ds(rows + row, group), :])
                    values.append(bottom - top * halves if minus else -bottom - top * halves)
                at = 2 * minus + start // quarter_rows
                for x, value in enumerate(transform(values, -1.0, halves)):
                    out_ref[at, x, pl.ds(start % quarter_rows, group), :] = value


def inverse_x_kernel(place_ref, spectrum_ref, own_ref, first_ref, second_ref, *refs):
    *outs, near_ref = refs
    cells_x, quarter_rows = spectrum_ref.shape[1:3]
    group = min(8, quarter_rows)
    halves = half_sign()
    lane = lax.broadcasted_iota(jnp.int32, (1, LANES), 1)
    side = 1.0 - 2.0 * place_ref[3].astype(F32)

    def rows_of(step, carry):
        rows = pl.ds(pl.multiple_of(step * group, group), group)
        for quarter in range(4):
            values = []
            for kx in range(cells_x):
                if quarter < 2:
                    green = own_ref[kx, rows, :]
                elif kx < first_ref.shape[0]:
                    green = first_ref[kx, rows, :]
                else:
                    green = second_ref[kx - first_ref.shape[0], rows, :]
                keep = lane < LANES // 2 if quarter % 2 == 0 else lane >= LANES // 2
                values.append(spectrum_ref[quarter, kx, rows, :] * jnp.where(keep, green, swap(green)))
            even = transform(values[0::2], 1.0, halves)
            odd = transform(values[1::2], 1.0, halves)
            for x in range(cells_x // 2):
                turned = rotate(odd[x], x, cells_x, 1.0, halves) * side
                near_ref[x, quarter, rows, :] = even[x] + turned
                if x < 3:
                    near_ref[cells_x // 2 + x, quarter, rows, :] = even[x] - turned
        return carry

    lax.fori_loop(0, quarter_rows // group, rows_of, 0)
    for k, out_ref in enumerate(outs):
        out_ref[...] = near_ref[pl.ds(lax.bitwise_xor(place_ref[4], k) * XD, XD)]


def inverse_y_kernel(sources, chunk, place_ref, *refs):
    ins, (high_ref, low_ref) = refs[:sources], refs[sources : sources + 2]
    outs, (lines_ref, turned_ref) = refs[sources + 2 : -2], refs[-2:]
    for k in range(sources):
        lines_ref[lax.bitwise_xor(place_ref[4], k)] = ins[k][pl.ds(chunk * DEPTH, DEPTH)]
    parts = []
    for x in range(DEPTH):
        lines = jnp.concatenate([lines_ref[source, x] for source in range(sources)], 0)
        pairs = jnp.concatenate([lines, swap(lines) * half_sign()], 0)
        parts.append(split(pairs))
    both = jnp.concatenate([value for part in parts for value in part], 1)
    main = jnp.dot(high_ref[...], both, preferred_element_type=F32)
    high = jnp.concatenate([part[0] for part in parts], 1)
    rest = jnp.dot(low_ref[...], high, preferred_element_type=F32)
    row = lax.broadcasted_iota(jnp.int32, (NY, 1), 0)
    sign = jnp.where((row % 2 == 1) & (place_ref[3] == 1), -1.0, 1.0)
    for x in range(DEPTH):
        total = main[:, 2 * x * LANES : (2 * x + 1) * LANES] + main[:, (2 * x + 1) * LANES : (2 * x + 2) * LANES]
        total = (total + rest[:, x * LANES : (x + 1) * LANES]) * sign
        turned_ref[:, x] = total.reshape(len(outs), -1, LANES)
    for k in range(len(outs)):
        outs[k][...] = turned_ref[lax.bitwise_xor(place_ref[5], k)]


def inverse_z_kernel(sources, place_ref, *refs):
    ins, (high_ref, low_ref) = refs[:sources], refs[sources : sources + 2]
    out_ref, lines_ref = refs[-2:]
    for k in range(sources):
        lines_ref[lax.bitwise_xor(place_ref[5], k)] = ins[k][...]
    for x in range(DEPTH):
        lines = jnp.concatenate([lines_ref[source, x] for source in range(sources)], 1)
        high, low = split(lines)
        total = jnp.dot(high, high_ref[...], preferred_element_type=F32)
        total += jnp.dot(low, high_ref[...], preferred_element_type=F32)
        total += jnp.dot(high, low_ref[...], preferred_element_type=F32)
        out_ref[x] = total


def gather_kernel(
    place_ref, same_ref, other_ref, table_y, table_z, near_ref, out_ref, shift_ref, fields_ref, stack_ref
):
    step = pl.program_id(0)
    half = LANES // 2
    rows = table_y.shape[1] // 2
    ky_local = rows - 8
    width = same_ref.shape[2]
    doms = table_y.shape[2] // width
    planes = near_ref.shape[0]
    slabs = 2 * (planes - 3) // XD
    halves = half_sign()

    @pl.when(step == 0)
    def _():
        stack_ref[...] = jnp.zeros_like(stack_ref)
        shift_ref[...] = jnp.zeros_like(shift_ref)
        row = lax.broadcasted_iota(jnp.int32, (8, LANES), 0)

        def build(x, carry):
            plus = near_ref[x, pl.ds(0, ky_local), :]
            shift_ref[pl.ds(1, ky_local), :] = near_ref[x, pl.ds(ky_local, ky_local), :]
            minus = shift_ref[pl.ds(0, ky_local), :]
            last = shift_ref[pl.ds(ky_local, 8), :][0:1]
            main = [plus + minus, swap(plus - minus) * halves]
            if 2 * ky_local < LANES:
                main.append(jnp.zeros((LANES - 2 * ky_local, LANES), F32))
            rest = jnp.where(row % 2 == 0, last, -swap(jnp.broadcast_to(last, (8, LANES))) * halves)
            rest = jnp.where(row < 6, rest, 0.0)
            rest_high = rest.astype(BF16).astype(F32)
            rest = jnp.where((row == 2) | (row == 3), rest - rest_high, rest_high)
            high, low = split(jnp.concatenate(main, 0).T)
            fields_ref[x, :, pl.ds(0, LANES)] = high
            fields_ref[x, :, pl.ds(LANES, LANES)] = low
            fields_ref[x, :, pl.ds(2 * LANES, LANES)] = high
            rest = jnp.concatenate([rest, jnp.zeros((LANES - 8, LANES), F32)], 0)
            fields_ref[x, :, pl.ds(3 * LANES, LANES)] = rest.T.astype(BF16)
            return carry

        lax.fori_loop(0, planes, build, 0)

    first_z = place_ref[1].astype(F32)
    twice = jnp.where(first_z + iota((half, 1), 0) == 0.0, 1.0, 2.0)
    fields = fields_ref[pl.ds(step * XD, SPAN)].reshape(SPAN * LANES, 4 * LANES)
    distance = lax.bitwise_xor(place_ref[4], step)
    for slot in range(doms):
        lanes = pl.ds(slot * width, width)
        cosine = table_y[step, pl.ds(0, ky_local), lanes]
        sine = table_y[step, pl.ds(rows, ky_local), lanes]
        high, low = split(jnp.concatenate([cosine, sine], 0))
        for part, value in enumerate((high, high, low)):
            stack_ref[pl.ds(LANES * part, 2 * ky_local), lanes] = value
        cosine = table_y[step, pl.ds(ky_local, 8), lanes][0:1]
        sine = table_y[step, pl.ds(rows + ky_local, 8), lanes][0:1]
        row = lax.broadcasted_iota(jnp.int32, (16, width), 0)
        rest = jnp.where(row % 2 == 0, cosine, sine)
        rest_high = rest.astype(BF16).astype(F32)
        rest = jnp.where(row < 4, rest_high, jnp.where(row < 6, rest - rest_high, 0.0))
        stack_ref[pl.ds(3 * LANES, 16), lanes] = rest.astype(BF16)
    product = jnp.dot(fields, stack_ref[...], preferred_element_type=F32)
    for slot in range(doms):
        atoms, dom_distance = atoms_of((same_ref, other_ref), distance, slot, slabs, doms)
        along_x = plane_weights(atoms, spline(atoms))
        lanes = pl.ds(slot * width, width)
        field = product[:, slot * width : (slot + 1) * width]
        total = along_x[0:1] * field[:LANES]
        for plane in range(1, SPAN):
            total += along_x[plane : plane + 1] * field[plane * LANES : (plane + 1) * LANES]
        waves = total * table_z[step, :, lanes]
        sampled = jnp.sum((waves[:half] - waves[half:]) * twice, axis=0, keepdims=True)
        out_ref[step * doms + lax.bitwise_xor(place_ref[5], dom_distance)] = sampled


def bf16_pair(table):
    high = table.astype(ml_dtypes.bfloat16)
    low = (table - high.astype(np.float64)).astype(ml_dtypes.bfloat16)
    return jnp.asarray(high), jnp.asarray(low)


def inverse_y_table(slab_half, ky_local):
    waves = []
    for slab in range(slab_half):
        first = slab * ky_local
        waves += [first + i for i in range(ky_local)] + [-(first + i + 1) for i in range(ky_local)]
    angle = 2.0 * np.pi * (np.outer(np.arange(NY), np.array(waves)) % NY) / NY
    return bf16_pair(np.concatenate([np.cos(angle), np.sin(angle)], 1))


def inverse_z_table(dom_count):
    kz = np.arange(KH)
    angle = 2.0 * np.pi * (np.outer(kz, np.arange(NZ)) % NZ) / NZ
    weight = np.where(kz == 0, 1.0, 2.0)[:, None]
    parts = [weight * np.cos(angle), -weight * np.sin(angle)]
    return bf16_pair(
        np.stack([p.reshape(dom_count, KH // dom_count, NZ) for p in parts], 1).reshape(2 * KH, NZ)
    )


def whole_spec(shape):
    return pl.BlockSpec(shape, lambda *_: (0,) * len(shape))


SMALL = pl.CostEstimate(flops=10**6, bytes_accessed=10**4, transcendentals=0)
SMEM = pl.BlockSpec(memory_space=pltpu.SMEM)


def params(mib):
    return pltpu.CompilerParams(vmem_limit_bytes=mib * MIB)


def swapped(value, axis, distance):
    if distance == 0:
        return value
    return lax.ppermute(value, axis, [(i, i ^ distance) for i in range(lax.axis_size(axis))])


def per_device(base_cells, offsets, charges, bias_coupling, counts, green):
    slabs = lax.axis_size("slab")
    doms = lax.axis_size("dom")
    slab = lax.axis_index("slab")
    dom = lax.axis_index("dom")
    atoms_local = charges.shape[0]
    cells_x = XD * slabs
    ky_local = NY // slabs
    kz_local = KH // doms
    slab_half = slabs // 2
    rows_local = NY // doms
    rows = ky_local + 8
    quarter_rows = ky_local // 2
    normalize = 1.0 / (cells_x * NY * NZ)
    upper = slab // slab_half
    place = jnp.stack(
        [slab * ky_local, dom * kz_local, upper * slab_half, upper, slab % slab_half, dom, slab]
    ).astype(jnp.int32)

    vmem = pl.BlockSpec(memory_space=pltpu.VMEM)
    atoms = pl.pallas_call(
        pack_kernel,
        in_specs=[SMEM, vmem, vmem, vmem],
        out_specs=vmem,
        out_shape=jax.ShapeDtypeStruct((1, 8, atoms_local), F32),
        compiler_params=params(4),
        name="pack",
    )(counts, base_cells, offsets, charges.reshape(1, atoms_local))
    factors_y, factors_z = pl.pallas_call(
        wave_kernel,
        in_specs=[SMEM],
        out_specs=[vmem] * 2,
        out_shape=[jax.ShapeDtypeStruct((4 * count, TERMS), BF16) for count in (rows, LANES // 2)],
        compiler_params=params(8),
        name="waves",
    )(place)
    same = atoms
    for number, (axis, distance) in enumerate(exchange_order(slabs, doms)):
        same = jnp.concatenate([same, swapped(same, axis, distance)], 0)
        if number == 1:
            same, factors_y, factors_z = lax.optimization_barrier((same, factors_y, factors_z))
    other = swapped(same, "dom", 1)

    early = cells_x * 3 // 8
    mirror = [(s, slabs - 1 - s) for s in range(slabs)]

    def halves_beside(value):
        return jnp.concatenate([value[:, :quarter_rows], value[:, quarter_rows:]], 2) * normalize

    own = halves_beside(green)
    first_part = lax.ppermute(halves_beside(green[:early, ::-1]), "slab", mirror)
    same, late = lax.optimization_barrier((same, halves_beside(green[early:, ::-1])))
    second_part = lax.ppermute(late, "slab", mirror)

    atoms_slab = doms * atoms_local
    table_bytes = 4 * (slab_half + 1) * (2 * rows + LANES) * atoms_slab
    spectrum_bytes = 16 * cells_x * max(8, quarter_rows) * LANES
    spectrum, table_y, table_z = pl.pallas_call(
        forward_kernel,
        grid=(slabs,),
        in_specs=[SMEM] + [vmem] * 4,
        out_specs=[vmem] * 3,
        out_shape=[
            jax.ShapeDtypeStruct((4, cells_x, quarter_rows, LANES), F32),
            jax.ShapeDtypeStruct((slab_half + 1, 2 * rows, atoms_slab), F32),
            jax.ShapeDtypeStruct((slab_half + 1, LANES, atoms_slab), F32),
        ],
        scratch_shapes=[
            pltpu.VMEM((SPAN * 4 * rows, atoms_slab), BF16),
            pltpu.VMEM((atoms_slab, 2 * LANES), BF16),
            pltpu.VMEM((cells_x, 2 * rows, LANES), F32),
            pltpu.VMEM((8, atoms_slab), F32),
            pltpu.VMEM((doms, TERMS, atoms_local), BF16),
            pltpu.VMEM((doms, TERMS, atoms_local), BF16),
        ],
        compiler_params=params(16 + (table_bytes + spectrum_bytes) // MIB),
        cost_estimate=SMALL,
        name="forward",
    )(place, same, other, factors_y, factors_z)

    near_planes = cells_x // 2 + 3
    piece = (XD, 4, quarter_rows, LANES)
    *pieces, near = pl.pallas_call(
        inverse_x_kernel,
        in_specs=[SMEM] + [vmem] * 4,
        out_specs=[vmem] * (slab_half + 1),
        out_shape=[jax.ShapeDtypeStruct(piece, F32)] * slab_half
        + [jax.ShapeDtypeStruct((near_planes, 4, quarter_rows, LANES), F32)],
        compiler_params=params(32),
        cost_estimate=SMALL,
        name="inverse_x",
    )(place, spectrum, own, first_part, second_part)

    partial = pl.pallas_call(
        gather_kernel,
        grid=(slab_half,),
        in_specs=[SMEM] + [vmem] * 5,
        out_specs=vmem,
        out_shape=jax.ShapeDtypeStruct((slab_half * doms, 1, atoms_local), F32),
        scratch_shapes=[
            pltpu.VMEM((rows, LANES), F32),
            pltpu.VMEM((near_planes, LANES, 4 * LANES), BF16),
            pltpu.VMEM((4 * LANES, atoms_slab), BF16),
        ],
        compiler_params=params(12 + (table_bytes + 8 * near_planes * LANES * LANES) // MIB),
        cost_estimate=SMALL,
        name="gather",
    )(place, same, other, table_y, table_z, near.reshape(near_planes, 2 * ky_local, LANES))

    high_y, low_y = inverse_y_table(slab_half, ky_local)
    high_z, low_z = inverse_z_table(doms)
    members = slab_half * doms
    sampled = lax.all_to_all(
        partial.reshape(members, atoms_local),
        ("slab", "dom"),
        0,
        0,
        axis_index_groups=[list(range(members)), list(range(members, 2 * members))],
        tiled=True,
    )
    lines = [swapped(value.reshape(XD, 2 * ky_local, LANES), "slab", k) for k, value in enumerate(pieces)]
    sampled, *lines = lax.optimization_barrier((sampled, *lines))

    potential = None
    for chunk in range(CHUNKS):
        turned = pl.pallas_call(
            functools.partial(inverse_y_kernel, slab_half, chunk),
            in_specs=[SMEM] + [vmem] * (slab_half + 2),
            out_specs=[vmem] * doms,
            out_shape=[jax.ShapeDtypeStruct((DEPTH, rows_local, LANES), F32)] * doms,
            scratch_shapes=[
                pltpu.VMEM((slab_half, DEPTH, 2 * ky_local, LANES), F32),
                pltpu.VMEM((doms, DEPTH, rows_local, LANES), F32),
            ],
            compiler_params=params(24),
            cost_estimate=SMALL,
            name="inverse_y",
        )(place, *lines, high_y, low_y)
        columns = [swapped(value, "dom", k) for k, value in enumerate(turned)]
        earlier = [] if potential is None else [potential]
        potential = pl.pallas_call(
            functools.partial(inverse_z_kernel, doms),
            grid=(1,),
            in_specs=[SMEM]
            + [whole_spec((DEPTH, rows_local, LANES))] * doms
            + [whole_spec((2 * KH, NZ))] * 2
            + [pl.BlockSpec(memory_space=pl.ANY)] * len(earlier),
            out_specs=pl.BlockSpec((DEPTH, rows_local, NZ), lambda _, at=chunk: (at, 0, 0)),
            out_shape=jax.ShapeDtypeStruct((XD, rows_local, NZ), F32),
            scratch_shapes=[pltpu.VMEM((doms, DEPTH, rows_local, LANES), F32)],
            input_output_aliases={doms + 3: 0} if earlier else {},
            compiler_params=params(24),
            cost_estimate=SMALL,
            name="inverse_z",
        )(place, *columns, high_z, low_z, *earlier)

    alive = jnp.arange(atoms_local, dtype=jnp.int32) < counts[0]
    gradient = jnp.where(alive, bias_coupling * jnp.sum(sampled, 0), 0.0)
    return (potential, gradient)


def solution(mesh):
    placed = (
        P(None, ("slab", "dom")),
        P(None, ("slab", "dom")),
        P(("slab", "dom")),
        P(("slab", "dom")),
        P(("slab", "dom")),
        P(None, "slab", "dom"),
    )
    return jax.shard_map(
        per_device,
        mesh=mesh,
        in_specs=placed,
        out_specs=(P("slab", "dom", None), P(("slab", "dom"))),
        check_vma=False,
    )
```

```python
import functools

import jax
import jax.numpy as jnp
import ml_dtypes
import numpy as np
from jax import lax
from jax.experimental import pallas as pl
from jax.experimental.pallas import tpu as pltpu
from jax.sharding import PartitionSpec as P

XD = 4
NY = 512
NZ = 512
KH = NZ // 2
LANES = 128
SPAN = XD + 3
CHUNKS = 2
DEPTH = XD // CHUNKS
MIB = 1 << 20
BF16 = jnp.bfloat16
F32 = jnp.float32


def polynomial(function, terms):
    nodes = 0.125 * (1.0 - np.cos(np.pi * (np.arange(64) + 0.5) / 64))
    powers = nodes[:, None] ** np.arange(terms)[None, :]
    return [float(v) for v in np.linalg.lstsq(powers, function(np.sqrt(nodes)), rcond=None)[0]]


SINE_TERMS = polynomial(lambda r: np.sin(np.pi * r) / r, 6)
COSINE_TERMS = polynomial(lambda r: np.cos(np.pi * r), 6)


def horner(terms, square):
    total = jnp.full_like(square, terms[-1])
    for term in terms[-2::-1]:
        total = total * square + term
    return total


def turn(fraction):
    left = fraction - jnp.floor(fraction + 0.5)
    square = left * left
    sine = left * horner(SINE_TERMS, square)
    cosine = horner(COSINE_TERMS, square)
    return 1.0 - 2.0 * sine * sine, 2.0 * sine * cosine


def spline(frac):
    inner = 1.0 - frac
    square = frac * frac
    cube = square * frac
    sixth = 1.0 / 6.0
    return (
        inner * inner * inner * sixth,
        (3.0 * cube - 6.0 * square + 4.0) * sixth,
        (-3.0 * cube + 3.0 * square + 3.0 * frac + 1.0) * sixth,
        cube * sixth,
    )


def split(value):
    high = value.astype(BF16)
    return high, (value - high.astype(F32)).astype(BF16)


def iota(shape, axis):
    return lax.broadcasted_iota(jnp.int32, shape, axis).astype(F32)


RADIX = 16
DIGITS = 32
TERMS = 256


def wave_factors(first, rows, length):
    lane = lax.broadcasted_iota(jnp.int32, (rows, TERMS), 1)
    section = lane // DIGITS
    digit = (lane % DIGITS).astype(F32) * jnp.where(section < 2, float(RADIX), 1.0)
    parts = []
    for value in turn((first + iota((rows, TERMS), 0)) * digit * (1.0 / length)):
        high = value.astype(BF16).astype(F32)
        parts.append(jnp.where((section == 1) | (section == 3), value - high, high))
    upper, lower = section < 2, (section >= 2) & (section < 5)
    masked = [jnp.where(mask, part, 0.0) for mask in (upper, lower) for part in parts]
    return jnp.concatenate(masked, 0).astype(BF16)


def wave_kernel(place_ref, out_y_ref, out_z_ref):
    out_y_ref[...] = wave_factors(place_ref[0].astype(F32), out_y_ref.shape[0] // 4, NY)
    out_z_ref[...] = wave_factors(place_ref[1].astype(F32), out_z_ref.shape[0] // 4, NZ)


def atom_waves(base, weights, factors_ref, digits_ref):
    width = base.shape[1]
    high_digit = jnp.floor(base * (1.0 / RADIX))
    row = iota((DIGITS, width), 0)
    chosen = jnp.where(row == high_digit, 1.0, 0.0).astype(BF16)
    step = row - (base - RADIX * high_digit)
    spread = jnp.where(step == 3.0, weights[3], 0.0)
    for r in (2, 1, 0):
        spread = jnp.where(step == float(r), weights[r], spread)
    high, low = split(spread)
    for section, value in enumerate((chosen, chosen, high, high, low)):
        digits_ref[pl.ds(DIGITS * section, DIGITS), :] = value
    product = jnp.dot(factors_ref[...], digits_ref[...], preferred_element_type=F32)
    rows = product.shape[0] // 4
    cos_a, sin_a, cos_b, sin_b = (product[i * rows : (i + 1) * rows] for i in range(4))
    return cos_a * cos_b - sin_a * sin_b, sin_a * cos_b + cos_a * sin_b


def plane_weights(atoms, weights):
    row = iota((8, atoms.shape[1]), 0) - atoms[0:1]
    return sum(weights[r][3:4] * (row == float(r)).astype(F32) for r in range(4))


def swap(value):
    return pltpu.roll(value, LANES // 2, axis=value.ndim - 1)


def half_sign():
    lane = lax.broadcasted_iota(jnp.int32, (1, LANES), 1)
    return jnp.where(lane < LANES // 2, -1.0, 1.0).astype(F32)


def rotate(value, numer, denom, sign, halves):
    if numer == 0:
        return value
    if 4 * numer == denom:
        return swap(value) * (halves * sign)
    angle = 2.0 * np.pi * numer / denom
    return value * float(np.cos(angle)) + swap(value) * (halves * float(sign * np.sin(angle)))


def transform(values, sign, halves):
    count = len(values)
    if count == 1:
        return values
    even = transform(values[0::2], sign, halves)
    odd = transform(values[1::2], sign, halves)
    turned = [rotate(odd[k], k, count, sign, halves) for k in range(count // 2)]
    return [e + t for e, t in zip(even, turned)] + [e - t for e, t in zip(even, turned)]


def pack_kernel(counts_ref, cells_ref, offsets_ref, charges_ref, out_ref):
    width = offsets_ref.shape[1]
    alive = lax.broadcasted_iota(jnp.int32, (1, width), 1) < counts_ref[0]
    atoms = jnp.concatenate(
        [
            lax.bitwise_and(cells_ref[0:1, :], XD - 1).astype(F32),
            cells_ref[1:3, :].astype(F32),
            offsets_ref[...],
            jnp.where(alive, charges_ref[...], 0.0),
            jnp.zeros((1, width), F32),
        ],
        0,
    )
    for copy in range(out_ref.shape[0]):
        out_ref[copy] = atoms


def exchange_order(slabs, doms):
    steps = [("slab", slabs >> (i + 1)) for i in range(slabs.bit_length() - 1)]
    return steps + [("dom", doms >> (i + 1)) for i in range(doms.bit_length() - 2)]


def atoms_of(refs, distance, slot, slabs, doms):
    half = doms // 2
    bits = slabs.bit_length() - 1
    at = sum(((distance >> (bits - 1 - i)) & 1) << i for i in range(bits))
    number = slot % half
    dom_bits = doms.bit_length() - 2
    dom_distance = sum(((number >> i) & 1) * (doms >> (i + 1)) for i in range(dom_bits))
    return refs[slot // half][number * slabs + at], dom_distance ^ (slot // half)


def forward_kernel(
    place_ref,
    same_ref,
    other_ref,
    factors_y,
    factors_z,
    out_ref,
    table_y,
    table_z,
    left_ref,
    right_ref,
    grid_ref,
    digits_y,
    digits_z,
):
    step = pl.program_id(0)
    cells_x = grid_ref.shape[0]
    rows = grid_ref.shape[1] // 2
    ky_local = rows - 8
    width = same_ref.shape[2]
    doms = table_y.shape[2] // width
    slabs = cells_x // XD
    slab = lax.bitwise_xor(place_ref[6], step)
    kept = slab - place_ref[2]
    kept = jnp.where((kept >= 0) & (kept < table_y.shape[0] - 1), kept, table_y.shape[0] - 1)

    @pl.when(step == 0)
    def _():
        grid_ref[...] = jnp.zeros_like(grid_ref)
        digits_y[...] = jnp.zeros_like(digits_y)
        digits_z[...] = jnp.zeros_like(digits_z)

    for slot in range(doms):
        atoms, _ = atoms_of((same_ref, other_ref), step, slot, slabs, doms)
        lanes = pl.ds(slot * width, width)
        weights = spline(atoms)
        along_x = plane_weights(atoms, weights) * atoms[6:7]
        waves = atom_waves(atoms[2:3], [w[5:6] for w in weights], factors_z, digits_z.at[slot])
        waves = jnp.concatenate(waves, 0)
        table_z[kept, :, lanes] = waves
        high, low = split(waves.T)
        right_ref[slot, :, :LANES] = high
        right_ref[slot, :, LANES:] = low
        cosine, sine = atom_waves(atoms[1:2], [w[4:5] for w in weights], factors_y, digits_y.at[slot])
        waves = jnp.concatenate([cosine, sine], 0)
        table_y[kept, :, lanes] = waves
        for plane in range(SPAN):
            first = 4 * rows * plane
            high, low = split(waves * along_x[plane : plane + 1])
            left_ref[slot, pl.ds(first, 2 * rows), :] = high
            left_ref[slot, pl.ds(first + 2 * rows, 2 * rows), :] = low
        product = jnp.dot(left_ref[slot], right_ref[slot], preferred_element_type=F32)
        for plane in range(SPAN):
            first = 4 * rows * plane
            high, low = product[first : first + 2 * rows], product[first + 2 * rows : first + 4 * rows]
            at = lax.rem(slab * XD + plane, cells_x)
            grid_ref[at] += (high[:, :LANES] + high[:, LANES:]) + (low[:, :LANES] + low[:, LANES:])

    @pl.when(step == pl.num_programs(0) - 1)
    def _():
        halves = half_sign()
        quarter_rows = ky_local // 2
        group = min(8, quarter_rows)
        for minus in (0, 1):
            for start in range(0, ky_local, group):
                row = start + minus
                values = []
                for x in range(cells_x):
                    top = grid_ref[x, pl.ds(row, group), :]
                    bottom = swap(grid_ref[x, pl.ds(rows + row, group), :])
                    values.append(bottom - top * halves if minus else -bottom - top * halves)
                at = 2 * minus + start // quarter_rows
                for x, value in enumerate(transform(values, -1.0, halves)):
                    out_ref[at, x, pl.ds(start % quarter_rows, group), :] = value


def inverse_x_kernel(place_ref, spectrum_ref, own_ref, mirrored_ref, *refs):
    *outs, near_ref = refs
    cells_x, quarter_rows = spectrum_ref.shape[1:3]
    group = min(8, quarter_rows)
    halves = half_sign()
    lane = lax.broadcasted_iota(jnp.int32, (1, LANES), 1)
    side = 1.0 - 2.0 * place_ref[3].astype(F32)

    def rows_of(step, carry):
        rows = pl.ds(pl.multiple_of(step * group, group), group)
        for quarter in range(4):
            values = []
            for kx in range(cells_x):
                green = (own_ref if quarter < 2 else mirrored_ref)[kx, rows, :]
                keep = lane < LANES // 2 if quarter % 2 == 0 else lane >= LANES // 2
                values.append(spectrum_ref[quarter, kx, rows, :] * jnp.where(keep, green, swap(green)))
            even = transform(values[0::2], 1.0, halves)
            odd = transform(values[1::2], 1.0, halves)
            for x in range(cells_x // 2):
                turned = rotate(odd[x], x, cells_x, 1.0, halves) * side
                near_ref[x, quarter, rows, :] = even[x] + turned
                if x < 3:
                    near_ref[cells_x // 2 + x, quarter, rows, :] = even[x] - turned
        return carry

    lax.fori_loop(0, quarter_rows // group, rows_of, 0)
    for k, out_ref in enumerate(outs):
        out_ref[...] = near_ref[pl.ds(lax.bitwise_xor(place_ref[4], k) * XD, XD)]


def inverse_y_kernel(sources, chunk, place_ref, *refs):
    ins, (high_ref, low_ref) = refs[:sources], refs[sources : sources + 2]
    outs, (lines_ref, turned_ref) = refs[sources + 2 : -2], refs[-2:]
    for k in range(sources):
        lines_ref[lax.bitwise_xor(place_ref[4], k)] = ins[k][pl.ds(chunk * DEPTH, DEPTH)]
    parts = []
    for x in range(DEPTH):
        lines = jnp.concatenate([lines_ref[source, x] for source in range(sources)], 0)
        pairs = jnp.concatenate([lines, swap(lines) * half_sign()], 0)
        parts.append(split(pairs))
    both = jnp.concatenate([value for part in parts for value in part], 1)
    main = jnp.dot(high_ref[...], both, preferred_element_type=F32)
    high = jnp.concatenate([part[0] for part in parts], 1)
    rest = jnp.dot(low_ref[...], high, preferred_element_type=F32)
    row = lax.broadcasted_iota(jnp.int32, (NY, 1), 0)
    sign = jnp.where((row % 2 == 1) & (place_ref[3] == 1), -1.0, 1.0)
    for x in range(DEPTH):
        total = main[:, 2 * x * LANES : (2 * x + 1) * LANES] + main[:, (2 * x + 1) * LANES : (2 * x + 2) * LANES]
        total = (total + rest[:, x * LANES : (x + 1) * LANES]) * sign
        turned_ref[:, x] = total.reshape(len(outs), -1, LANES)
    for k in range(len(outs)):
        outs[k][...] = turned_ref[lax.bitwise_xor(place_ref[5], k)]


def inverse_z_kernel(sources, place_ref, *refs):
    ins, (high_ref, low_ref) = refs[:sources], refs[sources : sources + 2]
    out_ref, lines_ref = refs[-2:]
    for k in range(sources):
        lines_ref[lax.bitwise_xor(place_ref[5], k)] = ins[k][...]
    for x in range(DEPTH):
        lines = jnp.concatenate([lines_ref[source, x] for source in range(sources)], 1)
        high, low = split(lines)
        total = jnp.dot(high, high_ref[...], preferred_element_type=F32)
        total += jnp.dot(low, high_ref[...], preferred_element_type=F32)
        total += jnp.dot(high, low_ref[...], preferred_element_type=F32)
        out_ref[x] = total


def gather_kernel(
    place_ref, same_ref, other_ref, table_y, table_z, near_ref, out_ref, shift_ref, fields_ref, stack_ref
):
    step = pl.program_id(0)
    half = LANES // 2
    rows = table_y.shape[1] // 2
    ky_local = rows - 8
    width = same_ref.shape[2]
    doms = table_y.shape[2] // width
    planes = near_ref.shape[0]
    slabs = 2 * (planes - 3) // XD
    halves = half_sign()

    @pl.when(step == 0)
    def _():
        stack_ref[...] = jnp.zeros_like(stack_ref)
        shift_ref[...] = jnp.zeros_like(shift_ref)
        row = lax.broadcasted_iota(jnp.int32, (8, LANES), 0)

        def build(x, carry):
            plus = near_ref[x, pl.ds(0, ky_local), :]
            shift_ref[pl.ds(1, ky_local), :] = near_ref[x, pl.ds(ky_local, ky_local), :]
            minus = shift_ref[pl.ds(0, ky_local), :]
            last = shift_ref[pl.ds(ky_local, 8), :][0:1]
            main = [plus + minus, swap(plus - minus) * halves]
            if 2 * ky_local < LANES:
                main.append(jnp.zeros((LANES - 2 * ky_local, LANES), F32))
            rest = jnp.where(row % 2 == 0, last, -swap(jnp.broadcast_to(last, (8, LANES))) * halves)
            rest = jnp.where(row < 6, rest, 0.0)
            rest_high = rest.astype(BF16).astype(F32)
            rest = jnp.where((row == 2) | (row == 3), rest - rest_high, rest_high)
            high, low = split(jnp.concatenate(main, 0).T)
            fields_ref[x, :, pl.ds(0, LANES)] = high
            fields_ref[x, :, pl.ds(LANES, LANES)] = low
            fields_ref[x, :, pl.ds(2 * LANES, LANES)] = high
            rest = jnp.concatenate([rest, jnp.zeros((LANES - 8, LANES), F32)], 0)
            fields_ref[x, :, pl.ds(3 * LANES, LANES)] = rest.T.astype(BF16)
            return carry

        lax.fori_loop(0, planes, build, 0)

    first_z = place_ref[1].astype(F32)
    twice = jnp.where(first_z + iota((half, 1), 0) == 0.0, 1.0, 2.0)
    fields = fields_ref[pl.ds(step * XD, SPAN)].reshape(SPAN * LANES, 4 * LANES)
    distance = lax.bitwise_xor(place_ref[4], step)
    for slot in range(doms):
        lanes = pl.ds(slot * width, width)
        cosine = table_y[step, pl.ds(0, ky_local), lanes]
        sine = table_y[step, pl.ds(rows, ky_local), lanes]
        high, low = split(jnp.concatenate([cosine, sine], 0))
        for part, value in enumerate((high, high, low)):
            stack_ref[pl.ds(LANES * part, 2 * ky_local), lanes] = value
        cosine = table_y[step, pl.ds(ky_local, 8), lanes][0:1]
        sine = table_y[step, pl.ds(rows + ky_local, 8), lanes][0:1]
        row = lax.broadcasted_iota(jnp.int32, (16, width), 0)
        rest = jnp.where(row % 2 == 0, cosine, sine)
        rest_high = rest.astype(BF16).astype(F32)
        rest = jnp.where(row < 4, rest_high, jnp.where(row < 6, rest - rest_high, 0.0))
        stack_ref[pl.ds(3 * LANES, 16), lanes] = rest.astype(BF16)
    product = sum(
        jnp.dot(fields[:, part : part + 2 * LANES], stack_ref[pl.ds(part, 2 * LANES), :], preferred_element_type=F32)
        for part in (0, 2 * LANES)
    )
    for slot in range(doms):
        atoms, dom_distance = atoms_of((same_ref, other_ref), distance, slot, slabs, doms)
        along_x = plane_weights(atoms, spline(atoms))
        lanes = pl.ds(slot * width, width)
        field = product[:, slot * width : (slot + 1) * width]
        total = along_x[0:1] * field[:LANES]
        for plane in range(1, SPAN):
            total += along_x[plane : plane + 1] * field[plane * LANES : (plane + 1) * LANES]
        waves = total * table_z[step, :, lanes]
        sampled = jnp.sum((waves[:half] - waves[half:]) * twice, axis=0, keepdims=True)
        out_ref[step * doms + lax.bitwise_xor(place_ref[5], dom_distance)] = sampled


def bf16_pair(table):
    high = table.astype(ml_dtypes.bfloat16)
    low = (table - high.astype(np.float64)).astype(ml_dtypes.bfloat16)
    return jnp.asarray(high), jnp.asarray(low)


def inverse_y_table(slab_half, ky_local):
    waves = []
    for slab in range(slab_half):
        first = slab * ky_local
        waves += [first + i for i in range(ky_local)] + [-(first + i + 1) for i in range(ky_local)]
    angle = 2.0 * np.pi * (np.outer(np.arange(NY), np.array(waves)) % NY) / NY
    return bf16_pair(np.concatenate([np.cos(angle), np.sin(angle)], 1))


def inverse_z_table(dom_count):
    kz = np.arange(KH)
    angle = 2.0 * np.pi * (np.outer(kz, np.arange(NZ)) % NZ) / NZ
    weight = np.where(kz == 0, 1.0, 2.0)[:, None]
    parts = [weight * np.cos(angle), -weight * np.sin(angle)]
    return bf16_pair(
        np.stack([p.reshape(dom_count, KH // dom_count, NZ) for p in parts], 1).reshape(2 * KH, NZ)
    )


def whole_spec(shape):
    return pl.BlockSpec(shape, lambda *_: (0,) * len(shape))


SMALL = pl.CostEstimate(flops=10**6, bytes_accessed=10**4, transcendentals=0)
SMEM = pl.BlockSpec(memory_space=pltpu.SMEM)


def params(mib):
    return pltpu.CompilerParams(vmem_limit_bytes=mib * MIB)


def swapped(value, axis, distance):
    if distance == 0:
        return value
    return lax.ppermute(value, axis, [(i, i ^ distance) for i in range(lax.axis_size(axis))])


def per_device(base_cells, offsets, charges, bias_coupling, counts, green):
    slabs = lax.axis_size("slab")
    doms = lax.axis_size("dom")
    slab = lax.axis_index("slab")
    dom = lax.axis_index("dom")
    atoms_local = charges.shape[0]
    cells_x = XD * slabs
    ky_local = NY // slabs
    kz_local = KH // doms
    slab_half = slabs // 2
    rows_local = NY // doms
    rows = ky_local + 8
    quarter_rows = ky_local // 2
    normalize = 1.0 / (cells_x * NY * NZ)
    upper = slab // slab_half
    place = jnp.stack(
        [slab * ky_local, dom * kz_local, upper * slab_half, upper, slab % slab_half, dom, slab]
    ).astype(jnp.int32)

    vmem = pl.BlockSpec(memory_space=pltpu.VMEM)
    atoms = pl.pallas_call(
        pack_kernel,
        in_specs=[SMEM, vmem, vmem, vmem],
        out_specs=vmem,
        out_shape=jax.ShapeDtypeStruct((1, 8, atoms_local), F32),
        name="pack",
    )(counts, base_cells, offsets, charges.reshape(1, atoms_local))
    factors_y, factors_z = pl.pallas_call(
        wave_kernel,
        in_specs=[SMEM],
        out_specs=[vmem] * 2,
        out_shape=[jax.ShapeDtypeStruct((4 * count, TERMS), BF16) for count in (rows, LANES // 2)],
        compiler_params=params(8),
        name="waves",
    )(place)
    same = atoms
    for number, (axis, distance) in enumerate(exchange_order(slabs, doms)):
        same = jnp.concatenate([same, swapped(same, axis, distance)], 0)
        if number == 1:
            same, factors_y, factors_z = lax.optimization_barrier((same, factors_y, factors_z))
    other = swapped(same, "dom", 1)

    def halves_beside(value):
        return jnp.concatenate([value[:, :quarter_rows], value[:, quarter_rows:]], 2) * normalize

    own = halves_beside(green)
    same, flipped = lax.optimization_barrier((same, halves_beside(green[:, ::-1])))
    mirrored = lax.ppermute(flipped, "slab", [(s, slabs - 1 - s) for s in range(slabs)])

    atoms_slab = doms * atoms_local
    table_bytes = 4 * (slab_half + 1) * (2 * rows + LANES) * atoms_slab
    spectrum_bytes = 16 * cells_x * max(8, quarter_rows) * LANES
    spectrum, table_y, table_z = pl.pallas_call(
        forward_kernel,
        grid=(slabs,),
        in_specs=[SMEM] + [vmem] * 4,
        out_specs=[vmem] * 3,
        out_shape=[
            jax.ShapeDtypeStruct((4, cells_x, quarter_rows, LANES), F32),
            jax.ShapeDtypeStruct((slab_half + 1, 2 * rows, atoms_slab), F32),
            jax.ShapeDtypeStruct((slab_half + 1, LANES, atoms_slab), F32),
        ],
        scratch_shapes=[
            pltpu.VMEM((doms, SPAN * 4 * rows, atoms_local), BF16),
            pltpu.VMEM((doms, atoms_local, 2 * LANES), BF16),
            pltpu.VMEM((cells_x, 2 * rows, LANES), F32),
            pltpu.VMEM((doms, TERMS, atoms_local), BF16),
            pltpu.VMEM((doms, TERMS, atoms_local), BF16),
        ],
        compiler_params=params(16 + (table_bytes + spectrum_bytes) // MIB),
        cost_estimate=SMALL,
        name="forward",
    )(place, same, other, factors_y, factors_z)

    near_planes = cells_x // 2 + 3
    piece = (XD, 4, quarter_rows, LANES)
    *pieces, near = pl.pallas_call(
        inverse_x_kernel,
        in_specs=[SMEM] + [vmem] * 3,
        out_specs=[vmem] * (slab_half + 1),
        out_shape=[jax.ShapeDtypeStruct(piece, F32)] * slab_half
        + [jax.ShapeDtypeStruct((near_planes, 4, quarter_rows, LANES), F32)],
        compiler_params=params(32),
        cost_estimate=SMALL,
        name="inverse_x",
    )(place, spectrum, own, mirrored)

    partial = pl.pallas_call(
        gather_kernel,
        grid=(slab_half,),
        in_specs=[SMEM] + [vmem] * 5,
        out_specs=vmem,
        out_shape=jax.ShapeDtypeStruct((slab_half * doms, 1, atoms_local), F32),
        scratch_shapes=[
            pltpu.VMEM((rows, LANES), F32),
            pltpu.VMEM((near_planes, LANES, 4 * LANES), BF16),
            pltpu.VMEM((4 * LANES, atoms_slab), BF16),
        ],
        compiler_params=params(12 + (table_bytes + 8 * near_planes * LANES * LANES) // MIB),
        cost_estimate=SMALL,
        name="gather",
    )(place, same, other, table_y, table_z, near.reshape(near_planes, 2 * ky_local, LANES))

    high_y, low_y = inverse_y_table(slab_half, ky_local)
    high_z, low_z = inverse_z_table(doms)
    members = slab_half * doms
    sampled = lax.all_to_all(
        partial.reshape(members, atoms_local),
        ("slab", "dom"),
        0,
        0,
        axis_index_groups=[list(range(members)), list(range(members, 2 * members))],
        tiled=True,
    )
    lines = [swapped(value.reshape(XD, 2 * ky_local, LANES), "slab", k) for k, value in enumerate(pieces)]
    sampled, *lines = lax.optimization_barrier((sampled, *lines))

    potential = None
    for chunk in range(CHUNKS):
        turned = pl.pallas_call(
            functools.partial(inverse_y_kernel, slab_half, chunk),
            in_specs=[SMEM] + [vmem] * (slab_half + 2),
            out_specs=[vmem] * doms,
            out_shape=[jax.ShapeDtypeStruct((DEPTH, rows_local, LANES), F32)] * doms,
            scratch_shapes=[
                pltpu.VMEM((slab_half, DEPTH, 2 * ky_local, LANES), F32),
                pltpu.VMEM((doms, DEPTH, rows_local, LANES), F32),
            ],
            compiler_params=params(24),
            cost_estimate=SMALL,
            name="inverse_y",
        )(place, *lines, high_y, low_y)
        columns = [swapped(value, "dom", k) for k, value in enumerate(turned)]
        earlier = [] if potential is None else [potential]
        potential = pl.pallas_call(
            functools.partial(inverse_z_kernel, doms),
            grid=(1,),
            in_specs=[SMEM]
            + [whole_spec((DEPTH, rows_local, LANES))] * doms
            + [whole_spec((2 * KH, NZ))] * 2
            + [pl.BlockSpec(memory_space=pl.ANY)] * len(earlier),
            out_specs=pl.BlockSpec((DEPTH, rows_local, NZ), lambda _, at=chunk: (at, 0, 0)),
            out_shape=jax.ShapeDtypeStruct((XD, rows_local, NZ), F32),
            scratch_shapes=[pltpu.VMEM((doms, DEPTH, rows_local, LANES), F32)],
            input_output_aliases={doms + 3: 0} if earlier else {},
            compiler_params=params(24),
            cost_estimate=SMALL,
            name="inverse_z",
        )(place, *columns, high_z, low_z, *earlier)

    alive = jnp.arange(atoms_local, dtype=jnp.int32) < counts[0]
    gradient = jnp.where(alive, bias_coupling * jnp.sum(sampled, 0), 0.0)
    return (potential, gradient)


def solution(mesh):
    placed = (
        P(None, ("slab", "dom")),
        P(None, ("slab", "dom")),
        P(("slab", "dom")),
        P(("slab", "dom")),
        P(("slab", "dom")),
        P(None, "slab", "dom"),
    )
    return jax.shard_map(
        per_device,
        mesh=mesh,
        in_specs=placed,
        out_specs=(P("slab", "dom", None), P(("slab", "dom"))),
        check_vma=False,
    )
```

```python
import functools

import jax
import jax.numpy as jnp
import ml_dtypes
import numpy as np
from jax import lax
from jax.experimental import pallas as pl
from jax.experimental.pallas import tpu as pltpu
from jax.sharding import PartitionSpec as P

XD = 4
NY = 512
NZ = 512
KH = NZ // 2
LANES = 128
SPAN = XD + 3
CHUNKS = 2
DEPTH = XD // CHUNKS
MIB = 1 << 20
BF16 = jnp.bfloat16
F32 = jnp.float32


def polynomial(function, terms):
    nodes = 0.125 * (1.0 - np.cos(np.pi * (np.arange(64) + 0.5) / 64))
    powers = nodes[:, None] ** np.arange(terms)[None, :]
    return [float(v) for v in np.linalg.lstsq(powers, function(np.sqrt(nodes)), rcond=None)[0]]


SINE_TERMS = polynomial(lambda r: np.sin(np.pi * r) / r, 6)
COSINE_TERMS = polynomial(lambda r: np.cos(np.pi * r), 6)


def horner(terms, square):
    total = jnp.full_like(square, terms[-1])
    for term in terms[-2::-1]:
        total = total * square + term
    return total


def turn(fraction):
    left = fraction - jnp.floor(fraction + 0.5)
    square = left * left
    sine = left * horner(SINE_TERMS, square)
    cosine = horner(COSINE_TERMS, square)
    return 1.0 - 2.0 * sine * sine, 2.0 * sine * cosine


def spline(frac):
    inner = 1.0 - frac
    square = frac * frac
    cube = square * frac
    sixth = 1.0 / 6.0
    return (
        inner * inner * inner * sixth,
        (3.0 * cube - 6.0 * square + 4.0) * sixth,
        (-3.0 * cube + 3.0 * square + 3.0 * frac + 1.0) * sixth,
        cube * sixth,
    )


def split(value):
    high = value.astype(BF16)
    return high, (value - high.astype(F32)).astype(BF16)


def iota(shape, axis):
    return lax.broadcasted_iota(jnp.int32, shape, axis).astype(F32)


RADIX = 16
DIGITS = 32
TERMS = 256


def wave_factors(first, rows, length):
    lane = lax.broadcasted_iota(jnp.int32, (rows, TERMS), 1)
    section = lane // DIGITS
    digit = (lane % DIGITS).astype(F32) * jnp.where(section < 2, float(RADIX), 1.0)
    parts = []
    for value in turn((first + iota((rows, TERMS), 0)) * digit * (1.0 / length)):
        high = value.astype(BF16).astype(F32)
        parts.append(jnp.where((section == 1) | (section == 3), value - high, high))
    upper, lower = section < 2, (section >= 2) & (section < 5)
    masked = [jnp.where(mask, part, 0.0) for mask in (upper, lower) for part in parts]
    return jnp.concatenate(masked, 0).astype(BF16)


def wave_kernel(place_ref, out_y_ref, out_z_ref):
    out_y_ref[...] = wave_factors(place_ref[0].astype(F32), out_y_ref.shape[0] // 4, NY)
    out_z_ref[...] = wave_factors(place_ref[1].astype(F32), out_z_ref.shape[0] // 4, NZ)


def atom_waves(base, weights, factors_ref, digits_ref):
    width = base.shape[1]
    high_digit = jnp.floor(base * (1.0 / RADIX))
    row = iota((DIGITS, width), 0)
    chosen = jnp.where(row == high_digit, 1.0, 0.0).astype(BF16)
    step = row - (base - RADIX * high_digit)
    spread = jnp.where(step == 3.0, weights[3], 0.0)
    for r in (2, 1, 0):
        spread = jnp.where(step == float(r), weights[r], spread)
    high, low = split(spread)
    for section, value in enumerate((chosen, chosen, high, high, low)):
        digits_ref[pl.ds(DIGITS * section, DIGITS), :] = value
    product = jnp.dot(factors_ref[...], digits_ref[...], preferred_element_type=F32)
    rows = product.shape[0] // 4
    cos_a, sin_a, cos_b, sin_b = (product[i * rows : (i + 1) * rows] for i in range(4))
    return cos_a * cos_b - sin_a * sin_b, sin_a * cos_b + cos_a * sin_b


def plane_weights(atoms, weights):
    row = iota((8, atoms.shape[1]), 0) - atoms[0:1]
    return sum(weights[r][3:4] * (row == float(r)).astype(F32) for r in range(4))


def swap(value):
    return pltpu.roll(value, LANES // 2, axis=value.ndim - 1)


def half_sign():
    lane = lax.broadcasted_iota(jnp.int32, (1, LANES), 1)
    return jnp.where(lane < LANES // 2, -1.0, 1.0).astype(F32)


def rotate(value, numer, denom, sign, halves):
    if numer == 0:
        return value
    if 4 * numer == denom:
        return swap(value) * (halves * sign)
    angle = 2.0 * np.pi * numer / denom
    return value * float(np.cos(angle)) + swap(value) * (halves * float(sign * np.sin(angle)))


def transform(values, sign, halves):
    count = len(values)
    if count == 1:
        return values
    even = transform(values[0::2], sign, halves)
    odd = transform(values[1::2], sign, halves)
    turned = [rotate(odd[k], k, count, sign, halves) for k in range(count // 2)]
    return [e + t for e, t in zip(even, turned)] + [e - t for e, t in zip(even, turned)]


def pack_kernel(counts_ref, cells_ref, offsets_ref, charges_ref, out_ref):
    width = offsets_ref.shape[1]
    alive = lax.broadcasted_iota(jnp.int32, (1, width), 1) < counts_ref[0]
    atoms = jnp.concatenate(
        [
            lax.bitwise_and(cells_ref[0:1, :], XD - 1).astype(F32),
            cells_ref[1:3, :].astype(F32),
            offsets_ref[...],
            jnp.where(alive, charges_ref[...], 0.0),
            jnp.zeros((1, width), F32),
        ],
        0,
    )
    for copy in range(out_ref.shape[0]):
        out_ref[copy] = atoms


def forward_kernel(
    place_ref,
    atoms_ref,
    factors_y,
    factors_z,
    out_ref,
    table_y,
    table_z,
    left_ref,
    right_ref,
    grid_ref,
    digits_y,
    digits_z,
):
    step = pl.program_id(0)
    cells_x = grid_ref.shape[0]
    rows = grid_ref.shape[1] // 2
    ky_local = rows - 8
    width = atoms_ref.shape[2]
    doms = table_y.shape[2] // width
    kept = step - place_ref[2]
    kept = jnp.where((kept >= 0) & (kept < table_y.shape[0] - 1), kept, table_y.shape[0] - 1)

    @pl.when(step == 0)
    def _():
        grid_ref[...] = jnp.zeros_like(grid_ref)
        digits_y[...] = jnp.zeros_like(digits_y)
        digits_z[...] = jnp.zeros_like(digits_z)

    for slot in range(doms):
        atoms = atoms_ref[step * doms + slot]
        lanes = pl.ds(slot * width, width)
        weights = spline(atoms)
        along_x = plane_weights(atoms, weights) * atoms[6:7]
        waves = atom_waves(atoms[2:3], [w[5:6] for w in weights], factors_z, digits_z.at[slot])
        waves = jnp.concatenate(waves, 0)
        table_z[kept, :, lanes] = waves
        high, low = split(waves.T)
        right_ref[slot, :, :LANES] = high
        right_ref[slot, :, LANES:] = low
        cosine, sine = atom_waves(atoms[1:2], [w[4:5] for w in weights], factors_y, digits_y.at[slot])
        waves = jnp.concatenate([cosine, sine], 0)
        table_y[kept, :, lanes] = waves
        for plane in range(SPAN):
            first = 4 * rows * plane
            high, low = split(waves * along_x[plane : plane + 1])
            left_ref[slot, pl.ds(first, 2 * rows), :] = high
            left_ref[slot, pl.ds(first + 2 * rows, 2 * rows), :] = low
        product = jnp.dot(left_ref[slot], right_ref[slot], preferred_element_type=F32)
        for plane in range(SPAN):
            first = 4 * rows * plane
            high, low = product[first : first + 2 * rows], product[first + 2 * rows : first + 4 * rows]
            at = lax.rem(step * XD + plane, cells_x)
            grid_ref[at] += (high[:, :LANES] + high[:, LANES:]) + (low[:, :LANES] + low[:, LANES:])

    @pl.when(step == pl.num_programs(0) - 1)
    def _():
        halves = half_sign()
        quarter_rows = ky_local // 2
        group = min(8, quarter_rows)
        for minus in (0, 1):
            for start in range(0, ky_local, group):
                row = start + minus
                values = []
                for x in range(cells_x):
                    top = grid_ref[x, pl.ds(row, group), :]
                    bottom = swap(grid_ref[x, pl.ds(rows + row, group), :])
                    values.append(bottom - top * halves if minus else -bottom - top * halves)
                at = 2 * minus + start // quarter_rows
                for x, value in enumerate(transform(values, -1.0, halves)):
                    out_ref[at, x, pl.ds(start % quarter_rows, group), :] = value


def inverse_x_kernel(place_ref, spectrum_ref, own_ref, mirrored_ref, *refs):
    *outs, near_ref = refs
    cells_x, quarter_rows = spectrum_ref.shape[1:3]
    group = min(8, quarter_rows)
    halves = half_sign()
    lane = lax.broadcasted_iota(jnp.int32, (1, LANES), 1)
    side = 1.0 - 2.0 * place_ref[3].astype(F32)

    def rows_of(step, carry):
        rows = pl.ds(pl.multiple_of(step * group, group), group)
        for quarter in range(4):
            values = []
            for kx in range(cells_x):
                green = (own_ref if quarter < 2 else mirrored_ref)[kx, rows, :]
                keep = lane < LANES // 2 if quarter % 2 == 0 else lane >= LANES // 2
                values.append(spectrum_ref[quarter, kx, rows, :] * jnp.where(keep, green, swap(green)))
            even = transform(values[0::2], 1.0, halves)
            odd = transform(values[1::2], 1.0, halves)
            for x in range(cells_x // 2):
                turned = rotate(odd[x], x, cells_x, 1.0, halves) * side
                near_ref[x, quarter, rows, :] = even[x] + turned
                if x < 3:
                    near_ref[cells_x // 2 + x, quarter, rows, :] = even[x] - turned
        return carry

    lax.fori_loop(0, quarter_rows // group, rows_of, 0)
    for k, out_ref in enumerate(outs):
        out_ref[...] = near_ref[pl.ds(lax.bitwise_xor(place_ref[4], k) * XD, XD)]


def inverse_y_kernel(sources, chunk, place_ref, *refs):
    ins, (high_ref, low_ref) = refs[:sources], refs[sources : sources + 2]
    outs, (lines_ref, turned_ref) = refs[sources + 2 : -2], refs[-2:]
    for k in range(sources):
        lines_ref[lax.bitwise_xor(place_ref[4], k)] = ins[k][pl.ds(chunk * DEPTH, DEPTH)]
    parts = []
    for x in range(DEPTH):
        lines = jnp.concatenate([lines_ref[source, x] for source in range(sources)], 0)
        pairs = jnp.concatenate([lines, swap(lines) * half_sign()], 0)
        parts.append(split(pairs))
    both = jnp.concatenate([value for part in parts for value in part], 1)
    main = jnp.dot(high_ref[...], both, preferred_element_type=F32)
    high = jnp.concatenate([part[0] for part in parts], 1)
    rest = jnp.dot(low_ref[...], high, preferred_element_type=F32)
    row = lax.broadcasted_iota(jnp.int32, (NY, 1), 0)
    sign = jnp.where((row % 2 == 1) & (place_ref[3] == 1), -1.0, 1.0)
    for x in range(DEPTH):
        total = main[:, 2 * x * LANES : (2 * x + 1) * LANES] + main[:, (2 * x + 1) * LANES : (2 * x + 2) * LANES]
        total = (total + rest[:, x * LANES : (x + 1) * LANES]) * sign
        turned_ref[:, x] = total.reshape(len(outs), -1, LANES)
    for k in range(len(outs)):
        outs[k][...] = turned_ref[lax.bitwise_xor(place_ref[5], k)]


def inverse_z_kernel(sources, place_ref, *refs):
    ins, (high_ref, low_ref) = refs[:sources], refs[sources : sources + 2]
    out_ref, lines_ref = refs[-2:]
    for k in range(sources):
        lines_ref[lax.bitwise_xor(place_ref[5], k)] = ins[k][...]
    for x in range(DEPTH):
        lines = jnp.concatenate([lines_ref[source, x] for source in range(sources)], 1)
        high, low = split(lines)
        total = jnp.dot(high, high_ref[...], preferred_element_type=F32)
        total += jnp.dot(low, high_ref[...], preferred_element_type=F32)
        total += jnp.dot(high, low_ref[...], preferred_element_type=F32)
        out_ref[x] = total


def gather_kernel(
    place_ref, atoms_ref, table_y, table_z, near_ref, out_ref, shift_ref, fields_ref, stack_ref
):
    step = pl.program_id(0)
    half = LANES // 2
    rows = table_y.shape[1] // 2
    ky_local = rows - 8
    width = atoms_ref.shape[2]
    doms = table_y.shape[2] // width
    planes = near_ref.shape[0]
    halves = half_sign()

    @pl.when(step == 0)
    def _():
        stack_ref[...] = jnp.zeros_like(stack_ref)
        shift_ref[...] = jnp.zeros_like(shift_ref)
        row = lax.broadcasted_iota(jnp.int32, (8, LANES), 0)

        def build(x, carry):
            plus = near_ref[x, pl.ds(0, ky_local), :]
            shift_ref[pl.ds(1, ky_local), :] = near_ref[x, pl.ds(ky_local, ky_local), :]
            minus = shift_ref[pl.ds(0, ky_local), :]
            last = shift_ref[pl.ds(ky_local, 8), :][0:1]
            main = [plus + minus, swap(plus - minus) * halves]
            if 2 * ky_local < LANES:
                main.append(jnp.zeros((LANES - 2 * ky_local, LANES), F32))
            rest = jnp.where(row % 2 == 0, last, -swap(jnp.broadcast_to(last, (8, LANES))) * halves)
            rest = jnp.where(row < 6, rest, 0.0)
            rest_high = rest.astype(BF16).astype(F32)
            rest = jnp.where((row == 2) | (row == 3), rest - rest_high, rest_high)
            high, low = split(jnp.concatenate(main, 0).T)
            fields_ref[x, :, pl.ds(0, LANES)] = high
            fields_ref[x, :, pl.ds(LANES, LANES)] = low
            fields_ref[x, :, pl.ds(2 * LANES, LANES)] = high
            rest = jnp.concatenate([rest, jnp.zeros((LANES - 8, LANES), F32)], 0)
            fields_ref[x, :, pl.ds(3 * LANES, LANES)] = rest.T.astype(BF16)
            return carry

        lax.fori_loop(0, planes, build, 0)

    first_z = place_ref[1].astype(F32)
    twice = jnp.where(first_z + iota((half, 1), 0) == 0.0, 1.0, 2.0)
    fields = fields_ref[pl.ds(step * XD, SPAN)].reshape(SPAN * LANES, 4 * LANES)
    for slot in range(doms):
        lanes = pl.ds(slot * width, width)
        cosine = table_y[step, pl.ds(0, ky_local), lanes]
        sine = table_y[step, pl.ds(rows, ky_local), lanes]
        high, low = split(jnp.concatenate([cosine, sine], 0))
        for part, value in enumerate((high, high, low)):
            stack_ref[pl.ds(LANES * part, 2 * ky_local), lanes] = value
        cosine = table_y[step, pl.ds(ky_local, 8), lanes][0:1]
        sine = table_y[step, pl.ds(rows + ky_local, 8), lanes][0:1]
        row = lax.broadcasted_iota(jnp.int32, (16, width), 0)
        rest = jnp.where(row % 2 == 0, cosine, sine)
        rest_high = rest.astype(BF16).astype(F32)
        rest = jnp.where(row < 4, rest_high, jnp.where(row < 6, rest - rest_high, 0.0))
        stack_ref[pl.ds(3 * LANES, 16), lanes] = rest.astype(BF16)
    product = sum(
        jnp.dot(fields[:, part : part + 2 * LANES], stack_ref[pl.ds(part, 2 * LANES), :], preferred_element_type=F32)
        for part in (0, 2 * LANES)
    )
    for slot in range(doms):
        atoms = atoms_ref[(place_ref[2] + step) * doms + slot]
        along_x = plane_weights(atoms, spline(atoms))
        lanes = pl.ds(slot * width, width)
        field = product[:, slot * width : (slot + 1) * width]
        total = along_x[0:1] * field[:LANES]
        for plane in range(1, SPAN):
            total += along_x[plane : plane + 1] * field[plane * LANES : (plane + 1) * LANES]
        waves = total * table_z[step, :, lanes]
        sampled = jnp.sum((waves[:half] - waves[half:]) * twice, axis=0, keepdims=True)
        out_ref[step * doms + slot] = sampled


def bf16_pair(table):
    high = table.astype(ml_dtypes.bfloat16)
    low = (table - high.astype(np.float64)).astype(ml_dtypes.bfloat16)
    return jnp.asarray(high), jnp.asarray(low)


def inverse_y_table(slab_half, ky_local):
    waves = []
    for slab in range(slab_half):
        first = slab * ky_local
        waves += [first + i for i in range(ky_local)] + [-(first + i + 1) for i in range(ky_local)]
    angle = 2.0 * np.pi * (np.outer(np.arange(NY), np.array(waves)) % NY) / NY
    return bf16_pair(np.concatenate([np.cos(angle), np.sin(angle)], 1))


def inverse_z_table(dom_count):
    kz = np.arange(KH)
    angle = 2.0 * np.pi * (np.outer(kz, np.arange(NZ)) % NZ) / NZ
    weight = np.where(kz == 0, 1.0, 2.0)[:, None]
    parts = [weight * np.cos(angle), -weight * np.sin(angle)]
    return bf16_pair(
        np.stack([p.reshape(dom_count, KH // dom_count, NZ) for p in parts], 1).reshape(2 * KH, NZ)
    )


def whole_spec(shape):
    return pl.BlockSpec(shape, lambda *_: (0,) * len(shape))


SMALL = pl.CostEstimate(flops=10**6, bytes_accessed=10**4, transcendentals=0)
SMEM = pl.BlockSpec(memory_space=pltpu.SMEM)


def params(mib):
    return pltpu.CompilerParams(vmem_limit_bytes=mib * MIB)


def swapped(value, axis, distance):
    if distance == 0:
        return value
    return lax.ppermute(value, axis, [(i, i ^ distance) for i in range(lax.axis_size(axis))])


def per_device(base_cells, offsets, charges, bias_coupling, counts, green):
    slabs = lax.axis_size("slab")
    doms = lax.axis_size("dom")
    slab = lax.axis_index("slab")
    dom = lax.axis_index("dom")
    atoms_local = charges.shape[0]
    cells_x = XD * slabs
    ky_local = NY // slabs
    kz_local = KH // doms
    slab_half = slabs // 2
    rows_local = NY // doms
    rows = ky_local + 8
    quarter_rows = ky_local // 2
    normalize = 1.0 / (cells_x * NY * NZ)
    upper = slab // slab_half
    place = jnp.stack(
        [slab * ky_local, dom * kz_local, upper * slab_half, upper, slab % slab_half, dom]
    ).astype(jnp.int32)

    vmem = pl.BlockSpec(memory_space=pltpu.VMEM)
    atoms = pl.pallas_call(
        pack_kernel,
        in_specs=[SMEM, vmem, vmem, vmem],
        out_specs=vmem,
        out_shape=jax.ShapeDtypeStruct((slabs * doms, 8, atoms_local), F32),
        name="pack",
    )(counts, base_cells, offsets, charges.reshape(1, atoms_local))
    factors_y, factors_z = pl.pallas_call(
        wave_kernel,
        in_specs=[SMEM],
        out_specs=[vmem] * 2,
        out_shape=[jax.ShapeDtypeStruct((4 * count, TERMS), BF16) for count in (rows, LANES // 2)],
        compiler_params=params(8),
        name="waves",
    )(place)
    gathered = lax.all_to_all(atoms, ("slab", "dom"), 0, 0, tiled=True)

    def halves_beside(value):
        return jnp.concatenate([value[:, :quarter_rows], value[:, quarter_rows:]], 2) * normalize

    own = halves_beside(green)
    gathered, flipped, factors_y, factors_z = lax.optimization_barrier(
        (gathered, halves_beside(green[:, ::-1]), factors_y, factors_z)
    )
    mirrored = lax.ppermute(flipped, "slab", [(s, slabs - 1 - s) for s in range(slabs)])

    atoms_slab = doms * atoms_local
    table_bytes = 4 * (slab_half + 1) * (2 * rows + LANES) * atoms_slab
    spectrum_bytes = 16 * cells_x * max(8, quarter_rows) * LANES
    spectrum, table_y, table_z = pl.pallas_call(
        forward_kernel,
        grid=(slabs,),
        in_specs=[SMEM] + [vmem] * 3,
        out_specs=[vmem] * 3,
        out_shape=[
            jax.ShapeDtypeStruct((4, cells_x, quarter_rows, LANES), F32),
            jax.ShapeDtypeStruct((slab_half + 1, 2 * rows, atoms_slab), F32),
            jax.ShapeDtypeStruct((slab_half + 1, LANES, atoms_slab), F32),
        ],
        scratch_shapes=[
            pltpu.VMEM((doms, SPAN * 4 * rows, atoms_local), BF16),
            pltpu.VMEM((doms, atoms_local, 2 * LANES), BF16),
            pltpu.VMEM((cells_x, 2 * rows, LANES), F32),
            pltpu.VMEM((doms, TERMS, atoms_local), BF16),
            pltpu.VMEM((doms, TERMS, atoms_local), BF16),
        ],
        compiler_params=params(16 + (table_bytes + spectrum_bytes) // MIB),
        cost_estimate=SMALL,
        name="forward",
    )(place, gathered, factors_y, factors_z)

    near_planes = cells_x // 2 + 3
    piece = (XD, 4, quarter_rows, LANES)
    *pieces, near = pl.pallas_call(
        inverse_x_kernel,
        in_specs=[SMEM] + [vmem] * 3,
        out_specs=[vmem] * (slab_half + 1),
        out_shape=[jax.ShapeDtypeStruct(piece, F32)] * slab_half
        + [jax.ShapeDtypeStruct((near_planes, 4, quarter_rows, LANES), F32)],
        compiler_params=params(32),
        cost_estimate=SMALL,
        name="inverse_x",
    )(place, spectrum, own, mirrored)

    partial = pl.pallas_call(
        gather_kernel,
        grid=(slab_half,),
        in_specs=[SMEM] + [vmem] * 4,
        out_specs=vmem,
        out_shape=jax.ShapeDtypeStruct((slab_half * doms, 1, atoms_local), F32),
        scratch_shapes=[
            pltpu.VMEM((rows, LANES), F32),
            pltpu.VMEM((near_planes, LANES, 4 * LANES), BF16),
            pltpu.VMEM((4 * LANES, atoms_slab), BF16),
        ],
        compiler_params=params(12 + (table_bytes + 8 * near_planes * LANES * LANES) // MIB),
        cost_estimate=SMALL,
        name="gather",
    )(place, gathered, table_y, table_z, near.reshape(near_planes, 2 * ky_local, LANES))

    high_y, low_y = inverse_y_table(slab_half, ky_local)
    high_z, low_z = inverse_z_table(doms)
    lines = [swapped(value.reshape(XD, 2 * ky_local, LANES), "slab", k) for k, value in enumerate(pieces)]
    partial, *lines = lax.optimization_barrier((partial, *lines))

    potential = None
    for chunk in range(CHUNKS):
        turned = pl.pallas_call(
            functools.partial(inverse_y_kernel, slab_half, chunk),
            in_specs=[SMEM] + [vmem] * (slab_half + 2),
            out_specs=[vmem] * doms,
            out_shape=[jax.ShapeDtypeStruct((DEPTH, rows_local, LANES), F32)] * doms,
            scratch_shapes=[
                pltpu.VMEM((slab_half, DEPTH, 2 * ky_local, LANES), F32),
                pltpu.VMEM((doms, DEPTH, rows_local, LANES), F32),
            ],
            compiler_params=params(24),
            cost_estimate=SMALL,
            name="inverse_y",
        )(place, *lines, high_y, low_y)
        if chunk == CHUNKS - 1:
            partial, *turned = lax.optimization_barrier((partial, *turned))
        columns = [swapped(value, "dom", k) for k, value in enumerate(turned)]
        earlier = [] if potential is None else [potential]
        potential = pl.pallas_call(
            functools.partial(inverse_z_kernel, doms),
            grid=(1,),
            in_specs=[SMEM]
            + [whole_spec((DEPTH, rows_local, LANES))] * doms
            + [whole_spec((2 * KH, NZ))] * 2
            + [pl.BlockSpec(memory_space=pl.ANY)] * len(earlier),
            out_specs=pl.BlockSpec((DEPTH, rows_local, NZ), lambda _, at=chunk: (at, 0, 0)),
            out_shape=jax.ShapeDtypeStruct((XD, rows_local, NZ), F32),
            scratch_shapes=[pltpu.VMEM((doms, DEPTH, rows_local, LANES), F32)],
            input_output_aliases={doms + 3: 0} if earlier else {},
            compiler_params=params(24),
            cost_estimate=SMALL,
            name="inverse_z",
        )(place, *columns, high_z, low_z, *earlier)

    members = slab_half * doms
    sampled = lax.all_to_all(
        partial.reshape(members, atoms_local),
        ("slab", "dom"),
        0,
        0,
        axis_index_groups=[list(range(members)), list(range(members, 2 * members))],
        tiled=True,
    )
    alive = jnp.arange(atoms_local, dtype=jnp.int32) < counts[0]
    gradient = jnp.where(alive, bias_coupling * jnp.sum(sampled, 0), 0.0)
    return (potential, gradient)


def solution(mesh):
    placed = (
        P(None, ("slab", "dom")),
        P(None, ("slab", "dom")),
        P(("slab", "dom")),
        P(("slab", "dom")),
        P(("slab", "dom")),
        P(None, "slab", "dom"),
    )
    return jax.shard_map(
        per_device,
        mesh=mesh,
        in_specs=placed,
        out_specs=(P("slab", "dom", None), P(("slab", "dom"))),
        check_vma=False,
    )
```

```python
import functools

import jax
import jax.numpy as jnp
import ml_dtypes
import numpy as np
from jax import lax
from jax.experimental import pallas as pl
from jax.experimental.pallas import tpu as pltpu
from jax.sharding import PartitionSpec as P

XD = 4
NY = 512
NZ = 512
KH = NZ // 2
LANES = 128
SPAN = XD + 3
CHUNKS = 1
DEPTH = XD // CHUNKS
MIB = 1 << 20
BF16 = jnp.bfloat16
F32 = jnp.float32


def polynomial(function, terms):
    nodes = 0.125 * (1.0 - np.cos(np.pi * (np.arange(64) + 0.5) / 64))
    powers = nodes[:, None] ** np.arange(terms)[None, :]
    return [float(v) for v in np.linalg.lstsq(powers, function(np.sqrt(nodes)), rcond=None)[0]]


SINE_TERMS = polynomial(lambda r: np.sin(np.pi * r) / r, 6)
COSINE_TERMS = polynomial(lambda r: np.cos(np.pi * r), 6)


def horner(terms, square):
    total = jnp.full_like(square, terms[-1])
    for term in terms[-2::-1]:
        total = total * square + term
    return total


def turn(fraction):
    left = fraction - jnp.floor(fraction + 0.5)
    square = left * left
    sine = left * horner(SINE_TERMS, square)
    cosine = horner(COSINE_TERMS, square)
    return 1.0 - 2.0 * sine * sine, 2.0 * sine * cosine


def spline(frac):
    inner = 1.0 - frac
    square = frac * frac
    cube = square * frac
    sixth = 1.0 / 6.0
    return (
        inner * inner * inner * sixth,
        (3.0 * cube - 6.0 * square + 4.0) * sixth,
        (-3.0 * cube + 3.0 * square + 3.0 * frac + 1.0) * sixth,
        cube * sixth,
    )


def split(value):
    high = value.astype(BF16)
    return high, (value - high.astype(F32)).astype(BF16)


def iota(shape, axis):
    return lax.broadcasted_iota(jnp.int32, shape, axis).astype(F32)


RADIX = 16
DIGITS = 32
TERMS = 256


def wave_factors(first, rows, length):
    lane = lax.broadcasted_iota(jnp.int32, (rows, TERMS), 1)
    section = lane // DIGITS
    digit = (lane % DIGITS).astype(F32) * jnp.where(section < 2, float(RADIX), 1.0)
    parts = []
    for value in turn((first + iota((rows, TERMS), 0)) * digit * (1.0 / length)):
        high = value.astype(BF16).astype(F32)
        parts.append(jnp.where((section == 1) | (section == 3), value - high, high))
    upper, lower = section < 2, (section >= 2) & (section < 5)
    masked = [jnp.where(mask, part, 0.0) for mask in (upper, lower) for part in parts]
    return jnp.concatenate(masked, 0).astype(BF16)


def wave_kernel(place_ref, out_y_ref, out_z_ref):
    out_y_ref[...] = wave_factors(place_ref[0].astype(F32), out_y_ref.shape[0] // 4, NY)
    out_z_ref[...] = wave_factors(place_ref[1].astype(F32), out_z_ref.shape[0] // 4, NZ)


def atom_waves(base, weights, factors_ref, digits_ref):
    width = base.shape[1]
    high_digit = jnp.floor(base * (1.0 / RADIX))
    row = iota((DIGITS, width), 0)
    chosen = jnp.where(row == high_digit, 1.0, 0.0).astype(BF16)
    step = row - (base - RADIX * high_digit)
    spread = jnp.where(step == 3.0, weights[3], 0.0)
    for r in (2, 1, 0):
        spread = jnp.where(step == float(r), weights[r], spread)
    high, low = split(spread)
    for section, value in enumerate((chosen, chosen, high, high, low)):
        digits_ref[pl.ds(DIGITS * section, DIGITS), :] = value
    product = jnp.dot(factors_ref[...], digits_ref[...], preferred_element_type=F32)
    rows = product.shape[0] // 4
    cos_a, sin_a, cos_b, sin_b = (product[i * rows : (i + 1) * rows] for i in range(4))
    return cos_a * cos_b - sin_a * sin_b, sin_a * cos_b + cos_a * sin_b


def plane_weights(atoms, weights):
    row = iota((8, atoms.shape[1]), 0) - atoms[0:1]
    return sum(weights[r][3:4] * (row == float(r)).astype(F32) for r in range(4))


def swap(value):
    return pltpu.roll(value, LANES // 2, axis=value.ndim - 1)


def half_sign():
    lane = lax.broadcasted_iota(jnp.int32, (1, LANES), 1)
    return jnp.where(lane < LANES // 2, -1.0, 1.0).astype(F32)


def rotate(value, numer, denom, sign):
    real, imag = value
    if numer == 0:
        return value
    if 4 * numer == denom:
        return (-imag, real) if sign > 0 else (imag, -real)
    angle = 2.0 * np.pi * numer / denom
    cosine, sine = float(np.cos(angle)), float(sign * np.sin(angle))
    if 8 * numer in (denom, 3 * denom):
        size = abs(cosine)
        cos_sign, sin_sign = (1 if cosine > 0 else -1), (1 if sine > 0 else -1)
        if cos_sign == sin_sign:
            return ((real - imag) * (cos_sign * size), (real + imag) * (cos_sign * size))
        return ((real + imag) * (cos_sign * size), (imag - real) * (cos_sign * size))
    return real * cosine - imag * sine, imag * cosine + real * sine


def butterfly(even, turned):
    plus = (even[0] + turned[0], even[1] + turned[1])
    return plus, (even[0] - turned[0], even[1] - turned[1])


def transform(values, sign):
    count = len(values)
    if count == 1:
        return values
    even = transform(values[0::2], sign)
    odd = transform(values[1::2], sign)
    both = [butterfly(even[k], rotate(odd[k], k, count, sign)) for k in range(count // 2)]
    return [pair[0] for pair in both] + [pair[1] for pair in both]


def regroup(low, high):
    first = lax.broadcasted_iota(jnp.int32, low.shape, 1) < LANES // 2
    crossed = swap(jnp.where(first, high, low))
    return jnp.where(first, low, crossed), jnp.where(first, crossed, high)


def pack_kernel(counts_ref, cells_ref, offsets_ref, charges_ref, out_ref):
    width = offsets_ref.shape[1]
    alive = lax.broadcasted_iota(jnp.int32, (1, width), 1) < counts_ref[0]
    atoms = jnp.concatenate(
        [
            lax.bitwise_and(cells_ref[0:1, :], XD - 1).astype(F32),
            cells_ref[1:3, :].astype(F32),
            offsets_ref[...],
            jnp.where(alive, charges_ref[...], 0.0),
            jnp.zeros((1, width), F32),
        ],
        0,
    )
    for copy in range(out_ref.shape[0]):
        out_ref[copy] = atoms


def forward_kernel(
    place_ref,
    atoms_ref,
    factors_y,
    factors_z,
    out_ref,
    table_y,
    table_z,
    left_ref,
    right_ref,
    grid_ref,
    digits_y,
    digits_z,
):
    step = pl.program_id(0)
    cells_x = grid_ref.shape[0]
    rows = grid_ref.shape[1] // 2
    ky_local = rows - 8
    width = atoms_ref.shape[2]
    doms = table_y.shape[2] // width
    kept = step - place_ref[2]
    kept = jnp.where((kept >= 0) & (kept < table_y.shape[0] - 1), kept, table_y.shape[0] - 1)

    @pl.when(step == 0)
    def _():
        grid_ref[...] = jnp.zeros_like(grid_ref)
        digits_y[...] = jnp.zeros_like(digits_y)
        digits_z[...] = jnp.zeros_like(digits_z)

    for slot in range(doms):
        atoms = atoms_ref[step * doms + slot]
        lanes = pl.ds(slot * width, width)
        weights = spline(atoms)
        along_x = plane_weights(atoms, weights) * atoms[6:7]
        waves = atom_waves(atoms[2:3], [w[5:6] for w in weights], factors_z, digits_z.at[slot])
        waves = jnp.concatenate(waves, 0)
        table_z[kept, :, lanes] = waves
        high, low = split(waves.T)
        right_ref[slot, :, :LANES] = high
        right_ref[slot, :, LANES:] = low
        cosine, sine = atom_waves(atoms[1:2], [w[4:5] for w in weights], factors_y, digits_y.at[slot])
        waves = jnp.concatenate([cosine, sine], 0)
        table_y[kept, :, lanes] = waves
        for plane in range(SPAN):
            first = 4 * rows * plane
            high, low = split(waves * along_x[plane : plane + 1])
            left_ref[slot, pl.ds(first, 2 * rows), :] = high
            left_ref[slot, pl.ds(first + 2 * rows, 2 * rows), :] = low
        product = jnp.dot(left_ref[slot], right_ref[slot], preferred_element_type=F32)
        for plane in range(SPAN):
            first = 4 * rows * plane
            high, low = product[first : first + 2 * rows], product[first + 2 * rows : first + 4 * rows]
            at = lax.rem(step * XD + plane, cells_x)
            grid_ref[at] += (high[:, :LANES] + high[:, LANES:]) + (low[:, :LANES] + low[:, LANES:])

    @pl.when(step == pl.num_programs(0) - 1)
    def _():
        quarter_rows = ky_local // 2
        group = min(8, quarter_rows)
        for minus in (0, 1):
            for start in range(0, quarter_rows, group):
                values = []
                for x in range(cells_x):
                    parts = [
                        grid_ref[x, pl.ds(minus + start + offset, group), :]
                        for offset in (0, quarter_rows, rows, rows + quarter_rows)
                    ]
                    cos_cos, cos_sin = regroup(parts[0], parts[1])
                    sin_cos, sin_sin = regroup(parts[2], parts[3])
                    if minus:
                        values.append((cos_cos + sin_sin, sin_cos - cos_sin))
                    else:
                        values.append((cos_cos - sin_sin, -cos_sin - sin_cos))
                for x, value in enumerate(transform(values, -1)):
                    for part in (0, 1):
                        out_ref[2 * minus + part, x, pl.ds(start, group), :] = value[part]


def inverse_x_kernel(place_ref, spectrum_ref, own_ref, mirrored_ref, *refs):
    *outs, near_ref = refs
    cells_x, quarter_rows = spectrum_ref.shape[1:3]
    group = min(8, quarter_rows)
    side = 1.0 - 2.0 * place_ref[3].astype(F32)

    def rows_of(step, carry):
        rows = pl.ds(pl.multiple_of(step * group, group), group)
        for minus, green_ref in enumerate((own_ref, mirrored_ref)):
            values = []
            for kx in range(cells_x):
                green = green_ref[kx, rows, :]
                values.append(tuple(spectrum_ref[2 * minus + part, kx, rows, :] * green for part in (0, 1)))
            even = transform(values[0::2], 1)
            odd = transform([(value[0] * side, value[1] * side) for value in values[1::2]], 1)
            for x in range(cells_x // 2):
                here, there = butterfly(even[x], rotate(odd[x], x, cells_x, 1))
                wanted = [(x, here)] + ([(cells_x // 2 + x, there)] if x < 3 else [])
                for plane, value in wanted:
                    low, high = regroup(value[0], value[1])
                    near_ref[plane, 2 * minus, rows, :] = low
                    near_ref[plane, 2 * minus + 1, rows, :] = high
        return carry

    lax.fori_loop(0, quarter_rows // group, rows_of, 0)
    for k, out_ref in enumerate(outs):
        out_ref[...] = near_ref[pl.ds(lax.bitwise_xor(place_ref[4], k) * XD, XD)]


def inverse_y_kernel(sources, chunk, place_ref, *refs):
    ins, (high_ref, low_ref) = refs[:sources], refs[sources : sources + 2]
    outs, (lines_ref, turned_ref) = refs[sources + 2 : -2], refs[-2:]
    for k in range(sources):
        lines_ref[lax.bitwise_xor(place_ref[4], k)] = ins[k][pl.ds(chunk * DEPTH, DEPTH)]
    parts = []
    for x in range(DEPTH):
        lines = jnp.concatenate([lines_ref[source, x] for source in range(sources)], 0)
        pairs = jnp.concatenate([lines, swap(lines) * half_sign()], 0)
        parts.append(split(pairs))
    both = jnp.concatenate([value for part in parts for value in part], 1)
    main = jnp.dot(high_ref[...], both, preferred_element_type=F32)
    high = jnp.concatenate([part[0] for part in parts], 1)
    rest = jnp.dot(low_ref[...], high, preferred_element_type=F32)
    row = lax.broadcasted_iota(jnp.int32, (NY, 1), 0)
    sign = jnp.where((row % 2 == 1) & (place_ref[3] == 1), -1.0, 1.0)
    for x in range(DEPTH):
        total = main[:, 2 * x * LANES : (2 * x + 1) * LANES] + main[:, (2 * x + 1) * LANES : (2 * x + 2) * LANES]
        total = (total + rest[:, x * LANES : (x + 1) * LANES]) * sign
        turned_ref[:, x] = total.reshape(len(outs), -1, LANES)
    for k in range(len(outs)):
        outs[k][...] = turned_ref[lax.bitwise_xor(place_ref[5], k)]


def inverse_z_kernel(sources, place_ref, *refs):
    ins, (high_ref, low_ref) = refs[:sources], refs[sources : sources + 2]
    out_ref, lines_ref = refs[-2:]
    for k in range(sources):
        lines_ref[lax.bitwise_xor(place_ref[5], k)] = ins[k][...]
    for x in range(DEPTH):
        lines = jnp.concatenate([lines_ref[source, x] for source in range(sources)], 1)
        high, low = split(lines)
        total = jnp.dot(high, high_ref[...], preferred_element_type=F32)
        total += jnp.dot(low, high_ref[...], preferred_element_type=F32)
        total += jnp.dot(high, low_ref[...], preferred_element_type=F32)
        out_ref[x] = total


def gather_kernel(
    place_ref, atoms_ref, table_y, table_z, near_ref, out_ref, shift_ref, fields_ref, stack_ref
):
    step = pl.program_id(0)
    half = LANES // 2
    rows = table_y.shape[1] // 2
    ky_local = rows - 8
    width = atoms_ref.shape[2]
    doms = table_y.shape[2] // width
    planes = near_ref.shape[0]
    halves = half_sign()

    @pl.when(step == 0)
    def _():
        stack_ref[...] = jnp.zeros_like(stack_ref)
        shift_ref[...] = jnp.zeros_like(shift_ref)
        row = lax.broadcasted_iota(jnp.int32, (8, LANES), 0)

        def build(x, carry):
            plus = near_ref[x, pl.ds(0, ky_local), :]
            shift_ref[pl.ds(1, ky_local), :] = near_ref[x, pl.ds(ky_local, ky_local), :]
            minus = shift_ref[pl.ds(0, ky_local), :]
            last = shift_ref[pl.ds(ky_local, 8), :][0:1]
            main = [plus + minus, swap(plus - minus) * halves]
            if 2 * ky_local < LANES:
                main.append(jnp.zeros((LANES - 2 * ky_local, LANES), F32))
            rest = jnp.where(row % 2 == 0, last, -swap(jnp.broadcast_to(last, (8, LANES))) * halves)
            rest = jnp.where(row < 6, rest, 0.0)
            rest_high = rest.astype(BF16).astype(F32)
            rest = jnp.where((row == 2) | (row == 3), rest - rest_high, rest_high)
            high, low = split(jnp.concatenate(main, 0).T)
            fields_ref[x, :, pl.ds(0, LANES)] = high
            fields_ref[x, :, pl.ds(LANES, LANES)] = low
            fields_ref[x, :, pl.ds(2 * LANES, LANES)] = high
            rest = jnp.concatenate([rest, jnp.zeros((LANES - 8, LANES), F32)], 0)
            fields_ref[x, :, pl.ds(3 * LANES, LANES)] = rest.T.astype(BF16)
            return carry

        lax.fori_loop(0, planes, build, 0)

    first_z = place_ref[1].astype(F32)
    twice = jnp.where(first_z + iota((half, 1), 0) == 0.0, 1.0, 2.0)
    fields = fields_ref[pl.ds(step * XD, SPAN)].reshape(SPAN * LANES, 4 * LANES)
    for slot in range(doms):
        lanes = pl.ds(slot * width, width)
        cosine = table_y[step, pl.ds(0, ky_local), lanes]
        sine = table_y[step, pl.ds(rows, ky_local), lanes]
        high, low = split(jnp.concatenate([cosine, sine], 0))
        for part, value in enumerate((high, high, low)):
            stack_ref[pl.ds(LANES * part, 2 * ky_local), lanes] = value
        cosine = table_y[step, pl.ds(ky_local, 8), lanes][0:1]
        sine = table_y[step, pl.ds(rows + ky_local, 8), lanes][0:1]
        row = lax.broadcasted_iota(jnp.int32, (16, width), 0)
        rest = jnp.where(row % 2 == 0, cosine, sine)
        rest_high = rest.astype(BF16).astype(F32)
        rest = jnp.where(row < 4, rest_high, jnp.where(row < 6, rest - rest_high, 0.0))
        stack_ref[pl.ds(3 * LANES, 16), lanes] = rest.astype(BF16)
    product = sum(
        jnp.dot(fields[:, part : part + 2 * LANES], stack_ref[pl.ds(part, 2 * LANES), :], preferred_element_type=F32)
        for part in (0, 2 * LANES)
    )
    for slot in range(doms):
        atoms = atoms_ref[(place_ref[2] + step) * doms + slot]
        along_x = plane_weights(atoms, spline(atoms))
        lanes = pl.ds(slot * width, width)
        field = product[:, slot * width : (slot + 1) * width]
        total = along_x[0:1] * field[:LANES]
        for plane in range(1, SPAN):
            total += along_x[plane : plane + 1] * field[plane * LANES : (plane + 1) * LANES]
        waves = total * table_z[step, :, lanes]
        sampled = jnp.sum((waves[:half] - waves[half:]) * twice, axis=0, keepdims=True)
        out_ref[step * doms + slot] = sampled


def bf16_pair(table):
    high = table.astype(ml_dtypes.bfloat16)
    low = (table - high.astype(np.float64)).astype(ml_dtypes.bfloat16)
    return jnp.asarray(high), jnp.asarray(low)


def inverse_y_table(slab_half, ky_local):
    waves = []
    for slab in range(slab_half):
        first = slab * ky_local
        waves += [first + i for i in range(ky_local)] + [-(first + i + 1) for i in range(ky_local)]
    angle = 2.0 * np.pi * (np.outer(np.arange(NY), np.array(waves)) % NY) / NY
    return bf16_pair(np.concatenate([np.cos(angle), np.sin(angle)], 1))


def inverse_z_table(dom_count):
    kz = np.arange(KH)
    angle = 2.0 * np.pi * (np.outer(kz, np.arange(NZ)) % NZ) / NZ
    weight = np.where(kz == 0, 1.0, 2.0)[:, None]
    parts = [weight * np.cos(angle), -weight * np.sin(angle)]
    return bf16_pair(
        np.stack([p.reshape(dom_count, KH // dom_count, NZ) for p in parts], 1).reshape(2 * KH, NZ)
    )


def whole_spec(shape):
    return pl.BlockSpec(shape, lambda *_: (0,) * len(shape))


SMALL = pl.CostEstimate(flops=10**6, bytes_accessed=10**4, transcendentals=0)
SMEM = pl.BlockSpec(memory_space=pltpu.SMEM)


def params(mib):
    return pltpu.CompilerParams(vmem_limit_bytes=mib * MIB)


def swapped(value, axis, distance):
    if distance == 0:
        return value
    return lax.ppermute(value, axis, [(i, i ^ distance) for i in range(lax.axis_size(axis))])


def per_device(base_cells, offsets, charges, bias_coupling, counts, green):
    slabs = lax.axis_size("slab")
    doms = lax.axis_size("dom")
    slab = lax.axis_index("slab")
    dom = lax.axis_index("dom")
    atoms_local = charges.shape[0]
    cells_x = XD * slabs
    ky_local = NY // slabs
    kz_local = KH // doms
    slab_half = slabs // 2
    rows_local = NY // doms
    rows = ky_local + 8
    quarter_rows = ky_local // 2
    normalize = 1.0 / (cells_x * NY * NZ)
    upper = slab // slab_half
    place = jnp.stack(
        [slab * ky_local, dom * kz_local, upper * slab_half, upper, slab % slab_half, dom]
    ).astype(jnp.int32)

    vmem = pl.BlockSpec(memory_space=pltpu.VMEM)
    atoms = pl.pallas_call(
        pack_kernel,
        in_specs=[SMEM, vmem, vmem, vmem],
        out_specs=vmem,
        out_shape=jax.ShapeDtypeStruct((slabs * doms, 8, atoms_local), F32),
        name="pack",
    )(counts, base_cells, offsets, charges.reshape(1, atoms_local))
    factors_y, factors_z = pl.pallas_call(
        wave_kernel,
        in_specs=[SMEM],
        out_specs=[vmem] * 2,
        out_shape=[jax.ShapeDtypeStruct((4 * count, TERMS), BF16) for count in (rows, LANES // 2)],
        compiler_params=params(8),
        name="waves",
    )(place)
    gathered = lax.all_to_all(atoms, ("slab", "dom"), 0, 0, tiled=True)

    def halves_beside(value):
        return jnp.concatenate([value[:, :quarter_rows], value[:, quarter_rows:]], 2) * normalize

    own = halves_beside(green)
    gathered, flipped, factors_y, factors_z = lax.optimization_barrier(
        (gathered, halves_beside(green[:, ::-1]), factors_y, factors_z)
    )
    mirrored = lax.ppermute(flipped, "slab", [(s, slabs - 1 - s) for s in range(slabs)])

    atoms_slab = doms * atoms_local
    table_bytes = 4 * (slab_half + 1) * (2 * rows + LANES) * atoms_slab
    spectrum_bytes = 16 * cells_x * max(8, quarter_rows) * LANES
    spectrum, table_y, table_z = pl.pallas_call(
        forward_kernel,
        grid=(slabs,),
        in_specs=[SMEM] + [vmem] * 3,
        out_specs=[vmem] * 3,
        out_shape=[
            jax.ShapeDtypeStruct((4, cells_x, quarter_rows, LANES), F32),
            jax.ShapeDtypeStruct((slab_half + 1, 2 * rows, atoms_slab), F32),
            jax.ShapeDtypeStruct((slab_half + 1, LANES, atoms_slab), F32),
        ],
        scratch_shapes=[
            pltpu.VMEM((doms, SPAN * 4 * rows, atoms_local), BF16),
            pltpu.VMEM((doms, atoms_local, 2 * LANES), BF16),
            pltpu.VMEM((cells_x, 2 * rows, LANES), F32),
            pltpu.VMEM((doms, TERMS, atoms_local), BF16),
            pltpu.VMEM((doms, TERMS, atoms_local), BF16),
        ],
        compiler_params=params(16 + (table_bytes + spectrum_bytes) // MIB),
        cost_estimate=SMALL,
        name="forward",
    )(place, gathered, factors_y, factors_z)

    near_planes = cells_x // 2 + 3
    piece = (XD, 4, quarter_rows, LANES)
    *pieces, near = pl.pallas_call(
        inverse_x_kernel,
        in_specs=[SMEM] + [vmem] * 3,
        out_specs=[vmem] * (slab_half + 1),
        out_shape=[jax.ShapeDtypeStruct(piece, F32)] * slab_half
        + [jax.ShapeDtypeStruct((near_planes, 4, quarter_rows, LANES), F32)],
        compiler_params=params(32),
        cost_estimate=SMALL,
        name="inverse_x",
    )(place, spectrum, own, mirrored)

    partial = pl.pallas_call(
        gather_kernel,
        grid=(slab_half,),
        in_specs=[SMEM] + [vmem] * 4,
        out_specs=vmem,
        out_shape=jax.ShapeDtypeStruct((slab_half * doms, 1, atoms_local), F32),
        scratch_shapes=[
            pltpu.VMEM((rows, LANES), F32),
            pltpu.VMEM((near_planes, LANES, 4 * LANES), BF16),
            pltpu.VMEM((4 * LANES, atoms_slab), BF16),
        ],
        compiler_params=params(12 + (table_bytes + 8 * near_planes * LANES * LANES) // MIB),
        cost_estimate=SMALL,
        name="gather",
    )(place, gathered, table_y, table_z, near.reshape(near_planes, 2 * ky_local, LANES))

    high_y, low_y = inverse_y_table(slab_half, ky_local)
    high_z, low_z = inverse_z_table(doms)
    lines = [swapped(value.reshape(XD, 2 * ky_local, LANES), "slab", k) for k, value in enumerate(pieces)]
    partial, *lines = lax.optimization_barrier((partial, *lines))

    potential = None
    for chunk in range(CHUNKS):
        turned = pl.pallas_call(
            functools.partial(inverse_y_kernel, slab_half, chunk),
            in_specs=[SMEM] + [vmem] * (slab_half + 2),
            out_specs=[vmem] * doms,
            out_shape=[jax.ShapeDtypeStruct((DEPTH, rows_local, LANES), F32)] * doms,
            scratch_shapes=[
                pltpu.VMEM((slab_half, DEPTH, 2 * ky_local, LANES), F32),
                pltpu.VMEM((doms, DEPTH, rows_local, LANES), F32),
            ],
            compiler_params=params(32),
            cost_estimate=SMALL,
            name="inverse_y",
        )(place, *lines, high_y, low_y)
        columns = [swapped(value, "dom", k) for k, value in enumerate(turned)]
        if chunk == CHUNKS - 1:
            partial, columns[1] = lax.optimization_barrier((partial, columns[1]))
        earlier = [] if potential is None else [potential]
        potential = pl.pallas_call(
            functools.partial(inverse_z_kernel, doms),
            grid=(1,),
            in_specs=[SMEM]
            + [whole_spec((DEPTH, rows_local, LANES))] * doms
            + [whole_spec((2 * KH, NZ))] * 2
            + [pl.BlockSpec(memory_space=pl.ANY)] * len(earlier),
            out_specs=pl.BlockSpec((DEPTH, rows_local, NZ), lambda _, at=chunk: (at, 0, 0)),
            out_shape=jax.ShapeDtypeStruct((XD, rows_local, NZ), F32),
            scratch_shapes=[pltpu.VMEM((doms, DEPTH, rows_local, LANES), F32)],
            input_output_aliases={doms + 3: 0} if earlier else {},
            compiler_params=params(24),
            cost_estimate=SMALL,
            name="inverse_z",
        )(place, *columns, high_z, low_z, *earlier)

    members = slab_half * doms
    sampled = lax.all_to_all(
        partial.reshape(members, atoms_local),
        ("slab", "dom"),
        0,
        0,
        axis_index_groups=[list(range(members)), list(range(members, 2 * members))],
        tiled=True,
    )
    alive = jnp.arange(atoms_local, dtype=jnp.int32) < counts[0]
    gradient = jnp.where(alive, bias_coupling * jnp.sum(sampled, 0), 0.0)
    return (potential, gradient)


def solution(mesh):
    placed = (
        P(None, ("slab", "dom")),
        P(None, ("slab", "dom")),
        P(("slab", "dom")),
        P(("slab", "dom")),
        P(("slab", "dom")),
        P(None, "slab", "dom"),
    )
    return jax.shard_map(
        per_device,
        mesh=mesh,
        in_specs=placed,
        out_specs=(P("slab", "dom", None), P(("slab", "dom"))),
        check_vma=False,
    )
```

```python
import functools

import jax
import jax.numpy as jnp
import ml_dtypes
import numpy as np
from jax import lax
from jax.experimental import pallas as pl
from jax.experimental.pallas import tpu as pltpu
from jax.sharding import PartitionSpec as P

XD = 4
NY = 512
NZ = 512
KH = NZ // 2
LANES = 128
SPAN = XD + 3
CHUNKS = 1
DEPTH = XD // CHUNKS
MIB = 1 << 20
BF16 = jnp.bfloat16
F32 = jnp.float32


def polynomial(function, terms):
    nodes = 0.125 * (1.0 - np.cos(np.pi * (np.arange(64) + 0.5) / 64))
    powers = nodes[:, None] ** np.arange(terms)[None, :]
    return [float(v) for v in np.linalg.lstsq(powers, function(np.sqrt(nodes)), rcond=None)[0]]


SINE_TERMS = polynomial(lambda r: np.sin(np.pi * r) / r, 6)
COSINE_TERMS = polynomial(lambda r: np.cos(np.pi * r), 6)


def horner(terms, square):
    total = jnp.full_like(square, terms[-1])
    for term in terms[-2::-1]:
        total = total * square + term
    return total


def turn(fraction):
    left = fraction - jnp.floor(fraction + 0.5)
    square = left * left
    sine = left * horner(SINE_TERMS, square)
    cosine = horner(COSINE_TERMS, square)
    return 1.0 - 2.0 * sine * sine, 2.0 * sine * cosine


def spline(frac):
    inner = 1.0 - frac
    square = frac * frac
    cube = square * frac
    sixth = 1.0 / 6.0
    return (
        inner * inner * inner * sixth,
        (3.0 * cube - 6.0 * square + 4.0) * sixth,
        (-3.0 * cube + 3.0 * square + 3.0 * frac + 1.0) * sixth,
        cube * sixth,
    )


def split(value):
    high = value.astype(BF16)
    return high, (value - high.astype(F32)).astype(BF16)


def iota(shape, axis):
    return lax.broadcasted_iota(jnp.int32, shape, axis).astype(F32)


RADIX = 16
DIGITS = 32
TERMS = 256


def wave_factors(first, rows, length):
    lane = lax.broadcasted_iota(jnp.int32, (rows, TERMS), 1)
    section = lane // DIGITS
    digit = (lane % DIGITS).astype(F32) * jnp.where(section < 2, float(RADIX), 1.0)
    parts = []
    for value in turn((first + iota((rows, TERMS), 0)) * digit * (1.0 / length)):
        high = value.astype(BF16).astype(F32)
        parts.append(jnp.where((section == 1) | (section == 3), value - high, high))
    upper, lower = section < 2, (section >= 2) & (section < 5)
    masked = [jnp.where(mask, part, 0.0) for mask in (upper, lower) for part in parts]
    return jnp.concatenate(masked, 0).astype(BF16)


def wave_kernel(place_ref, out_y_ref, out_z_ref):
    out_y_ref[...] = wave_factors(place_ref[0].astype(F32), out_y_ref.shape[0] // 4, NY)
    out_z_ref[...] = wave_factors(place_ref[1].astype(F32), out_z_ref.shape[0] // 4, NZ)


def atom_waves(base, weights, factors_ref, digits_ref):
    width = base.shape[1]
    high_digit = jnp.floor(base * (1.0 / RADIX))
    row = iota((DIGITS, width), 0)
    chosen = jnp.where(row == high_digit, 1.0, 0.0).astype(BF16)
    step = row - (base - RADIX * high_digit)
    spread = jnp.where(step == 3.0, weights[3], 0.0)
    for r in (2, 1, 0):
        spread = jnp.where(step == float(r), weights[r], spread)
    high, low = split(spread)
    for section, value in enumerate((chosen, chosen, high, high, low)):
        digits_ref[pl.ds(DIGITS * section, DIGITS), :] = value
    product = jnp.dot(factors_ref[...], digits_ref[...], preferred_element_type=F32)
    rows = product.shape[0] // 4
    cos_a, sin_a, cos_b, sin_b = (product[i * rows : (i + 1) * rows] for i in range(4))
    return cos_a * cos_b - sin_a * sin_b, sin_a * cos_b + cos_a * sin_b


def plane_weights(atoms, weights):
    row = iota((8, atoms.shape[1]), 0) - atoms[0:1]
    return sum(weights[r][3:4] * (row == float(r)).astype(F32) for r in range(4))


def swap(value):
    return pltpu.roll(value, LANES // 2, axis=value.ndim - 1)


def half_sign():
    lane = lax.broadcasted_iota(jnp.int32, (1, LANES), 1)
    return jnp.where(lane < LANES // 2, -1.0, 1.0).astype(F32)


def rotate(value, numer, denom, sign):
    real, imag = value
    if numer == 0:
        return value
    if 4 * numer == denom:
        return (-imag, real) if sign > 0 else (imag, -real)
    angle = 2.0 * np.pi * numer / denom
    cosine, sine = float(np.cos(angle)), float(sign * np.sin(angle))
    if 8 * numer in (denom, 3 * denom):
        size = abs(cosine)
        cos_sign, sin_sign = (1 if cosine > 0 else -1), (1 if sine > 0 else -1)
        if cos_sign == sin_sign:
            return ((real - imag) * (cos_sign * size), (real + imag) * (cos_sign * size))
        return ((real + imag) * (cos_sign * size), (imag - real) * (cos_sign * size))
    return real * cosine - imag * sine, imag * cosine + real * sine


def butterfly(even, turned):
    plus = (even[0] + turned[0], even[1] + turned[1])
    return plus, (even[0] - turned[0], even[1] - turned[1])


def transform(values, sign):
    count = len(values)
    if count == 1:
        return values
    even = transform(values[0::2], sign)
    odd = transform(values[1::2], sign)
    both = [butterfly(even[k], rotate(odd[k], k, count, sign)) for k in range(count // 2)]
    return [pair[0] for pair in both] + [pair[1] for pair in both]


def regroup(low, high):
    first = lax.broadcasted_iota(jnp.int32, low.shape, 1) < LANES // 2
    crossed = swap(jnp.where(first, high, low))
    return jnp.where(first, low, crossed), jnp.where(first, crossed, high)


def pack_kernel(counts_ref, cells_ref, offsets_ref, charges_ref, out_ref):
    width = offsets_ref.shape[1]
    alive = lax.broadcasted_iota(jnp.int32, (1, width), 1) < counts_ref[0]
    atoms = jnp.concatenate(
        [
            lax.bitwise_and(cells_ref[0:1, :], XD - 1).astype(F32),
            cells_ref[1:3, :].astype(F32),
            offsets_ref[...],
            jnp.where(alive, charges_ref[...], 0.0),
            jnp.zeros((1, width), F32),
        ],
        0,
    )
    for copy in range(out_ref.shape[0]):
        out_ref[copy] = atoms


def atoms_of(same_ref, other_ref, slab, slot, doms):
    half = doms // 2
    return (same_ref, other_ref)[slot // half][slab * half + slot % half]


def forward_kernel(
    place_ref,
    same_ref,
    other_ref,
    factors_y,
    factors_z,
    plus_ref,
    minus_ref,
    table_y,
    table_z,
    left_ref,
    right_ref,
    grid_ref,
    digits_y,
    digits_z,
):
    step = pl.program_id(0)
    cells_x = grid_ref.shape[0]
    rows = grid_ref.shape[1] // 2
    ky_local = rows - 8
    width = same_ref.shape[2]
    doms = table_y.shape[2] // width
    kept = step - place_ref[2]
    kept = jnp.where((kept >= 0) & (kept < table_y.shape[0] - 1), kept, table_y.shape[0] - 1)

    @pl.when(step == 0)
    def _():
        grid_ref[...] = jnp.zeros_like(grid_ref)
        digits_y[...] = jnp.zeros_like(digits_y)
        digits_z[...] = jnp.zeros_like(digits_z)

    for slot in range(doms):
        atoms = atoms_of(same_ref, other_ref, step, slot, doms)
        lanes = pl.ds(slot * width, width)
        weights = spline(atoms)
        along_x = plane_weights(atoms, weights) * atoms[6:7]
        waves = atom_waves(atoms[2:3], [w[5:6] for w in weights], factors_z, digits_z.at[slot])
        waves = jnp.concatenate(waves, 0)
        table_z[kept, :, lanes] = waves
        high, low = split(waves)
        right_ref[slot, pl.ds(0, LANES), :] = high
        right_ref[slot, pl.ds(LANES, LANES), :] = low
        cosine, sine = atom_waves(atoms[1:2], [w[4:5] for w in weights], factors_y, digits_y.at[slot])
        waves = jnp.concatenate([cosine, sine], 0)
        table_y[kept, :, lanes] = waves
        for plane in range(SPAN):
            first = 4 * rows * plane
            high, low = split(waves * along_x[plane : plane + 1])
            left_ref[slot, pl.ds(first, 2 * rows), :] = high
            left_ref[slot, pl.ds(first + 2 * rows, 2 * rows), :] = low
        product = lax.dot_general(
            left_ref[slot], right_ref[slot], (((1,), (1,)), ((), ())), preferred_element_type=F32
        )
        for plane in range(SPAN):
            first = 4 * rows * plane
            high, low = product[first : first + 2 * rows], product[first + 2 * rows : first + 4 * rows]
            at = lax.rem(step * XD + plane, cells_x)
            grid_ref[at] += (high[:, :LANES] + high[:, LANES:]) + (low[:, :LANES] + low[:, LANES:])

    @pl.when(step == pl.num_programs(0) - 1)
    def _():
        quarter_rows = ky_local // 2
        group = min(8, quarter_rows)
        for minus, out_ref in enumerate((plus_ref, minus_ref)):
            for start in range(0, quarter_rows, group):
                values = []
                for x in range(cells_x):
                    parts = [
                        grid_ref[x, pl.ds(minus + start + offset, group), :]
                        for offset in (0, quarter_rows, rows, rows + quarter_rows)
                    ]
                    cos_cos, cos_sin = regroup(parts[0], parts[1])
                    sin_cos, sin_sin = regroup(parts[2], parts[3])
                    if minus:
                        values.append((cos_cos + sin_sin, sin_cos - cos_sin))
                    else:
                        values.append((cos_cos - sin_sin, -cos_sin - sin_cos))
                for x, value in enumerate(transform(values, -1)):
                    for part in (0, 1):
                        out_ref[part, x, pl.ds(start, group), :] = value[part]


def inverse_x_kernel(place_ref, spectrum_ref, green_ref, *refs):
    *outs, near_ref = refs
    cells_x, quarter_rows = spectrum_ref.shape[1:3]
    group = min(8, quarter_rows)
    side = 1.0 - 2.0 * place_ref[3].astype(F32)

    def rows_of(step, carry):
        rows = pl.ds(pl.multiple_of(step * group, group), group)
        values = []
        for kx in range(cells_x):
            green = green_ref[kx, rows, :]
            values.append(tuple(spectrum_ref[part, kx, rows, :] * green for part in (0, 1)))
        even = transform(values[0::2], 1)
        odd = transform([(value[0] * side, value[1] * side) for value in values[1::2]], 1)
        for x in range(cells_x // 2):
            here, there = butterfly(even[x], rotate(odd[x], x, cells_x, 1))
            wanted = [(x, here)] + ([(cells_x // 2 + x, there)] if x < 3 else [])
            for plane, value in wanted:
                for part, row_group in enumerate(regroup(value[0], value[1])):
                    near_ref[plane, part, rows, :] = row_group
        return carry

    lax.fori_loop(0, quarter_rows // group, rows_of, 0)
    for k, out_ref in enumerate(outs):
        out_ref[...] = near_ref[pl.ds(lax.bitwise_xor(place_ref[4], k) * XD, XD)]


def inverse_y_kernel(sources, chunk, place_ref, *refs):
    ins, (high_ref, low_ref) = refs[: 2 * sources], refs[2 * sources : 2 * sources + 2]
    outs, (lines_ref, turned_ref) = refs[2 * sources + 2 : -2], refs[-2:]
    for number, in_ref in enumerate(ins):
        source = lax.bitwise_xor(place_ref[4], number % sources)
        half = in_ref.shape[1]
        rows = pl.ds(half * (number // sources), half)
        lines_ref[source, :, rows, :] = in_ref[pl.ds(chunk * DEPTH, DEPTH)]
    parts = []
    for x in range(DEPTH):
        lines = jnp.concatenate([lines_ref[source, x] for source in range(sources)], 0)
        pairs = jnp.concatenate([lines, swap(lines) * half_sign()], 0)
        parts.append(split(pairs))
    both = jnp.concatenate([value for part in parts for value in part], 1)
    main = jnp.dot(high_ref[...], both, preferred_element_type=F32)
    high = jnp.concatenate([part[0] for part in parts], 1)
    rest = jnp.dot(low_ref[...], high, preferred_element_type=F32)
    row = lax.broadcasted_iota(jnp.int32, (NY, 1), 0)
    sign = jnp.where((row % 2 == 1) & (place_ref[3] == 1), -1.0, 1.0)
    for x in range(DEPTH):
        total = main[:, 2 * x * LANES : (2 * x + 1) * LANES] + main[:, (2 * x + 1) * LANES : (2 * x + 2) * LANES]
        total = (total + rest[:, x * LANES : (x + 1) * LANES]) * sign
        turned_ref[:, x] = total.reshape(len(outs), -1, LANES)
    for k in range(len(outs)):
        outs[k][...] = turned_ref[lax.bitwise_xor(place_ref[5], k)]


def inverse_z_kernel(sources, place_ref, *refs):
    ins, (high_ref, low_ref) = refs[:sources], refs[sources : sources + 2]
    out_ref, lines_ref = refs[-2:]
    for k in range(sources):
        lines_ref[lax.bitwise_xor(place_ref[5], k)] = ins[k][...]
    for x in range(DEPTH):
        lines = jnp.concatenate([lines_ref[source, x] for source in range(sources)], 1)
        high, low = split(lines)
        total = jnp.dot(high, high_ref[...], preferred_element_type=F32)
        total += jnp.dot(low, high_ref[...], preferred_element_type=F32)
        total += jnp.dot(high, low_ref[...], preferred_element_type=F32)
        out_ref[x] = total


def gather_kernel(
    place_ref, same_ref, other_ref, table_y, table_z, plus_ref, minus_ref, out_ref, shift_ref, fields_ref, stack_ref
):
    step = pl.program_id(0)
    half = LANES // 2
    rows = table_y.shape[1] // 2
    ky_local = rows - 8
    width = same_ref.shape[2]
    doms = table_y.shape[2] // width
    planes = plus_ref.shape[0]
    halves = half_sign()

    @pl.when(step == 0)
    def _():
        stack_ref[...] = jnp.zeros_like(stack_ref)
        shift_ref[...] = jnp.zeros_like(shift_ref)
        row = lax.broadcasted_iota(jnp.int32, (8, LANES), 0)

        def build(x, carry):
            plus = plus_ref[x]
            shift_ref[pl.ds(1, ky_local), :] = minus_ref[x]
            minus = shift_ref[pl.ds(0, ky_local), :]
            last = shift_ref[pl.ds(ky_local, 8), :][0:1]
            main = [plus + minus, swap(plus - minus) * halves]
            if 2 * ky_local < LANES:
                main.append(jnp.zeros((LANES - 2 * ky_local, LANES), F32))
            rest = jnp.where(row % 2 == 0, last, -swap(jnp.broadcast_to(last, (8, LANES))) * halves)
            rest = jnp.where(row < 6, rest, 0.0)
            rest_high = rest.astype(BF16).astype(F32)
            rest = jnp.where((row == 2) | (row == 3), rest - rest_high, rest_high)
            high, low = split(jnp.concatenate(main, 0).T)
            fields_ref[x, :, pl.ds(0, LANES)] = high
            fields_ref[x, :, pl.ds(LANES, LANES)] = low
            fields_ref[x, :, pl.ds(2 * LANES, LANES)] = high
            rest = jnp.concatenate([rest, jnp.zeros((LANES - 8, LANES), F32)], 0)
            fields_ref[x, :, pl.ds(3 * LANES, LANES)] = rest.T.astype(BF16)
            return carry

        lax.fori_loop(0, planes, build, 0)

    first_z = place_ref[1].astype(F32)
    twice = jnp.where(first_z + iota((half, 1), 0) == 0.0, 1.0, 2.0)
    fields = fields_ref[pl.ds(step * XD, SPAN)].reshape(SPAN * LANES, 4 * LANES)
    for slot in range(doms):
        lanes = pl.ds(slot * width, width)
        cosine = table_y[step, pl.ds(0, ky_local), lanes]
        sine = table_y[step, pl.ds(rows, ky_local), lanes]
        high, low = split(jnp.concatenate([cosine, sine], 0))
        for part, value in enumerate((high, high, low)):
            stack_ref[pl.ds(LANES * part, 2 * ky_local), lanes] = value
        cosine = table_y[step, pl.ds(ky_local, 8), lanes][0:1]
        sine = table_y[step, pl.ds(rows + ky_local, 8), lanes][0:1]
        row = lax.broadcasted_iota(jnp.int32, (16, width), 0)
        rest = jnp.where(row % 2 == 0, cosine, sine)
        rest_high = rest.astype(BF16).astype(F32)
        rest = jnp.where(row < 4, rest_high, jnp.where(row < 6, rest - rest_high, 0.0))
        stack_ref[pl.ds(3 * LANES, 16), lanes] = rest.astype(BF16)
    product = sum(
        jnp.dot(fields[:, part : part + 2 * LANES], stack_ref[pl.ds(part, 2 * LANES), :], preferred_element_type=F32)
        for part in (0, 2 * LANES)
    )
    for slot in range(doms):
        atoms = atoms_of(same_ref, other_ref, place_ref[2] + step, slot, doms)
        along_x = plane_weights(atoms, spline(atoms))
        lanes = pl.ds(slot * width, width)
        field = product[:, slot * width : (slot + 1) * width]
        total = along_x[0:1] * field[:LANES]
        for plane in range(1, SPAN):
            total += along_x[plane : plane + 1] * field[plane * LANES : (plane + 1) * LANES]
        waves = total * table_z[step, :, lanes]
        sampled = jnp.sum((waves[:half] - waves[half:]) * twice, axis=0, keepdims=True)
        core = place_ref[5] % 2 if slot < doms // 2 else 1 - place_ref[5] % 2
        out_ref[step * doms + 2 * (slot % (doms // 2)) + core] = sampled


def bf16_pair(table):
    high = table.astype(ml_dtypes.bfloat16)
    low = (table - high.astype(np.float64)).astype(ml_dtypes.bfloat16)
    return jnp.asarray(high), jnp.asarray(low)


def inverse_y_table(slab_half, ky_local):
    waves = []
    for slab in range(slab_half):
        first = slab * ky_local
        waves += [first + i for i in range(ky_local)] + [-(first + i + 1) for i in range(ky_local)]
    angle = 2.0 * np.pi * (np.outer(np.arange(NY), np.array(waves)) % NY) / NY
    return bf16_pair(np.concatenate([np.cos(angle), np.sin(angle)], 1))


def inverse_z_table(dom_count):
    kz = np.arange(KH)
    angle = 2.0 * np.pi * (np.outer(kz, np.arange(NZ)) % NZ) / NZ
    weight = np.where(kz == 0, 1.0, 2.0)[:, None]
    parts = [weight * np.cos(angle), -weight * np.sin(angle)]
    return bf16_pair(
        np.stack([p.reshape(dom_count, KH // dom_count, NZ) for p in parts], 1).reshape(2 * KH, NZ)
    )


def whole_spec(shape):
    return pl.BlockSpec(shape, lambda *_: (0,) * len(shape))


SMALL = pl.CostEstimate(flops=10**6, bytes_accessed=10**4, transcendentals=0)
SMEM = pl.BlockSpec(memory_space=pltpu.SMEM)


def params(mib):
    return pltpu.CompilerParams(vmem_limit_bytes=mib * MIB)


def swapped(value, axis, distance):
    if distance == 0:
        return value
    return lax.ppermute(value, axis, [(i, i ^ distance) for i in range(lax.axis_size(axis))])


def per_device(base_cells, offsets, charges, bias_coupling, counts, green):
    slabs = lax.axis_size("slab")
    doms = lax.axis_size("dom")
    slab = lax.axis_index("slab")
    dom = lax.axis_index("dom")
    atoms_local = charges.shape[0]
    cells_x = XD * slabs
    ky_local = NY // slabs
    kz_local = KH // doms
    slab_half = slabs // 2
    rows_local = NY // doms
    rows = ky_local + 8
    quarter_rows = ky_local // 2
    normalize = 1.0 / (cells_x * NY * NZ)
    upper = slab // slab_half
    place = jnp.stack(
        [slab * ky_local, dom * kz_local, upper * slab_half, upper, slab % slab_half, dom]
    ).astype(jnp.int32)

    vmem = pl.BlockSpec(memory_space=pltpu.VMEM)
    atoms = pl.pallas_call(
        pack_kernel,
        in_specs=[SMEM, vmem, vmem, vmem],
        out_specs=vmem,
        out_shape=jax.ShapeDtypeStruct((slabs * doms // 2, 8, atoms_local), F32),
        name="pack",
    )(counts, base_cells, offsets, charges.reshape(1, atoms_local))
    factors_y, factors_z = pl.pallas_call(
        wave_kernel,
        in_specs=[SMEM],
        out_specs=[vmem] * 2,
        out_shape=[jax.ShapeDtypeStruct((4 * count, TERMS), BF16) for count in (rows, LANES // 2)],
        compiler_params=params(8),
        name="waves",
    )(place)
    everyone = list(range(slabs * doms))
    same = lax.all_to_all(
        atoms, ("slab", "dom"), 0, 0, axis_index_groups=[everyone[0::2], everyone[1::2]], tiled=True
    )

    def halves_beside(value):
        return jnp.concatenate([value[:, :quarter_rows], value[:, quarter_rows:]], 2) * normalize

    own = halves_beside(green)
    same, flipped, factors_y, factors_z = lax.optimization_barrier(
        (same, halves_beside(green[:, ::-1]), factors_y, factors_z)
    )
    other = swapped(same, "dom", 1)
    mirrored = lax.ppermute(flipped, "slab", [(s, slabs - 1 - s) for s in range(slabs)])

    atoms_slab = doms * atoms_local
    table_bytes = 4 * (slab_half + 1) * (2 * rows + LANES) * atoms_slab
    spectrum_bytes = 16 * cells_x * max(8, quarter_rows) * LANES
    plus, minus, table_y, table_z = pl.pallas_call(
        forward_kernel,
        grid=(slabs,),
        in_specs=[SMEM] + [vmem] * 4,
        out_specs=[vmem] * 4,
        out_shape=[
            jax.ShapeDtypeStruct((2, cells_x, quarter_rows, LANES), F32),
            jax.ShapeDtypeStruct((2, cells_x, quarter_rows, LANES), F32),
            jax.ShapeDtypeStruct((slab_half + 1, 2 * rows, atoms_slab), F32),
            jax.ShapeDtypeStruct((slab_half + 1, LANES, atoms_slab), F32),
        ],
        scratch_shapes=[
            pltpu.VMEM((doms, SPAN * 4 * rows, atoms_local), BF16),
            pltpu.VMEM((doms, 2 * LANES, atoms_local), BF16),
            pltpu.VMEM((cells_x, 2 * rows, LANES), F32),
            pltpu.VMEM((doms, TERMS, atoms_local), BF16),
            pltpu.VMEM((doms, TERMS, atoms_local), BF16),
        ],
        compiler_params=params(16 + (table_bytes + spectrum_bytes) // MIB),
        cost_estimate=SMALL,
        name="forward",
    )(place, same, other, factors_y, factors_z)

    near_planes = cells_x // 2 + 3
    lines, near = [], []
    for spectrum, influence in ((plus, own), (minus, mirrored)):
        *pieces, planes = pl.pallas_call(
            inverse_x_kernel,
            in_specs=[SMEM] + [vmem] * 2,
            out_specs=[vmem] * (slab_half + 1),
            out_shape=[jax.ShapeDtypeStruct((XD, 2, quarter_rows, LANES), F32)] * slab_half
            + [jax.ShapeDtypeStruct((near_planes, 2, quarter_rows, LANES), F32)],
            compiler_params=params(24),
            cost_estimate=SMALL,
            name="inverse_x",
        )(place, spectrum, influence)
        near.append(planes.reshape(near_planes, ky_local, LANES))
        lines += [swapped(value.reshape(XD, ky_local, LANES), "slab", k) for k, value in enumerate(pieces)]

    partial = pl.pallas_call(
        gather_kernel,
        grid=(slab_half,),
        in_specs=[SMEM] + [vmem] * 6,
        out_specs=vmem,
        out_shape=jax.ShapeDtypeStruct((slab_half * doms, 1, atoms_local), F32),
        scratch_shapes=[
            pltpu.VMEM((rows, LANES), F32),
            pltpu.VMEM((near_planes, LANES, 4 * LANES), BF16),
            pltpu.VMEM((4 * LANES, atoms_slab), BF16),
        ],
        compiler_params=params(12 + (table_bytes + 8 * near_planes * LANES * LANES) // MIB),
        cost_estimate=SMALL,
        name="gather",
    )(place, same, other, table_y, table_z, *near)

    high_y, low_y = inverse_y_table(slab_half, ky_local)
    high_z, low_z = inverse_z_table(doms)
    partial, *lines = lax.optimization_barrier((partial, *lines))

    potential = None
    for chunk in range(CHUNKS):
        turned = pl.pallas_call(
            functools.partial(inverse_y_kernel, slab_half, chunk),
            in_specs=[SMEM] + [vmem] * (2 * slab_half + 2),
            out_specs=[vmem] * doms,
            out_shape=[jax.ShapeDtypeStruct((DEPTH, rows_local, LANES), F32)] * doms,
            scratch_shapes=[
                pltpu.VMEM((slab_half, DEPTH, 2 * ky_local, LANES), F32),
                pltpu.VMEM((doms, DEPTH, rows_local, LANES), F32),
            ],
            compiler_params=params(32),
            cost_estimate=SMALL,
            name="inverse_y",
        )(place, *lines, high_y, low_y)
        columns = [swapped(value, "dom", k) for k, value in enumerate(turned)]
        if chunk == CHUNKS - 1:
            partial, columns[1] = lax.optimization_barrier((partial, columns[1]))
        earlier = [] if potential is None else [potential]
        potential = pl.pallas_call(
            functools.partial(inverse_z_kernel, doms),
            grid=(1,),
            in_specs=[SMEM]
            + [whole_spec((DEPTH, rows_local, LANES))] * doms
            + [whole_spec((2 * KH, NZ))] * 2
            + [pl.BlockSpec(memory_space=pl.ANY)] * len(earlier),
            out_specs=pl.BlockSpec((DEPTH, rows_local, NZ), lambda _, at=chunk: (at, 0, 0)),
            out_shape=jax.ShapeDtypeStruct((XD, rows_local, NZ), F32),
            scratch_shapes=[pltpu.VMEM((doms, DEPTH, rows_local, LANES), F32)],
            input_output_aliases={doms + 3: 0} if earlier else {},
            compiler_params=params(24),
            cost_estimate=SMALL,
            name="inverse_z",
        )(place, *columns, high_z, low_z, *earlier)

    members = slab_half * doms
    sampled = lax.all_to_all(
        partial.reshape(members, atoms_local),
        ("slab", "dom"),
        0,
        0,
        axis_index_groups=[list(range(members)), list(range(members, 2 * members))],
        tiled=True,
    )
    alive = jnp.arange(atoms_local, dtype=jnp.int32) < counts[0]
    gradient = jnp.where(alive, bias_coupling * jnp.sum(sampled, 0), 0.0)
    return (potential, gradient)


def solution(mesh):
    placed = (
        P(None, ("slab", "dom")),
        P(None, ("slab", "dom")),
        P(("slab", "dom")),
        P(("slab", "dom")),
        P(("slab", "dom")),
        P(None, "slab", "dom"),
    )
    return jax.shard_map(
        per_device,
        mesh=mesh,
        in_specs=placed,
        out_specs=(P("slab", "dom", None), P(("slab", "dom"))),
        check_vma=False,
    )
```

```python
import functools

import jax
import jax.numpy as jnp
import ml_dtypes
import numpy as np
from jax import lax
from jax.experimental import pallas as pl
from jax.experimental.pallas import tpu as pltpu
from jax.sharding import PartitionSpec as P

XD = 4
NY = 512
NZ = 512
KH = NZ // 2
LANES = 128
SPAN = XD + 3
DEPTH = 2
GATHERS = 2
MIB = 1 << 20
BF16 = jnp.bfloat16
F32 = jnp.float32


def polynomial(function, terms):
    nodes = 0.125 * (1.0 - np.cos(np.pi * (np.arange(64) + 0.5) / 64))
    powers = nodes[:, None] ** np.arange(terms)[None, :]
    return [float(v) for v in np.linalg.lstsq(powers, function(np.sqrt(nodes)), rcond=None)[0]]


SINE_TERMS = polynomial(lambda r: np.sin(np.pi * r) / r, 6)
COSINE_TERMS = polynomial(lambda r: np.cos(np.pi * r), 6)


def horner(terms, square):
    total = jnp.full_like(square, terms[-1])
    for term in terms[-2::-1]:
        total = total * square + term
    return total


def turn(fraction):
    left = fraction - jnp.floor(fraction + 0.5)
    square = left * left
    sine = left * horner(SINE_TERMS, square)
    cosine = horner(COSINE_TERMS, square)
    return 1.0 - 2.0 * sine * sine, 2.0 * sine * cosine


def spline(frac):
    inner = 1.0 - frac
    square = frac * frac
    cube = square * frac
    sixth = 1.0 / 6.0
    return (
        inner * inner * inner * sixth,
        (3.0 * cube - 6.0 * square + 4.0) * sixth,
        (-3.0 * cube + 3.0 * square + 3.0 * frac + 1.0) * sixth,
        cube * sixth,
    )


def split(value):
    high = value.astype(BF16)
    return high, (value - high.astype(F32)).astype(BF16)


def iota(shape, axis):
    return lax.broadcasted_iota(jnp.int32, shape, axis).astype(F32)


RADIX = 16
DIGITS = 32
TERMS = 256


def wave_factors(first, rows, length):
    lane = lax.broadcasted_iota(jnp.int32, (rows, TERMS), 1)
    section = lane // DIGITS
    digit = (lane % DIGITS).astype(F32) * jnp.where(section < 2, float(RADIX), 1.0)
    parts = []
    for value in turn((first + iota((rows, TERMS), 0)) * digit * (1.0 / length)):
        high = value.astype(BF16).astype(F32)
        parts.append(jnp.where((section == 1) | (section == 3), value - high, high))
    upper, lower = section < 2, (section >= 2) & (section < 5)
    masked = [jnp.where(mask, part, 0.0) for mask in (upper, lower) for part in parts]
    return jnp.concatenate(masked, 0).astype(BF16)


def wave_kernel(place_ref, out_y_ref, out_z_ref):
    out_y_ref[...] = wave_factors(place_ref[0].astype(F32), out_y_ref.shape[0] // 4, NY)
    out_z_ref[...] = wave_factors(place_ref[1].astype(F32), out_z_ref.shape[0] // 4, NZ)


def atom_waves(base, weights, factors_ref, digits_ref):
    width = base.shape[1]
    high_digit = jnp.floor(base * (1.0 / RADIX))
    row = iota((DIGITS, width), 0)
    chosen = jnp.where(row == high_digit, 1.0, 0.0).astype(BF16)
    step = row - (base - RADIX * high_digit)
    spread = jnp.where(step == 3.0, weights[3], 0.0)
    for r in (2, 1, 0):
        spread = jnp.where(step == float(r), weights[r], spread)
    high, low = split(spread)
    for section, value in enumerate((chosen, chosen, high, high, low)):
        digits_ref[pl.ds(DIGITS * section, DIGITS), :] = value
    product = jnp.dot(factors_ref[...], digits_ref[...], preferred_element_type=F32)
    rows = product.shape[0] // 4
    cos_a, sin_a, cos_b, sin_b = (product[i * rows : (i + 1) * rows] for i in range(4))
    return cos_a * cos_b - sin_a * sin_b, sin_a * cos_b + cos_a * sin_b


def plane_weights(atoms, weights):
    row = iota((8, atoms.shape[1]), 0) - atoms[0:1]
    return sum(weights[r][3:4] * (row == float(r)).astype(F32) for r in range(4))


def swap(value):
    return pltpu.roll(value, LANES // 2, axis=value.ndim - 1)


def half_sign():
    lane = lax.broadcasted_iota(jnp.int32, (1, LANES), 1)
    return jnp.where(lane < LANES // 2, -1.0, 1.0).astype(F32)


def rotate(value, numer, denom, sign):
    real, imag = value
    if numer == 0:
        return value
    if 4 * numer == denom:
        return (-imag, real) if sign > 0 else (imag, -real)
    angle = 2.0 * np.pi * numer / denom
    cosine, sine = float(np.cos(angle)), float(sign * np.sin(angle))
    if 8 * numer in (denom, 3 * denom):
        size = abs(cosine)
        cos_sign, sin_sign = (1 if cosine > 0 else -1), (1 if sine > 0 else -1)
        if cos_sign == sin_sign:
            return ((real - imag) * (cos_sign * size), (real + imag) * (cos_sign * size))
        return ((real + imag) * (cos_sign * size), (imag - real) * (cos_sign * size))
    return real * cosine - imag * sine, imag * cosine + real * sine


def butterfly(even, turned):
    plus = (even[0] + turned[0], even[1] + turned[1])
    return plus, (even[0] - turned[0], even[1] - turned[1])


def transform(values, sign):
    count = len(values)
    if count == 1:
        return values
    even = transform(values[0::2], sign)
    odd = transform(values[1::2], sign)
    both = [butterfly(even[k], rotate(odd[k], k, count, sign)) for k in range(count // 2)]
    return [pair[0] for pair in both] + [pair[1] for pair in both]


def regroup(low, high):
    first = lax.broadcasted_iota(jnp.int32, low.shape, 1) < LANES // 2
    crossed = swap(jnp.where(first, high, low))
    return jnp.where(first, low, crossed), jnp.where(first, crossed, high)


def pack_kernel(counts_ref, cells_ref, offsets_ref, charges_ref, out_ref):
    width = offsets_ref.shape[1]
    alive = lax.broadcasted_iota(jnp.int32, (1, width), 1) < counts_ref[0]
    atoms = jnp.concatenate(
        [
            lax.bitwise_and(cells_ref[0:1, :], XD - 1).astype(F32),
            cells_ref[1:3, :].astype(F32),
            offsets_ref[...],
            jnp.where(alive, charges_ref[...], 0.0),
            jnp.zeros((1, width), F32),
        ],
        0,
    )
    for copy in range(out_ref.shape[0]):
        out_ref[copy] = atoms


def atoms_of(same_ref, other_ref, slab, slot, doms):
    half = doms // 2
    return (same_ref, other_ref)[slot // half][slab * half + slot % half]


def forward_kernel(
    place_ref,
    same_ref,
    other_ref,
    factors_y,
    factors_z,
    plus_ref,
    minus_ref,
    table_y,
    table_z,
    left_ref,
    right_ref,
    grid_ref,
    digits_y,
    digits_z,
):
    step = pl.program_id(0)
    cells_x = grid_ref.shape[0]
    rows = grid_ref.shape[1] // 2
    ky_local = rows - 8
    width = same_ref.shape[2]
    doms = table_y.shape[2] // width
    kept = step - place_ref[2]
    kept = jnp.where((kept >= 0) & (kept < table_y.shape[0] - 1), kept, table_y.shape[0] - 1)

    @pl.when(step == 0)
    def _():
        grid_ref[...] = jnp.zeros_like(grid_ref)
        digits_y[...] = jnp.zeros_like(digits_y)
        digits_z[...] = jnp.zeros_like(digits_z)

    for slot in range(doms):
        atoms = atoms_of(same_ref, other_ref, step, slot, doms)
        lanes = pl.ds(slot * width, width)
        weights = spline(atoms)
        along_x = plane_weights(atoms, weights) * atoms[6:7]
        waves = atom_waves(atoms[2:3], [w[5:6] for w in weights], factors_z, digits_z.at[slot])
        waves = jnp.concatenate(waves, 0)
        table_z[kept, :, lanes] = waves
        high, low = split(waves)
        right_ref[slot, pl.ds(0, LANES), :] = high
        right_ref[slot, pl.ds(LANES, LANES), :] = low
        cosine, sine = atom_waves(atoms[1:2], [w[4:5] for w in weights], factors_y, digits_y.at[slot])
        waves = jnp.concatenate([cosine, sine], 0)
        table_y[kept, :, lanes] = waves
        for plane in range(SPAN):
            first = 4 * rows * plane
            high, low = split(waves * along_x[plane : plane + 1])
            left_ref[slot, pl.ds(first, 2 * rows), :] = high
            left_ref[slot, pl.ds(first + 2 * rows, 2 * rows), :] = low
        product = lax.dot_general(
            left_ref[slot], right_ref[slot], (((1,), (1,)), ((), ())), preferred_element_type=F32
        )
        for plane in range(SPAN):
            first = 4 * rows * plane
            high, low = product[first : first + 2 * rows], product[first + 2 * rows : first + 4 * rows]
            at = lax.rem(step * XD + plane, cells_x)
            grid_ref[at] += (high[:, :LANES] + high[:, LANES:]) + (low[:, :LANES] + low[:, LANES:])

    @pl.when(step == pl.num_programs(0) - 1)
    def _():
        quarter_rows = ky_local // 2
        group = min(8, quarter_rows)
        for minus, out_ref in enumerate((plus_ref, minus_ref)):
            for start in range(0, quarter_rows, group):
                values = []
                for x in range(cells_x):
                    parts = [
                        grid_ref[x, pl.ds(minus + start + offset, group), :]
                        for offset in (0, quarter_rows, rows, rows + quarter_rows)
                    ]
                    cos_cos, cos_sin = regroup(parts[0], parts[1])
                    sin_cos, sin_sin = regroup(parts[2], parts[3])
                    if minus:
                        values.append((cos_cos + sin_sin, sin_cos - cos_sin))
                    else:
                        values.append((cos_cos - sin_sin, -cos_sin - sin_cos))
                for x, value in enumerate(transform(values, -1)):
                    for part in (0, 1):
                        out_ref[part, x, pl.ds(start, group), :] = value[part]


def inverse_x_kernel(place_ref, spectrum_ref, green_ref, *refs):
    *outs, near_ref = refs
    cells_x, quarter_rows = spectrum_ref.shape[1:3]
    group = min(8, quarter_rows)
    side = 1.0 - 2.0 * place_ref[3].astype(F32)

    def rows_of(step, carry):
        rows = pl.ds(pl.multiple_of(step * group, group), group)
        values = []
        for kx in range(cells_x):
            green = green_ref[kx, rows, :]
            values.append(tuple(spectrum_ref[part, kx, rows, :] * green for part in (0, 1)))
        even = transform(values[0::2], 1)
        odd = transform([(value[0] * side, value[1] * side) for value in values[1::2]], 1)
        for x in range(cells_x // 2):
            here, there = butterfly(even[x], rotate(odd[x], x, cells_x, 1))
            wanted = [(x, here)] + ([(cells_x // 2 + x, there)] if x < 3 else [])
            for plane, value in wanted:
                for part, row_group in enumerate(regroup(value[0], value[1])):
                    near_ref[plane, part, rows, :] = row_group
        return carry

    lax.fori_loop(0, quarter_rows // group, rows_of, 0)
    for k, out_ref in enumerate(outs):
        out_ref[...] = near_ref[pl.ds(lax.bitwise_xor(place_ref[4], k) * XD, XD)]


def inverse_y_kernel(sources, place_ref, *refs):
    ins, (high_ref, low_ref) = refs[: 2 * sources], refs[2 * sources : 2 * sources + 2]
    outs, (lines_ref, turned_ref) = refs[2 * sources + 2 : -2], refs[-2:]
    for number, in_ref in enumerate(ins):
        source = lax.bitwise_xor(place_ref[4], number % sources)
        half = in_ref.shape[1]
        rows = pl.ds(half * (number // sources), half)
        lines_ref[source, :, rows, :] = in_ref[...]
    parts = []
    for x in range(XD):
        lines = jnp.concatenate([lines_ref[source, x] for source in range(sources)], 0)
        pairs = jnp.concatenate([lines, swap(lines) * half_sign()], 0)
        parts.append(split(pairs))
    both = jnp.concatenate([value for part in parts for value in part], 1)
    main = jnp.dot(high_ref[...], both, preferred_element_type=F32)
    high = jnp.concatenate([part[0] for part in parts], 1)
    rest = jnp.dot(low_ref[...], high, preferred_element_type=F32)
    row = lax.broadcasted_iota(jnp.int32, (NY, 1), 0)
    sign = jnp.where((row % 2 == 1) & (place_ref[3] == 1), -1.0, 1.0)
    for x in range(XD):
        total = main[:, 2 * x * LANES : (2 * x + 1) * LANES] + main[:, (2 * x + 1) * LANES : (2 * x + 2) * LANES]
        total = (total + rest[:, x * LANES : (x + 1) * LANES]) * sign
        turned_ref[:, x] = total.reshape(len(outs), -1, LANES)
    for k in range(len(outs)):
        outs[k][...] = turned_ref[lax.bitwise_xor(place_ref[5], k)]


def inverse_z_kernel(sources, place_ref, *refs):
    ins, (high_ref, low_ref) = refs[:sources], refs[sources : sources + 2]
    out_ref, lines_ref = refs[-2:]
    first = pl.program_id(0) * DEPTH
    for k in range(sources):
        lines_ref[lax.bitwise_xor(place_ref[5], k)] = ins[k][pl.ds(first, DEPTH)]
    rows = DEPTH * lines_ref.shape[2]
    lines = jnp.concatenate([lines_ref[source].reshape(rows, LANES) for source in range(sources)], 1)
    high, low = split(lines)
    total = jnp.dot(high, high_ref[...], preferred_element_type=F32)
    total += jnp.dot(low, high_ref[...], preferred_element_type=F32)
    total += jnp.dot(high, low_ref[...], preferred_element_type=F32)
    out_ref[...] = total.reshape(out_ref.shape)


def gather_kernel(
    first, place_ref, same_ref, other_ref, table_y, table_z, plus_ref, minus_ref, out_ref, shift_ref, fields_ref, stack_ref
):
    step = pl.program_id(0)
    half = LANES // 2
    rows = table_y.shape[1] // 2
    ky_local = rows - 8
    width = same_ref.shape[2]
    doms = table_y.shape[2] // width
    planes = fields_ref.shape[0]
    halves = half_sign()

    @pl.when(step == 0)
    def _():
        stack_ref[...] = jnp.zeros_like(stack_ref)
        shift_ref[...] = jnp.zeros_like(shift_ref)
        row = lax.broadcasted_iota(jnp.int32, (8, LANES), 0)

        def build(x, carry):
            plus = plus_ref[first * XD + x]
            shift_ref[pl.ds(1, ky_local), :] = minus_ref[first * XD + x]
            minus = shift_ref[pl.ds(0, ky_local), :]
            last = shift_ref[pl.ds(ky_local, 8), :][0:1]
            main = [plus + minus, swap(plus - minus) * halves]
            if 2 * ky_local < LANES:
                main.append(jnp.zeros((LANES - 2 * ky_local, LANES), F32))
            rest = jnp.where(row % 2 == 0, last, -swap(jnp.broadcast_to(last, (8, LANES))) * halves)
            rest = jnp.where(row < 6, rest, 0.0)
            rest_high = rest.astype(BF16).astype(F32)
            rest = jnp.where((row == 2) | (row == 3), rest - rest_high, rest_high)
            high, low = split(jnp.concatenate(main, 0).T)
            fields_ref[x, :, pl.ds(0, LANES)] = high
            fields_ref[x, :, pl.ds(LANES, LANES)] = low
            fields_ref[x, :, pl.ds(2 * LANES, LANES)] = high
            rest = jnp.concatenate([rest, jnp.zeros((LANES - 8, LANES), F32)], 0)
            fields_ref[x, :, pl.ds(3 * LANES, LANES)] = rest.T.astype(BF16)
            return carry

        lax.fori_loop(0, planes, build, 0)

    first_z = place_ref[1].astype(F32)
    twice = jnp.where(first_z + iota((half, 1), 0) == 0.0, 1.0, 2.0)
    fields = fields_ref[pl.ds(step * XD, SPAN)].reshape(SPAN * LANES, 4 * LANES)
    for slot in range(doms):
        lanes = pl.ds(slot * width, width)
        cosine = table_y[first + step, pl.ds(0, ky_local), lanes]
        sine = table_y[first + step, pl.ds(rows, ky_local), lanes]
        high, low = split(jnp.concatenate([cosine, sine], 0))
        for part, value in enumerate((high, high, low)):
            stack_ref[pl.ds(LANES * part, 2 * ky_local), lanes] = value
        cosine = table_y[first + step, pl.ds(ky_local, 8), lanes][0:1]
        sine = table_y[first + step, pl.ds(rows + ky_local, 8), lanes][0:1]
        row = lax.broadcasted_iota(jnp.int32, (16, width), 0)
        rest = jnp.where(row % 2 == 0, cosine, sine)
        rest_high = rest.astype(BF16).astype(F32)
        rest = jnp.where(row < 4, rest_high, jnp.where(row < 6, rest - rest_high, 0.0))
        stack_ref[pl.ds(3 * LANES, 16), lanes] = rest.astype(BF16)
    product = sum(
        jnp.dot(fields[:, part : part + 2 * LANES], stack_ref[pl.ds(part, 2 * LANES), :], preferred_element_type=F32)
        for part in (0, 2 * LANES)
    )
    for slot in range(doms):
        atoms = atoms_of(same_ref, other_ref, place_ref[2] + first + step, slot, doms)
        along_x = plane_weights(atoms, spline(atoms))
        lanes = pl.ds(slot * width, width)
        field = product[:, slot * width : (slot + 1) * width]
        total = along_x[0:1] * field[:LANES]
        for plane in range(1, SPAN):
            total += along_x[plane : plane + 1] * field[plane * LANES : (plane + 1) * LANES]
        waves = total * table_z[first + step, :, lanes]
        sampled = jnp.sum((waves[:half] - waves[half:]) * twice, axis=0, keepdims=True)
        core = place_ref[5] % 2 if slot < doms // 2 else 1 - place_ref[5] % 2
        out_ref[step * doms + 2 * (slot % (doms // 2)) + core] = sampled


def bf16_pair(table):
    high = table.astype(ml_dtypes.bfloat16)
    low = (table - high.astype(np.float64)).astype(ml_dtypes.bfloat16)
    return jnp.asarray(high), jnp.asarray(low)


def inverse_y_table(slab_half, ky_local):
    waves = []
    for slab in range(slab_half):
        first = slab * ky_local
        waves += [first + i for i in range(ky_local)] + [-(first + i + 1) for i in range(ky_local)]
    angle = 2.0 * np.pi * (np.outer(np.arange(NY), np.array(waves)) % NY) / NY
    return bf16_pair(np.concatenate([np.cos(angle), np.sin(angle)], 1))


def inverse_z_table(dom_count):
    kz = np.arange(KH)
    angle = 2.0 * np.pi * (np.outer(kz, np.arange(NZ)) % NZ) / NZ
    weight = np.where(kz == 0, 1.0, 2.0)[:, None]
    parts = [weight * np.cos(angle), -weight * np.sin(angle)]
    return bf16_pair(
        np.stack([p.reshape(dom_count, KH // dom_count, NZ) for p in parts], 1).reshape(2 * KH, NZ)
    )


def whole_spec(shape):
    return pl.BlockSpec(shape, lambda *_: (0,) * len(shape))


SMALL = pl.CostEstimate(flops=10**6, bytes_accessed=10**4, transcendentals=0)
SMEM = pl.BlockSpec(memory_space=pltpu.SMEM)


def params(mib):
    return pltpu.CompilerParams(vmem_limit_bytes=mib * MIB)


def swapped(value, axis, distance):
    if distance == 0:
        return value
    return lax.ppermute(value, axis, [(i, i ^ distance) for i in range(lax.axis_size(axis))])


def per_device(base_cells, offsets, charges, bias_coupling, counts, green):
    slabs = lax.axis_size("slab")
    doms = lax.axis_size("dom")
    slab = lax.axis_index("slab")
    dom = lax.axis_index("dom")
    atoms_local = charges.shape[0]
    cells_x = XD * slabs
    ky_local = NY // slabs
    kz_local = KH // doms
    slab_half = slabs // 2
    rows_local = NY // doms
    rows = ky_local + 8
    quarter_rows = ky_local // 2
    normalize = 1.0 / (cells_x * NY * NZ)
    upper = slab // slab_half
    place = jnp.stack(
        [slab * ky_local, dom * kz_local, upper * slab_half, upper, slab % slab_half, dom]
    ).astype(jnp.int32)

    vmem = pl.BlockSpec(memory_space=pltpu.VMEM)
    atoms = pl.pallas_call(
        pack_kernel,
        in_specs=[SMEM, vmem, vmem, vmem],
        out_specs=vmem,
        out_shape=jax.ShapeDtypeStruct((slabs * doms // 2, 8, atoms_local), F32),
        name="pack",
    )(counts, base_cells, offsets, charges.reshape(1, atoms_local))
    factors_y, factors_z = pl.pallas_call(
        wave_kernel,
        in_specs=[SMEM],
        out_specs=[vmem] * 2,
        out_shape=[jax.ShapeDtypeStruct((4 * count, TERMS), BF16) for count in (rows, LANES // 2)],
        compiler_params=params(8),
        name="waves",
    )(place)
    everyone = list(range(slabs * doms))
    same = lax.all_to_all(
        atoms, ("slab", "dom"), 0, 0, axis_index_groups=[everyone[0::2], everyone[1::2]], tiled=True
    )

    def halves_beside(value):
        return jnp.concatenate([value[:, :quarter_rows], value[:, quarter_rows:]], 2) * normalize

    own = halves_beside(green)
    same, flipped, factors_y, factors_z = lax.optimization_barrier(
        (same, halves_beside(green[:, ::-1]), factors_y, factors_z)
    )
    other = swapped(same, "dom", 1)
    mirrored = lax.ppermute(flipped, "slab", [(s, slabs - 1 - s) for s in range(slabs)])

    atoms_slab = doms * atoms_local
    table_bytes = 4 * (slab_half + 1) * (2 * rows + LANES) * atoms_slab
    spectrum_bytes = 16 * cells_x * max(8, quarter_rows) * LANES
    plus, minus, table_y, table_z = pl.pallas_call(
        forward_kernel,
        grid=(slabs,),
        in_specs=[SMEM] + [vmem] * 4,
        out_specs=[vmem] * 4,
        out_shape=[
            jax.ShapeDtypeStruct((2, cells_x, quarter_rows, LANES), F32),
            jax.ShapeDtypeStruct((2, cells_x, quarter_rows, LANES), F32),
            jax.ShapeDtypeStruct((slab_half + 1, 2 * rows, atoms_slab), F32),
            jax.ShapeDtypeStruct((slab_half + 1, LANES, atoms_slab), F32),
        ],
        scratch_shapes=[
            pltpu.VMEM((doms, SPAN * 4 * rows, atoms_local), BF16),
            pltpu.VMEM((doms, 2 * LANES, atoms_local), BF16),
            pltpu.VMEM((cells_x, 2 * rows, LANES), F32),
            pltpu.VMEM((doms, TERMS, atoms_local), BF16),
            pltpu.VMEM((doms, TERMS, atoms_local), BF16),
        ],
        compiler_params=params(16 + (table_bytes + spectrum_bytes) // MIB),
        cost_estimate=SMALL,
        name="forward",
    )(place, same, other, factors_y, factors_z)

    near_planes = cells_x // 2 + 3
    lines, near = [], []
    for spectrum, influence in ((plus, own), (minus, mirrored)):
        *pieces, planes = pl.pallas_call(
            inverse_x_kernel,
            in_specs=[SMEM] + [vmem] * 2,
            out_specs=[vmem] * (slab_half + 1),
            out_shape=[jax.ShapeDtypeStruct((XD, 2, quarter_rows, LANES), F32)] * slab_half
            + [jax.ShapeDtypeStruct((near_planes, 2, quarter_rows, LANES), F32)],
            compiler_params=params(24),
            cost_estimate=SMALL,
            name="inverse_x",
        )(place, spectrum, influence)
        near.append(planes.reshape(near_planes, ky_local, LANES))
        lines += [swapped(value.reshape(XD, ky_local, LANES), "slab", k) for k, value in enumerate(pieces)]

    steps = slab_half // GATHERS

    def gather(part, place):
        return pl.pallas_call(
            functools.partial(gather_kernel, part * steps),
            grid=(steps,),
            in_specs=[SMEM] + [vmem] * 6,
            out_specs=vmem,
            out_shape=jax.ShapeDtypeStruct((steps * doms, 1, atoms_local), F32),
            scratch_shapes=[
                pltpu.VMEM((rows, LANES), F32),
                pltpu.VMEM((steps * XD + 3, LANES, 4 * LANES), BF16),
                pltpu.VMEM((4 * LANES, atoms_slab), BF16),
            ],
            compiler_params=params(12 + (table_bytes + 8 * near_planes * LANES * LANES) // MIB),
            cost_estimate=SMALL,
            name="gather",
        )(place, same, other, table_y, table_z, *near)

    earlier, *lines = lax.optimization_barrier((gather(0, place), *lines))

    high_y, low_y = inverse_y_table(slab_half, ky_local)
    high_z, low_z = inverse_z_table(doms)

    turned = pl.pallas_call(
        functools.partial(inverse_y_kernel, slab_half),
        in_specs=[SMEM] + [vmem] * (2 * slab_half + 2),
        out_specs=[vmem] * doms,
        out_shape=[jax.ShapeDtypeStruct((XD, rows_local, LANES), F32)] * doms,
        scratch_shapes=[
            pltpu.VMEM((slab_half, XD, 2 * ky_local, LANES), F32),
            pltpu.VMEM((doms, XD, rows_local, LANES), F32),
        ],
        compiler_params=params(32),
        cost_estimate=SMALL,
        name="inverse_y",
    )(place, *lines, high_y, low_y)
    columns = [swapped(value, "dom", k) for k, value in enumerate(turned)]

    columns[1], late_place = lax.optimization_barrier((columns[1], place))
    partial = jnp.concatenate([earlier] + [gather(part, late_place) for part in range(1, GATHERS)], 0)
    members = slab_half * doms
    sampled = lax.all_to_all(
        partial.reshape(members, atoms_local),
        ("slab", "dom"),
        0,
        0,
        axis_index_groups=[list(range(members)), list(range(members, 2 * members))],
        tiled=True,
    )
    alive = jnp.arange(atoms_local, dtype=jnp.int32) < counts[0]
    gradient = jnp.where(alive, bias_coupling * jnp.sum(sampled, 0), 0.0)
    gradient, *columns = lax.optimization_barrier((gradient, *columns))

    potential = pl.pallas_call(
        functools.partial(inverse_z_kernel, doms),
        grid=(XD // DEPTH,),
        in_specs=[SMEM] + [vmem] * (doms + 2),
        out_specs=pl.BlockSpec((DEPTH, rows_local, NZ), lambda step: (step, 0, 0)),
        out_shape=jax.ShapeDtypeStruct((XD, rows_local, NZ), F32),
        scratch_shapes=[pltpu.VMEM((doms, DEPTH, rows_local, LANES), F32)],
        compiler_params=params(24),
        cost_estimate=SMALL,
        name="inverse_z",
    )(place, *columns, high_z, low_z)
    return (potential, gradient)


def solution(mesh):
    placed = (
        P(None, ("slab", "dom")),
        P(None, ("slab", "dom")),
        P(("slab", "dom")),
        P(("slab", "dom")),
        P(("slab", "dom")),
        P(None, "slab", "dom"),
    )
    return jax.shard_map(
        per_device,
        mesh=mesh,
        in_specs=placed,
        out_specs=(P("slab", "dom", None), P(("slab", "dom"))),
        check_vma=False,
    )
```

```python
import functools

import jax
import jax.numpy as jnp
import ml_dtypes
import numpy as np
from jax import lax
from jax.experimental import pallas as pl
from jax.experimental.pallas import tpu as pltpu
from jax.sharding import PartitionSpec as P

XD = 4
NY = 512
NZ = 512
KH = NZ // 2
LANES = 128
SPAN = XD + 3
DEPTH = 2
GATHERS = 2
MIB = 1 << 20
BF16 = jnp.bfloat16
F32 = jnp.float32


def polynomial(function, terms):
    nodes = 0.125 * (1.0 - np.cos(np.pi * (np.arange(64) + 0.5) / 64))
    powers = nodes[:, None] ** np.arange(terms)[None, :]
    return [float(v) for v in np.linalg.lstsq(powers, function(np.sqrt(nodes)), rcond=None)[0]]


SINE_TERMS = polynomial(lambda r: np.sin(np.pi * r) / r, 6)
COSINE_TERMS = polynomial(lambda r: np.cos(np.pi * r), 6)


def horner(terms, square):
    total = jnp.full_like(square, terms[-1])
    for term in terms[-2::-1]:
        total = total * square + term
    return total


def turn(fraction):
    left = fraction - jnp.floor(fraction + 0.5)
    square = left * left
    sine = left * horner(SINE_TERMS, square)
    cosine = horner(COSINE_TERMS, square)
    return 1.0 - 2.0 * sine * sine, 2.0 * sine * cosine


def spline(frac):
    inner = 1.0 - frac
    square = frac * frac
    cube = square * frac
    sixth = 1.0 / 6.0
    return (
        inner * inner * inner * sixth,
        (3.0 * cube - 6.0 * square + 4.0) * sixth,
        (-3.0 * cube + 3.0 * square + 3.0 * frac + 1.0) * sixth,
        cube * sixth,
    )


def split(value):
    high = value.astype(BF16)
    return high, (value - high.astype(F32)).astype(BF16)


def iota(shape, axis):
    return lax.broadcasted_iota(jnp.int32, shape, axis).astype(F32)


RADIX = 16
DIGITS = 32
TERMS = 256


def wave_factors(first, rows, length):
    lane = lax.broadcasted_iota(jnp.int32, (rows, TERMS), 1)
    section = lane // DIGITS
    digit = (lane % DIGITS).astype(F32) * jnp.where(section < 2, float(RADIX), 1.0)
    parts = []
    for value in turn((first + iota((rows, TERMS), 0)) * digit * (1.0 / length)):
        high = value.astype(BF16).astype(F32)
        parts.append(jnp.where((section == 1) | (section == 3), value - high, high))
    upper, lower = section < 2, (section >= 2) & (section < 5)
    masked = [jnp.where(mask, part, 0.0) for mask in (upper, lower) for part in parts]
    return jnp.concatenate(masked, 0).astype(BF16)


def wave_kernel(place_ref, out_y_ref, out_z_ref):
    out_y_ref[...] = wave_factors(place_ref[0].astype(F32), out_y_ref.shape[0] // 4, NY)
    out_z_ref[...] = wave_factors(place_ref[1].astype(F32), out_z_ref.shape[0] // 4, NZ)


def atom_waves(base, weights, factors_ref, digits_ref):
    width = base.shape[1]
    high_digit = jnp.floor(base * (1.0 / RADIX))
    row = iota((DIGITS, width), 0)
    chosen = jnp.where(row == high_digit, 1.0, 0.0).astype(BF16)
    step = row - (base - RADIX * high_digit)
    spread = jnp.where(step == 3.0, weights[3], 0.0)
    for r in (2, 1, 0):
        spread = jnp.where(step == float(r), weights[r], spread)
    high, low = split(spread)
    for section, value in enumerate((chosen, chosen, high, high, low)):
        digits_ref[pl.ds(DIGITS * section, DIGITS), :] = value
    product = jnp.dot(factors_ref[...], digits_ref[...], preferred_element_type=F32)
    rows = product.shape[0] // 4
    cos_a, sin_a, cos_b, sin_b = (product[i * rows : (i + 1) * rows] for i in range(4))
    return cos_a * cos_b - sin_a * sin_b, sin_a * cos_b + cos_a * sin_b


def plane_weights(atoms, weights):
    row = iota((8, atoms.shape[1]), 0) - atoms[0:1]
    return sum(weights[r][3:4] * (row == float(r)).astype(F32) for r in range(4))


def swap(value):
    return pltpu.roll(value, LANES // 2, axis=value.ndim - 1)


def half_sign():
    lane = lax.broadcasted_iota(jnp.int32, (1, LANES), 1)
    return jnp.where(lane < LANES // 2, -1.0, 1.0).astype(F32)


def rotate(value, numer, denom, sign):
    real, imag = value
    if numer == 0:
        return value
    if 4 * numer == denom:
        return (-imag, real) if sign > 0 else (imag, -real)
    angle = 2.0 * np.pi * numer / denom
    cosine, sine = float(np.cos(angle)), float(sign * np.sin(angle))
    if 8 * numer in (denom, 3 * denom):
        size = abs(cosine)
        cos_sign, sin_sign = (1 if cosine > 0 else -1), (1 if sine > 0 else -1)
        if cos_sign == sin_sign:
            return ((real - imag) * (cos_sign * size), (real + imag) * (cos_sign * size))
        return ((real + imag) * (cos_sign * size), (imag - real) * (cos_sign * size))
    return real * cosine - imag * sine, imag * cosine + real * sine


def butterfly(even, turned):
    plus = (even[0] + turned[0], even[1] + turned[1])
    return plus, (even[0] - turned[0], even[1] - turned[1])


def transform(values, sign):
    count = len(values)
    if count == 1:
        return values
    even = transform(values[0::2], sign)
    odd = transform(values[1::2], sign)
    both = [butterfly(even[k], rotate(odd[k], k, count, sign)) for k in range(count // 2)]
    return [pair[0] for pair in both] + [pair[1] for pair in both]


def regroup(low, high):
    first = lax.broadcasted_iota(jnp.int32, low.shape, 1) < LANES // 2
    crossed = swap(jnp.where(first, high, low))
    return jnp.where(first, low, crossed), jnp.where(first, crossed, high)


def pack_kernel(counts_ref, cells_ref, offsets_ref, charges_ref, out_ref):
    width = offsets_ref.shape[1]
    alive = lax.broadcasted_iota(jnp.int32, (1, width), 1) < counts_ref[0]
    atoms = jnp.concatenate(
        [
            lax.bitwise_and(cells_ref[0:1, :], XD - 1).astype(F32),
            cells_ref[1:3, :].astype(F32),
            offsets_ref[...],
            jnp.where(alive, charges_ref[...], 0.0),
            jnp.full((1, width), counts_ref[0].astype(F32)),
        ],
        0,
    )
    for copy in range(out_ref.shape[0]):
        out_ref[copy] = atoms


def atoms_of(same_ref, other_ref, slab, slot, doms):
    half = doms // 2
    return (same_ref, other_ref)[slot // half][slab * half + slot % half]


def forward_kernel(
    place_ref,
    live_ref,
    same_ref,
    other_ref,
    factors_y,
    factors_z,
    plus_ref,
    minus_ref,
    table_y,
    table_z,
    left_ref,
    right_ref,
    grid_ref,
    atoms_ref,
    digits_y,
    digits_z,
):
    step = pl.program_id(0)
    cells_x = grid_ref.shape[0]
    rows = grid_ref.shape[1] // 2
    ky_local = rows - 8
    half_slot = same_ref.shape[2] // 2
    doms = table_y.shape[2] // (2 * half_slot)
    kept = step - place_ref[2]
    kept = jnp.where((kept >= 0) & (kept < table_y.shape[0] - 1), kept, table_y.shape[0] - 1)

    @pl.when(step == 0)
    def _():
        grid_ref[...] = jnp.zeros_like(grid_ref)
        digits_y[...] = jnp.zeros_like(digits_y)
        digits_z[...] = jnp.zeros_like(digits_z)

    for slot in range(doms):
        atoms_ref[slot] = atoms_of(same_ref, other_ref, step, slot, doms)

    def add_tile(tile, halves):
        atoms = jnp.concatenate([atoms_ref[slot, :, pl.ds(part * half_slot, half_slot)] for slot, part, _ in halves], 1)
        counted = jnp.concatenate([jnp.full((1, half_slot), weight) for _, _, weight in halves], 1)
        weights = spline(atoms)
        along_x = plane_weights(atoms, weights) * (atoms[6:7] * counted)
        waves_z = atom_waves(atoms[2:3], [w[5:6] for w in weights], factors_z, digits_z.at[tile])
        waves_z = jnp.concatenate(waves_z, 0)
        waves_y = atom_waves(atoms[1:2], [w[4:5] for w in weights], factors_y, digits_y.at[tile])
        waves_y = jnp.concatenate(waves_y, 0)
        for number, (slot, part, _) in enumerate(halves):
            lanes = slice(number * half_slot, (number + 1) * half_slot)
            start = pl.multiple_of((2 * slot + part) * half_slot, half_slot)
            table_z[kept, :, pl.ds(start, half_slot)] = waves_z[:, lanes]
            table_y[kept, :, pl.ds(start, half_slot)] = waves_y[:, lanes]
        high, low = split(waves_z)
        right_ref[tile, pl.ds(0, LANES), :] = high
        right_ref[tile, pl.ds(LANES, LANES), :] = low
        for plane in range(SPAN):
            first = 4 * rows * plane
            high, low = split(waves_y * along_x[plane : plane + 1])
            left_ref[tile, pl.ds(first, 2 * rows), :] = high
            left_ref[tile, pl.ds(first + 2 * rows, 2 * rows), :] = low
        product = lax.dot_general(
            left_ref[tile], right_ref[tile], (((1,), (1,)), ((), ())), preferred_element_type=F32
        )
        for plane in range(SPAN):
            first = 4 * rows * plane
            high, low = product[first : first + 2 * rows], product[first + 2 * rows : first + 4 * rows]
            at = lax.rem(step * XD + plane, cells_x)
            grid_ref[at] += (high[:, :LANES] + high[:, LANES:]) + (low[:, :LANES] + low[:, LANES:])

    for tile in range(doms // 2):
        add_tile(tile, [(2 * tile, 0, 1.0), (2 * tile + 1, 0, 1.0)])

    reach = [live_ref[step * doms + slot] for slot in range(doms)]
    reach = [sum(reach[: slot + 1]) for slot in range(doms)]
    for tile in range(doms // 2):

        @pl.when(reach[-1] > 2 * tile)
        def _(tile=tile):
            chosen = []
            for place in (2 * tile, 2 * tile + 1):
                slot = sum((total <= place).astype(jnp.int32) for total in reach)
                weight = jnp.where(slot < doms, 1.0, 0.0).astype(F32)
                chosen.append((jnp.minimum(slot, doms - 1), 1, weight))
            add_tile(doms // 2 + tile, chosen)

    @pl.when(step == pl.num_programs(0) - 1)
    def _():
        quarter_rows = ky_local // 2
        group = min(8, quarter_rows)
        for minus, out_ref in enumerate((plus_ref, minus_ref)):
            for start in range(0, quarter_rows, group):
                values = []
                for x in range(cells_x):
                    parts = [
                        grid_ref[x, pl.ds(minus + start + offset, group), :]
                        for offset in (0, quarter_rows, rows, rows + quarter_rows)
                    ]
                    cos_cos, cos_sin = regroup(parts[0], parts[1])
                    sin_cos, sin_sin = regroup(parts[2], parts[3])
                    if minus:
                        values.append((cos_cos + sin_sin, sin_cos - cos_sin))
                    else:
                        values.append((cos_cos - sin_sin, -cos_sin - sin_cos))
                for x, value in enumerate(transform(values, -1)):
                    for part in (0, 1):
                        out_ref[part, x, pl.ds(start, group), :] = value[part]


def inverse_x_kernel(place_ref, spectrum_ref, green_ref, *refs):
    *outs, near_ref = refs
    cells_x, quarter_rows = spectrum_ref.shape[1:3]
    group = min(8, quarter_rows)
    side = 1.0 - 2.0 * place_ref[3].astype(F32)

    def rows_of(step, carry):
        rows = pl.ds(pl.multiple_of(step * group, group), group)
        values = []
        for kx in range(cells_x):
            green = green_ref[kx, rows, :]
            values.append(tuple(spectrum_ref[part, kx, rows, :] * green for part in (0, 1)))
        even = transform(values[0::2], 1)
        odd = transform([(value[0] * side, value[1] * side) for value in values[1::2]], 1)
        for x in range(cells_x // 2):
            here, there = butterfly(even[x], rotate(odd[x], x, cells_x, 1))
            wanted = [(x, here)] + ([(cells_x // 2 + x, there)] if x < 3 else [])
            for plane, value in wanted:
                for part, row_group in enumerate(regroup(value[0], value[1])):
                    near_ref[plane, part, rows, :] = row_group
        return carry

    lax.fori_loop(0, quarter_rows // group, rows_of, 0)
    for k, out_ref in enumerate(outs):
        out_ref[...] = near_ref[pl.ds(lax.bitwise_xor(place_ref[4], k) * XD, XD)]


def inverse_y_kernel(sources, place_ref, *refs):
    ins, (high_ref, low_ref) = refs[: 2 * sources], refs[2 * sources : 2 * sources + 2]
    outs, (lines_ref, turned_ref) = refs[2 * sources + 2 : -2], refs[-2:]
    for number, in_ref in enumerate(ins):
        source = lax.bitwise_xor(place_ref[4], number % sources)
        half = in_ref.shape[1]
        rows = pl.ds(half * (number // sources), half)
        lines_ref[source, :, rows, :] = in_ref[...]
    parts = []
    for x in range(XD):
        lines = jnp.concatenate([lines_ref[source, x] for source in range(sources)], 0)
        pairs = jnp.concatenate([lines, swap(lines) * half_sign()], 0)
        parts.append(split(pairs))
    both = jnp.concatenate([value for part in parts for value in part], 1)
    main = jnp.dot(high_ref[...], both, preferred_element_type=F32)
    high = jnp.concatenate([part[0] for part in parts], 1)
    rest = jnp.dot(low_ref[...], high, preferred_element_type=F32)
    row = lax.broadcasted_iota(jnp.int32, (NY, 1), 0)
    sign = jnp.where((row % 2 == 1) & (place_ref[3] == 1), -1.0, 1.0)
    for x in range(XD):
        total = main[:, 2 * x * LANES : (2 * x + 1) * LANES] + main[:, (2 * x + 1) * LANES : (2 * x + 2) * LANES]
        total = (total + rest[:, x * LANES : (x + 1) * LANES]) * sign
        turned_ref[:, x] = total.reshape(len(outs), -1, LANES)
    for k in range(len(outs)):
        outs[k][...] = turned_ref[lax.bitwise_xor(place_ref[5], k)]


def inverse_z_kernel(sources, place_ref, *refs):
    ins, (high_ref, low_ref) = refs[:sources], refs[sources : sources + 2]
    out_ref, lines_ref = refs[-2:]
    first = pl.program_id(0) * DEPTH
    for k in range(sources):
        lines_ref[lax.bitwise_xor(place_ref[5], k)] = ins[k][pl.ds(first, DEPTH)]
    rows = DEPTH * lines_ref.shape[2]
    lines = jnp.concatenate([lines_ref[source].reshape(rows, LANES) for source in range(sources)], 1)
    high, low = split(lines)
    total = jnp.dot(high, high_ref[...], preferred_element_type=F32)
    total += jnp.dot(low, high_ref[...], preferred_element_type=F32)
    total += jnp.dot(high, low_ref[...], preferred_element_type=F32)
    out_ref[...] = total.reshape(out_ref.shape)


def gather_kernel(
    first, place_ref, same_ref, other_ref, table_y, table_z, plus_ref, minus_ref, out_ref, shift_ref, fields_ref, stack_ref
):
    step = pl.program_id(0)
    half = LANES // 2
    rows = table_y.shape[1] // 2
    ky_local = rows - 8
    width = same_ref.shape[2]
    doms = table_y.shape[2] // width
    planes = fields_ref.shape[0]
    halves = half_sign()

    @pl.when(step == 0)
    def _():
        stack_ref[...] = jnp.zeros_like(stack_ref)
        shift_ref[...] = jnp.zeros_like(shift_ref)
        row = lax.broadcasted_iota(jnp.int32, (8, LANES), 0)

        def build(x, carry):
            plus = plus_ref[first * XD + x]
            shift_ref[pl.ds(1, ky_local), :] = minus_ref[first * XD + x]
            minus = shift_ref[pl.ds(0, ky_local), :]
            last = shift_ref[pl.ds(ky_local, 8), :][0:1]
            main = [plus + minus, swap(plus - minus) * halves]
            if 2 * ky_local < LANES:
                main.append(jnp.zeros((LANES - 2 * ky_local, LANES), F32))
            rest = jnp.where(row % 2 == 0, last, -swap(jnp.broadcast_to(last, (8, LANES))) * halves)
            rest = jnp.where(row < 6, rest, 0.0)
            rest_high = rest.astype(BF16).astype(F32)
            rest = jnp.where((row == 2) | (row == 3), rest - rest_high, rest_high)
            high, low = split(jnp.concatenate(main, 0).T)
            fields_ref[x, :, pl.ds(0, LANES)] = high
            fields_ref[x, :, pl.ds(LANES, LANES)] = low
            fields_ref[x, :, pl.ds(2 * LANES, LANES)] = high
            rest = jnp.concatenate([rest, jnp.zeros((LANES - 8, LANES), F32)], 0)
            fields_ref[x, :, pl.ds(3 * LANES, LANES)] = rest.T.astype(BF16)
            return carry

        lax.fori_loop(0, planes, build, 0)

    first_z = place_ref[1].astype(F32)
    twice = jnp.where(first_z + iota((half, 1), 0) == 0.0, 1.0, 2.0)
    fields = fields_ref[pl.ds(step * XD, SPAN)].reshape(SPAN * LANES, 4 * LANES)
    for slot in range(doms):
        lanes = pl.ds(slot * width, width)
        cosine = table_y[first + step, pl.ds(0, ky_local), lanes]
        sine = table_y[first + step, pl.ds(rows, ky_local), lanes]
        high, low = split(jnp.concatenate([cosine, sine], 0))
        for part, value in enumerate((high, high, low)):
            stack_ref[pl.ds(LANES * part, 2 * ky_local), lanes] = value
        cosine = table_y[first + step, pl.ds(ky_local, 8), lanes][0:1]
        sine = table_y[first + step, pl.ds(rows + ky_local, 8), lanes][0:1]
        row = lax.broadcasted_iota(jnp.int32, (16, width), 0)
        rest = jnp.where(row % 2 == 0, cosine, sine)
        rest_high = rest.astype(BF16).astype(F32)
        rest = jnp.where(row < 4, rest_high, jnp.where(row < 6, rest - rest_high, 0.0))
        stack_ref[pl.ds(3 * LANES, 16), lanes] = rest.astype(BF16)
    product = sum(
        jnp.dot(fields[:, part : part + 2 * LANES], stack_ref[pl.ds(part, 2 * LANES), :], preferred_element_type=F32)
        for part in (0, 2 * LANES)
    )
    for slot in range(doms):
        atoms = atoms_of(same_ref, other_ref, place_ref[2] + first + step, slot, doms)
        along_x = plane_weights(atoms, spline(atoms))
        lanes = pl.ds(slot * width, width)
        field = product[:, slot * width : (slot + 1) * width]
        total = along_x[0:1] * field[:LANES]
        for plane in range(1, SPAN):
            total += along_x[plane : plane + 1] * field[plane * LANES : (plane + 1) * LANES]
        waves = total * table_z[first + step, :, lanes]
        sampled = jnp.sum((waves[:half] - waves[half:]) * twice, axis=0, keepdims=True)
        core = place_ref[5] % 2 if slot < doms // 2 else 1 - place_ref[5] % 2
        out_ref[step * doms + 2 * (slot % (doms // 2)) + core] = sampled


def bf16_pair(table):
    high = table.astype(ml_dtypes.bfloat16)
    low = (table - high.astype(np.float64)).astype(ml_dtypes.bfloat16)
    return jnp.asarray(high), jnp.asarray(low)


def inverse_y_table(slab_half, ky_local):
    waves = []
    for slab in range(slab_half):
        first = slab * ky_local
        waves += [first + i for i in range(ky_local)] + [-(first + i + 1) for i in range(ky_local)]
    angle = 2.0 * np.pi * (np.outer(np.arange(NY), np.array(waves)) % NY) / NY
    return bf16_pair(np.concatenate([np.cos(angle), np.sin(angle)], 1))


def inverse_z_table(dom_count):
    kz = np.arange(KH)
    angle = 2.0 * np.pi * (np.outer(kz, np.arange(NZ)) % NZ) / NZ
    weight = np.where(kz == 0, 1.0, 2.0)[:, None]
    parts = [weight * np.cos(angle), -weight * np.sin(angle)]
    return bf16_pair(
        np.stack([p.reshape(dom_count, KH // dom_count, NZ) for p in parts], 1).reshape(2 * KH, NZ)
    )


def whole_spec(shape):
    return pl.BlockSpec(shape, lambda *_: (0,) * len(shape))


SMALL = pl.CostEstimate(flops=10**6, bytes_accessed=10**4, transcendentals=0)
SMEM = pl.BlockSpec(memory_space=pltpu.SMEM)


def params(mib):
    return pltpu.CompilerParams(vmem_limit_bytes=mib * MIB)


def swapped(value, axis, distance):
    if distance == 0:
        return value
    return lax.ppermute(value, axis, [(i, i ^ distance) for i in range(lax.axis_size(axis))])


def per_device(base_cells, offsets, charges, bias_coupling, counts, green):
    slabs = lax.axis_size("slab")
    doms = lax.axis_size("dom")
    slab = lax.axis_index("slab")
    dom = lax.axis_index("dom")
    atoms_local = charges.shape[0]
    cells_x = XD * slabs
    ky_local = NY // slabs
    kz_local = KH // doms
    slab_half = slabs // 2
    rows_local = NY // doms
    rows = ky_local + 8
    quarter_rows = ky_local // 2
    normalize = 1.0 / (cells_x * NY * NZ)
    upper = slab // slab_half
    place = jnp.stack(
        [slab * ky_local, dom * kz_local, upper * slab_half, upper, slab % slab_half, dom]
    ).astype(jnp.int32)

    vmem = pl.BlockSpec(memory_space=pltpu.VMEM)
    atoms = pl.pallas_call(
        pack_kernel,
        in_specs=[SMEM, vmem, vmem, vmem],
        out_specs=vmem,
        out_shape=jax.ShapeDtypeStruct((slabs * doms // 2, 8, atoms_local), F32),
        name="pack",
    )(counts, base_cells, offsets, charges.reshape(1, atoms_local))
    factors_y, factors_z = pl.pallas_call(
        wave_kernel,
        in_specs=[SMEM],
        out_specs=[vmem] * 2,
        out_shape=[jax.ShapeDtypeStruct((4 * count, TERMS), BF16) for count in (rows, LANES // 2)],
        compiler_params=params(8),
        name="waves",
    )(place)
    everyone = list(range(slabs * doms))
    same = lax.all_to_all(
        atoms, ("slab", "dom"), 0, 0, axis_index_groups=[everyone[0::2], everyone[1::2]], tiled=True
    )

    def halves_beside(value):
        return jnp.concatenate([value[:, :quarter_rows], value[:, quarter_rows:]], 2) * normalize

    own = halves_beside(green)
    same, flipped, factors_y, factors_z = lax.optimization_barrier(
        (same, halves_beside(green[:, ::-1]), factors_y, factors_z)
    )
    other = swapped(same, "dom", 1)
    mirrored = lax.ppermute(flipped, "slab", [(s, slabs - 1 - s) for s in range(slabs)])

    reaches = [value[:, 7, 0].reshape(slabs, doms // 2) for value in (same, other)]
    live = (jnp.concatenate(reaches, 1).reshape(-1) > atoms_local // 2).astype(jnp.int32)
    atoms_slab = doms * atoms_local
    table_bytes = 4 * (slab_half + 1) * (2 * rows + LANES) * atoms_slab
    spectrum_bytes = 16 * cells_x * max(8, quarter_rows) * LANES
    plus, minus, table_y, table_z = pl.pallas_call(
        forward_kernel,
        grid=(slabs,),
        in_specs=[SMEM] * 2 + [vmem] * 4,
        out_specs=[vmem] * 4,
        out_shape=[
            jax.ShapeDtypeStruct((2, cells_x, quarter_rows, LANES), F32),
            jax.ShapeDtypeStruct((2, cells_x, quarter_rows, LANES), F32),
            jax.ShapeDtypeStruct((slab_half + 1, 2 * rows, atoms_slab), F32),
            jax.ShapeDtypeStruct((slab_half + 1, LANES, atoms_slab), F32),
        ],
        scratch_shapes=[
            pltpu.VMEM((doms, SPAN * 4 * rows, atoms_local), BF16),
            pltpu.VMEM((doms, 2 * LANES, atoms_local), BF16),
            pltpu.VMEM((cells_x, 2 * rows, LANES), F32),
            pltpu.VMEM((doms, 8, atoms_local), F32),
            pltpu.VMEM((doms, TERMS, atoms_local), BF16),
            pltpu.VMEM((doms, TERMS, atoms_local), BF16),
        ],
        compiler_params=params(16 + (table_bytes + spectrum_bytes) // MIB),
        cost_estimate=SMALL,
        name="forward",
    )(place, live, same, other, factors_y, factors_z)

    near_planes = cells_x // 2 + 3
    lines, near = [], []
    for spectrum, influence in ((plus, own), (minus, mirrored)):
        *pieces, planes = pl.pallas_call(
            inverse_x_kernel,
            in_specs=[SMEM] + [vmem] * 2,
            out_specs=[vmem] * (slab_half + 1),
            out_shape=[jax.ShapeDtypeStruct((XD, 2, quarter_rows, LANES), F32)] * slab_half
            + [jax.ShapeDtypeStruct((near_planes, 2, quarter_rows, LANES), F32)],
            compiler_params=params(24),
            cost_estimate=SMALL,
            name="inverse_x",
        )(place, spectrum, influence)
        near.append(planes.reshape(near_planes, ky_local, LANES))
        lines += [swapped(value.reshape(XD, ky_local, LANES), "slab", k) for k, value in enumerate(pieces)]

    steps = slab_half // GATHERS

    def gather(part, place):
        return pl.pallas_call(
            functools.partial(gather_kernel, part * steps),
            grid=(steps,),
            in_specs=[SMEM] + [vmem] * 6,
            out_specs=vmem,
            out_shape=jax.ShapeDtypeStruct((steps * doms, 1, atoms_local), F32),
            scratch_shapes=[
                pltpu.VMEM((rows, LANES), F32),
                pltpu.VMEM((steps * XD + 3, LANES, 4 * LANES), BF16),
                pltpu.VMEM((4 * LANES, atoms_slab), BF16),
            ],
            compiler_params=params(12 + (table_bytes + 8 * near_planes * LANES * LANES) // MIB),
            cost_estimate=SMALL,
            name="gather",
        )(place, same, other, table_y, table_z, *near)

    earlier, *lines = lax.optimization_barrier((gather(0, place), *lines))

    high_y, low_y = inverse_y_table(slab_half, ky_local)
    high_z, low_z = inverse_z_table(doms)

    turned = pl.pallas_call(
        functools.partial(inverse_y_kernel, slab_half),
        in_specs=[SMEM] + [vmem] * (2 * slab_half + 2),
        out_specs=[vmem] * doms,
        out_shape=[jax.ShapeDtypeStruct((XD, rows_local, LANES), F32)] * doms,
        scratch_shapes=[
            pltpu.VMEM((slab_half, XD, 2 * ky_local, LANES), F32),
            pltpu.VMEM((doms, XD, rows_local, LANES), F32),
        ],
        compiler_params=params(32),
        cost_estimate=SMALL,
        name="inverse_y",
    )(place, *lines, high_y, low_y)
    columns = [swapped(value, "dom", k) for k, value in enumerate(turned)]

    columns[1], late_place = lax.optimization_barrier((columns[1], place))
    partial = jnp.concatenate([earlier] + [gather(part, late_place) for part in range(1, GATHERS)], 0)
    members = slab_half * doms
    sampled = lax.all_to_all(
        partial.reshape(members, atoms_local),
        ("slab", "dom"),
        0,
        0,
        axis_index_groups=[list(range(members)), list(range(members, 2 * members))],
        tiled=True,
    )
    alive = jnp.arange(atoms_local, dtype=jnp.int32) < counts[0]
    gradient = jnp.where(alive, bias_coupling * jnp.sum(sampled, 0), 0.0)
    gradient, *columns = lax.optimization_barrier((gradient, *columns))

    potential = pl.pallas_call(
        functools.partial(inverse_z_kernel, doms),
        grid=(XD // DEPTH,),
        in_specs=[SMEM] + [vmem] * (doms + 2),
        out_specs=pl.BlockSpec((DEPTH, rows_local, NZ), lambda step: (step, 0, 0)),
        out_shape=jax.ShapeDtypeStruct((XD, rows_local, NZ), F32),
        scratch_shapes=[pltpu.VMEM((doms, DEPTH, rows_local, LANES), F32)],
        compiler_params=params(24),
        cost_estimate=SMALL,
        name="inverse_z",
    )(place, *columns, high_z, low_z)
    return (potential, gradient)


def solution(mesh):
    placed = (
        P(None, ("slab", "dom")),
        P(None, ("slab", "dom")),
        P(("slab", "dom")),
        P(("slab", "dom")),
        P(("slab", "dom")),
        P(None, "slab", "dom"),
    )
    return jax.shard_map(
        per_device,
        mesh=mesh,
        in_specs=placed,
        out_specs=(P("slab", "dom", None), P(("slab", "dom"))),
        check_vma=False,
    )
```

```python
import functools

import jax
import jax.numpy as jnp
import ml_dtypes
import numpy as np
from jax import lax
from jax.experimental import pallas as pl
from jax.experimental.pallas import tpu as pltpu
from jax.sharding import PartitionSpec as P

XD = 4
NY = 512
NZ = 512
KH = NZ // 2
LANES = 128
SPAN = XD + 3
DEPTH = 2
GATHERS = 2
MIB = 1 << 20
BF16 = jnp.bfloat16
F32 = jnp.float32


def polynomial(function, terms):
    nodes = 0.125 * (1.0 - np.cos(np.pi * (np.arange(64) + 0.5) / 64))
    powers = nodes[:, None] ** np.arange(terms)[None, :]
    return [float(v) for v in np.linalg.lstsq(powers, function(np.sqrt(nodes)), rcond=None)[0]]


SINE_TERMS = polynomial(lambda r: np.sin(np.pi * r) / r, 6)
COSINE_TERMS = polynomial(lambda r: np.cos(np.pi * r), 6)


def horner(terms, square):
    total = jnp.full_like(square, terms[-1])
    for term in terms[-2::-1]:
        total = total * square + term
    return total


def turn(fraction):
    left = fraction - jnp.floor(fraction + 0.5)
    square = left * left
    sine = left * horner(SINE_TERMS, square)
    cosine = horner(COSINE_TERMS, square)
    return 1.0 - 2.0 * sine * sine, 2.0 * sine * cosine


def spline(frac):
    inner = 1.0 - frac
    square = frac * frac
    cube = square * frac
    sixth = 1.0 / 6.0
    return (
        inner * inner * inner * sixth,
        (3.0 * cube - 6.0 * square + 4.0) * sixth,
        (-3.0 * cube + 3.0 * square + 3.0 * frac + 1.0) * sixth,
        cube * sixth,
    )


def split(value):
    high = value.astype(BF16)
    return high, (value - high.astype(F32)).astype(BF16)


def iota(shape, axis):
    return lax.broadcasted_iota(jnp.int32, shape, axis).astype(F32)


RADIX = 16
DIGITS = 32
TERMS = 256


def wave_factors(first, rows, length):
    lane = lax.broadcasted_iota(jnp.int32, (rows, TERMS), 1)
    section = lane // DIGITS
    digit = (lane % DIGITS).astype(F32) * jnp.where(section < 2, float(RADIX), 1.0)
    parts = []
    for value in turn((first + iota((rows, TERMS), 0)) * digit * (1.0 / length)):
        high = value.astype(BF16).astype(F32)
        parts.append(jnp.where((section == 1) | (section == 3), value - high, high))
    upper, lower = section < 2, (section >= 2) & (section < 5)
    masked = [jnp.where(mask, part, 0.0) for mask in (upper, lower) for part in parts]
    return jnp.concatenate(masked, 0).astype(BF16)


def wave_kernel(place_ref, out_y_ref, out_z_ref):
    out_y_ref[...] = wave_factors(place_ref[0].astype(F32), out_y_ref.shape[0] // 4, NY)
    out_z_ref[...] = wave_factors(place_ref[1].astype(F32), out_z_ref.shape[0] // 4, NZ)


def atom_waves(base, weights, factors_ref, digits_ref):
    width = base.shape[1]
    high_digit = jnp.floor(base * (1.0 / RADIX))
    row = iota((DIGITS, width), 0)
    chosen = jnp.where(row == high_digit, 1.0, 0.0).astype(BF16)
    step = row - (base - RADIX * high_digit)
    spread = jnp.where(step == 3.0, weights[3], 0.0)
    for r in (2, 1, 0):
        spread = jnp.where(step == float(r), weights[r], spread)
    high, low = split(spread)
    for section, value in enumerate((chosen, chosen, high, high, low)):
        digits_ref[pl.ds(DIGITS * section, DIGITS), :] = value
    product = jnp.dot(factors_ref[...], digits_ref[...], preferred_element_type=F32)
    rows = product.shape[0] // 4
    cos_a, sin_a, cos_b, sin_b = (product[i * rows : (i + 1) * rows] for i in range(4))
    return cos_a * cos_b - sin_a * sin_b, sin_a * cos_b + cos_a * sin_b


def plane_weights(atoms, weights):
    row = iota((8, atoms.shape[1]), 0) - atoms[0:1]
    return sum(weights[r][3:4] * (row == float(r)).astype(F32) for r in range(4))


def swap(value):
    return pltpu.roll(value, LANES // 2, axis=value.ndim - 1)


def half_sign():
    lane = lax.broadcasted_iota(jnp.int32, (1, LANES), 1)
    return jnp.where(lane < LANES // 2, -1.0, 1.0).astype(F32)


def rotate(value, numer, denom, sign):
    real, imag = value
    if numer == 0:
        return value
    if 4 * numer == denom:
        return (-imag, real) if sign > 0 else (imag, -real)
    angle = 2.0 * np.pi * numer / denom
    cosine, sine = float(np.cos(angle)), float(sign * np.sin(angle))
    if 8 * numer in (denom, 3 * denom):
        size = abs(cosine)
        cos_sign, sin_sign = (1 if cosine > 0 else -1), (1 if sine > 0 else -1)
        if cos_sign == sin_sign:
            return ((real - imag) * (cos_sign * size), (real + imag) * (cos_sign * size))
        return ((real + imag) * (cos_sign * size), (imag - real) * (cos_sign * size))
    return real * cosine - imag * sine, imag * cosine + real * sine


def butterfly(even, turned):
    plus = (even[0] + turned[0], even[1] + turned[1])
    return plus, (even[0] - turned[0], even[1] - turned[1])


def transform(values, sign):
    count = len(values)
    if count == 1:
        return values
    even = transform(values[0::2], sign)
    odd = transform(values[1::2], sign)
    both = [butterfly(even[k], rotate(odd[k], k, count, sign)) for k in range(count // 2)]
    return [pair[0] for pair in both] + [pair[1] for pair in both]


def regroup(low, high):
    first = lax.broadcasted_iota(jnp.int32, low.shape, 1) < LANES // 2
    crossed = swap(jnp.where(first, high, low))
    return jnp.where(first, low, crossed), jnp.where(first, crossed, high)


def pack_kernel(counts_ref, cells_ref, offsets_ref, charges_ref, out_ref):
    width = offsets_ref.shape[1]
    alive = lax.broadcasted_iota(jnp.int32, (1, width), 1) < counts_ref[0]
    atoms = jnp.concatenate(
        [
            lax.bitwise_and(cells_ref[0:1, :], XD - 1).astype(F32),
            cells_ref[1:3, :].astype(F32),
            offsets_ref[...],
            jnp.where(alive, charges_ref[...], 0.0),
            jnp.full((1, width), counts_ref[0].astype(F32)),
        ],
        0,
    )
    for copy in range(out_ref.shape[0]):
        out_ref[copy] = atoms


def atoms_of(same_ref, other_ref, slab, slot, doms):
    half = doms // 2
    return (same_ref, other_ref)[slot // half][slab * half + slot % half]


def forward_kernel(
    place_ref,
    live_ref,
    same_ref,
    other_ref,
    factors_y,
    factors_z,
    plus_ref,
    minus_ref,
    table_y,
    table_z,
    left_ref,
    right_ref,
    grid_ref,
    atoms_ref,
    digits_y,
    digits_z,
):
    step = pl.program_id(0)
    cells_x = grid_ref.shape[0]
    rows = grid_ref.shape[1] // 2
    ky_local = rows - 8
    half_slot = same_ref.shape[2] // 2
    doms = table_y.shape[2] // (2 * half_slot)
    kept = step - place_ref[2]
    kept = jnp.where((kept >= 0) & (kept < table_y.shape[0] - 1), kept, table_y.shape[0] - 1)

    @pl.when(step == 0)
    def _():
        grid_ref[...] = jnp.zeros_like(grid_ref)
        digits_y[...] = jnp.zeros_like(digits_y)
        digits_z[...] = jnp.zeros_like(digits_z)

    for slot in range(doms):
        atoms_ref[slot] = atoms_of(same_ref, other_ref, step, slot, doms)

    def add_tile(tile, halves):
        atoms = jnp.concatenate([atoms_ref[slot, :, pl.ds(part * half_slot, half_slot)] for slot, part, _ in halves], 1)
        counted = jnp.concatenate([jnp.full((1, half_slot), weight) for _, _, weight in halves], 1)
        weights = spline(atoms)
        along_x = plane_weights(atoms, weights) * (atoms[6:7] * counted)
        waves_z = atom_waves(atoms[2:3], [w[5:6] for w in weights], factors_z, digits_z.at[tile])
        waves_z = jnp.concatenate(waves_z, 0)
        waves_y = atom_waves(atoms[1:2], [w[4:5] for w in weights], factors_y, digits_y.at[tile])
        waves_y = jnp.concatenate(waves_y, 0)
        for number, (slot, part, _) in enumerate(halves):
            lanes = slice(number * half_slot, (number + 1) * half_slot)
            start = pl.multiple_of((2 * slot + part) * half_slot, half_slot)
            table_z[kept, :, pl.ds(start, half_slot)] = waves_z[:, lanes]
            table_y[kept, :, pl.ds(start, half_slot)] = waves_y[:, lanes]
        high, low = split(waves_z)
        right_ref[tile, pl.ds(0, LANES), :] = high
        right_ref[tile, pl.ds(LANES, LANES), :] = low
        for plane in range(SPAN):
            first = 4 * rows * plane
            high, low = split(waves_y * along_x[plane : plane + 1])
            left_ref[tile, pl.ds(first, 2 * rows), :] = high
            left_ref[tile, pl.ds(first + 2 * rows, 2 * rows), :] = low
        product = lax.dot_general(
            left_ref[tile], right_ref[tile], (((1,), (1,)), ((), ())), preferred_element_type=F32
        )
        for plane in range(SPAN):
            first = 4 * rows * plane
            high, low = product[first : first + 2 * rows], product[first + 2 * rows : first + 4 * rows]
            at = lax.rem(step * XD + plane, cells_x)
            grid_ref[at] += (high[:, :LANES] + high[:, LANES:]) + (low[:, :LANES] + low[:, LANES:])

    reach = [live_ref[step * doms + slot] for slot in range(doms)]
    reach = [sum(reach[: slot + 1]) for slot in range(doms)]
    for extra in range(doms // 2 + 1):

        @pl.when((reach[-1] + 1) // 2 == extra)
        def _(extra=extra):
            for tile in range(doms // 2):
                add_tile(tile, [(2 * tile, 0, 1.0), (2 * tile + 1, 0, 1.0)])
            for tile in range(extra):
                chosen = []
                for place in (2 * tile, 2 * tile + 1):
                    slot = sum((total <= place).astype(jnp.int32) for total in reach)
                    weight = jnp.where(slot < doms, 1.0, 0.0).astype(F32)
                    chosen.append((jnp.minimum(slot, doms - 1), 1, weight))
                add_tile(doms // 2 + tile, chosen)

    @pl.when(step == pl.num_programs(0) - 1)
    def _():
        quarter_rows = ky_local // 2
        group = min(8, quarter_rows)
        for minus, out_ref in enumerate((plus_ref, minus_ref)):
            for start in range(0, quarter_rows, group):
                values = []
                for x in range(cells_x):
                    parts = [
                        grid_ref[x, pl.ds(minus + start + offset, group), :]
                        for offset in (0, quarter_rows, rows, rows + quarter_rows)
                    ]
                    cos_cos, cos_sin = regroup(parts[0], parts[1])
                    sin_cos, sin_sin = regroup(parts[2], parts[3])
                    if minus:
                        values.append((cos_cos + sin_sin, sin_cos - cos_sin))
                    else:
                        values.append((cos_cos - sin_sin, -cos_sin - sin_cos))
                for x, value in enumerate(transform(values, -1)):
                    for part in (0, 1):
                        out_ref[part, x, pl.ds(start, group), :] = value[part]


def inverse_x_kernel(place_ref, spectrum_ref, green_ref, *refs):
    *outs, near_ref = refs
    cells_x, quarter_rows = spectrum_ref.shape[1:3]
    group = min(8, quarter_rows)
    side = 1.0 - 2.0 * place_ref[3].astype(F32)

    def rows_of(step, carry):
        rows = pl.ds(pl.multiple_of(step * group, group), group)
        values = []
        for kx in range(cells_x):
            green = green_ref[kx, rows, :]
            values.append(tuple(spectrum_ref[part, kx, rows, :] * green for part in (0, 1)))
        even = transform(values[0::2], 1)
        odd = transform([(value[0] * side, value[1] * side) for value in values[1::2]], 1)
        for x in range(cells_x // 2):
            here, there = butterfly(even[x], rotate(odd[x], x, cells_x, 1))
            wanted = [(x, here)] + ([(cells_x // 2 + x, there)] if x < 3 else [])
            for plane, value in wanted:
                for part, row_group in enumerate(regroup(value[0], value[1])):
                    near_ref[plane, part, rows, :] = row_group
        return carry

    lax.fori_loop(0, quarter_rows // group, rows_of, 0)
    for k, out_ref in enumerate(outs):
        out_ref[...] = near_ref[pl.ds(lax.bitwise_xor(place_ref[4], k) * XD, XD)]


def inverse_y_kernel(sources, place_ref, *refs):
    ins, (high_ref, low_ref) = refs[: 2 * sources], refs[2 * sources : 2 * sources + 2]
    outs, (lines_ref, turned_ref) = refs[2 * sources + 2 : -2], refs[-2:]
    for number, in_ref in enumerate(ins):
        source = lax.bitwise_xor(place_ref[4], number % sources)
        half = in_ref.shape[1]
        rows = pl.ds(half * (number // sources), half)
        lines_ref[source, :, rows, :] = in_ref[...]
    parts = []
    for x in range(XD):
        lines = jnp.concatenate([lines_ref[source, x] for source in range(sources)], 0)
        pairs = jnp.concatenate([lines, swap(lines) * half_sign()], 0)
        parts.append(split(pairs))
    both = jnp.concatenate([value for part in parts for value in part], 1)
    main = jnp.dot(high_ref[...], both, preferred_element_type=F32)
    high = jnp.concatenate([part[0] for part in parts], 1)
    rest = jnp.dot(low_ref[...], high, preferred_element_type=F32)
    row = lax.broadcasted_iota(jnp.int32, (NY, 1), 0)
    sign = jnp.where((row % 2 == 1) & (place_ref[3] == 1), -1.0, 1.0)
    for x in range(XD):
        total = main[:, 2 * x * LANES : (2 * x + 1) * LANES] + main[:, (2 * x + 1) * LANES : (2 * x + 2) * LANES]
        total = (total + rest[:, x * LANES : (x + 1) * LANES]) * sign
        turned_ref[:, x] = total.reshape(len(outs), -1, LANES)
    for k in range(len(outs)):
        outs[k][...] = turned_ref[lax.bitwise_xor(place_ref[5], k)]


def inverse_z_kernel(sources, place_ref, *refs):
    ins, (high_ref, low_ref) = refs[:sources], refs[sources : sources + 2]
    out_ref, lines_ref = refs[-2:]
    first = pl.program_id(0) * DEPTH
    for k in range(sources):
        lines_ref[lax.bitwise_xor(place_ref[5], k)] = ins[k][pl.ds(first, DEPTH)]
    rows = DEPTH * lines_ref.shape[2]
    lines = jnp.concatenate([lines_ref[source].reshape(rows, LANES) for source in range(sources)], 1)
    high, low = split(lines)
    total = jnp.dot(high, high_ref[...], preferred_element_type=F32)
    total += jnp.dot(low, high_ref[...], preferred_element_type=F32)
    total += jnp.dot(high, low_ref[...], preferred_element_type=F32)
    out_ref[...] = total.reshape(out_ref.shape)


def gather_kernel(
    first, place_ref, same_ref, other_ref, table_y, table_z, plus_ref, minus_ref, out_ref, shift_ref, fields_ref, stack_ref
):
    step = pl.program_id(0)
    half = LANES // 2
    rows = table_y.shape[1] // 2
    ky_local = rows - 8
    width = same_ref.shape[2]
    doms = table_y.shape[2] // width
    planes = fields_ref.shape[0]
    halves = half_sign()

    @pl.when(step == 0)
    def _():
        stack_ref[...] = jnp.zeros_like(stack_ref)
        shift_ref[...] = jnp.zeros_like(shift_ref)
        row = lax.broadcasted_iota(jnp.int32, (8, LANES), 0)

        def build(x, carry):
            plus = plus_ref[first * XD + x]
            shift_ref[pl.ds(1, ky_local), :] = minus_ref[first * XD + x]
            minus = shift_ref[pl.ds(0, ky_local), :]
            last = shift_ref[pl.ds(ky_local, 8), :][0:1]
            main = [plus + minus, swap(plus - minus) * halves]
            if 2 * ky_local < LANES:
                main.append(jnp.zeros((LANES - 2 * ky_local, LANES), F32))
            rest = jnp.where(row % 2 == 0, last, -swap(jnp.broadcast_to(last, (8, LANES))) * halves)
            rest = jnp.where(row < 6, rest, 0.0)
            rest_high = rest.astype(BF16).astype(F32)
            rest = jnp.where((row == 2) | (row == 3), rest - rest_high, rest_high)
            high, low = split(jnp.concatenate(main, 0).T)
            fields_ref[x, :, pl.ds(0, LANES)] = high
            fields_ref[x, :, pl.ds(LANES, LANES)] = low
            fields_ref[x, :, pl.ds(2 * LANES, LANES)] = high
            rest = jnp.concatenate([rest, jnp.zeros((LANES - 8, LANES), F32)], 0)
            fields_ref[x, :, pl.ds(3 * LANES, LANES)] = rest.T.astype(BF16)
            return carry

        lax.fori_loop(0, planes, build, 0)

    first_z = place_ref[1].astype(F32)
    twice = jnp.where(first_z + iota((half, 1), 0) == 0.0, 1.0, 2.0)
    fields = fields_ref[pl.ds(step * XD, SPAN)].reshape(SPAN * LANES, 4 * LANES)
    for slot in range(doms):
        lanes = pl.ds(slot * width, width)
        cosine = table_y[first + step, pl.ds(0, ky_local), lanes]
        sine = table_y[first + step, pl.ds(rows, ky_local), lanes]
        high, low = split(jnp.concatenate([cosine, sine], 0))
        for part, value in enumerate((high, high, low)):
            stack_ref[pl.ds(LANES * part, 2 * ky_local), lanes] = value
        cosine = table_y[first + step, pl.ds(ky_local, 8), lanes][0:1]
        sine = table_y[first + step, pl.ds(rows + ky_local, 8), lanes][0:1]
        row = lax.broadcasted_iota(jnp.int32, (16, width), 0)
        rest = jnp.where(row % 2 == 0, cosine, sine)
        rest_high = rest.astype(BF16).astype(F32)
        rest = jnp.where(row < 4, rest_high, jnp.where(row < 6, rest - rest_high, 0.0))
        stack_ref[pl.ds(3 * LANES, 16), lanes] = rest.astype(BF16)
    product = sum(
        jnp.dot(fields[:, part : part + 2 * LANES], stack_ref[pl.ds(part, 2 * LANES), :], preferred_element_type=F32)
        for part in (0, 2 * LANES)
    )
    for slot in range(doms):
        atoms = atoms_of(same_ref, other_ref, place_ref[2] + first + step, slot, doms)
        along_x = plane_weights(atoms, spline(atoms))
        lanes = pl.ds(slot * width, width)
        field = product[:, slot * width : (slot + 1) * width]
        total = along_x[0:1] * field[:LANES]
        for plane in range(1, SPAN):
            total += along_x[plane : plane + 1] * field[plane * LANES : (plane + 1) * LANES]
        waves = total * table_z[first + step, :, lanes]
        sampled = jnp.sum((waves[:half] - waves[half:]) * twice, axis=0, keepdims=True)
        core = place_ref[5] % 2 if slot < doms // 2 else 1 - place_ref[5] % 2
        out_ref[step * doms + 2 * (slot % (doms // 2)) + core] = sampled


def bf16_pair(table):
    high = table.astype(ml_dtypes.bfloat16)
    low = (table - high.astype(np.float64)).astype(ml_dtypes.bfloat16)
    return jnp.asarray(high), jnp.asarray(low)


def inverse_y_table(slab_half, ky_local):
    waves = []
    for slab in range(slab_half):
        first = slab * ky_local
        waves += [first + i for i in range(ky_local)] + [-(first + i + 1) for i in range(ky_local)]
    angle = 2.0 * np.pi * (np.outer(np.arange(NY), np.array(waves)) % NY) / NY
    return bf16_pair(np.concatenate([np.cos(angle), np.sin(angle)], 1))


def inverse_z_table(dom_count):
    kz = np.arange(KH)
    angle = 2.0 * np.pi * (np.outer(kz, np.arange(NZ)) % NZ) / NZ
    weight = np.where(kz == 0, 1.0, 2.0)[:, None]
    parts = [weight * np.cos(angle), -weight * np.sin(angle)]
    return bf16_pair(
        np.stack([p.reshape(dom_count, KH // dom_count, NZ) for p in parts], 1).reshape(2 * KH, NZ)
    )


def whole_spec(shape):
    return pl.BlockSpec(shape, lambda *_: (0,) * len(shape))


SMALL = pl.CostEstimate(flops=10**6, bytes_accessed=10**4, transcendentals=0)
SMEM = pl.BlockSpec(memory_space=pltpu.SMEM)


def params(mib):
    return pltpu.CompilerParams(vmem_limit_bytes=mib * MIB)


def swapped(value, axis, distance):
    if distance == 0:
        return value
    return lax.ppermute(value, axis, [(i, i ^ distance) for i in range(lax.axis_size(axis))])


def per_device(base_cells, offsets, charges, bias_coupling, counts, green):
    slabs = lax.axis_size("slab")
    doms = lax.axis_size("dom")
    slab = lax.axis_index("slab")
    dom = lax.axis_index("dom")
    atoms_local = charges.shape[0]
    cells_x = XD * slabs
    ky_local = NY // slabs
    kz_local = KH // doms
    slab_half = slabs // 2
    rows_local = NY // doms
    rows = ky_local + 8
    quarter_rows = ky_local // 2
    normalize = 1.0 / (cells_x * NY * NZ)
    upper = slab // slab_half
    place = jnp.stack(
        [slab * ky_local, dom * kz_local, upper * slab_half, upper, slab % slab_half, dom]
    ).astype(jnp.int32)

    vmem = pl.BlockSpec(memory_space=pltpu.VMEM)
    atoms = pl.pallas_call(
        pack_kernel,
        in_specs=[SMEM, vmem, vmem, vmem],
        out_specs=vmem,
        out_shape=jax.ShapeDtypeStruct((slabs * doms // 2, 8, atoms_local), F32),
        name="pack",
    )(counts, base_cells, offsets, charges.reshape(1, atoms_local))
    factors_y, factors_z = pl.pallas_call(
        wave_kernel,
        in_specs=[SMEM],
        out_specs=[vmem] * 2,
        out_shape=[jax.ShapeDtypeStruct((4 * count, TERMS), BF16) for count in (rows, LANES // 2)],
        compiler_params=params(8),
        name="waves",
    )(place)
    everyone = list(range(slabs * doms))
    same = lax.all_to_all(
        atoms, ("slab", "dom"), 0, 0, axis_index_groups=[everyone[0::2], everyone[1::2]], tiled=True
    )

    def halves_beside(value):
        return jnp.concatenate([value[:, :quarter_rows], value[:, quarter_rows:]], 2) * normalize

    own = halves_beside(green)
    same, flipped, factors_y, factors_z = lax.optimization_barrier(
        (same, halves_beside(green[:, ::-1]), factors_y, factors_z)
    )
    other = swapped(same, "dom", 1)
    mirrored = lax.ppermute(flipped, "slab", [(s, slabs - 1 - s) for s in range(slabs)])

    reaches = [value[:, 7, 0].reshape(slabs, doms // 2) for value in (same, other)]
    live = (jnp.concatenate(reaches, 1).reshape(-1) > atoms_local // 2).astype(jnp.int32)
    atoms_slab = doms * atoms_local
    table_bytes = 4 * (slab_half + 1) * (2 * rows + LANES) * atoms_slab
    spectrum_bytes = 16 * cells_x * max(8, quarter_rows) * LANES
    plus, minus, table_y, table_z = pl.pallas_call(
        forward_kernel,
        grid=(slabs,),
        in_specs=[SMEM] * 2 + [vmem] * 4,
        out_specs=[vmem] * 4,
        out_shape=[
            jax.ShapeDtypeStruct((2, cells_x, quarter_rows, LANES), F32),
            jax.ShapeDtypeStruct((2, cells_x, quarter_rows, LANES), F32),
            jax.ShapeDtypeStruct((slab_half + 1, 2 * rows, atoms_slab), F32),
            jax.ShapeDtypeStruct((slab_half + 1, LANES, atoms_slab), F32),
        ],
        scratch_shapes=[
            pltpu.VMEM((doms, SPAN * 4 * rows, atoms_local), BF16),
            pltpu.VMEM((doms, 2 * LANES, atoms_local), BF16),
            pltpu.VMEM((cells_x, 2 * rows, LANES), F32),
            pltpu.VMEM((doms, 8, atoms_local), F32),
            pltpu.VMEM((doms, TERMS, atoms_local), BF16),
            pltpu.VMEM((doms, TERMS, atoms_local), BF16),
        ],
        compiler_params=params(16 + (table_bytes + spectrum_bytes) // MIB),
        cost_estimate=SMALL,
        name="forward",
    )(place, live, same, other, factors_y, factors_z)

    near_planes = cells_x // 2 + 3
    lines, near = [], []
    for spectrum, influence in ((plus, own), (minus, mirrored)):
        *pieces, planes = pl.pallas_call(
            inverse_x_kernel,
            in_specs=[SMEM] + [vmem] * 2,
            out_specs=[vmem] * (slab_half + 1),
            out_shape=[jax.ShapeDtypeStruct((XD, 2, quarter_rows, LANES), F32)] * slab_half
            + [jax.ShapeDtypeStruct((near_planes, 2, quarter_rows, LANES), F32)],
            compiler_params=params(24),
            cost_estimate=SMALL,
            name="inverse_x",
        )(place, spectrum, influence)
        near.append(planes.reshape(near_planes, ky_local, LANES))
        lines += [swapped(value.reshape(XD, ky_local, LANES), "slab", k) for k, value in enumerate(pieces)]

    steps = slab_half // GATHERS

    def gather(part, place):
        return pl.pallas_call(
            functools.partial(gather_kernel, part * steps),
            grid=(steps,),
            in_specs=[SMEM] + [vmem] * 6,
            out_specs=vmem,
            out_shape=jax.ShapeDtypeStruct((steps * doms, 1, atoms_local), F32),
            scratch_shapes=[
                pltpu.VMEM((rows, LANES), F32),
                pltpu.VMEM((steps * XD + 3, LANES, 4 * LANES), BF16),
                pltpu.VMEM((4 * LANES, atoms_slab), BF16),
            ],
            compiler_params=params(12 + (table_bytes + 8 * near_planes * LANES * LANES) // MIB),
            cost_estimate=SMALL,
            name="gather",
        )(place, same, other, table_y, table_z, *near)

    earlier, *lines = lax.optimization_barrier((gather(0, place), *lines))

    high_y, low_y = inverse_y_table(slab_half, ky_local)
    high_z, low_z = inverse_z_table(doms)

    turned = pl.pallas_call(
        functools.partial(inverse_y_kernel, slab_half),
        in_specs=[SMEM] + [vmem] * (2 * slab_half + 2),
        out_specs=[vmem] * doms,
        out_shape=[jax.ShapeDtypeStruct((XD, rows_local, LANES), F32)] * doms,
        scratch_shapes=[
            pltpu.VMEM((slab_half, XD, 2 * ky_local, LANES), F32),
            pltpu.VMEM((doms, XD, rows_local, LANES), F32),
        ],
        compiler_params=params(32),
        cost_estimate=SMALL,
        name="inverse_y",
    )(place, *lines, high_y, low_y)
    columns = [swapped(value, "dom", k) for k, value in enumerate(turned)]

    columns[1], late_place = lax.optimization_barrier((columns[1], place))
    partial = jnp.concatenate([earlier] + [gather(part, late_place) for part in range(1, GATHERS)], 0)
    members = slab_half * doms
    sampled = lax.all_to_all(
        partial.reshape(members, atoms_local),
        ("slab", "dom"),
        0,
        0,
        axis_index_groups=[list(range(members)), list(range(members, 2 * members))],
        tiled=True,
    )
    alive = jnp.arange(atoms_local, dtype=jnp.int32) < counts[0]
    gradient = jnp.where(alive, bias_coupling * jnp.sum(sampled, 0), 0.0)
    gradient, *columns = lax.optimization_barrier((gradient, *columns))

    potential = pl.pallas_call(
        functools.partial(inverse_z_kernel, doms),
        grid=(XD // DEPTH,),
        in_specs=[SMEM] + [vmem] * (doms + 2),
        out_specs=pl.BlockSpec((DEPTH, rows_local, NZ), lambda step: (step, 0, 0)),
        out_shape=jax.ShapeDtypeStruct((XD, rows_local, NZ), F32),
        scratch_shapes=[pltpu.VMEM((doms, DEPTH, rows_local, LANES), F32)],
        compiler_params=params(24),
        cost_estimate=SMALL,
        name="inverse_z",
    )(place, *columns, high_z, low_z)
    return (potential, gradient)


def solution(mesh):
    placed = (
        P(None, ("slab", "dom")),
        P(None, ("slab", "dom")),
        P(("slab", "dom")),
        P(("slab", "dom")),
        P(("slab", "dom")),
        P(None, "slab", "dom"),
    )
    return jax.shard_map(
        per_device,
        mesh=mesh,
        in_specs=placed,
        out_specs=(P("slab", "dom", None), P(("slab", "dom"))),
        check_vma=False,
    )
```

```python
import functools

import jax
import jax.numpy as jnp
import ml_dtypes
import numpy as np
from jax import lax
from jax.experimental import pallas as pl
from jax.experimental.pallas import tpu as pltpu
from jax.sharding import PartitionSpec as P

XD = 4
NY = 512
NZ = 512
KH = NZ // 2
LANES = 128
SPAN = XD + 3
DEPTH = 2
GATHERS = 2
MIB = 1 << 20
BF16 = jnp.bfloat16
F32 = jnp.float32


def polynomial(function, terms):
    nodes = 0.125 * (1.0 - np.cos(np.pi * (np.arange(64) + 0.5) / 64))
    powers = nodes[:, None] ** np.arange(terms)[None, :]
    return [float(v) for v in np.linalg.lstsq(powers, function(np.sqrt(nodes)), rcond=None)[0]]


SINE_TERMS = polynomial(lambda r: np.sin(np.pi * r) / r, 6)
COSINE_TERMS = polynomial(lambda r: np.cos(np.pi * r), 6)


def horner(terms, square):
    total = jnp.full_like(square, terms[-1])
    for term in terms[-2::-1]:
        total = total * square + term
    return total


def turn(fraction):
    left = fraction - jnp.floor(fraction + 0.5)
    square = left * left
    sine = left * horner(SINE_TERMS, square)
    cosine = horner(COSINE_TERMS, square)
    return 1.0 - 2.0 * sine * sine, 2.0 * sine * cosine


def spline(frac):
    inner = 1.0 - frac
    square = frac * frac
    cube = square * frac
    sixth = 1.0 / 6.0
    return (
        inner * inner * inner * sixth,
        (3.0 * cube - 6.0 * square + 4.0) * sixth,
        (-3.0 * cube + 3.0 * square + 3.0 * frac + 1.0) * sixth,
        cube * sixth,
    )


def split(value):
    high = value.astype(BF16)
    return high, (value - high.astype(F32)).astype(BF16)


def iota(shape, axis):
    return lax.broadcasted_iota(jnp.int32, shape, axis).astype(F32)


RADIX = 16
DIGITS = 32
TERMS = 256


def wave_factors(first, rows, length):
    lane = lax.broadcasted_iota(jnp.int32, (rows, TERMS), 1)
    section = lane // DIGITS
    digit = (lane % DIGITS).astype(F32) * jnp.where(section < 2, float(RADIX), 1.0)
    parts = []
    for value in turn((first + iota((rows, TERMS), 0)) * digit * (1.0 / length)):
        high = value.astype(BF16).astype(F32)
        parts.append(jnp.where((section == 1) | (section == 3), value - high, high))
    upper, lower = section < 2, (section >= 2) & (section < 5)
    masked = [jnp.where(mask, part, 0.0) for mask in (upper, lower) for part in parts]
    return jnp.concatenate(masked, 0).astype(BF16)


def wave_kernel(place_ref, out_y_ref, out_z_ref):
    out_y_ref[...] = wave_factors(place_ref[0].astype(F32), out_y_ref.shape[0] // 4, NY)
    out_z_ref[...] = wave_factors(place_ref[1].astype(F32), out_z_ref.shape[0] // 4, NZ)


def atom_waves(base, weights, factors_ref, digits_ref):
    width = base.shape[1]
    high_digit = jnp.floor(base * (1.0 / RADIX))
    row = iota((DIGITS, width), 0)
    chosen = jnp.where(row == high_digit, 1.0, 0.0).astype(BF16)
    step = row - (base - RADIX * high_digit)
    spread = jnp.where(step == 3.0, weights[3], 0.0)
    for r in (2, 1, 0):
        spread = jnp.where(step == float(r), weights[r], spread)
    high, low = split(spread)
    for section, value in enumerate((chosen, chosen, high, high, low)):
        digits_ref[pl.ds(DIGITS * section, DIGITS), :] = value
    product = jnp.dot(factors_ref[...], digits_ref[...], preferred_element_type=F32)
    rows = product.shape[0] // 4
    cos_a, sin_a, cos_b, sin_b = (product[i * rows : (i + 1) * rows] for i in range(4))
    return cos_a * cos_b - sin_a * sin_b, sin_a * cos_b + cos_a * sin_b


def plane_weights(atoms, weights):
    row = iota((8, atoms.shape[1]), 0) - atoms[0:1]
    return sum(weights[r][3:4] * (row == float(r)).astype(F32) for r in range(4))


def swap(value):
    return pltpu.roll(value, LANES // 2, axis=value.ndim - 1)


def half_sign():
    lane = lax.broadcasted_iota(jnp.int32, (1, LANES), 1)
    return jnp.where(lane < LANES // 2, -1.0, 1.0).astype(F32)


def rotate(value, numer, denom, sign):
    real, imag = value
    if numer == 0:
        return value
    if 4 * numer == denom:
        return (-imag, real) if sign > 0 else (imag, -real)
    angle = 2.0 * np.pi * numer / denom
    cosine, sine = float(np.cos(angle)), float(sign * np.sin(angle))
    if 8 * numer in (denom, 3 * denom):
        size = abs(cosine)
        cos_sign, sin_sign = (1 if cosine > 0 else -1), (1 if sine > 0 else -1)
        if cos_sign == sin_sign:
            return ((real - imag) * (cos_sign * size), (real + imag) * (cos_sign * size))
        return ((real + imag) * (cos_sign * size), (imag - real) * (cos_sign * size))
    return real * cosine - imag * sine, imag * cosine + real * sine


def butterfly(even, turned):
    plus = (even[0] + turned[0], even[1] + turned[1])
    return plus, (even[0] - turned[0], even[1] - turned[1])


def transform(values, sign):
    count = len(values)
    if count == 1:
        return values
    even = transform(values[0::2], sign)
    odd = transform(values[1::2], sign)
    both = [butterfly(even[k], rotate(odd[k], k, count, sign)) for k in range(count // 2)]
    return [pair[0] for pair in both] + [pair[1] for pair in both]


def regroup(low, high):
    first = lax.broadcasted_iota(jnp.int32, low.shape, 1) < LANES // 2
    crossed = swap(jnp.where(first, high, low))
    return jnp.where(first, low, crossed), jnp.where(first, crossed, high)


def pack_kernel(counts_ref, cells_ref, offsets_ref, charges_ref, out_ref):
    width = offsets_ref.shape[1]
    alive = lax.broadcasted_iota(jnp.int32, (1, width), 1) < counts_ref[0]
    atoms = jnp.concatenate(
        [
            lax.bitwise_and(cells_ref[0:1, :], XD - 1).astype(F32),
            cells_ref[1:3, :].astype(F32),
            offsets_ref[...],
            jnp.where(alive, charges_ref[...], 0.0),
            jnp.full((1, width), counts_ref[0].astype(F32)),
        ],
        0,
    )
    for copy in range(out_ref.shape[0]):
        out_ref[copy] = atoms


def atoms_of(same_ref, other_ref, slab, slot, doms):
    half = doms // 2
    return (same_ref, other_ref)[slot // half][slab * half + slot % half]


def forward_kernel(
    place_ref,
    live_ref,
    same_ref,
    other_ref,
    factors_y,
    factors_z,
    plus_ref,
    minus_ref,
    table_y,
    table_z,
    left_ref,
    right_ref,
    grid_ref,
    atoms_ref,
    digits_y,
    digits_z,
):
    step = pl.program_id(0)
    cells_x = grid_ref.shape[0]
    rows = grid_ref.shape[1] // 2
    ky_local = rows - 8
    half_slot = same_ref.shape[2] // 2
    doms = table_y.shape[2] // (2 * half_slot)
    kept = step - place_ref[2]
    kept = jnp.where((kept >= 0) & (kept < table_y.shape[0] - 1), kept, table_y.shape[0] - 1)

    @pl.when(step == 0)
    def _():
        grid_ref[...] = jnp.zeros_like(grid_ref)
        digits_y[...] = jnp.zeros_like(digits_y)
        digits_z[...] = jnp.zeros_like(digits_z)

    for slot in range(doms):
        atoms_ref[slot] = atoms_of(same_ref, other_ref, step, slot, doms)

    def add_tile(tile, halves):
        atoms = jnp.concatenate([atoms_ref[slot, :, pl.ds(part * half_slot, half_slot)] for slot, part, _ in halves], 1)
        counted = jnp.concatenate([jnp.full((1, half_slot), weight) for _, _, weight in halves], 1)
        weights = spline(atoms)
        along_x = plane_weights(atoms, weights) * (atoms[6:7] * counted)
        waves_z = atom_waves(atoms[2:3], [w[5:6] for w in weights], factors_z, digits_z.at[tile])
        waves_z = jnp.concatenate(waves_z, 0)
        waves_y = atom_waves(atoms[1:2], [w[4:5] for w in weights], factors_y, digits_y.at[tile])
        waves_y = jnp.concatenate(waves_y, 0)
        for number, (slot, part, _) in enumerate(halves):
            lanes = slice(number * half_slot, (number + 1) * half_slot)
            start = pl.multiple_of((2 * slot + part) * half_slot, half_slot)
            table_z[kept, :, pl.ds(start, half_slot)] = waves_z[:, lanes]
            table_y[kept, :, pl.ds(start, half_slot)] = waves_y[:, lanes]
        high, low = split(waves_z)
        right_ref[tile, pl.ds(0, LANES), :] = high
        right_ref[tile, pl.ds(LANES, LANES), :] = low
        for plane in range(SPAN):
            first = 4 * rows * plane
            high, low = split(waves_y * along_x[plane : plane + 1])
            left_ref[tile, pl.ds(first, 2 * rows), :] = high
            left_ref[tile, pl.ds(first + 2 * rows, 2 * rows), :] = low
        product = lax.dot_general(
            left_ref[tile], right_ref[tile], (((1,), (1,)), ((), ())), preferred_element_type=F32
        )
        for plane in range(SPAN):
            first = 4 * rows * plane
            high, low = product[first : first + 2 * rows], product[first + 2 * rows : first + 4 * rows]
            at = lax.rem(step * XD + plane, cells_x)
            grid_ref[at] += (high[:, :LANES] + high[:, LANES:]) + (low[:, :LANES] + low[:, LANES:])

    reach = [live_ref[step * doms + slot] for slot in range(doms)]
    reach = [sum(reach[: slot + 1]) for slot in range(doms)]
    for extra in range(doms // 2 + 1):

        @pl.when((reach[-1] + 1) // 2 == extra)
        def _(extra=extra):
            for tile in range(doms // 2):
                add_tile(tile, [(2 * tile, 0, 1.0), (2 * tile + 1, 0, 1.0)])
            for tile in range(extra):
                chosen = []
                for place in (2 * tile, 2 * tile + 1):
                    slot = sum((total <= place).astype(jnp.int32) for total in reach)
                    weight = jnp.where(slot < doms, 1.0, 0.0).astype(F32)
                    chosen.append((jnp.minimum(slot, doms - 1), 1, weight))
                add_tile(doms // 2 + tile, chosen)

    @pl.when(step == pl.num_programs(0) - 1)
    def _():
        quarter_rows = ky_local // 2
        group = min(8, quarter_rows)
        for minus, out_ref in enumerate((plus_ref, minus_ref)):
            for start in range(0, quarter_rows, group):
                values = []
                for x in range(cells_x):
                    parts = [
                        grid_ref[x, pl.ds(minus + start + offset, group), :]
                        for offset in (0, quarter_rows, rows, rows + quarter_rows)
                    ]
                    cos_cos, cos_sin = regroup(parts[0], parts[1])
                    sin_cos, sin_sin = regroup(parts[2], parts[3])
                    if minus:
                        values.append((cos_cos + sin_sin, sin_cos - cos_sin))
                    else:
                        values.append((cos_cos - sin_sin, -cos_sin - sin_cos))
                for x, value in enumerate(transform(values, -1)):
                    for part in (0, 1):
                        out_ref[part, x, pl.ds(start, group), :] = value[part]


def inverse_x_kernel(place_ref, spectrum_ref, green_ref, *refs):
    *outs, near_ref = refs
    cells_x, quarter_rows = spectrum_ref.shape[1:3]
    group = min(8, quarter_rows)
    side = 1.0 - 2.0 * place_ref[3].astype(F32)

    def rows_of(step, carry):
        rows = pl.ds(pl.multiple_of(step * group, group), group)
        values = []
        for kx in range(cells_x):
            green = green_ref[kx, rows, :]
            values.append(tuple(spectrum_ref[part, kx, rows, :] * green for part in (0, 1)))
        even = transform(values[0::2], 1)
        odd = transform([(value[0] * side, value[1] * side) for value in values[1::2]], 1)
        for x in range(cells_x // 2):
            here, there = butterfly(even[x], rotate(odd[x], x, cells_x, 1))
            wanted = [(x, here)] + ([(cells_x // 2 + x, there)] if x < 3 else [])
            for plane, value in wanted:
                for part, row_group in enumerate(regroup(value[0], value[1])):
                    near_ref[plane, part, rows, :] = row_group
        return carry

    lax.fori_loop(0, quarter_rows // group, rows_of, 0)
    for k, out_ref in enumerate(outs):
        out_ref[...] = near_ref[pl.ds(lax.bitwise_xor(place_ref[4], k) * XD, XD)]


def inverse_y_kernel(sources, place_ref, *refs):
    ins, (high_ref, low_ref) = refs[: 2 * sources], refs[2 * sources : 2 * sources + 2]
    outs, (plus_ref, minus_ref, turned_ref) = refs[2 * sources + 2 : -3], refs[-3:]
    waves = NY // 2
    halves = half_sign()
    minus_ref[:, pl.ds(0, 8), :] = jnp.zeros((XD, 8, LANES), F32)
    for number, in_ref in enumerate(ins):
        count = in_ref.shape[1]
        start = lax.bitwise_xor(place_ref[4], number % sources) * count
        if number < sources:
            plus_ref[:, pl.ds(pl.multiple_of(start, 8), count), :] = in_ref[...]
        else:
            minus_ref[:, pl.ds(pl.multiple_of(start + 8, 8), count), :] = in_ref[...]
    sums = []
    for parity in (0, 1):
        parts = []
        for x in range(XD):
            plus = plus_ref[x, pl.ds(parity, waves // 2, stride=2), :]
            minus = minus_ref[x, pl.ds(7 + parity, waves // 2, stride=2), :]
            parts.append(split(jnp.concatenate([plus + minus, swap(plus - minus) * halves], 0)))
        both = jnp.concatenate([value for part in parts for value in part], 1)
        main = jnp.dot(high_ref[parity], both, preferred_element_type=F32)
        high = jnp.concatenate([part[0] for part in parts], 1)
        rest = jnp.dot(low_ref[parity], high, preferred_element_type=F32)
        sums.append(
            [
                main[:, 2 * x * LANES : (2 * x + 1) * LANES]
                + main[:, (2 * x + 1) * LANES : (2 * x + 2) * LANES]
                + rest[:, x * LANES : (x + 1) * LANES]
                for x in range(XD)
            ]
        )
    row = lax.broadcasted_iota(jnp.int32, (waves, 1), 0)
    alternate = jnp.where(row % 2 == 0, 1.0, -1.0)
    sign = jnp.where(place_ref[3] == 1, alternate, 1.0)
    for x in range(XD):
        last = minus_ref[x, pl.ds(waves, 8), :][7:8]
        even, odd = sums[0][x] + alternate * last, sums[1][x]
        total = jnp.concatenate([(even + odd) * sign, (even - odd) * sign], 0)
        turned_ref[:, x] = total.reshape(len(outs), -1, LANES)
    for k in range(len(outs)):
        outs[k][...] = turned_ref[lax.bitwise_xor(place_ref[5], k)]


def inverse_z_kernel(sources, place_ref, *refs):
    ins, (high_ref, low_ref) = refs[:sources], refs[sources : sources + 2]
    out_ref, lines_ref = refs[-2:]
    first = pl.program_id(0) * DEPTH
    for k in range(sources):
        lines_ref[lax.bitwise_xor(place_ref[5], k)] = ins[k][pl.ds(first, DEPTH)]
    rows = DEPTH * lines_ref.shape[2]
    lines = jnp.concatenate([lines_ref[source].reshape(rows, LANES) for source in range(sources)], 1)
    high, low = split(lines)
    total = jnp.dot(high, high_ref[...], preferred_element_type=F32)
    total += jnp.dot(low, high_ref[...], preferred_element_type=F32)
    total += jnp.dot(high, low_ref[...], preferred_element_type=F32)
    out_ref[...] = total.reshape(out_ref.shape)


def gather_kernel(
    first, place_ref, same_ref, other_ref, table_y, table_z, plus_ref, minus_ref, out_ref, shift_ref, fields_ref, stack_ref
):
    step = pl.program_id(0)
    half = LANES // 2
    rows = table_y.shape[1] // 2
    ky_local = rows - 8
    width = same_ref.shape[2]
    doms = table_y.shape[2] // width
    planes = fields_ref.shape[0]
    halves = half_sign()

    @pl.when(step == 0)
    def _():
        stack_ref[...] = jnp.zeros_like(stack_ref)
        shift_ref[...] = jnp.zeros_like(shift_ref)
        row = lax.broadcasted_iota(jnp.int32, (8, LANES), 0)

        def build(x, carry):
            plus = plus_ref[first * XD + x]
            shift_ref[pl.ds(1, ky_local), :] = minus_ref[first * XD + x]
            minus = shift_ref[pl.ds(0, ky_local), :]
            last = shift_ref[pl.ds(ky_local, 8), :][0:1]
            main = [plus + minus, swap(plus - minus) * halves]
            if 2 * ky_local < LANES:
                main.append(jnp.zeros((LANES - 2 * ky_local, LANES), F32))
            rest = jnp.where(row % 2 == 0, last, -swap(jnp.broadcast_to(last, (8, LANES))) * halves)
            rest = jnp.where(row < 6, rest, 0.0)
            rest_high = rest.astype(BF16).astype(F32)
            rest = jnp.where((row == 2) | (row == 3), rest - rest_high, rest_high)
            high, low = split(jnp.concatenate(main, 0).T)
            fields_ref[x, :, pl.ds(0, LANES)] = high
            fields_ref[x, :, pl.ds(LANES, LANES)] = low
            fields_ref[x, :, pl.ds(2 * LANES, LANES)] = high
            rest = jnp.concatenate([rest, jnp.zeros((LANES - 8, LANES), F32)], 0)
            fields_ref[x, :, pl.ds(3 * LANES, LANES)] = rest.T.astype(BF16)
            return carry

        lax.fori_loop(0, planes, build, 0)

    first_z = place_ref[1].astype(F32)
    twice = jnp.where(first_z + iota((half, 1), 0) == 0.0, 1.0, 2.0)
    fields = fields_ref[pl.ds(step * XD, SPAN)].reshape(SPAN * LANES, 4 * LANES)
    for slot in range(doms):
        lanes = pl.ds(slot * width, width)
        cosine = table_y[first + step, pl.ds(0, ky_local), lanes]
        sine = table_y[first + step, pl.ds(rows, ky_local), lanes]
        high, low = split(jnp.concatenate([cosine, sine], 0))
        for part, value in enumerate((high, high, low)):
            stack_ref[pl.ds(LANES * part, 2 * ky_local), lanes] = value
        cosine = table_y[first + step, pl.ds(ky_local, 8), lanes][0:1]
        sine = table_y[first + step, pl.ds(rows + ky_local, 8), lanes][0:1]
        row = lax.broadcasted_iota(jnp.int32, (16, width), 0)
        rest = jnp.where(row % 2 == 0, cosine, sine)
        rest_high = rest.astype(BF16).astype(F32)
        rest = jnp.where(row < 4, rest_high, jnp.where(row < 6, rest - rest_high, 0.0))
        stack_ref[pl.ds(3 * LANES, 16), lanes] = rest.astype(BF16)
    product = sum(
        jnp.dot(fields[:, part : part + 2 * LANES], stack_ref[pl.ds(part, 2 * LANES), :], preferred_element_type=F32)
        for part in (0, 2 * LANES)
    )
    for slot in range(doms):
        atoms = atoms_of(same_ref, other_ref, place_ref[2] + first + step, slot, doms)
        along_x = plane_weights(atoms, spline(atoms))
        lanes = pl.ds(slot * width, width)
        field = product[:, slot * width : (slot + 1) * width]
        total = along_x[0:1] * field[:LANES]
        for plane in range(1, SPAN):
            total += along_x[plane : plane + 1] * field[plane * LANES : (plane + 1) * LANES]
        waves = total * table_z[first + step, :, lanes]
        sampled = jnp.sum((waves[:half] - waves[half:]) * twice, axis=0, keepdims=True)
        core = place_ref[5] % 2 if slot < doms // 2 else 1 - place_ref[5] % 2
        out_ref[step * doms + 2 * (slot % (doms // 2)) + core] = sampled


def bf16_pair(table):
    high = table.astype(ml_dtypes.bfloat16)
    low = (table - high.astype(np.float64)).astype(ml_dtypes.bfloat16)
    return jnp.asarray(high), jnp.asarray(low)


def inverse_y_table():
    tables = []
    for parity in (0, 1):
        waves = np.arange(parity, NY // 2, 2)
        angle = 2.0 * np.pi * (np.outer(np.arange(NY // 2), waves) % NY) / NY
        tables.append(np.concatenate([np.cos(angle), np.sin(angle)], 1))
    return bf16_pair(np.stack(tables))


def inverse_z_table(dom_count):
    kz = np.arange(KH)
    angle = 2.0 * np.pi * (np.outer(kz, np.arange(NZ)) % NZ) / NZ
    weight = np.where(kz == 0, 1.0, 2.0)[:, None]
    parts = [weight * np.cos(angle), -weight * np.sin(angle)]
    return bf16_pair(
        np.stack([p.reshape(dom_count, KH // dom_count, NZ) for p in parts], 1).reshape(2 * KH, NZ)
    )


def whole_spec(shape):
    return pl.BlockSpec(shape, lambda *_: (0,) * len(shape))


SMALL = pl.CostEstimate(flops=10**6, bytes_accessed=10**4, transcendentals=0)
SMEM = pl.BlockSpec(memory_space=pltpu.SMEM)


def params(mib):
    return pltpu.CompilerParams(vmem_limit_bytes=mib * MIB)


def swapped(value, axis, distance):
    if distance == 0:
        return value
    return lax.ppermute(value, axis, [(i, i ^ distance) for i in range(lax.axis_size(axis))])


def per_device(base_cells, offsets, charges, bias_coupling, counts, green):
    slabs = lax.axis_size("slab")
    doms = lax.axis_size("dom")
    slab = lax.axis_index("slab")
    dom = lax.axis_index("dom")
    atoms_local = charges.shape[0]
    cells_x = XD * slabs
    ky_local = NY // slabs
    kz_local = KH // doms
    slab_half = slabs // 2
    rows_local = NY // doms
    rows = ky_local + 8
    quarter_rows = ky_local // 2
    normalize = 1.0 / (cells_x * NY * NZ)
    upper = slab // slab_half
    place = jnp.stack(
        [slab * ky_local, dom * kz_local, upper * slab_half, upper, slab % slab_half, dom]
    ).astype(jnp.int32)

    vmem = pl.BlockSpec(memory_space=pltpu.VMEM)
    atoms = pl.pallas_call(
        pack_kernel,
        in_specs=[SMEM, vmem, vmem, vmem],
        out_specs=vmem,
        out_shape=jax.ShapeDtypeStruct((slabs * doms // 2, 8, atoms_local), F32),
        name="pack",
    )(counts, base_cells, offsets, charges.reshape(1, atoms_local))
    factors_y, factors_z = pl.pallas_call(
        wave_kernel,
        in_specs=[SMEM],
        out_specs=[vmem] * 2,
        out_shape=[jax.ShapeDtypeStruct((4 * count, TERMS), BF16) for count in (rows, LANES // 2)],
        compiler_params=params(8),
        name="waves",
    )(place)
    everyone = list(range(slabs * doms))
    same = lax.all_to_all(
        atoms, ("slab", "dom"), 0, 0, axis_index_groups=[everyone[0::2], everyone[1::2]], tiled=True
    )

    def halves_beside(value):
        return jnp.concatenate([value[:, :quarter_rows], value[:, quarter_rows:]], 2) * normalize

    own = halves_beside(green)
    same, flipped, factors_y, factors_z = lax.optimization_barrier(
        (same, halves_beside(green[:, ::-1]), factors_y, factors_z)
    )
    other = swapped(same, "dom", 1)
    mirrored = lax.ppermute(flipped, "slab", [(s, slabs - 1 - s) for s in range(slabs)])

    reaches = [value[:, 7, 0].reshape(slabs, doms // 2) for value in (same, other)]
    live = (jnp.concatenate(reaches, 1).reshape(-1) > atoms_local // 2).astype(jnp.int32)
    atoms_slab = doms * atoms_local
    table_bytes = 4 * (slab_half + 1) * (2 * rows + LANES) * atoms_slab
    spectrum_bytes = 16 * cells_x * max(8, quarter_rows) * LANES
    plus, minus, table_y, table_z = pl.pallas_call(
        forward_kernel,
        grid=(slabs,),
        in_specs=[SMEM] * 2 + [vmem] * 4,
        out_specs=[vmem] * 4,
        out_shape=[
            jax.ShapeDtypeStruct((2, cells_x, quarter_rows, LANES), F32),
            jax.ShapeDtypeStruct((2, cells_x, quarter_rows, LANES), F32),
            jax.ShapeDtypeStruct((slab_half + 1, 2 * rows, atoms_slab), F32),
            jax.ShapeDtypeStruct((slab_half + 1, LANES, atoms_slab), F32),
        ],
        scratch_shapes=[
            pltpu.VMEM((doms, SPAN * 4 * rows, atoms_local), BF16),
            pltpu.VMEM((doms, 2 * LANES, atoms_local), BF16),
            pltpu.VMEM((cells_x, 2 * rows, LANES), F32),
            pltpu.VMEM((doms, 8, atoms_local), F32),
            pltpu.VMEM((doms, TERMS, atoms_local), BF16),
            pltpu.VMEM((doms, TERMS, atoms_local), BF16),
        ],
        compiler_params=params(16 + (table_bytes + spectrum_bytes) // MIB),
        cost_estimate=SMALL,
        name="forward",
    )(place, live, same, other, factors_y, factors_z)

    near_planes = cells_x // 2 + 3
    lines, near = [], []
    for spectrum, influence in ((plus, own), (minus, mirrored)):
        *pieces, planes = pl.pallas_call(
            inverse_x_kernel,
            in_specs=[SMEM] + [vmem] * 2,
            out_specs=[vmem] * (slab_half + 1),
            out_shape=[jax.ShapeDtypeStruct((XD, 2, quarter_rows, LANES), F32)] * slab_half
            + [jax.ShapeDtypeStruct((near_planes, 2, quarter_rows, LANES), F32)],
            compiler_params=params(24),
            cost_estimate=SMALL,
            name="inverse_x",
        )(place, spectrum, influence)
        near.append(planes.reshape(near_planes, ky_local, LANES))
        lines += [swapped(value.reshape(XD, ky_local, LANES), "slab", k) for k, value in enumerate(pieces)]

    steps = slab_half // GATHERS

    def gather(part, place):
        return pl.pallas_call(
            functools.partial(gather_kernel, part * steps),
            grid=(steps,),
            in_specs=[SMEM] + [vmem] * 6,
            out_specs=vmem,
            out_shape=jax.ShapeDtypeStruct((steps * doms, 1, atoms_local), F32),
            scratch_shapes=[
                pltpu.VMEM((rows, LANES), F32),
                pltpu.VMEM((steps * XD + 3, LANES, 4 * LANES), BF16),
                pltpu.VMEM((4 * LANES, atoms_slab), BF16),
            ],
            compiler_params=params(12 + (table_bytes + 8 * near_planes * LANES * LANES) // MIB),
            cost_estimate=SMALL,
            name="gather",
        )(place, same, other, table_y, table_z, *near)

    earlier, *lines = lax.optimization_barrier((gather(0, place), *lines))

    high_y, low_y = inverse_y_table()
    high_z, low_z = inverse_z_table(doms)

    turned = pl.pallas_call(
        functools.partial(inverse_y_kernel, slab_half),
        in_specs=[SMEM] + [vmem] * (2 * slab_half + 2),
        out_specs=[vmem] * doms,
        out_shape=[jax.ShapeDtypeStruct((XD, rows_local, LANES), F32)] * doms,
        scratch_shapes=[
            pltpu.VMEM((XD, NY // 2, LANES), F32),
            pltpu.VMEM((XD, NY // 2 + 8, LANES), F32),
            pltpu.VMEM((doms, XD, rows_local, LANES), F32),
        ],
        compiler_params=params(32),
        cost_estimate=SMALL,
        name="inverse_y",
    )(place, *lines, high_y, low_y)
    columns = [swapped(value, "dom", k) for k, value in enumerate(turned)]

    columns[1], late_place = lax.optimization_barrier((columns[1], place))
    partial = jnp.concatenate([earlier] + [gather(part, late_place) for part in range(1, GATHERS)], 0)
    members = slab_half * doms
    sampled = lax.all_to_all(
        partial.reshape(members, atoms_local),
        ("slab", "dom"),
        0,
        0,
        axis_index_groups=[list(range(members)), list(range(members, 2 * members))],
        tiled=True,
    )
    alive = jnp.arange(atoms_local, dtype=jnp.int32) < counts[0]
    gradient = jnp.where(alive, bias_coupling * jnp.sum(sampled, 0), 0.0)

    potential = pl.pallas_call(
        functools.partial(inverse_z_kernel, doms),
        grid=(XD // DEPTH,),
        in_specs=[SMEM] + [vmem] * (doms + 2),
        out_specs=pl.BlockSpec((DEPTH, rows_local, NZ), lambda step: (step, 0, 0)),
        out_shape=jax.ShapeDtypeStruct((XD, rows_local, NZ), F32),
        scratch_shapes=[pltpu.VMEM((doms, DEPTH, rows_local, LANES), F32)],
        compiler_params=params(24),
        cost_estimate=SMALL,
        name="inverse_z",
    )(place, *columns, high_z, low_z)
    return (potential, gradient)


def solution(mesh):
    placed = (
        P(None, ("slab", "dom")),
        P(None, ("slab", "dom")),
        P(("slab", "dom")),
        P(("slab", "dom")),
        P(("slab", "dom")),
        P(None, "slab", "dom"),
    )
    return jax.shard_map(
        per_device,
        mesh=mesh,
        in_specs=placed,
        out_specs=(P("slab", "dom", None), P(("slab", "dom"))),
        check_vma=False,
    )
```

```python
import functools

import jax
import jax.numpy as jnp
import ml_dtypes
import numpy as np
from jax import lax
from jax.experimental import pallas as pl
from jax.experimental.pallas import tpu as pltpu
from jax.sharding import PartitionSpec as P

XD = 4
NY = 512
NZ = 512
KH = NZ // 2
LANES = 128
SPAN = XD + 3
DEPTH = 2
GATHERS = 2
MIB = 1 << 20
BF16 = jnp.bfloat16
F32 = jnp.float32


def polynomial(function, terms):
    nodes = 0.125 * (1.0 - np.cos(np.pi * (np.arange(64) + 0.5) / 64))
    powers = nodes[:, None] ** np.arange(terms)[None, :]
    return [float(v) for v in np.linalg.lstsq(powers, function(np.sqrt(nodes)), rcond=None)[0]]


SINE_TERMS = polynomial(lambda r: np.sin(np.pi * r) / r, 6)
COSINE_TERMS = polynomial(lambda r: np.cos(np.pi * r), 6)


def horner(terms, square):
    total = jnp.full_like(square, terms[-1])
    for term in terms[-2::-1]:
        total = total * square + term
    return total


def turn(fraction):
    left = fraction - jnp.floor(fraction + 0.5)
    square = left * left
    sine = left * horner(SINE_TERMS, square)
    cosine = horner(COSINE_TERMS, square)
    return 1.0 - 2.0 * sine * sine, 2.0 * sine * cosine


def spline(frac):
    inner = 1.0 - frac
    square = frac * frac
    cube = square * frac
    sixth = 1.0 / 6.0
    return (
        inner * inner * inner * sixth,
        (3.0 * cube - 6.0 * square + 4.0) * sixth,
        (-3.0 * cube + 3.0 * square + 3.0 * frac + 1.0) * sixth,
        cube * sixth,
    )


def split(value):
    high = value.astype(BF16)
    return high, (value - high.astype(F32)).astype(BF16)


def iota(shape, axis):
    return lax.broadcasted_iota(jnp.int32, shape, axis).astype(F32)


RADIX = 16
DIGITS = 32
TERMS = 256


def wave_factors(first, rows, length):
    lane = lax.broadcasted_iota(jnp.int32, (rows, TERMS), 1)
    section = lane // DIGITS
    digit = (lane % DIGITS).astype(F32) * jnp.where(section < 2, float(RADIX), 1.0)
    parts = []
    for value in turn((first + iota((rows, TERMS), 0)) * digit * (1.0 / length)):
        high = value.astype(BF16).astype(F32)
        parts.append(jnp.where((section == 1) | (section == 3), value - high, high))
    upper, lower = section < 2, (section >= 2) & (section < 5)
    masked = [jnp.where(mask, part, 0.0) for mask in (upper, lower) for part in parts]
    return jnp.concatenate(masked, 0).astype(BF16)


def wave_kernel(place_ref, out_y_ref, out_z_ref):
    out_y_ref[...] = wave_factors(place_ref[0].astype(F32), out_y_ref.shape[0] // 4, NY)
    out_z_ref[...] = wave_factors(place_ref[1].astype(F32), out_z_ref.shape[0] // 4, NZ)


def atom_waves(base, weights, factors_ref, digits_ref):
    width = base.shape[1]
    high_digit = jnp.floor(base * (1.0 / RADIX))
    row = iota((DIGITS, width), 0)
    chosen = jnp.where(row == high_digit, 1.0, 0.0).astype(BF16)
    step = row - (base - RADIX * high_digit)
    spread = jnp.where(step == 3.0, weights[3], 0.0)
    for r in (2, 1, 0):
        spread = jnp.where(step == float(r), weights[r], spread)
    high, low = split(spread)
    for section, value in enumerate((chosen, chosen, high, high, low)):
        digits_ref[pl.ds(DIGITS * section, DIGITS), :] = value
    product = jnp.dot(factors_ref[...], digits_ref[...], preferred_element_type=F32)
    rows = product.shape[0] // 4
    cos_a, sin_a, cos_b, sin_b = (product[i * rows : (i + 1) * rows] for i in range(4))
    return cos_a * cos_b - sin_a * sin_b, sin_a * cos_b + cos_a * sin_b


def plane_weights(atoms, weights):
    row = iota((8, atoms.shape[1]), 0) - atoms[0:1]
    return sum(weights[r][3:4] * (row == float(r)).astype(F32) for r in range(4))


def swap(value):
    return pltpu.roll(value, LANES // 2, axis=value.ndim - 1)


def half_sign():
    lane = lax.broadcasted_iota(jnp.int32, (1, LANES), 1)
    return jnp.where(lane < LANES // 2, -1.0, 1.0).astype(F32)


def rotate(value, numer, denom, sign):
    real, imag = value
    if numer == 0:
        return value
    if 4 * numer == denom:
        return (-imag, real) if sign > 0 else (imag, -real)
    angle = 2.0 * np.pi * numer / denom
    cosine, sine = float(np.cos(angle)), float(sign * np.sin(angle))
    if 8 * numer in (denom, 3 * denom):
        size = abs(cosine)
        cos_sign, sin_sign = (1 if cosine > 0 else -1), (1 if sine > 0 else -1)
        if cos_sign == sin_sign:
            return ((real - imag) * (cos_sign * size), (real + imag) * (cos_sign * size))
        return ((real + imag) * (cos_sign * size), (imag - real) * (cos_sign * size))
    return real * cosine - imag * sine, imag * cosine + real * sine


def butterfly(even, turned):
    plus = (even[0] + turned[0], even[1] + turned[1])
    return plus, (even[0] - turned[0], even[1] - turned[1])


def transform(values, sign):
    count = len(values)
    if count == 1:
        return values
    even = transform(values[0::2], sign)
    odd = transform(values[1::2], sign)
    both = [butterfly(even[k], rotate(odd[k], k, count, sign)) for k in range(count // 2)]
    return [pair[0] for pair in both] + [pair[1] for pair in both]


def regroup(low, high):
    first = lax.broadcasted_iota(jnp.int32, low.shape, 1) < LANES // 2
    crossed = swap(jnp.where(first, high, low))
    return jnp.where(first, low, crossed), jnp.where(first, crossed, high)


def pack_kernel(counts_ref, cells_ref, offsets_ref, charges_ref, out_ref):
    width = offsets_ref.shape[1]
    alive = lax.broadcasted_iota(jnp.int32, (1, width), 1) < counts_ref[0]
    atoms = jnp.concatenate(
        [
            lax.bitwise_and(cells_ref[0:1, :], XD - 1).astype(F32),
            cells_ref[1:3, :].astype(F32),
            offsets_ref[...],
            jnp.where(alive, charges_ref[...], 0.0),
            jnp.full((1, width), counts_ref[0].astype(F32)),
        ],
        0,
    )
    for copy in range(out_ref.shape[0]):
        out_ref[copy] = atoms


def atoms_of(same_ref, other_ref, slab, slot, doms):
    half = doms // 2
    return (same_ref, other_ref)[slot // half][slab * half + slot % half]


def forward_kernel(
    place_ref,
    live_ref,
    same_ref,
    other_ref,
    factors_y,
    factors_z,
    plus_ref,
    minus_ref,
    table_y,
    table_z,
    left_ref,
    right_ref,
    grid_ref,
    atoms_ref,
    digits_y,
    digits_z,
):
    step = pl.program_id(0)
    cells_x = grid_ref.shape[0]
    rows = grid_ref.shape[1] // 2
    ky_local = rows - 8
    half_slot = same_ref.shape[2] // 2
    doms = table_y.shape[2] // (2 * half_slot)
    slabs = cells_x // XD

    def kept(slab):
        at = slab - place_ref[2]
        return jnp.where((at >= 0) & (at < table_y.shape[0] - 1), at, table_y.shape[0] - 1)

    def build_tile(tile, slab, halves):
        lanes_of = [pl.ds(part * half_slot, half_slot) for _, part, _ in halves]
        atoms = [atoms_ref[slab * doms + slot, :, lanes] for (slot, _, _), lanes in zip(halves, lanes_of)]
        atoms = jnp.concatenate(atoms, 1)
        counted = jnp.concatenate([jnp.full((1, half_slot), weight) for _, _, weight in halves], 1)
        weights = spline(atoms)
        along_x = plane_weights(atoms, weights) * (atoms[6:7] * counted)
        waves_z = atom_waves(atoms[2:3], [w[5:6] for w in weights], factors_z, digits_z.at[tile])
        waves_z = jnp.concatenate(waves_z, 0)
        waves_y = atom_waves(atoms[1:2], [w[4:5] for w in weights], factors_y, digits_y.at[tile])
        waves_y = jnp.concatenate(waves_y, 0)
        for number, (slot, part, _) in enumerate(halves):
            lanes = slice(number * half_slot, (number + 1) * half_slot)
            start = pl.multiple_of((2 * slot + part) * half_slot, half_slot)
            table_z[kept(slab), :, pl.ds(start, half_slot)] = waves_z[:, lanes]
            table_y[kept(slab), :, pl.ds(start, half_slot)] = waves_y[:, lanes]
        high, low = split(waves_z)
        right_ref[tile, pl.ds(0, LANES), :] = high
        right_ref[tile, pl.ds(LANES, LANES), :] = low
        for plane in range(SPAN):
            first = 4 * rows * plane
            high, low = split(waves_y * along_x[plane : plane + 1])
            left_ref[tile, pl.ds(first, 2 * rows), :] = high
            left_ref[tile, pl.ds(first + 2 * rows, 2 * rows), :] = low

    def add_tile(tile):
        product = lax.dot_general(
            left_ref[tile], right_ref[tile], (((1,), (1,)), ((), ())), preferred_element_type=F32
        )
        for plane in range(SPAN):
            first = 4 * rows * plane
            high, low = product[first : first + 2 * rows], product[first + 2 * rows : first + 4 * rows]
            at = lax.rem(step * XD + plane, cells_x)
            grid_ref[at] += (high[:, :LANES] + high[:, LANES:]) + (low[:, :LANES] + low[:, LANES:])

    @pl.when(step == 0)
    def _():
        grid_ref[...] = jnp.zeros_like(grid_ref)
        digits_y[...] = jnp.zeros_like(digits_y)
        digits_z[...] = jnp.zeros_like(digits_z)
        for slab in range(slabs):
            for slot in range(doms):
                atoms_ref[slab * doms + slot] = atoms_of(same_ref, other_ref, slab, slot, doms)
        build_tile(0, 0, [(0, 0, 1.0), (1, 0, 1.0)])

    reach = [live_ref[step * doms + slot] for slot in range(doms)]
    reach = [sum(reach[: slot + 1]) for slot in range(doms)]
    for extra in range(doms // 2 + 1):

        @pl.when((reach[-1] + 1) // 2 == extra)
        def _(extra=extra):
            add_tile(0)
            for tile in range(1, doms // 2):
                build_tile(tile, step, [(2 * tile, 0, 1.0), (2 * tile + 1, 0, 1.0)])
                add_tile(tile)
            for tile in range(extra):
                chosen = []
                for place in (2 * tile, 2 * tile + 1):
                    slot = sum((total <= place).astype(jnp.int32) for total in reach)
                    weight = jnp.where(slot < doms, 1.0, 0.0).astype(F32)
                    chosen.append((jnp.minimum(slot, doms - 1), 1, weight))
                build_tile(doms // 2 + tile, step, chosen)
                add_tile(doms // 2 + tile)
            build_tile(0, jnp.minimum(step + 1, slabs - 1), [(0, 0, 1.0), (1, 0, 1.0)])

    @pl.when(step == pl.num_programs(0) - 1)
    def _():
        quarter_rows = ky_local // 2
        group = min(8, quarter_rows)
        for minus, out_ref in enumerate((plus_ref, minus_ref)):
            for start in range(0, quarter_rows, group):
                values = []
                for x in range(cells_x):
                    parts = [
                        grid_ref[x, pl.ds(minus + start + offset, group), :]
                        for offset in (0, quarter_rows, rows, rows + quarter_rows)
                    ]
                    cos_cos, cos_sin = regroup(parts[0], parts[1])
                    sin_cos, sin_sin = regroup(parts[2], parts[3])
                    if minus:
                        values.append((cos_cos + sin_sin, sin_cos - cos_sin))
                    else:
                        values.append((cos_cos - sin_sin, -cos_sin - sin_cos))
                for x, value in enumerate(transform(values, -1)):
                    for part in (0, 1):
                        out_ref[part, x, pl.ds(start, group), :] = value[part]


def inverse_x_kernel(place_ref, spectrum_ref, green_ref, *refs):
    *outs, near_ref = refs
    cells_x, quarter_rows = spectrum_ref.shape[1:3]
    group = min(8, quarter_rows)
    side = 1.0 - 2.0 * place_ref[3].astype(F32)

    def rows_of(step, carry):
        rows = pl.ds(pl.multiple_of(step * group, group), group)
        values = []
        for kx in range(cells_x):
            green = green_ref[kx, rows, :]
            values.append(tuple(spectrum_ref[part, kx, rows, :] * green for part in (0, 1)))
        even = transform(values[0::2], 1)
        odd = transform([(value[0] * side, value[1] * side) for value in values[1::2]], 1)
        for x in range(cells_x // 2):
            here, there = butterfly(even[x], rotate(odd[x], x, cells_x, 1))
            wanted = [(x, here)] + ([(cells_x // 2 + x, there)] if x < 3 else [])
            for plane, value in wanted:
                for part, row_group in enumerate(regroup(value[0], value[1])):
                    near_ref[plane, part, rows, :] = row_group
        return carry

    lax.fori_loop(0, quarter_rows // group, rows_of, 0)
    for k, out_ref in enumerate(outs):
        out_ref[...] = near_ref[pl.ds(lax.bitwise_xor(place_ref[4], k) * XD, XD)]


def inverse_y_kernel(sources, place_ref, *refs):
    ins, (high_ref, low_ref) = refs[: 2 * sources], refs[2 * sources : 2 * sources + 2]
    outs, (plus_ref, minus_ref, turned_ref) = refs[2 * sources + 2 : -3], refs[-3:]
    waves = NY // 2
    halves = half_sign()
    minus_ref[:, pl.ds(0, 8), :] = jnp.zeros((XD, 8, LANES), F32)
    for number, in_ref in enumerate(ins):
        count = in_ref.shape[1]
        start = lax.bitwise_xor(place_ref[4], number % sources) * count
        if number < sources:
            plus_ref[:, pl.ds(pl.multiple_of(start, 8), count), :] = in_ref[...]
        else:
            minus_ref[:, pl.ds(pl.multiple_of(start + 8, 8), count), :] = in_ref[...]
    sums = []
    for parity in (0, 1):
        parts = []
        for x in range(XD):
            plus = plus_ref[x, pl.ds(parity, waves // 2, stride=2), :]
            minus = minus_ref[x, pl.ds(7 + parity, waves // 2, stride=2), :]
            parts.append(split(jnp.concatenate([plus + minus, swap(plus - minus) * halves], 0)))
        both = jnp.concatenate([value for part in parts for value in part], 1)
        main = jnp.dot(high_ref[parity], both, preferred_element_type=F32)
        high = jnp.concatenate([part[0] for part in parts], 1)
        rest = jnp.dot(low_ref[parity], high, preferred_element_type=F32)
        sums.append(
            [
                main[:, 2 * x * LANES : (2 * x + 1) * LANES]
                + main[:, (2 * x + 1) * LANES : (2 * x + 2) * LANES]
                + rest[:, x * LANES : (x + 1) * LANES]
                for x in range(XD)
            ]
        )
    row = lax.broadcasted_iota(jnp.int32, (waves, 1), 0)
    alternate = jnp.where(row % 2 == 0, 1.0, -1.0)
    sign = jnp.where(place_ref[3] == 1, alternate, 1.0)
    for x in range(XD):
        last = minus_ref[x, pl.ds(waves, 8), :][7:8]
        even, odd = sums[0][x] + alternate * last, sums[1][x]
        total = jnp.concatenate([(even + odd) * sign, (even - odd) * sign], 0)
        turned_ref[:, x] = total.reshape(len(outs), -1, LANES)
    for k in range(len(outs)):
        outs[k][...] = turned_ref[lax.bitwise_xor(place_ref[5], k)]


def inverse_z_kernel(sources, place_ref, *refs):
    ins, (high_ref, low_ref) = refs[:sources], refs[sources : sources + 2]
    out_ref, lines_ref = refs[-2:]
    first = pl.program_id(0) * DEPTH
    for k in range(sources):
        lines_ref[lax.bitwise_xor(place_ref[5], k)] = ins[k][pl.ds(first, DEPTH)]
    rows = DEPTH * lines_ref.shape[2]
    lines = jnp.concatenate([lines_ref[source].reshape(rows, LANES) for source in range(sources)], 1)
    high, low = split(lines)
    total = jnp.dot(high, high_ref[...], preferred_element_type=F32)
    total += jnp.dot(low, high_ref[...], preferred_element_type=F32)
    total += jnp.dot(high, low_ref[...], preferred_element_type=F32)
    out_ref[...] = total.reshape(out_ref.shape)


def gather_kernel(
    first, place_ref, same_ref, other_ref, table_y, table_z, plus_ref, minus_ref, out_ref, shift_ref, fields_ref, stack_ref
):
    step = pl.program_id(0)
    half = LANES // 2
    rows = table_y.shape[1] // 2
    ky_local = rows - 8
    width = same_ref.shape[2]
    doms = table_y.shape[2] // width
    planes = fields_ref.shape[0]
    halves = half_sign()

    @pl.when(step == 0)
    def _():
        stack_ref[...] = jnp.zeros_like(stack_ref)
        shift_ref[...] = jnp.zeros_like(shift_ref)
        row = lax.broadcasted_iota(jnp.int32, (8, LANES), 0)

        def build(x, carry):
            plus = plus_ref[first * XD + x]
            shift_ref[pl.ds(1, ky_local), :] = minus_ref[first * XD + x]
            minus = shift_ref[pl.ds(0, ky_local), :]
            last = shift_ref[pl.ds(ky_local, 8), :][0:1]
            main = [plus + minus, swap(plus - minus) * halves]
            if 2 * ky_local < LANES:
                main.append(jnp.zeros((LANES - 2 * ky_local, LANES), F32))
            rest = jnp.where(row % 2 == 0, last, -swap(jnp.broadcast_to(last, (8, LANES))) * halves)
            rest = jnp.where(row < 6, rest, 0.0)
            rest_high = rest.astype(BF16).astype(F32)
            rest = jnp.where((row == 2) | (row == 3), rest - rest_high, rest_high)
            high, low = split(jnp.concatenate(main, 0).T)
            fields_ref[x, :, pl.ds(0, LANES)] = high
            fields_ref[x, :, pl.ds(LANES, LANES)] = low
            fields_ref[x, :, pl.ds(2 * LANES, LANES)] = high
            rest = jnp.concatenate([rest, jnp.zeros((LANES - 8, LANES), F32)], 0)
            fields_ref[x, :, pl.ds(3 * LANES, LANES)] = rest.T.astype(BF16)
            return carry

        lax.fori_loop(0, planes, build, 0)

    first_z = place_ref[1].astype(F32)
    twice = jnp.where(first_z + iota((half, 1), 0) == 0.0, 1.0, 2.0)
    fields = fields_ref[pl.ds(step * XD, SPAN)].reshape(SPAN * LANES, 4 * LANES)
    for slot in range(doms):
        lanes = pl.ds(slot * width, width)
        cosine = table_y[first + step, pl.ds(0, ky_local), lanes]
        sine = table_y[first + step, pl.ds(rows, ky_local), lanes]
        high, low = split(jnp.concatenate([cosine, sine], 0))
        for part, value in enumerate((high, high, low)):
            stack_ref[pl.ds(LANES * part, 2 * ky_local), lanes] = value
        cosine = table_y[first + step, pl.ds(ky_local, 8), lanes][0:1]
        sine = table_y[first + step, pl.ds(rows + ky_local, 8), lanes][0:1]
        row = lax.broadcasted_iota(jnp.int32, (16, width), 0)
        rest = jnp.where(row % 2 == 0, cosine, sine)
        rest_high = rest.astype(BF16).astype(F32)
        rest = jnp.where(row < 4, rest_high, jnp.where(row < 6, rest - rest_high, 0.0))
        stack_ref[pl.ds(3 * LANES, 16), lanes] = rest.astype(BF16)
    product = sum(
        jnp.dot(fields[:, part : part + 2 * LANES], stack_ref[pl.ds(part, 2 * LANES), :], preferred_element_type=F32)
        for part in (0, 2 * LANES)
    )
    for slot in range(doms):
        atoms = atoms_of(same_ref, other_ref, place_ref[2] + first + step, slot, doms)
        along_x = plane_weights(atoms, spline(atoms))
        lanes = pl.ds(slot * width, width)
        field = product[:, slot * width : (slot + 1) * width]
        total = along_x[0:1] * field[:LANES]
        for plane in range(1, SPAN):
            total += along_x[plane : plane + 1] * field[plane * LANES : (plane + 1) * LANES]
        waves = total * table_z[first + step, :, lanes]
        sampled = jnp.sum((waves[:half] - waves[half:]) * twice, axis=0, keepdims=True)
        core = place_ref[5] % 2 if slot < doms // 2 else 1 - place_ref[5] % 2
        out_ref[step * doms + 2 * (slot % (doms // 2)) + core] = sampled


def bf16_pair(table):
    high = table.astype(ml_dtypes.bfloat16)
    low = (table - high.astype(np.float64)).astype(ml_dtypes.bfloat16)
    return jnp.asarray(high), jnp.asarray(low)


def inverse_y_table():
    tables = []
    for parity in (0, 1):
        waves = np.arange(parity, NY // 2, 2)
        angle = 2.0 * np.pi * (np.outer(np.arange(NY // 2), waves) % NY) / NY
        tables.append(np.concatenate([np.cos(angle), np.sin(angle)], 1))
    return bf16_pair(np.stack(tables))


def inverse_z_table(dom_count):
    kz = np.arange(KH)
    angle = 2.0 * np.pi * (np.outer(kz, np.arange(NZ)) % NZ) / NZ
    weight = np.where(kz == 0, 1.0, 2.0)[:, None]
    parts = [weight * np.cos(angle), -weight * np.sin(angle)]
    return bf16_pair(
        np.stack([p.reshape(dom_count, KH // dom_count, NZ) for p in parts], 1).reshape(2 * KH, NZ)
    )


def whole_spec(shape):
    return pl.BlockSpec(shape, lambda *_: (0,) * len(shape))


SMALL = pl.CostEstimate(flops=10**6, bytes_accessed=10**4, transcendentals=0)
SMEM = pl.BlockSpec(memory_space=pltpu.SMEM)


def params(mib):
    return pltpu.CompilerParams(vmem_limit_bytes=mib * MIB)


def swapped(value, axis, distance):
    if distance == 0:
        return value
    return lax.ppermute(value, axis, [(i, i ^ distance) for i in range(lax.axis_size(axis))])


def partners(values, axis):
    received = [swapped(value, axis, k) for k, value in reversed(list(enumerate(values)))]
    return received[::-1]


def per_device(base_cells, offsets, charges, bias_coupling, counts, green):
    slabs = lax.axis_size("slab")
    doms = lax.axis_size("dom")
    slab = lax.axis_index("slab")
    dom = lax.axis_index("dom")
    atoms_local = charges.shape[0]
    cells_x = XD * slabs
    ky_local = NY // slabs
    kz_local = KH // doms
    slab_half = slabs // 2
    rows_local = NY // doms
    rows = ky_local + 8
    quarter_rows = ky_local // 2
    normalize = 1.0 / (cells_x * NY * NZ)
    upper = slab // slab_half
    place = jnp.stack(
        [slab * ky_local, dom * kz_local, upper * slab_half, upper, slab % slab_half, dom]
    ).astype(jnp.int32)

    vmem = pl.BlockSpec(memory_space=pltpu.VMEM)
    atoms = pl.pallas_call(
        pack_kernel,
        in_specs=[SMEM, vmem, vmem, vmem],
        out_specs=vmem,
        out_shape=jax.ShapeDtypeStruct((slabs * doms // 2, 8, atoms_local), F32),
        name="pack",
    )(counts, base_cells, offsets, charges.reshape(1, atoms_local))
    factors_y, factors_z = pl.pallas_call(
        wave_kernel,
        in_specs=[SMEM],
        out_specs=[vmem] * 2,
        out_shape=[jax.ShapeDtypeStruct((4 * count, TERMS), BF16) for count in (rows, LANES // 2)],
        compiler_params=params(8),
        name="waves",
    )(place)
    everyone = list(range(slabs * doms))
    same = lax.all_to_all(
        atoms, ("slab", "dom"), 0, 0, axis_index_groups=[everyone[0::2], everyone[1::2]], tiled=True
    )

    def halves_beside(value):
        return jnp.concatenate([value[:, :quarter_rows], value[:, quarter_rows:]], 2) * normalize

    own = halves_beside(green)
    same, flipped, factors_y, factors_z = lax.optimization_barrier(
        (same, halves_beside(green[:, ::-1]), factors_y, factors_z)
    )
    other = swapped(same, "dom", 1)
    mirrored = lax.ppermute(flipped, "slab", [(s, slabs - 1 - s) for s in range(slabs)])

    reaches = [value[:, 7, 0].reshape(slabs, doms // 2) for value in (same, other)]
    live = (jnp.concatenate(reaches, 1).reshape(-1) > atoms_local // 2).astype(jnp.int32)
    atoms_slab = doms * atoms_local
    table_bytes = 4 * (slab_half + 1) * (2 * rows + LANES) * atoms_slab
    spectrum_bytes = 16 * cells_x * max(8, quarter_rows) * LANES
    plus, minus, table_y, table_z = pl.pallas_call(
        forward_kernel,
        grid=(slabs,),
        in_specs=[SMEM] * 2 + [vmem] * 4,
        out_specs=[vmem] * 4,
        out_shape=[
            jax.ShapeDtypeStruct((2, cells_x, quarter_rows, LANES), F32),
            jax.ShapeDtypeStruct((2, cells_x, quarter_rows, LANES), F32),
            jax.ShapeDtypeStruct((slab_half + 1, 2 * rows, atoms_slab), F32),
            jax.ShapeDtypeStruct((slab_half + 1, LANES, atoms_slab), F32),
        ],
        scratch_shapes=[
            pltpu.VMEM((doms, SPAN * 4 * rows, atoms_local), BF16),
            pltpu.VMEM((doms, 2 * LANES, atoms_local), BF16),
            pltpu.VMEM((cells_x, 2 * rows, LANES), F32),
            pltpu.VMEM((slabs * doms, 8, atoms_local), F32),
            pltpu.VMEM((doms, TERMS, atoms_local), BF16),
            pltpu.VMEM((doms, TERMS, atoms_local), BF16),
        ],
        compiler_params=params(16 + (table_bytes + spectrum_bytes) // MIB),
        cost_estimate=SMALL,
        name="forward",
    )(place, live, same, other, factors_y, factors_z)

    near_planes = cells_x // 2 + 3
    lines, near = [], []
    for spectrum, influence in ((plus, own), (minus, mirrored)):
        *pieces, planes = pl.pallas_call(
            inverse_x_kernel,
            in_specs=[SMEM] + [vmem] * 2,
            out_specs=[vmem] * (slab_half + 1),
            out_shape=[jax.ShapeDtypeStruct((XD, 2, quarter_rows, LANES), F32)] * slab_half
            + [jax.ShapeDtypeStruct((near_planes, 2, quarter_rows, LANES), F32)],
            compiler_params=params(24),
            cost_estimate=SMALL,
            name="inverse_x",
        )(place, spectrum, influence)
        near.append(planes.reshape(near_planes, ky_local, LANES))
        lines += partners([value.reshape(XD, ky_local, LANES) for value in pieces], "slab")

    steps = slab_half // GATHERS

    def gather(part, place):
        return pl.pallas_call(
            functools.partial(gather_kernel, part * steps),
            grid=(steps,),
            in_specs=[SMEM] + [vmem] * 6,
            out_specs=vmem,
            out_shape=jax.ShapeDtypeStruct((steps * doms, 1, atoms_local), F32),
            scratch_shapes=[
                pltpu.VMEM((rows, LANES), F32),
                pltpu.VMEM((steps * XD + 3, LANES, 4 * LANES), BF16),
                pltpu.VMEM((4 * LANES, atoms_slab), BF16),
            ],
            compiler_params=params(12 + (table_bytes + 8 * near_planes * LANES * LANES) // MIB),
            cost_estimate=SMALL,
            name="gather",
        )(place, same, other, table_y, table_z, *near)

    earlier, *lines = lax.optimization_barrier((gather(0, place), *lines))

    high_y, low_y = inverse_y_table()
    high_z, low_z = inverse_z_table(doms)

    turned = pl.pallas_call(
        functools.partial(inverse_y_kernel, slab_half),
        in_specs=[SMEM] + [vmem] * (2 * slab_half + 2),
        out_specs=[vmem] * doms,
        out_shape=[jax.ShapeDtypeStruct((XD, rows_local, LANES), F32)] * doms,
        scratch_shapes=[
            pltpu.VMEM((XD, NY // 2, LANES), F32),
            pltpu.VMEM((XD, NY // 2 + 8, LANES), F32),
            pltpu.VMEM((doms, XD, rows_local, LANES), F32),
        ],
        compiler_params=params(32),
        cost_estimate=SMALL,
        name="inverse_y",
    )(place, *lines, high_y, low_y)
    columns = partners(turned, "dom")

    columns[1], late_place = lax.optimization_barrier((columns[1], place))
    partial = jnp.concatenate([earlier] + [gather(part, late_place) for part in range(1, GATHERS)], 0)
    members = slab_half * doms
    sampled = lax.all_to_all(
        partial.reshape(members, atoms_local),
        ("slab", "dom"),
        0,
        0,
        axis_index_groups=[list(range(members)), list(range(members, 2 * members))],
        tiled=True,
    )
    alive = jnp.arange(atoms_local, dtype=jnp.int32) < counts[0]
    gradient = jnp.where(alive, bias_coupling * jnp.sum(sampled, 0), 0.0)

    potential = pl.pallas_call(
        functools.partial(inverse_z_kernel, doms),
        grid=(XD // DEPTH,),
        in_specs=[SMEM] + [vmem] * (doms + 2),
        out_specs=pl.BlockSpec((DEPTH, rows_local, NZ), lambda step: (step, 0, 0)),
        out_shape=jax.ShapeDtypeStruct((XD, rows_local, NZ), F32),
        scratch_shapes=[pltpu.VMEM((doms, DEPTH, rows_local, LANES), F32)],
        compiler_params=params(24),
        cost_estimate=SMALL,
        name="inverse_z",
    )(place, *columns, high_z, low_z)
    return (potential, gradient)


def solution(mesh):
    placed = (
        P(None, ("slab", "dom")),
        P(None, ("slab", "dom")),
        P(("slab", "dom")),
        P(("slab", "dom")),
        P(("slab", "dom")),
        P(None, "slab", "dom"),
    )
    return jax.shard_map(
        per_device,
        mesh=mesh,
        in_specs=placed,
        out_specs=(P("slab", "dom", None), P(("slab", "dom"))),
        check_vma=False,
    )
```

```python
import functools

import jax
import jax.numpy as jnp
import ml_dtypes
import numpy as np
from jax import lax
from jax.experimental import pallas as pl
from jax.experimental.pallas import tpu as pltpu
from jax.sharding import PartitionSpec as P

XD = 4
NY = 512
NZ = 512
KH = NZ // 2
LANES = 128
SPAN = XD + 3
DEPTH = 2
GATHERS = 2
MIB = 1 << 20
BF16 = jnp.bfloat16
F32 = jnp.float32


def polynomial(function, terms):
    nodes = 0.125 * (1.0 - np.cos(np.pi * (np.arange(64) + 0.5) / 64))
    powers = nodes[:, None] ** np.arange(terms)[None, :]
    return [float(v) for v in np.linalg.lstsq(powers, function(np.sqrt(nodes)), rcond=None)[0]]


SINE_TERMS = polynomial(lambda r: np.sin(np.pi * r) / r, 6)
COSINE_TERMS = polynomial(lambda r: np.cos(np.pi * r), 6)


def horner(terms, square):
    total = jnp.full_like(square, terms[-1])
    for term in terms[-2::-1]:
        total = total * square + term
    return total


def turn(fraction):
    left = fraction - jnp.floor(fraction + 0.5)
    square = left * left
    sine = left * horner(SINE_TERMS, square)
    cosine = horner(COSINE_TERMS, square)
    return 1.0 - 2.0 * sine * sine, 2.0 * sine * cosine


def spline(frac):
    inner = 1.0 - frac
    square = frac * frac
    cube = square * frac
    sixth = 1.0 / 6.0
    return (
        inner * inner * inner * sixth,
        (3.0 * cube - 6.0 * square + 4.0) * sixth,
        (-3.0 * cube + 3.0 * square + 3.0 * frac + 1.0) * sixth,
        cube * sixth,
    )


def split(value):
    high = value.astype(BF16)
    return high, (value - high.astype(F32)).astype(BF16)


def iota(shape, axis):
    return lax.broadcasted_iota(jnp.int32, shape, axis).astype(F32)


RADIX = 16
DIGITS = 32
TERMS = 256


def wave_factors(first, rows, length):
    lane = lax.broadcasted_iota(jnp.int32, (rows, TERMS), 1)
    section = lane // DIGITS
    digit = (lane % DIGITS).astype(F32) * jnp.where(section < 2, float(RADIX), 1.0)
    parts = []
    for value in turn((first + iota((rows, TERMS), 0)) * digit * (1.0 / length)):
        high = value.astype(BF16).astype(F32)
        parts.append(jnp.where((section == 1) | (section == 3), value - high, high))
    upper, lower = section < 2, (section >= 2) & (section < 5)
    masked = [jnp.where(mask, part, 0.0) for mask in (upper, lower) for part in parts]
    return jnp.concatenate(masked, 0).astype(BF16)


def wave_kernel(place_ref, out_y_ref, out_z_ref):
    out_y_ref[...] = wave_factors(place_ref[0].astype(F32), out_y_ref.shape[0] // 4, NY)
    out_z_ref[...] = wave_factors(place_ref[1].astype(F32), out_z_ref.shape[0] // 4, NZ)


def atom_waves(base, weights, factors_ref, digits_ref):
    width = base.shape[1]
    high_digit = jnp.floor(base * (1.0 / RADIX))
    row = iota((DIGITS, width), 0)
    chosen = jnp.where(row == high_digit, 1.0, 0.0).astype(BF16)
    step = row - (base - RADIX * high_digit)
    spread = jnp.where(step == 3.0, weights[3], 0.0)
    for r in (2, 1, 0):
        spread = jnp.where(step == float(r), weights[r], spread)
    high, low = split(spread)
    for section, value in enumerate((chosen, chosen, high, high, low)):
        digits_ref[pl.ds(DIGITS * section, DIGITS), :] = value
    product = jnp.dot(factors_ref[...], digits_ref[...], preferred_element_type=F32)
    rows = product.shape[0] // 4
    cos_a, sin_a, cos_b, sin_b = (product[i * rows : (i + 1) * rows] for i in range(4))
    return cos_a * cos_b - sin_a * sin_b, sin_a * cos_b + cos_a * sin_b


def plane_weights(atoms, weights):
    row = iota((8, atoms.shape[1]), 0) - atoms[0:1]
    return sum(weights[r][3:4] * (row == float(r)).astype(F32) for r in range(4))


def swap(value):
    return pltpu.roll(value, LANES // 2, axis=value.ndim - 1)


def half_sign():
    lane = lax.broadcasted_iota(jnp.int32, (1, LANES), 1)
    return jnp.where(lane < LANES // 2, -1.0, 1.0).astype(F32)


def rotate(value, numer, denom, sign):
    real, imag = value
    if numer == 0:
        return value
    if 4 * numer == denom:
        return (-imag, real) if sign > 0 else (imag, -real)
    angle = 2.0 * np.pi * numer / denom
    cosine, sine = float(np.cos(angle)), float(sign * np.sin(angle))
    if 8 * numer in (denom, 3 * denom):
        size = abs(cosine)
        cos_sign, sin_sign = (1 if cosine > 0 else -1), (1 if sine > 0 else -1)
        if cos_sign == sin_sign:
            return ((real - imag) * (cos_sign * size), (real + imag) * (cos_sign * size))
        return ((real + imag) * (cos_sign * size), (imag - real) * (cos_sign * size))
    return real * cosine - imag * sine, imag * cosine + real * sine


def butterfly(even, turned):
    plus = (even[0] + turned[0], even[1] + turned[1])
    return plus, (even[0] - turned[0], even[1] - turned[1])


def transform(values, sign):
    count = len(values)
    if count == 1:
        return values
    even = transform(values[0::2], sign)
    odd = transform(values[1::2], sign)
    both = [butterfly(even[k], rotate(odd[k], k, count, sign)) for k in range(count // 2)]
    return [pair[0] for pair in both] + [pair[1] for pair in both]


def regroup(low, high):
    first = lax.broadcasted_iota(jnp.int32, low.shape, 1) < LANES // 2
    crossed = swap(jnp.where(first, high, low))
    return jnp.where(first, low, crossed), jnp.where(first, crossed, high)


def pack_kernel(counts_ref, cells_ref, offsets_ref, charges_ref, out_ref):
    width = offsets_ref.shape[1]
    alive = lax.broadcasted_iota(jnp.int32, (1, width), 1) < counts_ref[0]
    atoms = jnp.concatenate(
        [
            lax.bitwise_and(cells_ref[0:1, :], XD - 1).astype(F32),
            cells_ref[1:3, :].astype(F32),
            offsets_ref[...],
            jnp.where(alive, charges_ref[...], 0.0),
            jnp.full((1, width), counts_ref[0].astype(F32)),
        ],
        0,
    )
    for copy in range(out_ref.shape[0]):
        out_ref[copy] = atoms


def atoms_of(same_ref, other_ref, slab, slot, doms):
    half = doms // 2
    return (same_ref, other_ref)[slot // half][slab * half + slot % half]


def forward_kernel(
    place_ref,
    same_reach,
    other_reach,
    same_ref,
    other_ref,
    factors_y,
    factors_z,
    plus_ref,
    minus_ref,
    table_y,
    table_z,
    left_ref,
    right_ref,
    grid_ref,
    atoms_ref,
    digits_y,
    digits_z,
):
    step = pl.program_id(0)
    cells_x = grid_ref.shape[0]
    rows = grid_ref.shape[1] // 2
    ky_local = rows - 8
    half_slot = same_ref.shape[2] // 2
    doms = table_y.shape[2] // (2 * half_slot)
    kept = step - place_ref[2]
    kept = jnp.where((kept >= 0) & (kept < table_y.shape[0] - 1), kept, table_y.shape[0] - 1)

    @pl.when(step == 0)
    def _():
        grid_ref[...] = jnp.zeros_like(grid_ref)
        digits_y[...] = jnp.zeros_like(digits_y)
        digits_z[...] = jnp.zeros_like(digits_z)

    for slot in range(doms):
        atoms_ref[slot] = atoms_of(same_ref, other_ref, step, slot, doms)

    def add_tile(tile, halves):
        atoms = jnp.concatenate([atoms_ref[slot, :, pl.ds(part * half_slot, half_slot)] for slot, part, _ in halves], 1)
        counted = jnp.concatenate([jnp.full((1, half_slot), weight) for _, _, weight in halves], 1)
        weights = spline(atoms)
        along_x = plane_weights(atoms, weights) * (atoms[6:7] * counted)
        waves_z = atom_waves(atoms[2:3], [w[5:6] for w in weights], factors_z, digits_z.at[tile])
        waves_z = jnp.concatenate(waves_z, 0)
        waves_y = atom_waves(atoms[1:2], [w[4:5] for w in weights], factors_y, digits_y.at[tile])
        waves_y = jnp.concatenate(waves_y, 0)
        for number, (slot, part, _) in enumerate(halves):
            lanes = slice(number * half_slot, (number + 1) * half_slot)
            start = pl.multiple_of((2 * slot + part) * half_slot, half_slot)
            table_z[kept, :, pl.ds(start, half_slot)] = waves_z[:, lanes]
            table_y[kept, :, pl.ds(start, half_slot)] = waves_y[:, lanes]
        high, low = split(waves_z)
        right_ref[tile, pl.ds(0, LANES), :] = high
        right_ref[tile, pl.ds(LANES, LANES), :] = low
        for plane in range(SPAN):
            first = 4 * rows * plane
            high, low = split(waves_y * along_x[plane : plane + 1])
            left_ref[tile, pl.ds(first, 2 * rows), :] = high
            left_ref[tile, pl.ds(first + 2 * rows, 2 * rows), :] = low
        product = lax.dot_general(
            left_ref[tile], right_ref[tile], (((1,), (1,)), ((), ())), preferred_element_type=F32
        )
        for plane in range(SPAN):
            first = 4 * rows * plane
            high, low = product[first : first + 2 * rows], product[first + 2 * rows : first + 4 * rows]
            at = lax.rem(step * XD + plane, cells_x)
            grid_ref[at] += (high[:, :LANES] + high[:, LANES:]) + (low[:, :LANES] + low[:, LANES:])

    reach = [
        (same_reach, other_reach)[2 * slot // doms][step * (doms // 2) + slot % (doms // 2)] for slot in range(doms)
    ]
    reach = [sum(reach[: slot + 1]) for slot in range(doms)]
    for extra in range(doms // 2 + 1):

        @pl.when((reach[-1] + 1) // 2 == extra)
        def _(extra=extra):
            for tile in range(doms // 2):
                add_tile(tile, [(2 * tile, 0, 1.0), (2 * tile + 1, 0, 1.0)])
            for tile in range(extra):
                chosen = []
                for place in (2 * tile, 2 * tile + 1):
                    slot = sum((total <= place).astype(jnp.int32) for total in reach)
                    weight = jnp.where(slot < doms, 1.0, 0.0).astype(F32)
                    chosen.append((jnp.minimum(slot, doms - 1), 1, weight))
                add_tile(doms // 2 + tile, chosen)

    @pl.when(step == pl.num_programs(0) - 1)
    def _():
        quarter_rows = ky_local // 2
        group = min(8, quarter_rows)
        for minus, out_ref in enumerate((plus_ref, minus_ref)):
            for start in range(0, quarter_rows, group):
                values = []
                for x in range(cells_x):
                    parts = [
                        grid_ref[x, pl.ds(minus + start + offset, group), :]
                        for offset in (0, quarter_rows, rows, rows + quarter_rows)
                    ]
                    cos_cos, cos_sin = regroup(parts[0], parts[1])
                    sin_cos, sin_sin = regroup(parts[2], parts[3])
                    if minus:
                        values.append((cos_cos + sin_sin, sin_cos - cos_sin))
                    else:
                        values.append((cos_cos - sin_sin, -cos_sin - sin_cos))
                for x, value in enumerate(transform(values, -1)):
                    for part in (0, 1):
                        out_ref[part, x, pl.ds(start, group), :] = value[part]


def inverse_x_kernel(place_ref, spectrum_ref, green_ref, *refs):
    *outs, near_ref = refs
    cells_x, quarter_rows = spectrum_ref.shape[1:3]
    group = min(8, quarter_rows)
    side = 1.0 - 2.0 * place_ref[3].astype(F32)

    def rows_of(step, carry):
        rows = pl.ds(pl.multiple_of(step * group, group), group)
        values = []
        for kx in range(cells_x):
            green = green_ref[kx, rows, :]
            values.append(tuple(spectrum_ref[part, kx, rows, :] * green for part in (0, 1)))
        even = transform(values[0::2], 1)
        odd = transform([(value[0] * side, value[1] * side) for value in values[1::2]], 1)
        for x in range(cells_x // 2):
            here, there = butterfly(even[x], rotate(odd[x], x, cells_x, 1))
            wanted = [(x, here)] + ([(cells_x // 2 + x, there)] if x < 3 else [])
            for plane, value in wanted:
                for part, row_group in enumerate(regroup(value[0], value[1])):
                    near_ref[plane, part, rows, :] = row_group
        return carry

    lax.fori_loop(0, quarter_rows // group, rows_of, 0)
    for k, out_ref in enumerate(outs):
        out_ref[...] = near_ref[pl.ds(lax.bitwise_xor(place_ref[4], k) * XD, XD)]


def inverse_y_kernel(sources, place_ref, *refs):
    ins, (high_ref, low_ref) = refs[: 2 * sources], refs[2 * sources : 2 * sources + 2]
    outs, (plus_ref, minus_ref, turned_ref) = refs[2 * sources + 2 : -3], refs[-3:]
    waves = NY // 2
    halves = half_sign()
    minus_ref[:, pl.ds(0, 8), :] = jnp.zeros((XD, 8, LANES), F32)
    for number, in_ref in enumerate(ins):
        count = in_ref.shape[1]
        start = lax.bitwise_xor(place_ref[4], sources - 1 - number % sources) * count
        if number < sources:
            plus_ref[:, pl.ds(pl.multiple_of(start, 8), count), :] = in_ref[...]
        else:
            minus_ref[:, pl.ds(pl.multiple_of(start + 8, 8), count), :] = in_ref[...]
    sums = []
    for parity in (0, 1):
        parts = []
        for x in range(XD):
            plus = plus_ref[x, pl.ds(parity, waves // 2, stride=2), :]
            minus = minus_ref[x, pl.ds(7 + parity, waves // 2, stride=2), :]
            parts.append(split(jnp.concatenate([plus + minus, swap(plus - minus) * halves], 0)))
        both = jnp.concatenate([value for part in parts for value in part], 1)
        main = jnp.dot(high_ref[parity], both, preferred_element_type=F32)
        high = jnp.concatenate([part[0] for part in parts], 1)
        rest = jnp.dot(low_ref[parity], high, preferred_element_type=F32)
        sums.append(
            [
                main[:, 2 * x * LANES : (2 * x + 1) * LANES]
                + main[:, (2 * x + 1) * LANES : (2 * x + 2) * LANES]
                + rest[:, x * LANES : (x + 1) * LANES]
                for x in range(XD)
            ]
        )
    row = lax.broadcasted_iota(jnp.int32, (waves, 1), 0)
    alternate = jnp.where(row % 2 == 0, 1.0, -1.0)
    sign = jnp.where(place_ref[3] == 1, alternate, 1.0)
    for x in range(XD):
        last = minus_ref[x, pl.ds(waves, 8), :][7:8]
        even, odd = sums[0][x] + alternate * last, sums[1][x]
        total = jnp.concatenate([(even + odd) * sign, (even - odd) * sign], 0)
        turned_ref[:, x] = total.reshape(len(outs), -1, LANES)
    for k in range(len(outs)):
        outs[k][...] = turned_ref[lax.bitwise_xor(place_ref[5], k)]


def inverse_z_kernel(distances, place_ref, *refs):
    count = len(distances)
    ins, (high_ref, low_ref), (*total_refs, out_ref) = refs[:count], refs[count : count + 2], refs[count + 2 :]
    planes, rows, depth = out_ref.shape
    span = pl.ds(pl.program_id(0) * planes, planes)
    lines, tables = [], []
    for in_ref, distance in zip(ins, distances):
        lines.append(in_ref[span].reshape(planes * rows, LANES))
        start = pl.multiple_of(lax.bitwise_xor(place_ref[5], distance) * LANES, LANES)
        tables.append((high_ref[pl.ds(start, LANES), :], low_ref[pl.ds(start, LANES), :]))
    high, low = split(jnp.concatenate(lines, 1))
    table_high, table_low = (jnp.concatenate([pair[part] for pair in tables], 0) for part in (0, 1))
    total = jnp.dot(high, table_high, preferred_element_type=F32)
    total += jnp.dot(low, table_high, preferred_element_type=F32)
    total += jnp.dot(high, table_low, preferred_element_type=F32)
    total = total.reshape(planes, rows, depth)
    for total_ref in total_refs:
        total += total_ref[span]
    out_ref[...] = total


def gather_kernel(first, place_ref, same_ref, other_ref, table_y, table_z, plus_ref, minus_ref, *refs):
    *earlier, out_ref, shift_ref, fields_ref, stack_ref = refs
    step = pl.program_id(0)
    half = LANES // 2
    rows = table_y.shape[1] // 2
    ky_local = rows - 8
    width = same_ref.shape[2]
    doms = table_y.shape[2] // width
    planes = fields_ref.shape[0]
    halves = half_sign()

    @pl.when(step == 0)
    def _():
        for earlier_ref in earlier:
            out_ref[pl.ds(0, first * doms)] = earlier_ref[...]
        stack_ref[...] = jnp.zeros_like(stack_ref)
        shift_ref[...] = jnp.zeros_like(shift_ref)
        row = lax.broadcasted_iota(jnp.int32, (8, LANES), 0)

        def build(x, carry):
            plus = plus_ref[first * XD + x]
            shift_ref[pl.ds(1, ky_local), :] = minus_ref[first * XD + x]
            minus = shift_ref[pl.ds(0, ky_local), :]
            last = shift_ref[pl.ds(ky_local, 8), :][0:1]
            main = [plus + minus, swap(plus - minus) * halves]
            if 2 * ky_local < LANES:
                main.append(jnp.zeros((LANES - 2 * ky_local, LANES), F32))
            rest = jnp.where(row % 2 == 0, last, -swap(jnp.broadcast_to(last, (8, LANES))) * halves)
            rest = jnp.where(row < 6, rest, 0.0)
            rest_high = rest.astype(BF16).astype(F32)
            rest = jnp.where((row == 2) | (row == 3), rest - rest_high, rest_high)
            high, low = split(jnp.concatenate(main, 0).T)
            fields_ref[x, :, pl.ds(0, LANES)] = high
            fields_ref[x, :, pl.ds(LANES, LANES)] = low
            fields_ref[x, :, pl.ds(2 * LANES, LANES)] = high
            rest = jnp.concatenate([rest, jnp.zeros((LANES - 8, LANES), F32)], 0)
            fields_ref[x, :, pl.ds(3 * LANES, LANES)] = rest.T.astype(BF16)
            return carry

        lax.fori_loop(0, planes, build, 0)

    first_z = place_ref[1].astype(F32)
    twice = jnp.where(first_z + iota((half, 1), 0) == 0.0, 1.0, 2.0)
    fields = fields_ref[pl.ds(step * XD, SPAN)].reshape(SPAN * LANES, 4 * LANES)
    for slot in range(doms):
        lanes = pl.ds(slot * width, width)
        cosine = table_y[first + step, pl.ds(0, ky_local), lanes]
        sine = table_y[first + step, pl.ds(rows, ky_local), lanes]
        high, low = split(jnp.concatenate([cosine, sine], 0))
        for part, value in enumerate((high, high, low)):
            stack_ref[pl.ds(LANES * part, 2 * ky_local), lanes] = value
        cosine = table_y[first + step, pl.ds(ky_local, 8), lanes][0:1]
        sine = table_y[first + step, pl.ds(rows + ky_local, 8), lanes][0:1]
        row = lax.broadcasted_iota(jnp.int32, (16, width), 0)
        rest = jnp.where(row % 2 == 0, cosine, sine)
        rest_high = rest.astype(BF16).astype(F32)
        rest = jnp.where(row < 4, rest_high, jnp.where(row < 6, rest - rest_high, 0.0))
        stack_ref[pl.ds(3 * LANES, 16), lanes] = rest.astype(BF16)
    product = sum(
        jnp.dot(fields[:, part : part + 2 * LANES], stack_ref[pl.ds(part, 2 * LANES), :], preferred_element_type=F32)
        for part in (0, 2 * LANES)
    )
    for slot in range(doms):
        atoms = atoms_of(same_ref, other_ref, place_ref[2] + first + step, slot, doms)
        along_x = plane_weights(atoms, spline(atoms))
        lanes = pl.ds(slot * width, width)
        field = product[:, slot * width : (slot + 1) * width]
        total = along_x[0:1] * field[:LANES]
        for plane in range(1, SPAN):
            total += along_x[plane : plane + 1] * field[plane * LANES : (plane + 1) * LANES]
        waves = total * table_z[first + step, :, lanes]
        sampled = jnp.sum((waves[:half] - waves[half:]) * twice, axis=0, keepdims=True)
        core = place_ref[5] % 2 if slot < doms // 2 else 1 - place_ref[5] % 2
        out_ref[(first + step) * doms + 2 * (slot % (doms // 2)) + core] = sampled


def bf16_pair(table):
    high = table.astype(ml_dtypes.bfloat16)
    low = (table - high.astype(np.float64)).astype(ml_dtypes.bfloat16)
    return jnp.asarray(high), jnp.asarray(low)


def inverse_y_table():
    tables = []
    for parity in (0, 1):
        waves = np.arange(parity, NY // 2, 2)
        angle = 2.0 * np.pi * (np.outer(np.arange(NY // 2), waves) % NY) / NY
        tables.append(np.concatenate([np.cos(angle), np.sin(angle)], 1))
    return bf16_pair(np.stack(tables))


def inverse_z_table(dom_count):
    kz = np.arange(KH)
    angle = 2.0 * np.pi * (np.outer(kz, np.arange(NZ)) % NZ) / NZ
    weight = np.where(kz == 0, 1.0, 2.0)[:, None]
    parts = [weight * np.cos(angle), -weight * np.sin(angle)]
    return bf16_pair(
        np.stack([p.reshape(dom_count, KH // dom_count, NZ) for p in parts], 1).reshape(2 * KH, NZ)
    )


def whole_spec(shape):
    return pl.BlockSpec(shape, lambda *_: (0,) * len(shape))


SMALL = pl.CostEstimate(flops=10**6, bytes_accessed=10**4, transcendentals=0)
SMEM = pl.BlockSpec(memory_space=pltpu.SMEM)


def params(mib):
    return pltpu.CompilerParams(vmem_limit_bytes=mib * MIB)


def swapped(value, axis, distance):
    if distance == 0:
        return value
    return lax.ppermute(value, axis, [(i, i ^ distance) for i in range(lax.axis_size(axis))])


def per_device(base_cells, offsets, charges, bias_coupling, counts, green):
    slabs = lax.axis_size("slab")
    doms = lax.axis_size("dom")
    slab = lax.axis_index("slab")
    dom = lax.axis_index("dom")
    atoms_local = charges.shape[0]
    cells_x = XD * slabs
    ky_local = NY // slabs
    kz_local = KH // doms
    slab_half = slabs // 2
    rows_local = NY // doms
    rows = ky_local + 8
    quarter_rows = ky_local // 2
    normalize = 1.0 / (cells_x * NY * NZ)
    upper = slab // slab_half
    place = jnp.stack(
        [slab * ky_local, dom * kz_local, upper * slab_half, upper, slab % slab_half, dom]
    ).astype(jnp.int32)

    vmem = pl.BlockSpec(memory_space=pltpu.VMEM)
    atoms = pl.pallas_call(
        pack_kernel,
        in_specs=[SMEM, vmem, vmem, vmem],
        out_specs=vmem,
        out_shape=jax.ShapeDtypeStruct((slabs * doms // 2, 8, atoms_local), F32),
        name="pack",
    )(counts, base_cells, offsets, charges.reshape(1, atoms_local))
    factors_y, factors_z = pl.pallas_call(
        wave_kernel,
        in_specs=[SMEM],
        out_specs=[vmem] * 2,
        out_shape=[jax.ShapeDtypeStruct((4 * count, TERMS), BF16) for count in (rows, LANES // 2)],
        compiler_params=params(8),
        name="waves",
    )(place)
    everyone = list(range(slabs * doms))
    same = lax.all_to_all(
        atoms, ("slab", "dom"), 0, 0, axis_index_groups=[everyone[0::2], everyone[1::2]], tiled=True
    )

    def halves_beside(value):
        return jnp.concatenate([value[:, :quarter_rows], value[:, quarter_rows:]], 2) * normalize

    own = halves_beside(green)
    same, flipped, factors_y, factors_z = lax.optimization_barrier(
        (same, halves_beside(green[:, ::-1]), factors_y, factors_z)
    )
    other = swapped(same, "dom", 1)
    mirrored = lax.ppermute(flipped, "slab", [(s, slabs - 1 - s) for s in range(slabs)])

    reaches = [(value[:, 7, 0] > atoms_local // 2).astype(jnp.int32) for value in (same, other)]
    atoms_slab = doms * atoms_local
    table_bytes = 4 * (slab_half + 1) * (2 * rows + LANES) * atoms_slab
    spectrum_bytes = 16 * cells_x * max(8, quarter_rows) * LANES
    plus, minus, table_y, table_z = pl.pallas_call(
        forward_kernel,
        grid=(slabs,),
        in_specs=[SMEM] * 3 + [vmem] * 4,
        out_specs=[vmem] * 4,
        out_shape=[
            jax.ShapeDtypeStruct((2, cells_x, quarter_rows, LANES), F32),
            jax.ShapeDtypeStruct((2, cells_x, quarter_rows, LANES), F32),
            jax.ShapeDtypeStruct((slab_half + 1, 2 * rows, atoms_slab), F32),
            jax.ShapeDtypeStruct((slab_half + 1, LANES, atoms_slab), F32),
        ],
        scratch_shapes=[
            pltpu.VMEM((doms, SPAN * 4 * rows, atoms_local), BF16),
            pltpu.VMEM((doms, 2 * LANES, atoms_local), BF16),
            pltpu.VMEM((cells_x, 2 * rows, LANES), F32),
            pltpu.VMEM((doms, 8, atoms_local), F32),
            pltpu.VMEM((doms, TERMS, atoms_local), BF16),
            pltpu.VMEM((doms, TERMS, atoms_local), BF16),
        ],
        compiler_params=params(16 + (table_bytes + spectrum_bytes) // MIB),
        cost_estimate=SMALL,
        name="forward",
    )(place, *reaches, same, other, factors_y, factors_z)

    near_planes = cells_x // 2 + 3
    lines, near = [], []
    for spectrum, influence in ((plus, own), (minus, mirrored)):
        *pieces, planes = pl.pallas_call(
            inverse_x_kernel,
            in_specs=[SMEM] + [vmem] * 2,
            out_specs=[vmem] * (slab_half + 1),
            out_shape=[jax.ShapeDtypeStruct((XD, 2, quarter_rows, LANES), F32)] * slab_half
            + [jax.ShapeDtypeStruct((near_planes, 2, quarter_rows, LANES), F32)],
            compiler_params=params(24),
            cost_estimate=SMALL,
            name="inverse_x",
        )(place, spectrum, influence)
        near.append(planes.reshape(near_planes, ky_local, LANES))
        lines += [swapped(value.reshape(XD, ky_local, LANES), "slab", k) for k, value in enumerate(pieces)][::-1]

    steps = slab_half // GATHERS

    def gather(part, place, *earlier):
        return pl.pallas_call(
            functools.partial(gather_kernel, part * steps),
            grid=(steps,),
            in_specs=[SMEM] + [vmem] * (6 + len(earlier)),
            out_specs=vmem,
            out_shape=jax.ShapeDtypeStruct(((part + 1) * steps * doms, 1, atoms_local), F32),
            scratch_shapes=[
                pltpu.VMEM((rows, LANES), F32),
                pltpu.VMEM((steps * XD + 3, LANES, 4 * LANES), BF16),
                pltpu.VMEM((4 * LANES, atoms_slab), BF16),
            ],
            compiler_params=params(12 + (table_bytes + 8 * near_planes * LANES * LANES) // MIB),
            cost_estimate=SMALL,
            name="gather",
        )(place, same, other, table_y, table_z, *near, *earlier)

    partial, *lines = lax.optimization_barrier((gather(0, place), *lines))

    high_y, low_y = inverse_y_table()
    high_z, low_z = inverse_z_table(doms)

    turned = pl.pallas_call(
        functools.partial(inverse_y_kernel, slab_half),
        in_specs=[SMEM] + [vmem] * (2 * slab_half + 2),
        out_specs=[vmem] * doms,
        out_shape=[jax.ShapeDtypeStruct((XD, rows_local, LANES), F32)] * doms,
        scratch_shapes=[
            pltpu.VMEM((XD, NY // 2, LANES), F32),
            pltpu.VMEM((XD, NY // 2 + 8, LANES), F32),
            pltpu.VMEM((doms, XD, rows_local, LANES), F32),
        ],
        compiler_params=params(32),
        cost_estimate=SMALL,
        name="inverse_y",
    )(place, *lines, high_y, low_y)
    columns = [swapped(value, "dom", k) for k, value in enumerate(turned)]

    columns[1], late_place = lax.optimization_barrier((columns[1], place))
    for part in range(1, GATHERS):
        partial = gather(part, late_place, partial)
    partial, columns[0] = lax.optimization_barrier((partial, columns[0]))
    members = slab_half * doms
    sampled = lax.all_to_all(
        partial.reshape(members, atoms_local),
        ("slab", "dom"),
        0,
        0,
        axis_index_groups=[list(range(members)), list(range(members, 2 * members))],
        tiled=True,
    )
    alive = jnp.arange(atoms_local, dtype=jnp.int32) < counts[0]
    gradient = jnp.where(alive, bias_coupling * jnp.sum(sampled, 0), 0.0)

    total = []
    for distances in (range(doms // 2), range(doms - 1, doms // 2 - 1, -1)):
        last = len(total) == 1
        total = [
            pl.pallas_call(
                functools.partial(inverse_z_kernel, distances),
                grid=(XD // DEPTH if last else 1,),
                in_specs=[SMEM] + [vmem] * (len(distances) + 2 + len(total)),
                out_specs=pl.BlockSpec((DEPTH, rows_local, NZ), lambda step: (step, 0, 0)) if last else vmem,
                out_shape=jax.ShapeDtypeStruct((XD, rows_local, NZ), F32),
                compiler_params=params(24),
                cost_estimate=SMALL,
                name="inverse_z",
            )(place, *[columns[k] for k in distances], high_z, low_z, *total)
        ]
    potential = total[0]
    return (potential, gradient)


def solution(mesh):
    placed = (
        P(None, ("slab", "dom")),
        P(None, ("slab", "dom")),
        P(("slab", "dom")),
        P(("slab", "dom")),
        P(("slab", "dom")),
        P(None, "slab", "dom"),
    )
    return jax.shard_map(
        per_device,
        mesh=mesh,
        in_specs=placed,
        out_specs=(P("slab", "dom", None), P(("slab", "dom"))),
        check_vma=False,
    )
```

```python
import functools

import jax
import jax.numpy as jnp
import ml_dtypes
import numpy as np
from jax import lax
from jax.experimental import pallas as pl
from jax.experimental.pallas import tpu as pltpu
from jax.sharding import PartitionSpec as P

XD = 4
NY = 512
NZ = 512
KH = NZ // 2
LANES = 128
SPAN = XD + 3
DEPTH = 2
GATHERS = 2
MIB = 1 << 20
BF16 = jnp.bfloat16
F32 = jnp.float32


def polynomial(function, terms):
    nodes = 0.125 * (1.0 - np.cos(np.pi * (np.arange(64) + 0.5) / 64))
    powers = nodes[:, None] ** np.arange(terms)[None, :]
    return [float(v) for v in np.linalg.lstsq(powers, function(np.sqrt(nodes)), rcond=None)[0]]


SINE_TERMS = polynomial(lambda r: np.sin(np.pi * r) / r, 6)
COSINE_TERMS = polynomial(lambda r: np.cos(np.pi * r), 6)


def horner(terms, square):
    total = jnp.full_like(square, terms[-1])
    for term in terms[-2::-1]:
        total = total * square + term
    return total


def turn(fraction):
    left = fraction - jnp.floor(fraction + 0.5)
    square = left * left
    sine = left * horner(SINE_TERMS, square)
    cosine = horner(COSINE_TERMS, square)
    return 1.0 - 2.0 * sine * sine, 2.0 * sine * cosine


def spline(frac):
    inner = 1.0 - frac
    square = frac * frac
    cube = square * frac
    sixth = 1.0 / 6.0
    return (
        inner * inner * inner * sixth,
        (3.0 * cube - 6.0 * square + 4.0) * sixth,
        (-3.0 * cube + 3.0 * square + 3.0 * frac + 1.0) * sixth,
        cube * sixth,
    )


def split(value):
    high = value.astype(BF16)
    return high, (value - high.astype(F32)).astype(BF16)


def iota(shape, axis):
    return lax.broadcasted_iota(jnp.int32, shape, axis).astype(F32)


RADIX = 16
DIGITS = 32
TERMS = 256


def wave_factors(first, rows, length):
    lane = lax.broadcasted_iota(jnp.int32, (rows, TERMS), 1)
    section = lane // DIGITS
    digit = (lane % DIGITS).astype(F32) * jnp.where(section < 2, float(RADIX), 1.0)
    parts = []
    for value in turn((first + iota((rows, TERMS), 0)) * digit * (1.0 / length)):
        high = value.astype(BF16).astype(F32)
        parts.append(jnp.where((section == 1) | (section == 3), value - high, high))
    upper, lower = section < 2, (section >= 2) & (section < 5)
    masked = [jnp.where(mask, part, 0.0) for mask in (upper, lower) for part in parts]
    return jnp.concatenate(masked, 0).astype(BF16)


def wave_kernel(place_ref, out_y_ref, out_z_ref):
    out_y_ref[...] = wave_factors(place_ref[0].astype(F32), out_y_ref.shape[0] // 4, NY)
    out_z_ref[...] = wave_factors(place_ref[1].astype(F32), out_z_ref.shape[0] // 4, NZ)


def atom_waves(base, weights, factors_ref, digits_ref):
    width = base.shape[1]
    high_digit = jnp.floor(base * (1.0 / RADIX))
    row = iota((DIGITS, width), 0)
    chosen = jnp.where(row == high_digit, 1.0, 0.0).astype(BF16)
    step = row - (base - RADIX * high_digit)
    spread = jnp.where(step == 3.0, weights[3], 0.0)
    for r in (2, 1, 0):
        spread = jnp.where(step == float(r), weights[r], spread)
    high, low = split(spread)
    for section, value in enumerate((chosen, chosen, high, high, low)):
        digits_ref[pl.ds(DIGITS * section, DIGITS), :] = value
    product = jnp.dot(factors_ref[...], digits_ref[...], preferred_element_type=F32)
    rows = product.shape[0] // 4
    cos_a, sin_a, cos_b, sin_b = (product[i * rows : (i + 1) * rows] for i in range(4))
    return cos_a * cos_b - sin_a * sin_b, sin_a * cos_b + cos_a * sin_b


def plane_weights(atoms, weights):
    row = iota((8, atoms.shape[1]), 0) - atoms[0:1]
    return sum(weights[r][3:4] * (row == float(r)).astype(F32) for r in range(4))


def swap(value):
    return pltpu.roll(value, LANES // 2, axis=value.ndim - 1)


def half_sign():
    lane = lax.broadcasted_iota(jnp.int32, (1, LANES), 1)
    return jnp.where(lane < LANES // 2, -1.0, 1.0).astype(F32)


def rotate(value, numer, denom, sign):
    real, imag = value
    if numer == 0:
        return value
    if 4 * numer == denom:
        return (-imag, real) if sign > 0 else (imag, -real)
    angle = 2.0 * np.pi * numer / denom
    cosine, sine = float(np.cos(angle)), float(sign * np.sin(angle))
    if 8 * numer in (denom, 3 * denom):
        size = abs(cosine)
        cos_sign, sin_sign = (1 if cosine > 0 else -1), (1 if sine > 0 else -1)
        if cos_sign == sin_sign:
            return ((real - imag) * (cos_sign * size), (real + imag) * (cos_sign * size))
        return ((real + imag) * (cos_sign * size), (imag - real) * (cos_sign * size))
    return real * cosine - imag * sine, imag * cosine + real * sine


def butterfly(even, turned):
    plus = (even[0] + turned[0], even[1] + turned[1])
    return plus, (even[0] - turned[0], even[1] - turned[1])


def transform(values, sign):
    count = len(values)
    if count == 1:
        return values
    even = transform(values[0::2], sign)
    odd = transform(values[1::2], sign)
    both = [butterfly(even[k], rotate(odd[k], k, count, sign)) for k in range(count // 2)]
    return [pair[0] for pair in both] + [pair[1] for pair in both]


def regroup(low, high):
    first = lax.broadcasted_iota(jnp.int32, low.shape, 1) < LANES // 2
    crossed = swap(jnp.where(first, high, low))
    return jnp.where(first, low, crossed), jnp.where(first, crossed, high)


def pack_kernel(counts_ref, cells_ref, offsets_ref, charges_ref, out_ref):
    width = offsets_ref.shape[1]
    alive = lax.broadcasted_iota(jnp.int32, (1, width), 1) < counts_ref[0]
    atoms = jnp.concatenate(
        [
            lax.bitwise_and(cells_ref[0:1, :], XD - 1).astype(F32),
            cells_ref[1:3, :].astype(F32),
            offsets_ref[...],
            jnp.where(alive, charges_ref[...], 0.0),
            jnp.full((1, width), counts_ref[0].astype(F32)),
        ],
        0,
    )
    for copy in range(out_ref.shape[0]):
        out_ref[copy] = atoms


def atoms_of(same_ref, other_ref, slab, slot, doms):
    half = doms // 2
    return (same_ref, other_ref)[slot // half][slab * half + slot % half]


def forward_kernel(
    place_ref,
    live_ref,
    same_ref,
    other_ref,
    factors_y,
    factors_z,
    plus_ref,
    minus_ref,
    table_y,
    table_z,
    left_ref,
    right_ref,
    grid_ref,
    atoms_ref,
    digits_y,
    digits_z,
):
    step = pl.program_id(0)
    cells_x = grid_ref.shape[0]
    rows = grid_ref.shape[1] // 2
    ky_local = rows - 8
    half_slot = same_ref.shape[2] // 2
    doms = table_y.shape[2] // (2 * half_slot)
    kept = step - place_ref[2]
    kept = jnp.where((kept >= 0) & (kept < table_y.shape[0] - 1), kept, table_y.shape[0] - 1)

    @pl.when(step == 0)
    def _():
        grid_ref[...] = jnp.zeros_like(grid_ref)
        digits_y[...] = jnp.zeros_like(digits_y)
        digits_z[...] = jnp.zeros_like(digits_z)

    for slot in range(doms):
        atoms_ref[slot] = atoms_of(same_ref, other_ref, step, slot, doms)

    def add_tile(tile, halves):
        atoms = jnp.concatenate([atoms_ref[slot, :, pl.ds(part * half_slot, half_slot)] for slot, part, _ in halves], 1)
        counted = jnp.concatenate([jnp.full((1, half_slot), weight) for _, _, weight in halves], 1)
        weights = spline(atoms)
        along_x = plane_weights(atoms, weights) * (atoms[6:7] * counted)
        waves_z = atom_waves(atoms[2:3], [w[5:6] for w in weights], factors_z, digits_z.at[tile])
        waves_z = jnp.concatenate(waves_z, 0)
        waves_y = atom_waves(atoms[1:2], [w[4:5] for w in weights], factors_y, digits_y.at[tile])
        waves_y = jnp.concatenate(waves_y, 0)
        for number, (slot, part, _) in enumerate(halves):
            lanes = slice(number * half_slot, (number + 1) * half_slot)
            start = pl.multiple_of((2 * slot + part) * half_slot, half_slot)
            table_z[kept, :, pl.ds(start, half_slot)] = waves_z[:, lanes]
            table_y[kept, :, pl.ds(start, half_slot)] = waves_y[:, lanes]
        high, low = split(waves_z)
        right_ref[tile, pl.ds(0, LANES), :] = high
        right_ref[tile, pl.ds(LANES, LANES), :] = low
        for plane in range(SPAN):
            high, low = split(waves_y * along_x[plane : plane + 1])
            left_ref[tile, 0, pl.ds(2 * rows * plane, 2 * rows), :] = high
            left_ref[tile, 1, pl.ds(2 * rows * plane, 2 * rows), :] = low
        across = (((1,), (1,)), ((), ()))
        high = lax.dot_general(left_ref[tile, 0], right_ref[tile], across, preferred_element_type=F32)
        low = lax.dot_general(
            left_ref[tile, 1], right_ref[tile, pl.ds(0, LANES), :], across, preferred_element_type=F32
        )
        for plane in range(SPAN):
            span = slice(2 * rows * plane, 2 * rows * (plane + 1))
            at = lax.rem(step * XD + plane, cells_x)
            grid_ref[at] += (high[span, :LANES] + high[span, LANES:]) + low[span]

    slabs, pairs = cells_x // XD, doms // 2
    reach = [live_ref[(slot // pairs * slabs + step) * pairs + slot % pairs] for slot in range(doms)]
    reach = [sum(reach[: slot + 1]) for slot in range(doms)]
    for extra in range(doms // 2 + 1):

        @pl.when((reach[-1] + 1) // 2 == extra)
        def _(extra=extra):
            for tile in range(doms // 2):
                add_tile(tile, [(2 * tile, 0, 1.0), (2 * tile + 1, 0, 1.0)])
            for tile in range(extra):
                chosen = []
                for place in (2 * tile, 2 * tile + 1):
                    slot = sum((total <= place).astype(jnp.int32) for total in reach)
                    weight = jnp.where(slot < doms, 1.0, 0.0).astype(F32)
                    chosen.append((jnp.minimum(slot, doms - 1), 1, weight))
                add_tile(doms // 2 + tile, chosen)

    @pl.when(step == pl.num_programs(0) - 1)
    def _():
        quarter_rows = ky_local // 2
        group = min(8, quarter_rows)
        for minus, out_ref in enumerate((plus_ref, minus_ref)):
            for start in range(0, quarter_rows, group):
                values = []
                for x in range(cells_x):
                    parts = [
                        grid_ref[x, pl.ds(minus + start + offset, group), :]
                        for offset in (0, quarter_rows, rows, rows + quarter_rows)
                    ]
                    cos_cos, cos_sin = regroup(parts[0], parts[1])
                    sin_cos, sin_sin = regroup(parts[2], parts[3])
                    if minus:
                        values.append((cos_cos + sin_sin, sin_cos - cos_sin))
                    else:
                        values.append((cos_cos - sin_sin, -cos_sin - sin_cos))
                for x, value in enumerate(transform(values, -1)):
                    for part in (0, 1):
                        out_ref[part, x, pl.ds(start, group), :] = value[part]


def inverse_x_kernel(place_ref, spectrum_ref, green_ref, *refs):
    *outs, near_ref = refs
    cells_x, quarter_rows = spectrum_ref.shape[1:3]
    group = min(8, quarter_rows)
    side = 1.0 - 2.0 * place_ref[3].astype(F32)

    def rows_of(step, carry):
        rows = pl.ds(pl.multiple_of(step * group, group), group)
        values = []
        for kx in range(cells_x):
            green = green_ref[kx, rows, :]
            values.append(tuple(spectrum_ref[part, kx, rows, :] * green for part in (0, 1)))
        even = transform(values[0::2], 1)
        odd = transform([(value[0] * side, value[1] * side) for value in values[1::2]], 1)
        for x in range(cells_x // 2):
            here, there = butterfly(even[x], rotate(odd[x], x, cells_x, 1))
            wanted = [(x, here)] + ([(cells_x // 2 + x, there)] if x < 3 else [])
            for plane, value in wanted:
                for part, row_group in enumerate(regroup(value[0], value[1])):
                    near_ref[plane, part, rows, :] = row_group
        return carry

    lax.fori_loop(0, quarter_rows // group, rows_of, 0)
    for k, out_ref in enumerate(outs):
        out_ref[...] = near_ref[pl.ds(lax.bitwise_xor(place_ref[4], k) * XD, XD)]


def inverse_y_kernel(sources, place_ref, *refs):
    ins, (high_ref, low_ref) = refs[: 2 * sources], refs[2 * sources : 2 * sources + 2]
    outs, (plus_ref, minus_ref, turned_ref) = refs[2 * sources + 2 : -3], refs[-3:]
    waves = NY // 2
    halves = half_sign()
    minus_ref[:, pl.ds(0, 8), :] = jnp.zeros((XD, 8, LANES), F32)
    for number, in_ref in enumerate(ins):
        count = in_ref.shape[1]
        start = lax.bitwise_xor(place_ref[4], sources - 1 - number % sources) * count
        if number < sources:
            plus_ref[:, pl.ds(pl.multiple_of(start, 8), count), :] = in_ref[...]
        else:
            minus_ref[:, pl.ds(pl.multiple_of(start + 8, 8), count), :] = in_ref[...]
    sums = []
    for parity in (0, 1):
        parts = []
        for x in range(XD):
            plus = plus_ref[x, pl.ds(parity, waves // 2, stride=2), :]
            minus = minus_ref[x, pl.ds(7 + parity, waves // 2, stride=2), :]
            parts.append(split(jnp.concatenate([plus + minus, swap(plus - minus) * halves], 0)))
        both = jnp.concatenate([value for part in parts for value in part], 1)
        main = jnp.dot(high_ref[parity], both, preferred_element_type=F32)
        high = jnp.concatenate([part[0] for part in parts], 1)
        rest = jnp.dot(low_ref[parity], high, preferred_element_type=F32)
        sums.append(
            [
                main[:, 2 * x * LANES : (2 * x + 1) * LANES]
                + main[:, (2 * x + 1) * LANES : (2 * x + 2) * LANES]
                + rest[:, x * LANES : (x + 1) * LANES]
                for x in range(XD)
            ]
        )
    row = lax.broadcasted_iota(jnp.int32, (waves, 1), 0)
    alternate = jnp.where(row % 2 == 0, 1.0, -1.0)
    sign = jnp.where(place_ref[3] == 1, alternate, 1.0)
    for x in range(XD):
        last = minus_ref[x, pl.ds(waves, 8), :][7:8]
        even, odd = sums[0][x] + alternate * last, sums[1][x]
        total = jnp.concatenate([(even + odd) * sign, (even - odd) * sign], 0)
        turned_ref[:, x] = total.reshape(len(outs), -1, LANES)
    for k in range(len(outs)):
        outs[k][...] = turned_ref[lax.bitwise_xor(place_ref[5], k)]


def inverse_z_kernel(distances, place_ref, *refs):
    count = len(distances)
    ins, (high_ref, low_ref), (*total_refs, out_ref) = refs[:count], refs[count : count + 2], refs[count + 2 :]
    planes, rows, depth = out_ref.shape
    span = pl.ds(pl.program_id(0) * planes, planes)
    lines, tables = [], []
    for in_ref, distance in zip(ins, distances):
        lines.append(in_ref[span].reshape(planes * rows, LANES))
        start = pl.multiple_of(lax.bitwise_xor(place_ref[5], distance) * LANES, LANES)
        tables.append((high_ref[pl.ds(start, LANES), :], low_ref[pl.ds(start, LANES), :]))
    high, low = split(jnp.concatenate(lines, 1))
    table_high, table_low = (jnp.concatenate([pair[part] for pair in tables], 0) for part in (0, 1))
    total = jnp.dot(high, table_high, preferred_element_type=F32)
    total += jnp.dot(low, table_high, preferred_element_type=F32)
    total += jnp.dot(high, table_low, preferred_element_type=F32)
    total = total.reshape(planes, rows, depth)
    for total_ref in total_refs:
        total += total_ref[span]
    out_ref[...] = total


def gather_kernel(first, place_ref, same_ref, other_ref, table_y, table_z, plus_ref, minus_ref, *refs):
    *earlier, out_ref, shift_ref, fields_ref, stack_ref = refs
    step = pl.program_id(0)
    half = LANES // 2
    rows = table_y.shape[1] // 2
    ky_local = rows - 8
    width = same_ref.shape[2]
    doms = table_y.shape[2] // width
    planes = fields_ref.shape[0]
    halves = half_sign()

    @pl.when(step == 0)
    def _():
        for earlier_ref in earlier:
            out_ref[pl.ds(0, first * doms)] = earlier_ref[...]
        stack_ref[...] = jnp.zeros_like(stack_ref)
        shift_ref[...] = jnp.zeros_like(shift_ref)
        row = lax.broadcasted_iota(jnp.int32, (8, LANES), 0)

        def build(x, carry):
            plus = plus_ref[first * XD + x]
            shift_ref[pl.ds(1, ky_local), :] = minus_ref[first * XD + x]
            minus = shift_ref[pl.ds(0, ky_local), :]
            last = shift_ref[pl.ds(ky_local, 8), :][0:1]
            main = [plus + minus, swap(plus - minus) * halves]
            if 2 * ky_local < LANES:
                main.append(jnp.zeros((LANES - 2 * ky_local, LANES), F32))
            rest = jnp.where(row % 2 == 0, last, -swap(jnp.broadcast_to(last, (8, LANES))) * halves)
            rest = jnp.where(row < 6, rest, 0.0)
            rest_high = rest.astype(BF16).astype(F32)
            rest = jnp.where((row == 2) | (row == 3), rest - rest_high, rest_high)
            high, low = split(jnp.concatenate(main, 0).T)
            fields_ref[x, :, pl.ds(0, LANES)] = high
            fields_ref[x, :, pl.ds(LANES, LANES)] = low
            fields_ref[x, :, pl.ds(2 * LANES, LANES)] = high
            rest = jnp.concatenate([rest, jnp.zeros((LANES - 8, LANES), F32)], 0)
            fields_ref[x, :, pl.ds(3 * LANES, LANES)] = rest.T.astype(BF16)
            return carry

        lax.fori_loop(0, planes, build, 0)

    first_z = place_ref[1].astype(F32)
    twice = jnp.where(first_z + iota((half, 1), 0) == 0.0, 1.0, 2.0)
    fields = fields_ref[pl.ds(step * XD, SPAN)].reshape(SPAN * LANES, 4 * LANES)
    for slot in range(doms):
        lanes = pl.ds(slot * width, width)
        cosine = table_y[first + step, pl.ds(0, ky_local), lanes]
        sine = table_y[first + step, pl.ds(rows, ky_local), lanes]
        high, low = split(jnp.concatenate([cosine, sine], 0))
        for part, value in enumerate((high, high, low)):
            stack_ref[pl.ds(LANES * part, 2 * ky_local), lanes] = value
        cosine = table_y[first + step, pl.ds(ky_local, 8), lanes][0:1]
        sine = table_y[first + step, pl.ds(rows + ky_local, 8), lanes][0:1]
        row = lax.broadcasted_iota(jnp.int32, (16, width), 0)
        rest = jnp.where(row % 2 == 0, cosine, sine)
        rest_high = rest.astype(BF16).astype(F32)
        rest = jnp.where(row < 4, rest_high, jnp.where(row < 6, rest - rest_high, 0.0))
        stack_ref[pl.ds(3 * LANES, 16), lanes] = rest.astype(BF16)
    product = sum(
        jnp.dot(fields[:, part : part + 2 * LANES], stack_ref[pl.ds(part, 2 * LANES), :], preferred_element_type=F32)
        for part in (0, 2 * LANES)
    )
    for slot in range(doms):
        atoms = atoms_of(same_ref, other_ref, place_ref[2] + first + step, slot, doms)
        along_x = plane_weights(atoms, spline(atoms))
        lanes = pl.ds(slot * width, width)
        field = product[:, slot * width : (slot + 1) * width]
        total = along_x[0:1] * field[:LANES]
        for plane in range(1, SPAN):
            total += along_x[plane : plane + 1] * field[plane * LANES : (plane + 1) * LANES]
        waves = total * table_z[first + step, :, lanes]
        sampled = jnp.sum((waves[:half] - waves[half:]) * twice, axis=0, keepdims=True)
        core = place_ref[5] % 2 if slot < doms // 2 else 1 - place_ref[5] % 2
        out_ref[(first + step) * doms + 2 * (slot % (doms // 2)) + core] = sampled


def bf16_pair(table):
    high = table.astype(ml_dtypes.bfloat16)
    low = (table - high.astype(np.float64)).astype(ml_dtypes.bfloat16)
    return jnp.asarray(high), jnp.asarray(low)


def inverse_y_table():
    tables = []
    for parity in (0, 1):
        waves = np.arange(parity, NY // 2, 2)
        angle = 2.0 * np.pi * (np.outer(np.arange(NY // 2), waves) % NY) / NY
        tables.append(np.concatenate([np.cos(angle), np.sin(angle)], 1))
    return bf16_pair(np.stack(tables))


def inverse_z_table(dom_count):
    kz = np.arange(KH)
    angle = 2.0 * np.pi * (np.outer(kz, np.arange(NZ)) % NZ) / NZ
    weight = np.where(kz == 0, 1.0, 2.0)[:, None]
    parts = [weight * np.cos(angle), -weight * np.sin(angle)]
    return bf16_pair(
        np.stack([p.reshape(dom_count, KH // dom_count, NZ) for p in parts], 1).reshape(2 * KH, NZ)
    )


def whole_spec(shape):
    return pl.BlockSpec(shape, lambda *_: (0,) * len(shape))


SMALL = pl.CostEstimate(flops=10**6, bytes_accessed=10**4, transcendentals=0)
SMEM = pl.BlockSpec(memory_space=pltpu.SMEM)


def params(mib):
    return pltpu.CompilerParams(vmem_limit_bytes=mib * MIB)


def swapped(value, axis, distance):
    if distance == 0:
        return value
    return lax.ppermute(value, axis, [(i, i ^ distance) for i in range(lax.axis_size(axis))])


def per_device(base_cells, offsets, charges, bias_coupling, counts, green):
    slabs = lax.axis_size("slab")
    doms = lax.axis_size("dom")
    slab = lax.axis_index("slab")
    dom = lax.axis_index("dom")
    atoms_local = charges.shape[0]
    cells_x = XD * slabs
    ky_local = NY // slabs
    kz_local = KH // doms
    slab_half = slabs // 2
    rows_local = NY // doms
    rows = ky_local + 8
    quarter_rows = ky_local // 2
    normalize = 1.0 / (cells_x * NY * NZ)
    upper = slab // slab_half
    place = jnp.stack(
        [slab * ky_local, dom * kz_local, upper * slab_half, upper, slab % slab_half, dom]
    ).astype(jnp.int32)

    vmem = pl.BlockSpec(memory_space=pltpu.VMEM)
    atoms = pl.pallas_call(
        pack_kernel,
        in_specs=[SMEM, vmem, vmem, vmem],
        out_specs=vmem,
        out_shape=jax.ShapeDtypeStruct((slabs * doms // 2, 8, atoms_local), F32),
        name="pack",
    )(counts, base_cells, offsets, charges.reshape(1, atoms_local))
    factors_y, factors_z = pl.pallas_call(
        wave_kernel,
        in_specs=[SMEM],
        out_specs=[vmem] * 2,
        out_shape=[jax.ShapeDtypeStruct((4 * count, TERMS), BF16) for count in (rows, LANES // 2)],
        compiler_params=params(8),
        name="waves",
    )(place)
    everyone = list(range(slabs * doms))
    same = lax.all_to_all(
        atoms, ("slab", "dom"), 0, 0, axis_index_groups=[everyone[0::2], everyone[1::2]], tiled=True
    )

    def halves_beside(value):
        return jnp.concatenate([value[:, :quarter_rows], value[:, quarter_rows:]], 2) * normalize

    own = halves_beside(green)
    same, own, flipped, factors_y, factors_z = lax.optimization_barrier(
        (same, own, halves_beside(green[:, ::-1]), factors_y, factors_z)
    )
    other = swapped(same, "dom", 1)
    mirrored = lax.ppermute(flipped, "slab", [(s, slabs - 1 - s) for s in range(slabs)])

    live = jnp.concatenate([same[:, 7, 0], other[:, 7, 0]])
    live = (live > atoms_local // 2).astype(jnp.int32)
    atoms_slab = doms * atoms_local
    table_bytes = 4 * (slab_half + 1) * (2 * rows + LANES) * atoms_slab
    spectrum_bytes = 16 * cells_x * max(8, quarter_rows) * LANES
    plus, minus, table_y, table_z = pl.pallas_call(
        forward_kernel,
        grid=(slabs,),
        in_specs=[SMEM] * 2 + [vmem] * 4,
        out_specs=[vmem] * 4,
        out_shape=[
            jax.ShapeDtypeStruct((2, cells_x, quarter_rows, LANES), F32),
            jax.ShapeDtypeStruct((2, cells_x, quarter_rows, LANES), F32),
            jax.ShapeDtypeStruct((slab_half + 1, 2 * rows, atoms_slab), F32),
            jax.ShapeDtypeStruct((slab_half + 1, LANES, atoms_slab), F32),
        ],
        scratch_shapes=[
            pltpu.VMEM((doms, 2, SPAN * 2 * rows, atoms_local), BF16),
            pltpu.VMEM((doms, 2 * LANES, atoms_local), BF16),
            pltpu.VMEM((cells_x, 2 * rows, LANES), F32),
            pltpu.VMEM((doms, 8, atoms_local), F32),
            pltpu.VMEM((doms, TERMS, atoms_local), BF16),
            pltpu.VMEM((doms, TERMS, atoms_local), BF16),
        ],
        compiler_params=params(16 + (table_bytes + spectrum_bytes) // MIB),
        cost_estimate=SMALL,
        name="forward",
    )(place, live, same, other, factors_y, factors_z)

    near_planes = cells_x // 2 + 3
    lines, near = [], []
    for spectrum, influence in ((plus, own), (minus, mirrored)):
        *pieces, planes = pl.pallas_call(
            inverse_x_kernel,
            in_specs=[SMEM] + [vmem] * 2,
            out_specs=[vmem] * (slab_half + 1),
            out_shape=[jax.ShapeDtypeStruct((XD, 2, quarter_rows, LANES), F32)] * slab_half
            + [jax.ShapeDtypeStruct((near_planes, 2, quarter_rows, LANES), F32)],
            compiler_params=params(24),
            cost_estimate=SMALL,
            name="inverse_x",
        )(place, spectrum, influence)
        near.append(planes.reshape(near_planes, ky_local, LANES))
        lines += [swapped(value.reshape(XD, ky_local, LANES), "slab", k) for k, value in enumerate(pieces)][::-1]

    steps = slab_half // GATHERS

    def gather(part, place, *earlier):
        return pl.pallas_call(
            functools.partial(gather_kernel, part * steps),
            grid=(steps,),
            in_specs=[SMEM] + [vmem] * (6 + len(earlier)),
            out_specs=vmem,
            out_shape=jax.ShapeDtypeStruct(((part + 1) * steps * doms, 1, atoms_local), F32),
            scratch_shapes=[
                pltpu.VMEM((rows, LANES), F32),
                pltpu.VMEM((steps * XD + 3, LANES, 4 * LANES), BF16),
                pltpu.VMEM((4 * LANES, atoms_slab), BF16),
            ],
            compiler_params=params(12 + (table_bytes + 8 * near_planes * LANES * LANES) // MIB),
            cost_estimate=SMALL,
            name="gather",
        )(place, same, other, table_y, table_z, *near, *earlier)

    partial, *lines = lax.optimization_barrier((gather(0, place), *lines))

    high_y, low_y = inverse_y_table()
    high_z, low_z = inverse_z_table(doms)

    turned = pl.pallas_call(
        functools.partial(inverse_y_kernel, slab_half),
        in_specs=[SMEM] + [vmem] * (2 * slab_half + 2),
        out_specs=[vmem] * doms,
        out_shape=[jax.ShapeDtypeStruct((XD, rows_local, LANES), F32)] * doms,
        scratch_shapes=[
            pltpu.VMEM((XD, NY // 2, LANES), F32),
            pltpu.VMEM((XD, NY // 2 + 8, LANES), F32),
            pltpu.VMEM((doms, XD, rows_local, LANES), F32),
        ],
        compiler_params=params(32),
        cost_estimate=SMALL,
        name="inverse_y",
    )(place, *lines, high_y, low_y)
    columns = [swapped(value, "dom", k) for k, value in enumerate(turned)]

    columns[1], late_place = lax.optimization_barrier((columns[1], place))
    for part in range(1, GATHERS):
        partial = gather(part, late_place, partial)
    partial, columns[0] = lax.optimization_barrier((partial, columns[0]))
    members = slab_half * doms
    sampled = lax.all_to_all(
        partial.reshape(members, atoms_local),
        ("slab", "dom"),
        0,
        0,
        axis_index_groups=[list(range(members)), list(range(members, 2 * members))],
        tiled=True,
    )
    alive = jnp.arange(atoms_local, dtype=jnp.int32) < counts[0]
    gradient = jnp.where(alive, bias_coupling * jnp.sum(sampled, 0), 0.0)

    total = []
    for distances in (range(doms // 2), range(doms - 1, doms // 2 - 1, -1)):
        last = len(total) == 1
        total = [
            pl.pallas_call(
                functools.partial(inverse_z_kernel, distances),
                grid=(XD // DEPTH if last else 1,),
                in_specs=[SMEM] + [vmem] * (len(distances) + 2 + len(total)),
                out_specs=pl.BlockSpec((DEPTH, rows_local, NZ), lambda step: (step, 0, 0)) if last else vmem,
                out_shape=jax.ShapeDtypeStruct((XD, rows_local, NZ), F32),
                compiler_params=params(24),
                cost_estimate=SMALL,
                name="inverse_z",
            )(place, *[columns[k] for k in distances], high_z, low_z, *total)
        ]
    potential = total[0]
    return (potential, gradient)


def solution(mesh):
    placed = (
        P(None, ("slab", "dom")),
        P(None, ("slab", "dom")),
        P(("slab", "dom")),
        P(("slab", "dom")),
        P(("slab", "dom")),
        P(None, "slab", "dom"),
    )
    return jax.shard_map(
        per_device,
        mesh=mesh,
        in_specs=placed,
        out_specs=(P("slab", "dom", None), P(("slab", "dom"))),
        check_vma=False,
    )
```

```python
import functools

import jax
import jax.numpy as jnp
import ml_dtypes
import numpy as np
from jax import lax
from jax.experimental import pallas as pl
from jax.experimental.pallas import tpu as pltpu
from jax.sharding import PartitionSpec as P

XD = 4
NY = 512
NZ = 512
KH = NZ // 2
LANES = 128
SPAN = XD + 3
DEPTH = 2
GATHERS = 2
MIB = 1 << 20
BF16 = jnp.bfloat16
F32 = jnp.float32


def polynomial(function, terms):
    nodes = 0.125 * (1.0 - np.cos(np.pi * (np.arange(64) + 0.5) / 64))
    powers = nodes[:, None] ** np.arange(terms)[None, :]
    return [float(v) for v in np.linalg.lstsq(powers, function(np.sqrt(nodes)), rcond=None)[0]]


SINE_TERMS = polynomial(lambda r: np.sin(np.pi * r) / r, 6)
COSINE_TERMS = polynomial(lambda r: np.cos(np.pi * r), 6)


def horner(terms, square):
    total = jnp.full_like(square, terms[-1])
    for term in terms[-2::-1]:
        total = total * square + term
    return total


def turn(fraction):
    left = fraction - jnp.floor(fraction + 0.5)
    square = left * left
    sine = left * horner(SINE_TERMS, square)
    cosine = horner(COSINE_TERMS, square)
    return 1.0 - 2.0 * sine * sine, 2.0 * sine * cosine


def spline(frac):
    inner = 1.0 - frac
    square = frac * frac
    cube = square * frac
    sixth = 1.0 / 6.0
    return (
        inner * inner * inner * sixth,
        (3.0 * cube - 6.0 * square + 4.0) * sixth,
        (-3.0 * cube + 3.0 * square + 3.0 * frac + 1.0) * sixth,
        cube * sixth,
    )


def split(value):
    high = value.astype(BF16)
    return high, (value - high.astype(F32)).astype(BF16)


def iota(shape, axis):
    return lax.broadcasted_iota(jnp.int32, shape, axis).astype(F32)


RADIX = 16
DIGITS = 32
TERMS = 256


def wave_factors(first, rows, length):
    lane = lax.broadcasted_iota(jnp.int32, (rows, TERMS), 1)
    section = lane // DIGITS
    digit = (lane % DIGITS).astype(F32) * jnp.where(section < 2, float(RADIX), 1.0)
    parts = []
    for value in turn((first + iota((rows, TERMS), 0)) * digit * (1.0 / length)):
        high = value.astype(BF16).astype(F32)
        parts.append(jnp.where((section == 1) | (section == 3), value - high, high))
    upper, lower = section < 2, (section >= 2) & (section < 5)
    masked = [jnp.where(mask, part, 0.0) for mask in (upper, lower) for part in parts]
    return jnp.concatenate(masked, 0).astype(BF16)


def wave_kernel(place_ref, out_y_ref, out_z_ref):
    out_y_ref[...] = wave_factors(place_ref[0].astype(F32), out_y_ref.shape[0] // 4, NY)
    out_z_ref[...] = wave_factors(place_ref[1].astype(F32), out_z_ref.shape[0] // 4, NZ)


def atom_waves(base, weights, factors_ref, digits_ref):
    width = base.shape[1]
    high_digit = jnp.floor(base * (1.0 / RADIX))
    row = iota((DIGITS, width), 0)
    chosen = jnp.where(row == high_digit, 1.0, 0.0).astype(BF16)
    step = row - (base - RADIX * high_digit)
    spread = jnp.where(step == 3.0, weights[3], 0.0)
    for r in (2, 1, 0):
        spread = jnp.where(step == float(r), weights[r], spread)
    high, low = split(spread)
    for section, value in enumerate((chosen, chosen, high, high, low)):
        digits_ref[pl.ds(DIGITS * section, DIGITS), :] = value
    product = jnp.dot(factors_ref[...], digits_ref[...], preferred_element_type=F32)
    rows = product.shape[0] // 4
    cos_a, sin_a, cos_b, sin_b = (product[i * rows : (i + 1) * rows] for i in range(4))
    return cos_a * cos_b - sin_a * sin_b, sin_a * cos_b + cos_a * sin_b


def plane_weights(atoms, weights):
    row = iota((8, atoms.shape[1]), 0) - atoms[0:1]
    return sum(weights[r][3:4] * (row == float(r)).astype(F32) for r in range(4))


def swap(value):
    return pltpu.roll(value, LANES // 2, axis=value.ndim - 1)


def half_sign():
    lane = lax.broadcasted_iota(jnp.int32, (1, LANES), 1)
    return jnp.where(lane < LANES // 2, -1.0, 1.0).astype(F32)


def rotate(value, numer, denom, sign):
    real, imag = value
    if numer == 0:
        return value
    if 4 * numer == denom:
        return (-imag, real) if sign > 0 else (imag, -real)
    angle = 2.0 * np.pi * numer / denom
    cosine, sine = float(np.cos(angle)), float(sign * np.sin(angle))
    if 8 * numer in (denom, 3 * denom):
        size = abs(cosine)
        cos_sign, sin_sign = (1 if cosine > 0 else -1), (1 if sine > 0 else -1)
        if cos_sign == sin_sign:
            return ((real - imag) * (cos_sign * size), (real + imag) * (cos_sign * size))
        return ((real + imag) * (cos_sign * size), (imag - real) * (cos_sign * size))
    return real * cosine - imag * sine, imag * cosine + real * sine


def butterfly(even, turned):
    plus = (even[0] + turned[0], even[1] + turned[1])
    return plus, (even[0] - turned[0], even[1] - turned[1])


def transform(values, sign):
    count = len(values)
    if count == 1:
        return values
    even = transform(values[0::2], sign)
    odd = transform(values[1::2], sign)
    both = [butterfly(even[k], rotate(odd[k], k, count, sign)) for k in range(count // 2)]
    return [pair[0] for pair in both] + [pair[1] for pair in both]


def regroup(low, high):
    first = lax.broadcasted_iota(jnp.int32, low.shape, 1) < LANES // 2
    crossed = swap(jnp.where(first, high, low))
    return jnp.where(first, low, crossed), jnp.where(first, crossed, high)


def pack_kernel(counts_ref, cells_ref, offsets_ref, charges_ref, out_ref):
    width = offsets_ref.shape[1]
    alive = lax.broadcasted_iota(jnp.int32, (1, width), 1) < counts_ref[0]
    atoms = jnp.concatenate(
        [
            lax.bitwise_and(cells_ref[0:1, :], XD - 1).astype(F32),
            cells_ref[1:3, :].astype(F32),
            offsets_ref[...],
            jnp.where(alive, charges_ref[...], 0.0),
            jnp.full((1, width), counts_ref[0].astype(F32)),
        ],
        0,
    )
    for copy in range(out_ref.shape[0]):
        out_ref[copy] = atoms


def atoms_of(same_ref, other_ref, slab, slot, doms):
    half = doms // 2
    return (same_ref, other_ref)[slot // half][slab * half + slot % half]


def forward_kernel(
    place_ref,
    live_ref,
    same_ref,
    other_ref,
    factors_y,
    factors_z,
    plus_ref,
    minus_ref,
    table_y,
    table_z,
    left_ref,
    right_ref,
    grid_ref,
    atoms_ref,
    digits_y,
    digits_z,
):
    step = pl.program_id(0)
    cells_x = grid_ref.shape[0]
    rows = grid_ref.shape[1] // 2
    ky_local = rows - 8
    half_slot = same_ref.shape[2] // 2
    doms = table_y.shape[2] // (2 * half_slot)
    kept = step - place_ref[2]
    kept = jnp.where((kept >= 0) & (kept < table_y.shape[0] - 1), kept, table_y.shape[0] - 1)

    @pl.when(step == 0)
    def _():
        grid_ref[...] = jnp.zeros_like(grid_ref)
        digits_y[...] = jnp.zeros_like(digits_y)
        digits_z[...] = jnp.zeros_like(digits_z)

    for slot in range(doms):
        atoms_ref[slot] = atoms_of(same_ref, other_ref, step, slot, doms)

    def build_tile(tile, halves):
        atoms = jnp.concatenate([atoms_ref[slot, :, pl.ds(part * half_slot, half_slot)] for slot, part, _ in halves], 1)
        counted = jnp.concatenate([jnp.full((1, half_slot), weight) for _, _, weight in halves], 1)
        weights = spline(atoms)
        along_x = plane_weights(atoms, weights) * (atoms[6:7] * counted)
        waves_z = atom_waves(atoms[2:3], [w[5:6] for w in weights], factors_z, digits_z.at[tile])
        waves_z = jnp.concatenate(waves_z, 0)
        waves_y = atom_waves(atoms[1:2], [w[4:5] for w in weights], factors_y, digits_y.at[tile])
        waves_y = jnp.concatenate(waves_y, 0)
        for number, (slot, part, _) in enumerate(halves):
            lanes = slice(number * half_slot, (number + 1) * half_slot)
            start = pl.multiple_of((2 * slot + part) * half_slot, half_slot)
            table_z[kept, :, pl.ds(start, half_slot)] = waves_z[:, lanes]
            table_y[kept, :, pl.ds(start, half_slot)] = waves_y[:, lanes]
        high, low = split(waves_z)
        lanes = pl.ds(2 * half_slot * tile, 2 * half_slot)
        right_ref[pl.ds(0, LANES), lanes] = high
        right_ref[pl.ds(LANES, LANES), lanes] = low
        for plane in range(SPAN):
            first = 4 * rows * plane
            high, low = split(waves_y * along_x[plane : plane + 1])
            left_ref[pl.ds(first, 2 * rows), lanes] = high
            left_ref[pl.ds(first + 2 * rows, 2 * rows), lanes] = low

    def add_tiles(count):
        lanes = pl.ds(0, 2 * half_slot * count)
        product = lax.dot_general(
            left_ref[:, lanes], right_ref[:, lanes], (((1,), (1,)), ((), ())), preferred_element_type=F32
        )
        for plane in range(SPAN):
            first = 4 * rows * plane
            high, low = product[first : first + 2 * rows], product[first + 2 * rows : first + 4 * rows]
            at = lax.rem(step * XD + plane, cells_x)
            grid_ref[at] += (high[:, :LANES] + high[:, LANES:]) + (low[:, :LANES] + low[:, LANES:])

    slabs, pairs = cells_x // XD, doms // 2
    reach = [live_ref[(slot // pairs * slabs + step) * pairs + slot % pairs] for slot in range(doms)]
    reach = [sum(reach[: slot + 1]) for slot in range(doms)]
    for extra in range(doms // 2 + 1):

        @pl.when((reach[-1] + 1) // 2 == extra)
        def _(extra=extra):
            for tile in range(doms // 2):
                build_tile(tile, [(2 * tile, 0, 1.0), (2 * tile + 1, 0, 1.0)])
            for tile in range(extra):
                chosen = []
                for place in (2 * tile, 2 * tile + 1):
                    slot = sum((total <= place).astype(jnp.int32) for total in reach)
                    weight = jnp.where(slot < doms, 1.0, 0.0).astype(F32)
                    chosen.append((jnp.minimum(slot, doms - 1), 1, weight))
                build_tile(doms // 2 + tile, chosen)
            add_tiles(doms // 2 + extra)

    @pl.when(step == pl.num_programs(0) - 1)
    def _():
        quarter_rows = ky_local // 2
        group = min(8, quarter_rows)
        for minus, out_ref in enumerate((plus_ref, minus_ref)):
            for start in range(0, quarter_rows, group):
                values = []
                for x in range(cells_x):
                    parts = [
                        grid_ref[x, pl.ds(minus + start + offset, group), :]
                        for offset in (0, quarter_rows, rows, rows + quarter_rows)
                    ]
                    cos_cos, cos_sin = regroup(parts[0], parts[1])
                    sin_cos, sin_sin = regroup(parts[2], parts[3])
                    if minus:
                        values.append((cos_cos + sin_sin, sin_cos - cos_sin))
                    else:
                        values.append((cos_cos - sin_sin, -cos_sin - sin_cos))
                for x, value in enumerate(transform(values, -1)):
                    for part in (0, 1):
                        out_ref[part, x, pl.ds(start, group), :] = value[part]


def inverse_x_kernel(place_ref, spectrum_ref, green_ref, *refs):
    *outs, near_ref = refs
    cells_x, quarter_rows = spectrum_ref.shape[1:3]
    group = min(8, quarter_rows)
    side = 1.0 - 2.0 * place_ref[3].astype(F32)

    def rows_of(step, carry):
        rows = pl.ds(pl.multiple_of(step * group, group), group)
        values = []
        for kx in range(cells_x):
            green = green_ref[kx, rows, :]
            values.append(tuple(spectrum_ref[part, kx, rows, :] * green for part in (0, 1)))
        even = transform(values[0::2], 1)
        odd = transform([(value[0] * side, value[1] * side) for value in values[1::2]], 1)
        for x in range(cells_x // 2):
            here, there = butterfly(even[x], rotate(odd[x], x, cells_x, 1))
            wanted = [(x, here)] + ([(cells_x // 2 + x, there)] if x < 3 else [])
            for plane, value in wanted:
                for part, row_group in enumerate(regroup(value[0], value[1])):
                    near_ref[plane, part, rows, :] = row_group
        return carry

    lax.fori_loop(0, quarter_rows // group, rows_of, 0)
    for k, out_ref in enumerate(outs):
        out_ref[...] = near_ref[pl.ds(lax.bitwise_xor(place_ref[4], k) * XD, XD)]


def inverse_y_kernel(sources, place_ref, *refs):
    ins, (high_ref, low_ref) = refs[: 2 * sources], refs[2 * sources : 2 * sources + 2]
    outs, (plus_ref, minus_ref, turned_ref) = refs[2 * sources + 2 : -3], refs[-3:]
    waves = NY // 2
    halves = half_sign()
    minus_ref[:, pl.ds(0, 8), :] = jnp.zeros((XD, 8, LANES), F32)
    for number, in_ref in enumerate(ins):
        count = in_ref.shape[1]
        start = lax.bitwise_xor(place_ref[4], sources - 1 - number % sources) * count
        if number < sources:
            plus_ref[:, pl.ds(pl.multiple_of(start, 8), count), :] = in_ref[...]
        else:
            minus_ref[:, pl.ds(pl.multiple_of(start + 8, 8), count), :] = in_ref[...]
    sums = []
    for parity in (0, 1):
        parts = []
        for x in range(XD):
            plus = plus_ref[x, pl.ds(parity, waves // 2, stride=2), :]
            minus = minus_ref[x, pl.ds(7 + parity, waves // 2, stride=2), :]
            parts.append(split(jnp.concatenate([plus + minus, swap(plus - minus) * halves], 0)))
        both = jnp.concatenate([value for part in parts for value in part], 1)
        main = jnp.dot(high_ref[parity], both, preferred_element_type=F32)
        high = jnp.concatenate([part[0] for part in parts], 1)
        rest = jnp.dot(low_ref[parity], high, preferred_element_type=F32)
        sums.append(
            [
                main[:, 2 * x * LANES : (2 * x + 1) * LANES]
                + main[:, (2 * x + 1) * LANES : (2 * x + 2) * LANES]
                + rest[:, x * LANES : (x + 1) * LANES]
                for x in range(XD)
            ]
        )
    row = lax.broadcasted_iota(jnp.int32, (waves, 1), 0)
    alternate = jnp.where(row % 2 == 0, 1.0, -1.0)
    sign = jnp.where(place_ref[3] == 1, alternate, 1.0)
    for x in range(XD):
        last = minus_ref[x, pl.ds(waves, 8), :][7:8]
        even, odd = sums[0][x] + alternate * last, sums[1][x]
        total = jnp.concatenate([(even + odd) * sign, (even - odd) * sign], 0)
        turned_ref[:, x] = total.reshape(len(outs), -1, LANES)
    for k in range(len(outs)):
        outs[k][...] = turned_ref[lax.bitwise_xor(place_ref[5], k)]


def inverse_z_kernel(distances, place_ref, *refs):
    count = len(distances)
    ins, (high_ref, low_ref), (*total_refs, out_ref) = refs[:count], refs[count : count + 2], refs[count + 2 :]
    planes, rows, depth = out_ref.shape
    span = pl.ds(pl.program_id(0) * planes, planes)
    lines, tables = [], []
    for in_ref, distance in zip(ins, distances):
        lines.append(in_ref[span].reshape(planes * rows, LANES))
        start = pl.multiple_of(lax.bitwise_xor(place_ref[5], distance) * LANES, LANES)
        tables.append((high_ref[pl.ds(start, LANES), :], low_ref[pl.ds(start, LANES), :]))
    high, low = split(jnp.concatenate(lines, 1))
    table_high, table_low = (jnp.concatenate([pair[part] for pair in tables], 0) for part in (0, 1))
    total = jnp.dot(high, table_high, preferred_element_type=F32)
    total += jnp.dot(low, table_high, preferred_element_type=F32)
    total += jnp.dot(high, table_low, preferred_element_type=F32)
    total = total.reshape(planes, rows, depth)
    for total_ref in total_refs:
        total += total_ref[span]
    out_ref[...] = total


def gather_kernel(first, place_ref, same_ref, other_ref, table_y, table_z, plus_ref, minus_ref, *refs):
    *earlier, out_ref, shift_ref, fields_ref, stack_ref = refs
    step = pl.program_id(0)
    half = LANES // 2
    rows = table_y.shape[1] // 2
    ky_local = rows - 8
    width = same_ref.shape[2]
    doms = table_y.shape[2] // width
    planes = fields_ref.shape[0]
    halves = half_sign()

    @pl.when(step == 0)
    def _():
        for earlier_ref in earlier:
            out_ref[pl.ds(0, first * doms)] = earlier_ref[...]
        stack_ref[...] = jnp.zeros_like(stack_ref)
        shift_ref[...] = jnp.zeros_like(shift_ref)
        row = lax.broadcasted_iota(jnp.int32, (8, LANES), 0)

        def build(x, carry):
            plus = plus_ref[first * XD + x]
            shift_ref[pl.ds(1, ky_local), :] = minus_ref[first * XD + x]
            minus = shift_ref[pl.ds(0, ky_local), :]
            last = shift_ref[pl.ds(ky_local, 8), :][0:1]
            main = [plus + minus, swap(plus - minus) * halves]
            if 2 * ky_local < LANES:
                main.append(jnp.zeros((LANES - 2 * ky_local, LANES), F32))
            rest = jnp.where(row % 2 == 0, last, -swap(jnp.broadcast_to(last, (8, LANES))) * halves)
            rest = jnp.where(row < 6, rest, 0.0)
            rest_high = rest.astype(BF16).astype(F32)
            rest = jnp.where((row == 2) | (row == 3), rest - rest_high, rest_high)
            high, low = split(jnp.concatenate(main, 0).T)
            fields_ref[x, :, pl.ds(0, LANES)] = high
            fields_ref[x, :, pl.ds(LANES, LANES)] = low
            fields_ref[x, :, pl.ds(2 * LANES, LANES)] = high
            rest = jnp.concatenate([rest, jnp.zeros((LANES - 8, LANES), F32)], 0)
            fields_ref[x, :, pl.ds(3 * LANES, LANES)] = rest.T.astype(BF16)
            return carry

        lax.fori_loop(0, planes, build, 0)

    first_z = place_ref[1].astype(F32)
    twice = jnp.where(first_z + iota((half, 1), 0) == 0.0, 1.0, 2.0)
    fields = fields_ref[pl.ds(step * XD, SPAN)].reshape(SPAN * LANES, 4 * LANES)
    for slot in range(doms):
        lanes = pl.ds(slot * width, width)
        cosine = table_y[first + step, pl.ds(0, ky_local), lanes]
        sine = table_y[first + step, pl.ds(rows, ky_local), lanes]
        high, low = split(jnp.concatenate([cosine, sine], 0))
        for part, value in enumerate((high, high, low)):
            stack_ref[pl.ds(LANES * part, 2 * ky_local), lanes] = value
        cosine = table_y[first + step, pl.ds(ky_local, 8), lanes][0:1]
        sine = table_y[first + step, pl.ds(rows + ky_local, 8), lanes][0:1]
        row = lax.broadcasted_iota(jnp.int32, (16, width), 0)
        rest = jnp.where(row % 2 == 0, cosine, sine)
        rest_high = rest.astype(BF16).astype(F32)
        rest = jnp.where(row < 4, rest_high, jnp.where(row < 6, rest - rest_high, 0.0))
        stack_ref[pl.ds(3 * LANES, 16), lanes] = rest.astype(BF16)
    product = sum(
        jnp.dot(fields[:, part : part + 2 * LANES], stack_ref[pl.ds(part, 2 * LANES), :], preferred_element_type=F32)
        for part in (0, 2 * LANES)
    )
    for slot in range(doms):
        atoms = atoms_of(same_ref, other_ref, place_ref[2] + first + step, slot, doms)
        along_x = plane_weights(atoms, spline(atoms))
        lanes = pl.ds(slot * width, width)
        field = product[:, slot * width : (slot + 1) * width]
        total = along_x[0:1] * field[:LANES]
        for plane in range(1, SPAN):
            total += along_x[plane : plane + 1] * field[plane * LANES : (plane + 1) * LANES]
        waves = total * table_z[first + step, :, lanes]
        sampled = jnp.sum((waves[:half] - waves[half:]) * twice, axis=0, keepdims=True)
        core = place_ref[5] % 2 if slot < doms // 2 else 1 - place_ref[5] % 2
        out_ref[(first + step) * doms + 2 * (slot % (doms // 2)) + core] = sampled


def bf16_pair(table):
    high = table.astype(ml_dtypes.bfloat16)
    low = (table - high.astype(np.float64)).astype(ml_dtypes.bfloat16)
    return jnp.asarray(high), jnp.asarray(low)


def inverse_y_table():
    tables = []
    for parity in (0, 1):
        waves = np.arange(parity, NY // 2, 2)
        angle = 2.0 * np.pi * (np.outer(np.arange(NY // 2), waves) % NY) / NY
        tables.append(np.concatenate([np.cos(angle), np.sin(angle)], 1))
    return bf16_pair(np.stack(tables))


def inverse_z_table(dom_count):
    kz = np.arange(KH)
    angle = 2.0 * np.pi * (np.outer(kz, np.arange(NZ)) % NZ) / NZ
    weight = np.where(kz == 0, 1.0, 2.0)[:, None]
    parts = [weight * np.cos(angle), -weight * np.sin(angle)]
    return bf16_pair(
        np.stack([p.reshape(dom_count, KH // dom_count, NZ) for p in parts], 1).reshape(2 * KH, NZ)
    )


def whole_spec(shape):
    return pl.BlockSpec(shape, lambda *_: (0,) * len(shape))


SMALL = pl.CostEstimate(flops=10**6, bytes_accessed=10**4, transcendentals=0)
SMEM = pl.BlockSpec(memory_space=pltpu.SMEM)


def params(mib):
    return pltpu.CompilerParams(vmem_limit_bytes=mib * MIB)


def swapped(value, axis, distance):
    if distance == 0:
        return value
    return lax.ppermute(value, axis, [(i, i ^ distance) for i in range(lax.axis_size(axis))])


def per_device(base_cells, offsets, charges, bias_coupling, counts, green):
    slabs = lax.axis_size("slab")
    doms = lax.axis_size("dom")
    slab = lax.axis_index("slab")
    dom = lax.axis_index("dom")
    atoms_local = charges.shape[0]
    cells_x = XD * slabs
    ky_local = NY // slabs
    kz_local = KH // doms
    slab_half = slabs // 2
    rows_local = NY // doms
    rows = ky_local + 8
    quarter_rows = ky_local // 2
    normalize = 1.0 / (cells_x * NY * NZ)
    upper = slab // slab_half
    place = jnp.stack(
        [slab * ky_local, dom * kz_local, upper * slab_half, upper, slab % slab_half, dom]
    ).astype(jnp.int32)

    vmem = pl.BlockSpec(memory_space=pltpu.VMEM)
    atoms = pl.pallas_call(
        pack_kernel,
        in_specs=[SMEM, vmem, vmem, vmem],
        out_specs=vmem,
        out_shape=jax.ShapeDtypeStruct((slabs * doms // 2, 8, atoms_local), F32),
        name="pack",
    )(counts, base_cells, offsets, charges.reshape(1, atoms_local))
    factors_y, factors_z = pl.pallas_call(
        wave_kernel,
        in_specs=[SMEM],
        out_specs=[vmem] * 2,
        out_shape=[jax.ShapeDtypeStruct((4 * count, TERMS), BF16) for count in (rows, LANES // 2)],
        compiler_params=params(8),
        name="waves",
    )(place)
    everyone = list(range(slabs * doms))
    same = lax.all_to_all(
        atoms, ("slab", "dom"), 0, 0, axis_index_groups=[everyone[0::2], everyone[1::2]], tiled=True
    )

    def halves_beside(value):
        return jnp.concatenate([value[:, :quarter_rows], value[:, quarter_rows:]], 2) * normalize

    own = halves_beside(green)
    same, own, flipped, factors_y, factors_z = lax.optimization_barrier(
        (same, own, halves_beside(green[:, ::-1]), factors_y, factors_z)
    )
    other = swapped(same, "dom", 1)
    mirrored = lax.ppermute(flipped, "slab", [(s, slabs - 1 - s) for s in range(slabs)])

    live = jnp.concatenate([same[:, 7, 0], other[:, 7, 0]])
    live = (live > atoms_local // 2).astype(jnp.int32)
    atoms_slab = doms * atoms_local
    table_bytes = 4 * (slab_half + 1) * (2 * rows + LANES) * atoms_slab
    spectrum_bytes = 16 * cells_x * max(8, quarter_rows) * LANES
    plus, minus, table_y, table_z = pl.pallas_call(
        forward_kernel,
        grid=(slabs,),
        in_specs=[SMEM] * 2 + [vmem] * 4,
        out_specs=[vmem] * 4,
        out_shape=[
            jax.ShapeDtypeStruct((2, cells_x, quarter_rows, LANES), F32),
            jax.ShapeDtypeStruct((2, cells_x, quarter_rows, LANES), F32),
            jax.ShapeDtypeStruct((slab_half + 1, 2 * rows, atoms_slab), F32),
            jax.ShapeDtypeStruct((slab_half + 1, LANES, atoms_slab), F32),
        ],
        scratch_shapes=[
            pltpu.VMEM((SPAN * 4 * rows, atoms_slab), BF16),
            pltpu.VMEM((2 * LANES, atoms_slab), BF16),
            pltpu.VMEM((cells_x, 2 * rows, LANES), F32),
            pltpu.VMEM((doms, 8, atoms_local), F32),
            pltpu.VMEM((doms, TERMS, atoms_local), BF16),
            pltpu.VMEM((doms, TERMS, atoms_local), BF16),
        ],
        compiler_params=params(16 + (table_bytes + spectrum_bytes) // MIB),
        cost_estimate=SMALL,
        name="forward",
    )(place, live, same, other, factors_y, factors_z)

    near_planes = cells_x // 2 + 3
    lines, near = [], []
    for spectrum, influence in ((plus, own), (minus, mirrored)):
        *pieces, planes = pl.pallas_call(
            inverse_x_kernel,
            in_specs=[SMEM] + [vmem] * 2,
            out_specs=[vmem] * (slab_half + 1),
            out_shape=[jax.ShapeDtypeStruct((XD, 2, quarter_rows, LANES), F32)] * slab_half
            + [jax.ShapeDtypeStruct((near_planes, 2, quarter_rows, LANES), F32)],
            compiler_params=params(24),
            cost_estimate=SMALL,
            name="inverse_x",
        )(place, spectrum, influence)
        near.append(planes.reshape(near_planes, ky_local, LANES))
        lines += [swapped(value.reshape(XD, ky_local, LANES), "slab", k) for k, value in enumerate(pieces)][::-1]

    steps = slab_half // GATHERS

    def gather(part, place, *earlier):
        return pl.pallas_call(
            functools.partial(gather_kernel, part * steps),
            grid=(steps,),
            in_specs=[SMEM] + [vmem] * (6 + len(earlier)),
            out_specs=vmem,
            out_shape=jax.ShapeDtypeStruct(((part + 1) * steps * doms, 1, atoms_local), F32),
            scratch_shapes=[
                pltpu.VMEM((rows, LANES), F32),
                pltpu.VMEM((steps * XD + 3, LANES, 4 * LANES), BF16),
                pltpu.VMEM((4 * LANES, atoms_slab), BF16),
            ],
            compiler_params=params(12 + (table_bytes + 8 * near_planes * LANES * LANES) // MIB),
            cost_estimate=SMALL,
            name="gather",
        )(place, same, other, table_y, table_z, *near, *earlier)

    partial, *lines = lax.optimization_barrier((gather(0, place), *lines))

    high_y, low_y = inverse_y_table()
    high_z, low_z = inverse_z_table(doms)

    turned = pl.pallas_call(
        functools.partial(inverse_y_kernel, slab_half),
        in_specs=[SMEM] + [vmem] * (2 * slab_half + 2),
        out_specs=[vmem] * doms,
        out_shape=[jax.ShapeDtypeStruct((XD, rows_local, LANES), F32)] * doms,
        scratch_shapes=[
            pltpu.VMEM((XD, NY // 2, LANES), F32),
            pltpu.VMEM((XD, NY // 2 + 8, LANES), F32),
            pltpu.VMEM((doms, XD, rows_local, LANES), F32),
        ],
        compiler_params=params(32),
        cost_estimate=SMALL,
        name="inverse_y",
    )(place, *lines, high_y, low_y)
    columns = [swapped(value, "dom", k) for k, value in enumerate(turned)]

    columns[1], late_place = lax.optimization_barrier((columns[1], place))
    for part in range(1, GATHERS):
        partial = gather(part, late_place, partial)
    partial, columns[0] = lax.optimization_barrier((partial, columns[0]))
    members = slab_half * doms
    sampled = lax.all_to_all(
        partial.reshape(members, atoms_local),
        ("slab", "dom"),
        0,
        0,
        axis_index_groups=[list(range(members)), list(range(members, 2 * members))],
        tiled=True,
    )
    alive = jnp.arange(atoms_local, dtype=jnp.int32) < counts[0]
    gradient = jnp.where(alive, bias_coupling * jnp.sum(sampled, 0), 0.0)

    total = []
    for distances in (range(doms // 2), range(doms - 1, doms // 2 - 1, -1)):
        last = len(total) == 1
        total = [
            pl.pallas_call(
                functools.partial(inverse_z_kernel, distances),
                grid=(XD // DEPTH if last else 1,),
                in_specs=[SMEM] + [vmem] * (len(distances) + 2 + len(total)),
                out_specs=pl.BlockSpec((DEPTH, rows_local, NZ), lambda step: (step, 0, 0)) if last else vmem,
                out_shape=jax.ShapeDtypeStruct((XD, rows_local, NZ), F32),
                compiler_params=params(24),
                cost_estimate=SMALL,
                name="inverse_z",
            )(place, *[columns[k] for k in distances], high_z, low_z, *total)
        ]
    potential = total[0]
    return (potential, gradient)


def solution(mesh):
    placed = (
        P(None, ("slab", "dom")),
        P(None, ("slab", "dom")),
        P(("slab", "dom")),
        P(("slab", "dom")),
        P(("slab", "dom")),
        P(None, "slab", "dom"),
    )
    return jax.shard_map(
        per_device,
        mesh=mesh,
        in_specs=placed,
        out_specs=(P("slab", "dom", None), P(("slab", "dom"))),
        check_vma=False,
    )
```

```python
import functools

import jax
import jax.numpy as jnp
import ml_dtypes
import numpy as np
from jax import lax
from jax.experimental import pallas as pl
from jax.experimental.pallas import tpu as pltpu
from jax.sharding import PartitionSpec as P

XD = 4
NY = 512
NZ = 512
KH = NZ // 2
LANES = 128
SPAN = XD + 3
DEPTH = 2
GATHERS = 2
MIB = 1 << 20
BF16 = jnp.bfloat16
F32 = jnp.float32


def polynomial(function, terms):
    nodes = 0.125 * (1.0 - np.cos(np.pi * (np.arange(64) + 0.5) / 64))
    powers = nodes[:, None] ** np.arange(terms)[None, :]
    return [float(v) for v in np.linalg.lstsq(powers, function(np.sqrt(nodes)), rcond=None)[0]]


SINE_TERMS = polynomial(lambda r: np.sin(np.pi * r) / r, 6)
COSINE_TERMS = polynomial(lambda r: np.cos(np.pi * r), 6)


def horner(terms, square):
    total = jnp.full_like(square, terms[-1])
    for term in terms[-2::-1]:
        total = total * square + term
    return total


def turn(fraction):
    left = fraction - jnp.floor(fraction + 0.5)
    square = left * left
    sine = left * horner(SINE_TERMS, square)
    cosine = horner(COSINE_TERMS, square)
    return 1.0 - 2.0 * sine * sine, 2.0 * sine * cosine


def spline(frac):
    inner = 1.0 - frac
    square = frac * frac
    cube = square * frac
    sixth = 1.0 / 6.0
    return (
        inner * inner * inner * sixth,
        (3.0 * cube - 6.0 * square + 4.0) * sixth,
        (-3.0 * cube + 3.0 * square + 3.0 * frac + 1.0) * sixth,
        cube * sixth,
    )


def split(value):
    high = value.astype(BF16)
    return high, (value - high.astype(F32)).astype(BF16)


def iota(shape, axis):
    return lax.broadcasted_iota(jnp.int32, shape, axis).astype(F32)


RADIX = 16
DIGITS = 32
TERMS = 256


def wave_factors(first, rows, length):
    lane = lax.broadcasted_iota(jnp.int32, (rows, TERMS), 1)
    section = lane // DIGITS
    digit = (lane % DIGITS).astype(F32) * jnp.where(section < 2, float(RADIX), 1.0)
    parts = []
    for value in turn((first + iota((rows, TERMS), 0)) * digit * (1.0 / length)):
        high = value.astype(BF16).astype(F32)
        parts.append(jnp.where((section == 1) | (section == 3), value - high, high))
    upper, lower = section < 2, (section >= 2) & (section < 5)
    masked = [jnp.where(mask, part, 0.0) for mask in (upper, lower) for part in parts]
    return jnp.concatenate(masked, 0).astype(BF16)


def wave_kernel(place_ref, out_y_ref, out_z_ref):
    out_y_ref[...] = wave_factors(place_ref[0].astype(F32), out_y_ref.shape[0] // 4, NY)
    out_z_ref[...] = wave_factors(place_ref[1].astype(F32), out_z_ref.shape[0] // 4, NZ)


def atom_waves(base, weights, factors_ref, digits_ref):
    width = base.shape[1]
    high_digit = jnp.floor(base * (1.0 / RADIX))
    row = iota((DIGITS, width), 0)
    chosen = jnp.where(row == high_digit, 1.0, 0.0).astype(BF16)
    step = row - (base - RADIX * high_digit)
    spread = jnp.where(step == 3.0, weights[3], 0.0)
    for r in (2, 1, 0):
        spread = jnp.where(step == float(r), weights[r], spread)
    high, low = split(spread)
    for section, value in enumerate((chosen, chosen, high, high, low)):
        digits_ref[pl.ds(DIGITS * section, DIGITS), :] = value
    product = jnp.dot(factors_ref[...], digits_ref[...], preferred_element_type=F32)
    rows = product.shape[0] // 4
    cos_a, sin_a, cos_b, sin_b = (product[i * rows : (i + 1) * rows] for i in range(4))
    return cos_a * cos_b - sin_a * sin_b, sin_a * cos_b + cos_a * sin_b


def plane_weights(atoms, weights):
    row = iota((8, atoms.shape[1]), 0) - atoms[0:1]
    return sum(weights[r][3:4] * (row == float(r)).astype(F32) for r in range(4))


def swap(value):
    return pltpu.roll(value, LANES // 2, axis=value.ndim - 1)


def half_sign():
    lane = lax.broadcasted_iota(jnp.int32, (1, LANES), 1)
    return jnp.where(lane < LANES // 2, -1.0, 1.0).astype(F32)


def rotate(value, numer, denom, sign):
    real, imag = value
    if numer == 0:
        return value
    if 4 * numer == denom:
        return (-imag, real) if sign > 0 else (imag, -real)
    angle = 2.0 * np.pi * numer / denom
    cosine, sine = float(np.cos(angle)), float(sign * np.sin(angle))
    if 8 * numer in (denom, 3 * denom):
        size = abs(cosine)
        cos_sign, sin_sign = (1 if cosine > 0 else -1), (1 if sine > 0 else -1)
        if cos_sign == sin_sign:
            return ((real - imag) * (cos_sign * size), (real + imag) * (cos_sign * size))
        return ((real + imag) * (cos_sign * size), (imag - real) * (cos_sign * size))
    return real * cosine - imag * sine, imag * cosine + real * sine


def butterfly(even, turned):
    plus = (even[0] + turned[0], even[1] + turned[1])
    return plus, (even[0] - turned[0], even[1] - turned[1])


def transform(values, sign):
    count = len(values)
    if count == 1:
        return values
    even = transform(values[0::2], sign)
    odd = transform(values[1::2], sign)
    both = [butterfly(even[k], rotate(odd[k], k, count, sign)) for k in range(count // 2)]
    return [pair[0] for pair in both] + [pair[1] for pair in both]


def regroup(low, high):
    first = lax.broadcasted_iota(jnp.int32, low.shape, 1) < LANES // 2
    crossed = swap(jnp.where(first, high, low))
    return jnp.where(first, low, crossed), jnp.where(first, crossed, high)


def pack_kernel(counts_ref, cells_ref, offsets_ref, charges_ref, out_ref):
    width = offsets_ref.shape[1]
    alive = lax.broadcasted_iota(jnp.int32, (1, width), 1) < counts_ref[0]
    atoms = jnp.concatenate(
        [
            lax.bitwise_and(cells_ref[0:1, :], XD - 1).astype(F32),
            cells_ref[1:3, :].astype(F32),
            offsets_ref[...],
            jnp.where(alive, charges_ref[...], 0.0),
            jnp.full((1, width), counts_ref[0].astype(F32)),
        ],
        0,
    )
    for copy in range(out_ref.shape[0]):
        out_ref[copy] = atoms


def atoms_of(same_ref, other_ref, slab, slot, doms):
    half = doms // 2
    return (same_ref, other_ref)[slot // half][slab * half + slot % half]


def forward_kernel(
    place_ref,
    live_ref,
    same_ref,
    other_ref,
    factors_y,
    factors_z,
    plus_ref,
    minus_ref,
    table_y,
    table_z,
    left_ref,
    right_ref,
    grid_ref,
    atoms_ref,
    digits_y,
    digits_z,
):
    step = pl.program_id(0)
    cells_x = grid_ref.shape[0]
    rows = grid_ref.shape[1] // 2
    ky_local = rows - 8
    half_slot = same_ref.shape[2] // 2
    doms = table_y.shape[2] // (2 * half_slot)
    kept = step - place_ref[2]
    kept = jnp.where((kept >= 0) & (kept < table_y.shape[0] - 1), kept, table_y.shape[0] - 1)

    @pl.when(step == 0)
    def _():
        grid_ref[...] = jnp.zeros_like(grid_ref)
        digits_y[...] = jnp.zeros_like(digits_y)
        digits_z[...] = jnp.zeros_like(digits_z)

    for slot in range(doms):
        atoms_ref[slot] = atoms_of(same_ref, other_ref, step, slot, doms)

    def build_tile(tile, halves):
        atoms = jnp.concatenate([atoms_ref[slot, :, pl.ds(part * half_slot, half_slot)] for slot, part, _ in halves], 1)
        counted = jnp.concatenate([jnp.full((1, half_slot), weight) for _, _, weight in halves], 1)
        weights = spline(atoms)
        along_x = plane_weights(atoms, weights) * (atoms[6:7] * counted)
        waves_z = atom_waves(atoms[2:3], [w[5:6] for w in weights], factors_z, digits_z.at[tile])
        waves_z = jnp.concatenate(waves_z, 0)
        waves_y = atom_waves(atoms[1:2], [w[4:5] for w in weights], factors_y, digits_y.at[tile])
        waves_y = jnp.concatenate(waves_y, 0)
        for number, (slot, part, _) in enumerate(halves):
            lanes = slice(number * half_slot, (number + 1) * half_slot)
            start = pl.multiple_of((2 * slot + part) * half_slot, half_slot)
            table_z[kept, :, pl.ds(start, half_slot)] = waves_z[:, lanes]
            table_y[kept, :, pl.ds(start, half_slot)] = waves_y[:, lanes]
        high, low = split(waves_z)
        lanes = pl.ds(2 * half_slot * tile, 2 * half_slot)
        right_ref[pl.ds(0, LANES), lanes] = high
        right_ref[pl.ds(LANES, LANES), lanes] = low
        for plane in range(SPAN):
            first = 4 * rows * plane
            high, low = split(waves_y * along_x[plane : plane + 1])
            left_ref[pl.ds(first, 2 * rows), lanes] = high
            left_ref[pl.ds(first + 2 * rows, 2 * rows), lanes] = low

    def add_tiles(count):
        lanes = pl.ds(0, 2 * half_slot * count)
        product = lax.dot_general(
            left_ref[:, lanes], right_ref[:, lanes], (((1,), (1,)), ((), ())), preferred_element_type=F32
        )
        for plane in range(SPAN):
            first = 4 * rows * plane
            high, low = product[first : first + 2 * rows], product[first + 2 * rows : first + 4 * rows]
            at = lax.rem(step * XD + plane, cells_x)
            grid_ref[at] += (high[:, :LANES] + high[:, LANES:]) + (low[:, :LANES] + low[:, LANES:])

    slabs, pairs = cells_x // XD, doms // 2
    reach = [live_ref[(slot // pairs * slabs + step) * pairs + slot % pairs] for slot in range(doms)]
    reach = [sum(reach[: slot + 1]) for slot in range(doms)]
    for extra in range(doms // 2 + 1):

        @pl.when((reach[-1] + 1) // 2 == extra)
        def _(extra=extra):
            for tile in range(doms // 2):
                build_tile(tile, [(2 * tile, 0, 1.0), (2 * tile + 1, 0, 1.0)])
            for tile in range(extra):
                chosen = []
                for place in (2 * tile, 2 * tile + 1):
                    slot = sum((total <= place).astype(jnp.int32) for total in reach)
                    weight = jnp.where(slot < doms, 1.0, 0.0).astype(F32)
                    chosen.append((jnp.minimum(slot, doms - 1), 1, weight))
                build_tile(doms // 2 + tile, chosen)
            add_tiles(doms // 2 + extra)

    @pl.when(step == pl.num_programs(0) - 1)
    def _():
        quarter_rows = ky_local // 2
        group = min(8, quarter_rows)
        for minus, out_ref in enumerate((plus_ref, minus_ref)):
            for start in range(0, quarter_rows, group):
                values = []
                for x in range(cells_x):
                    parts = [
                        grid_ref[x, pl.ds(minus + start + offset, group), :]
                        for offset in (0, quarter_rows, rows, rows + quarter_rows)
                    ]
                    cos_cos, cos_sin = regroup(parts[0], parts[1])
                    sin_cos, sin_sin = regroup(parts[2], parts[3])
                    if minus:
                        values.append((cos_cos + sin_sin, sin_cos - cos_sin))
                    else:
                        values.append((cos_cos - sin_sin, -cos_sin - sin_cos))
                for x, value in enumerate(transform(values, -1)):
                    for part in (0, 1):
                        out_ref[part, x, pl.ds(start, group), :] = value[part]


def inverse_x_kernel(place_ref, spectrum_ref, green_ref, *refs):
    *outs, near_ref = refs
    cells_x, quarter_rows = spectrum_ref.shape[1:3]
    group = min(8, quarter_rows)
    side = 1.0 - 2.0 * place_ref[3].astype(F32)

    def rows_of(step, carry):
        rows = pl.ds(pl.multiple_of(step * group, group), group)
        values = []
        for kx in range(cells_x):
            green = green_ref[kx, rows, :]
            values.append(tuple(spectrum_ref[part, kx, rows, :] * green for part in (0, 1)))
        even = transform(values[0::2], 1)
        odd = transform([(value[0] * side, value[1] * side) for value in values[1::2]], 1)
        for x in range(cells_x // 2):
            here, there = butterfly(even[x], rotate(odd[x], x, cells_x, 1))
            wanted = [(x, here)] + ([(cells_x // 2 + x, there)] if x < 3 else [])
            for plane, value in wanted:
                for part, row_group in enumerate(regroup(value[0], value[1])):
                    near_ref[plane, part, rows, :] = row_group
        return carry

    lax.fori_loop(0, quarter_rows // group, rows_of, 0)
    for k, out_ref in enumerate(outs):
        out_ref[...] = near_ref[pl.ds(lax.bitwise_xor(place_ref[4], k) * XD, XD)]


def inverse_y_kernel(sources, place_ref, *refs):
    ins, (high_ref, low_ref) = refs[: 2 * sources], refs[2 * sources : 2 * sources + 2]
    outs, (plus_ref, minus_ref, turned_ref) = refs[2 * sources + 2 : -3], refs[-3:]
    waves = NY // 2
    halves = half_sign()
    minus_ref[:, pl.ds(0, 8), :] = jnp.zeros((XD, 8, LANES), F32)
    for number, in_ref in enumerate(ins):
        count = in_ref.shape[1]
        start = lax.bitwise_xor(place_ref[4], sources - 1 - number % sources) * count
        if number < sources:
            plus_ref[:, pl.ds(pl.multiple_of(start, 8), count), :] = in_ref[...]
        else:
            minus_ref[:, pl.ds(pl.multiple_of(start + 8, 8), count), :] = in_ref[...]
    sums = []
    for parity in (0, 1):
        parts = []
        for x in range(XD):
            plus = plus_ref[x, pl.ds(parity, waves // 2, stride=2), :]
            minus = minus_ref[x, pl.ds(7 + parity, waves // 2, stride=2), :]
            parts.append(split(jnp.concatenate([plus + minus, swap(plus - minus) * halves], 0)))
        high, low = (jnp.concatenate([part[i] for part in parts], 1) for i in (0, 1))
        left = jnp.concatenate([high_ref[parity], high_ref[parity], low_ref[parity]], 1)
        total = jnp.dot(left, jnp.concatenate([high, low, high], 0), preferred_element_type=F32)
        sums.append([total[:, x * LANES : (x + 1) * LANES] for x in range(XD)])
    row = lax.broadcasted_iota(jnp.int32, (waves, 1), 0)
    alternate = jnp.where(row % 2 == 0, 1.0, -1.0)
    sign = jnp.where(place_ref[3] == 1, alternate, 1.0)
    for x in range(XD):
        last = minus_ref[x, pl.ds(waves, 8), :][7:8]
        even, odd = sums[0][x] + alternate * last, sums[1][x]
        total = jnp.concatenate([(even + odd) * sign, (even - odd) * sign], 0)
        turned_ref[:, x] = total.reshape(len(outs), -1, LANES)
    for k in range(len(outs)):
        outs[k][...] = turned_ref[lax.bitwise_xor(place_ref[5], k)]


def inverse_z_kernel(distances, place_ref, *refs):
    count = len(distances)
    ins, (high_ref, low_ref), (*total_refs, out_ref) = refs[:count], refs[count : count + 2], refs[count + 2 :]
    planes, rows, depth = out_ref.shape
    span = pl.ds(pl.program_id(0) * planes, planes)
    lines, tables = [], []
    for in_ref, distance in zip(ins, distances):
        lines.append(in_ref[span].reshape(planes * rows, LANES))
        start = pl.multiple_of(lax.bitwise_xor(place_ref[5], distance) * LANES, LANES)
        tables.append((high_ref[pl.ds(start, LANES), :], low_ref[pl.ds(start, LANES), :]))
    high, low = split(jnp.concatenate(lines, 1))
    table_high, table_low = (jnp.concatenate([pair[part] for pair in tables], 0) for part in (0, 1))
    left, right = jnp.concatenate([high, low, high], 1), jnp.concatenate([table_high, table_high, table_low], 0)
    total = jnp.dot(left, right, preferred_element_type=F32).reshape(planes, rows, depth)
    for total_ref in total_refs:
        total += total_ref[span]
    out_ref[...] = total


def gather_kernel(first, place_ref, same_ref, other_ref, table_y, table_z, plus_ref, minus_ref, *refs):
    *earlier, out_ref, shift_ref, fields_ref, stack_ref = refs
    step = pl.program_id(0)
    half = LANES // 2
    rows = table_y.shape[1] // 2
    ky_local = rows - 8
    width = same_ref.shape[2]
    doms = table_y.shape[2] // width
    planes = fields_ref.shape[0]
    halves = half_sign()

    @pl.when(step == 0)
    def _():
        for earlier_ref in earlier:
            out_ref[pl.ds(0, first * doms)] = earlier_ref[...]
        stack_ref[...] = jnp.zeros_like(stack_ref)
        shift_ref[...] = jnp.zeros_like(shift_ref)
        row = lax.broadcasted_iota(jnp.int32, (8, LANES), 0)

        def build(x, carry):
            plus = plus_ref[first * XD + x]
            shift_ref[pl.ds(1, ky_local), :] = minus_ref[first * XD + x]
            minus = shift_ref[pl.ds(0, ky_local), :]
            last = shift_ref[pl.ds(ky_local, 8), :][0:1]
            main = [plus + minus, swap(plus - minus) * halves]
            if 2 * ky_local < LANES:
                main.append(jnp.zeros((LANES - 2 * ky_local, LANES), F32))
            rest = jnp.where(row % 2 == 0, last, -swap(jnp.broadcast_to(last, (8, LANES))) * halves)
            rest = jnp.where(row < 6, rest, 0.0)
            rest_high = rest.astype(BF16).astype(F32)
            rest = jnp.where((row == 2) | (row == 3), rest - rest_high, rest_high)
            high, low = split(jnp.concatenate(main, 0).T)
            fields_ref[x, :, pl.ds(0, LANES)] = high
            fields_ref[x, :, pl.ds(LANES, LANES)] = low
            fields_ref[x, :, pl.ds(2 * LANES, LANES)] = high
            rest = jnp.concatenate([rest, jnp.zeros((LANES - 8, LANES), F32)], 0)
            fields_ref[x, :, pl.ds(3 * LANES, LANES)] = rest.T.astype(BF16)
            return carry

        lax.fori_loop(0, planes, build, 0)

    first_z = place_ref[1].astype(F32)
    twice = jnp.where(first_z + iota((half, 1), 0) == 0.0, 1.0, 2.0)
    fields = fields_ref[pl.ds(step * XD, SPAN)].reshape(SPAN * LANES, 4 * LANES)
    for slot in range(doms):
        lanes = pl.ds(slot * width, width)
        cosine = table_y[first + step, pl.ds(0, ky_local), lanes]
        sine = table_y[first + step, pl.ds(rows, ky_local), lanes]
        high, low = split(jnp.concatenate([cosine, sine], 0))
        for part, value in enumerate((high, high, low)):
            stack_ref[pl.ds(LANES * part, 2 * ky_local), lanes] = value
        cosine = table_y[first + step, pl.ds(ky_local, 8), lanes][0:1]
        sine = table_y[first + step, pl.ds(rows + ky_local, 8), lanes][0:1]
        row = lax.broadcasted_iota(jnp.int32, (16, width), 0)
        rest = jnp.where(row % 2 == 0, cosine, sine)
        rest_high = rest.astype(BF16).astype(F32)
        rest = jnp.where(row < 4, rest_high, jnp.where(row < 6, rest - rest_high, 0.0))
        stack_ref[pl.ds(3 * LANES, 16), lanes] = rest.astype(BF16)
    product = jnp.dot(fields, stack_ref[...], preferred_element_type=F32)
    for slot in range(doms):
        atoms = atoms_of(same_ref, other_ref, place_ref[2] + first + step, slot, doms)
        along_x = plane_weights(atoms, spline(atoms))
        lanes = pl.ds(slot * width, width)
        field = product[:, slot * width : (slot + 1) * width]
        total = along_x[0:1] * field[:LANES]
        for plane in range(1, SPAN):
            total += along_x[plane : plane + 1] * field[plane * LANES : (plane + 1) * LANES]
        waves = total * table_z[first + step, :, lanes]
        sampled = jnp.sum((waves[:half] - waves[half:]) * twice, axis=0, keepdims=True)
        core = place_ref[5] % 2 if slot < doms // 2 else 1 - place_ref[5] % 2
        out_ref[(first + step) * doms + 2 * (slot % (doms // 2)) + core] = sampled


def bf16_pair(table):
    high = table.astype(ml_dtypes.bfloat16)
    low = (table - high.astype(np.float64)).astype(ml_dtypes.bfloat16)
    return jnp.asarray(high), jnp.asarray(low)


def inverse_y_table():
    tables = []
    for parity in (0, 1):
        waves = np.arange(parity, NY // 2, 2)
        angle = 2.0 * np.pi * (np.outer(np.arange(NY // 2), waves) % NY) / NY
        tables.append(np.concatenate([np.cos(angle), np.sin(angle)], 1))
    return bf16_pair(np.stack(tables))


def inverse_z_table(dom_count):
    kz = np.arange(KH)
    angle = 2.0 * np.pi * (np.outer(kz, np.arange(NZ)) % NZ) / NZ
    weight = np.where(kz == 0, 1.0, 2.0)[:, None]
    parts = [weight * np.cos(angle), -weight * np.sin(angle)]
    return bf16_pair(
        np.stack([p.reshape(dom_count, KH // dom_count, NZ) for p in parts], 1).reshape(2 * KH, NZ)
    )


def whole_spec(shape):
    return pl.BlockSpec(shape, lambda *_: (0,) * len(shape))


SMALL = pl.CostEstimate(flops=10**6, bytes_accessed=10**4, transcendentals=0)
SMEM = pl.BlockSpec(memory_space=pltpu.SMEM)


def params(mib):
    return pltpu.CompilerParams(vmem_limit_bytes=mib * MIB)


def swapped(value, axis, distance):
    if distance == 0:
        return value
    return lax.ppermute(value, axis, [(i, i ^ distance) for i in range(lax.axis_size(axis))])


def per_device(base_cells, offsets, charges, bias_coupling, counts, green):
    slabs = lax.axis_size("slab")
    doms = lax.axis_size("dom")
    slab = lax.axis_index("slab")
    dom = lax.axis_index("dom")
    atoms_local = charges.shape[0]
    cells_x = XD * slabs
    ky_local = NY // slabs
    kz_local = KH // doms
    slab_half = slabs // 2
    rows_local = NY // doms
    rows = ky_local + 8
    quarter_rows = ky_local // 2
    normalize = 1.0 / (cells_x * NY * NZ)
    upper = slab // slab_half
    place = jnp.stack(
        [slab * ky_local, dom * kz_local, upper * slab_half, upper, slab % slab_half, dom]
    ).astype(jnp.int32)

    vmem = pl.BlockSpec(memory_space=pltpu.VMEM)
    atoms = pl.pallas_call(
        pack_kernel,
        in_specs=[SMEM, vmem, vmem, vmem],
        out_specs=vmem,
        out_shape=jax.ShapeDtypeStruct((slabs * doms // 2, 8, atoms_local), F32),
        name="pack",
    )(counts, base_cells, offsets, charges.reshape(1, atoms_local))
    factors_y, factors_z = pl.pallas_call(
        wave_kernel,
        in_specs=[SMEM],
        out_specs=[vmem] * 2,
        out_shape=[jax.ShapeDtypeStruct((4 * count, TERMS), BF16) for count in (rows, LANES // 2)],
        compiler_params=params(8),
        name="waves",
    )(place)
    everyone = list(range(slabs * doms))
    same = lax.all_to_all(
        atoms, ("slab", "dom"), 0, 0, axis_index_groups=[everyone[0::2], everyone[1::2]], tiled=True
    )

    def halves_beside(value):
        return jnp.concatenate([value[:, :quarter_rows], value[:, quarter_rows:]], 2) * normalize

    own = halves_beside(green)
    same, own, flipped, factors_y, factors_z = lax.optimization_barrier(
        (same, own, halves_beside(green[:, ::-1]), factors_y, factors_z)
    )
    other = swapped(same, "dom", 1)
    mirrored = lax.ppermute(flipped, "slab", [(s, slabs - 1 - s) for s in range(slabs)])

    live = jnp.concatenate([same[:, 7, 0], other[:, 7, 0]])
    live = (live > atoms_local // 2).astype(jnp.int32)
    atoms_slab = doms * atoms_local
    table_bytes = 4 * (slab_half + 1) * (2 * rows + LANES) * atoms_slab
    spectrum_bytes = 16 * cells_x * max(8, quarter_rows) * LANES
    plus, minus, table_y, table_z = pl.pallas_call(
        forward_kernel,
        grid=(slabs,),
        in_specs=[SMEM] * 2 + [vmem] * 4,
        out_specs=[vmem] * 4,
        out_shape=[
            jax.ShapeDtypeStruct((2, cells_x, quarter_rows, LANES), F32),
            jax.ShapeDtypeStruct((2, cells_x, quarter_rows, LANES), F32),
            jax.ShapeDtypeStruct((slab_half + 1, 2 * rows, atoms_slab), F32),
            jax.ShapeDtypeStruct((slab_half + 1, LANES, atoms_slab), F32),
        ],
        scratch_shapes=[
            pltpu.VMEM((SPAN * 4 * rows, atoms_slab), BF16),
            pltpu.VMEM((2 * LANES, atoms_slab), BF16),
            pltpu.VMEM((cells_x, 2 * rows, LANES), F32),
            pltpu.VMEM((doms, 8, atoms_local), F32),
            pltpu.VMEM((doms, TERMS, atoms_local), BF16),
            pltpu.VMEM((doms, TERMS, atoms_local), BF16),
        ],
        compiler_params=params(16 + (table_bytes + spectrum_bytes) // MIB),
        cost_estimate=SMALL,
        name="forward",
    )(place, live, same, other, factors_y, factors_z)

    near_planes = cells_x // 2 + 3
    lines, near = [], []
    for spectrum, influence in ((plus, own), (minus, mirrored)):
        *pieces, planes = pl.pallas_call(
            inverse_x_kernel,
            in_specs=[SMEM] + [vmem] * 2,
            out_specs=[vmem] * (slab_half + 1),
            out_shape=[jax.ShapeDtypeStruct((XD, 2, quarter_rows, LANES), F32)] * slab_half
            + [jax.ShapeDtypeStruct((near_planes, 2, quarter_rows, LANES), F32)],
            compiler_params=params(24),
            cost_estimate=SMALL,
            name="inverse_x",
        )(place, spectrum, influence)
        near.append(planes.reshape(near_planes, ky_local, LANES))
        lines += [swapped(value.reshape(XD, ky_local, LANES), "slab", k) for k, value in enumerate(pieces)][::-1]

    steps = slab_half // GATHERS

    def gather(part, place, *earlier):
        return pl.pallas_call(
            functools.partial(gather_kernel, part * steps),
            grid=(steps,),
            in_specs=[SMEM] + [vmem] * (6 + len(earlier)),
            out_specs=vmem,
            out_shape=jax.ShapeDtypeStruct(((part + 1) * steps * doms, 1, atoms_local), F32),
            scratch_shapes=[
                pltpu.VMEM((rows, LANES), F32),
                pltpu.VMEM((steps * XD + 3, LANES, 4 * LANES), BF16),
                pltpu.VMEM((4 * LANES, atoms_slab), BF16),
            ],
            compiler_params=params(12 + (table_bytes + 8 * near_planes * LANES * LANES) // MIB),
            cost_estimate=SMALL,
            name="gather",
        )(place, same, other, table_y, table_z, *near, *earlier)

    partial, *lines = lax.optimization_barrier((gather(0, place), *lines))

    high_y, low_y = inverse_y_table()
    high_z, low_z = inverse_z_table(doms)

    turned = pl.pallas_call(
        functools.partial(inverse_y_kernel, slab_half),
        in_specs=[SMEM] + [vmem] * (2 * slab_half + 2),
        out_specs=[vmem] * doms,
        out_shape=[jax.ShapeDtypeStruct((XD, rows_local, LANES), F32)] * doms,
        scratch_shapes=[
            pltpu.VMEM((XD, NY // 2, LANES), F32),
            pltpu.VMEM((XD, NY // 2 + 8, LANES), F32),
            pltpu.VMEM((doms, XD, rows_local, LANES), F32),
        ],
        compiler_params=params(32),
        cost_estimate=SMALL,
        name="inverse_y",
    )(place, *lines, high_y, low_y)
    columns = [swapped(value, "dom", k) for k, value in enumerate(turned)]

    columns[1], late_place = lax.optimization_barrier((columns[1], place))
    for part in range(1, GATHERS):
        partial = gather(part, late_place, partial)
    partial, columns[0] = lax.optimization_barrier((partial, columns[0]))
    members = slab_half * doms
    sampled = lax.all_to_all(
        partial.reshape(members, atoms_local),
        ("slab", "dom"),
        0,
        0,
        axis_index_groups=[list(range(members)), list(range(members, 2 * members))],
        tiled=True,
    )
    alive = jnp.arange(atoms_local, dtype=jnp.int32) < counts[0]
    gradient = jnp.where(alive, bias_coupling * jnp.sum(sampled, 0), 0.0)

    total = []
    for distances in (range(doms // 2), range(doms - 1, doms // 2 - 1, -1)):
        last = len(total) == 1
        total = [
            pl.pallas_call(
                functools.partial(inverse_z_kernel, distances),
                grid=(XD // DEPTH if last else 1,),
                in_specs=[SMEM] + [vmem] * (len(distances) + 2 + len(total)),
                out_specs=pl.BlockSpec((DEPTH, rows_local, NZ), lambda step: (step, 0, 0)) if last else vmem,
                out_shape=jax.ShapeDtypeStruct((XD, rows_local, NZ), F32),
                compiler_params=params(24),
                cost_estimate=SMALL,
                name="inverse_z",
            )(place, *[columns[k] for k in distances], high_z, low_z, *total)
        ]
    potential = total[0]
    return (potential, gradient)


def solution(mesh):
    placed = (
        P(None, ("slab", "dom")),
        P(None, ("slab", "dom")),
        P(("slab", "dom")),
        P(("slab", "dom")),
        P(("slab", "dom")),
        P(None, "slab", "dom"),
    )
    return jax.shard_map(
        per_device,
        mesh=mesh,
        in_specs=placed,
        out_specs=(P("slab", "dom", None), P(("slab", "dom"))),
        check_vma=False,
    )
```
